32 devices in a mesh: rep: 2 (over core), wide: 4 (over z), narrow: 4 (over y, x).
Axes of the slice: x: 2, y: 2, z: 4, core: 2. Of those that a mesh axis runs over, the one named last changes fastest.
Arguments:
- byte_ids: int32 [64, 1152], P(('rep', 'wide', 'narrow')), may hold values from 0 to 255
- live_mask: int32 [64, 1152], P(('rep', 'wide', 'narrow')), may hold values from 0 to 1, as said below
- tables: float32 [2, 256, 512], P(None, ('wide', 'narrow')), may hold values from -6 to 6
- attention: float32 [2, 512, 2048], P(None, ('wide', 'narrow')), may hold values from -0.25 to 0.25
- feed_forward: float32 [2, 512, 4096], P(None, ('wide', 'narrow')), may hold values from -0.25 to 0.25
- vectors: float32 [21, 512], P(None, ('wide', 'narrow'))
- moment_tables: float32 [2, 2, 256, 512], P('rep', None, ('wide', 'narrow')), may hold values from -4.7683716e-06 to 4.7683716e-06
- moment_attention: float32 [2, 2, 512, 2048], P('rep', None, ('wide', 'narrow')), may hold values from -4.7683716e-06 to 4.7683716e-06
- moment_feed: float32 [2, 2, 512, 4096], P('rep', None, ('wide', 'narrow')), may hold values from -4.7683716e-06 to 4.7683716e-06
- moment_vectors: float32 [2, 21, 512], P('rep', None, ('wide', 'narrow')), may hold values from -1.5258789e-05 to 1.5258789e-05
- square_tables: float32 [2, 2, 256, 512], P('rep', None, ('wide', 'narrow')), may hold values from 3.1990972e-12 to 1.2796389e-11
- square_attention: float32 [2, 2, 512, 2048], P('rep', None, ('wide', 'narrow')), may hold values from 3.1990972e-12 to 1.2796389e-11
- square_feed: float32 [2, 2, 512, 4096], P('rep', None, ('wide', 'narrow')), may hold values from 3.1990972e-12 to 1.2796389e-11
- square_vectors: float32 [2, 21, 512], P('rep', None, ('wide', 'narrow')), may hold values from 2.8944213e-11 to 1.1577685e-10
- outer_tables: float32 [2, 256, 512], P(None, ('wide', 'narrow')), may hold values from -0.0625 to 0.0625
- outer_attention: float32 [2, 512, 2048], P(None, ('wide', 'narrow')), may hold values from -0.0625 to 0.0625
- outer_feed: float32 [2, 512, 4096], P(None, ('wide', 'narrow')), may hold values from -0.0625 to 0.0625
- outer_vectors: float32 [21, 512], P(None, ('wide', 'narrow')), may hold values from -0.0625 to 0.0625
- average_tables: float32 [2, 256, 512], P(None, ('wide', 'narrow')), may hold values from -6 to 6
- average_attention: float32 [2, 512, 2048], P(None, ('wide', 'narrow')), may hold values from -0.25 to 0.25
- average_feed: float32 [2, 512, 4096], P(None, ('wide', 'narrow')), may hold values from -0.25 to 0.25
- average_vectors: float32 [21, 512], P(None, ('wide', 'narrow'))
Outputs:
- loss_bits: float32 [2], P('rep')
- token_count: float32 [2], P('rep')
- gradient_norm: float32 [2], P('rep')
- new_moment_tables: float32 [2, 2, 256, 512], P('rep', None, ('wide', 'narrow'))
- new_moment_attention: float32 [2, 2, 512, 2048], P('rep', None, ('wide', 'narrow'))
- new_moment_feed: float32 [2, 2, 512, 4096], P('rep', None, ('wide', 'narrow'))
- new_moment_vectors: float32 [2, 21, 512], P('rep', None, ('wide', 'narrow'))
- new_square_tables: float32 [2, 2, 256, 512], P('rep', None, ('wide', 'narrow'))
- new_square_attention: float32 [2, 2, 512, 2048], P('rep', None, ('wide', 'narrow'))
- new_square_feed: float32 [2, 2, 512, 4096], P('rep', None, ('wide', 'narrow'))
- new_square_vectors: float32 [2, 21, 512], P('rep', None, ('wide', 'narrow'))
- new_tables: float32 [2, 256, 512], P(None, ('wide', 'narrow'))
- new_attention: float32 [2, 512, 2048], P(None, ('wide', 'narrow'))
- new_feed: float32 [2, 512, 4096], P(None, ('wide', 'narrow'))
- new_vectors: float32 [21, 512], P(None, ('wide', 'narrow'))
- new_outer_tables: float32 [2, 256, 512], P(None, ('wide', 'narrow'))
- new_outer_attention: float32 [2, 512, 2048], P(None, ('wide', 'narrow'))
- new_outer_feed: float32 [2, 512, 4096], P(None, ('wide', 'narrow'))
- new_outer_vectors: float32 [21, 512], P(None, ('wide', 'narrow'))
- new_average_tables: float32 [2, 256, 512], P(None, ('wide', 'narrow'))
- new_average_attention: float32 [2, 512, 2048], P(None, ('wide', 'narrow'))
- new_average_feed: float32 [2, 512, 4096], P(None, ('wide', 'narrow'))
- new_average_vectors: float32 [21, 512], P(None, ('wide', 'narrow'))
The draws below stay inside these ranges and needn't reach their ends.
Inputs may be any that keep to these rules, and one draw needn't show every extreme that they name: `live_mask`: each row is live (1) on a prefix of 2 or more positions and 0 after it; within one device's rows, those of even index hold at most 1152 live positions and those of odd index at most 288; the first row of the last device is live on all 1152 positions.
All inputs are finite; a program needn't handle non-finite values.
Results may differ from the reference program's by a relative error of at most 0.0078.
Values may be sent and summed in bfloat16 or wider, within the bound.
A program may use at most 704 MiB of HBM per device.

```python
import math
import jax
import jax.numpy as jnp
import numpy as np
from jax import lax

D = 512
HEADS = 8
HD = 64
FF = 2048
V = 256
NB = 32
SEQ = 1152
ROWS_DEV = 2
STEP = 10
ROWS = 64
REPS = 2
WIDE_DEVS = 4
NARROW_DEVS = 4
VEC = 21
PARAMS = 6564352
N_REP = 2


def vector_rows(key, spread):
    keys = jax.random.split(key, 3)
    row = jnp.arange(VEC, dtype=jnp.int32)[:, None]
    column_index = jnp.arange(D, dtype=jnp.int32)[None, :]
    column = column_index.astype(jnp.float32) / D
    gains = (0.6 + 0.8 * column) * jax.random.uniform(keys[0], (VEC, D), jnp.float32, 0.8, 1.2)
    shifts = 0.1 * jax.random.normal(keys[1], (VEC, D), jnp.float32)
    table_start = 12 + 2 * FF // D
    bucket = ((row - table_start) * D + column_index) % NB
    far_lift = jnp.where(bucket >= 24, 2.0, 0.0)
    tables_rel = spread * jax.random.normal(keys[2], (VEC, D), jnp.float32) + far_lift
    is_gain = (row == 0) | (row == 2) | (row == 4) | (row == 7) | (row == 9)
    is_table = row >= table_start
    return jnp.where(is_gain, gains, jnp.where(is_table, tables_rel, shifts))


def draw_vectors(key, part):
    key = jax.random.fold_in(key, 11)
    return vector_rows(key, 0.5)


def draw_average_vectors(key, part):
    key = jax.random.fold_in(key, 12)
    return vector_rows(key, 0.5)


def draw_byte_ids(key, part):
    key = jax.random.fold_in(key, 5)
    keys = jax.random.split(key, 2)
    places = jnp.arange(SEQ, dtype=jnp.int32)
    block = places * 4 // SEQ
    offsets = jax.random.randint(keys[0], (ROWS, 4), 0, V)
    inner = jax.random.randint(keys[1], (ROWS, SEQ), 0, 48)
    block_hot = (block[:, None] == jnp.arange(4, dtype=jnp.int32)[None, :]).astype(jnp.int32)
    chosen = jnp.sum(offsets[:, None, :] * block_hot[None, :, :], -1)
    ids = (chosen + inner) % V
    ids = ids.at[0, 0].set(V - 1).at[0, 1].set(0)
    return ids.astype(jnp.int32)


def draw_live_mask(key, part):
    key = jax.random.fold_in(key, 3)
    row_index = jnp.arange(ROWS, dtype=jnp.int32)
    device = row_index // ROWS_DEV
    narrow_at = device % NARROW_DEVS
    wide_at = device // NARROW_DEVS % WIDE_DEVS
    rep_at = device // (NARROW_DEVS * WIDE_DEVS)
    upper = jnp.where(row_index % ROWS_DEV % 2 == 0, SEQ, SEQ // 4)
    numer = (NARROW_DEVS - 1 + 2 * narrow_at) * (WIDE_DEVS - 1 + 2 * wide_at) * (1 + rep_at)
    denom = 9 * max(NARROW_DEVS - 1, 1) * max(WIDE_DEVS - 1, 1) * REPS
    planned = upper * numer // denom
    jitter = jax.random.randint(key, (ROWS,), 0, max(SEQ // 4, 2))
    jitter = jnp.where(row_index == ROWS - ROWS_DEV, 0, jitter)
    length = jnp.clip(planned - jitter, 2, upper)
    places = jnp.arange(SEQ, dtype=jnp.int32)
    return (places[None, :] < length[:, None]).astype(jnp.int32)


def level_of(stream_key, extent, cuts, least, high):
    loudness = 1.0
    for axis_at, parts in cuts:
        draws = jax.random.uniform(jax.random.fold_in(jax.random.fold_in(stream_key, 6), axis_at), (parts,), jnp.float32, least / len(cuts), high / len(cuts))
        loudness = loudness * jnp.repeat(jnp.exp(draws), extent[axis_at] // parts).reshape((-1,) + (1,) * (len(extent) - 1 - axis_at))
    return loudness


def noise(stream_key, extent, scale, reach, pieces=(), kind=jnp.bfloat16):
    gain = level_of(stream_key, extent, pieces, -0.22, 0.18) if pieces else 1.0
    drawn = jax.random.normal(stream_key, extent, jnp.float32) * scale * gain
    return jnp.minimum(jnp.maximum(drawn, -reach), reach).astype(kind)


def setup_inputs(seed: int = 0) -> dict:
    streams_of = jax.random.split(jax.random.key(seed), 23)
    byte_ids = draw_byte_ids(jax.random.fold_in(streams_of[22], 71), 0)
    live_mask = draw_live_mask(jax.random.fold_in(streams_of[22], 71), 0)
    tables = noise(streams_of[2], (2, V, D), 1.0, 6.0, ((1, 16),), jnp.float32)
    attention = noise(streams_of[3], (2, D, 4 * D), D ** -0.5, 0.25, ((1, 16),), jnp.float32)
    feed_forward = noise(streams_of[4], (2, D, 2 * FF), D ** -0.5, 0.25, ((1, 16),), jnp.float32)
    vectors = draw_vectors(jax.random.fold_in(streams_of[22], 71), 0)
    moment_tables = noise(streams_of[6], (REPS, 2, V, D), (0.00222 * PARAMS ** -0.5), 4.76837158203125e-06, ((0, 2), (2, 16)), jnp.float32)
    moment_attention = noise(streams_of[7], (REPS, 2, D, 4 * D), (0.00222 * PARAMS ** -0.5), 4.76837158203125e-06, ((0, 2), (2, 16)), jnp.float32)
    moment_feed = noise(streams_of[8], (REPS, 2, D, 2 * FF), (0.00222 * PARAMS ** -0.5), 4.76837158203125e-06, ((0, 2), (2, 16)), jnp.float32)
    moment_vectors = noise(streams_of[9], (REPS, VEC, D), (0.0067 * PARAMS ** -0.5), 1.52587890625e-05, ((0, 2), (2, 16)), jnp.float32)
    square_tables = jnp.clip(jnp.exp(math.log(1.2796388948466131e-11) - 1.3862944 * jax.random.uniform(streams_of[10], (REPS, 2, V, D), jnp.float32) ** level_of(streams_of[10], (REPS, 2, V, D), ((0, 2), (2, 16)), -0.2, 0.2)), 3.1990972371165327e-12, 1.2796388948466131e-11)
    square_attention = jnp.clip(jnp.exp(math.log(1.2796388948466131e-11) - 1.3862944 * jax.random.uniform(streams_of[11], (REPS, 2, D, 4 * D), jnp.float32) ** level_of(streams_of[11], (REPS, 2, D, 4 * D), ((0, 2), (2, 16)), -0.2, 0.2)), 3.1990972371165327e-12, 1.2796388948466131e-11)
    square_feed = jnp.clip(jnp.exp(math.log(1.2796388948466131e-11) - 1.3862944 * jax.random.uniform(streams_of[12], (REPS, 2, D, 2 * FF), jnp.float32) ** level_of(streams_of[12], (REPS, 2, D, 2 * FF), ((0, 2), (2, 16)), -0.2, 0.2)), 3.1990972371165327e-12, 1.2796388948466131e-11)
    square_vectors = jnp.clip(jnp.exp(math.log(1.157768533821546e-10) - 1.3862944 * jax.random.uniform(streams_of[13], (REPS, VEC, D), jnp.float32) ** level_of(streams_of[13], (REPS, VEC, D), ((0, 2), (2, 16)), -0.2, 0.2)), 2.894421334553865e-11, 1.157768533821546e-10)
    outer_tables = noise(streams_of[14], (2, V, D), 0.01, 0.0625, ((1, 16),), jnp.float32)
    outer_attention = noise(streams_of[15], (2, D, 4 * D), 0.01, 0.0625, ((1, 16),), jnp.float32)
    outer_feed = noise(streams_of[16], (2, D, 2 * FF), 0.01, 0.0625, ((1, 16),), jnp.float32)
    outer_vectors = noise(streams_of[17], (VEC, D), 0.01, 0.0625, ((1, 16),), jnp.float32)
    average_tables = noise(streams_of[18], (2, V, D), 1.0, 6.0, ((1, 16),), jnp.float32)
    average_attention = noise(streams_of[19], (2, D, 4 * D), D ** -0.5, 0.25, ((1, 16),), jnp.float32)
    average_feed = noise(streams_of[20], (2, D, 2 * FF), D ** -0.5, 0.25, ((1, 16),), jnp.float32)
    average_vectors = draw_average_vectors(jax.random.fold_in(streams_of[22], 71), 0)
    return {"byte_ids": byte_ids, "live_mask": live_mask, "tables": tables, "attention": attention, "feed_forward": feed_forward, "vectors": vectors, "moment_tables": moment_tables, "moment_attention": moment_attention, "moment_feed": moment_feed, "moment_vectors": moment_vectors, "square_tables": square_tables, "square_attention": square_attention, "square_feed": square_feed, "square_vectors": square_vectors, "outer_tables": outer_tables, "outer_attention": outer_attention, "outer_feed": outer_feed, "outer_vectors": outer_vectors, "average_tables": average_tables, "average_attention": average_attention, "average_feed": average_feed, "average_vectors": average_vectors}


@jax.custom_vjp
def low(v):
    return lax.optimization_barrier(v.astype(jnp.bfloat16)).astype(jnp.float32)

@jax.custom_vjp
def low_back(v):
    return v

def low_keep(v):
    return (low(v), None)

def low_pass(kept, grad):
    return (grad,)

def back_keep(v):
    return (v, None)

def back_low(kept, grad):
    return (low(grad),)
low.defvjp(low_keep, low_pass)
low_back.defvjp(back_keep, back_low)
HIGH = lax.Precision.HIGHEST
EDGES = np.array([1, 2, 3, 4, 5, 6, 7, 8, 10, 12, 14, 16, 20, 24, 28, 32, 40, 48, 64, 80, 96, 128, 160, 192, 256, 320, 384, 512, 640, 768, 1024], np.int32)
NEG = -1000000000.0
EPS = 1e-05
LOG_TWO = math.log(2.0)
RATE = 0.01
RATE_TABLE = 0.2
BETA_ONE = 0.9
BETA_TWO = 0.95
ADAM_EPS = 1e-08
DECAY = 0.1
CLIP_AT = 0.02
OUTER_RATE = 0.7
OUTER_MOM = 0.9
EVAL_KEEP = 0.9

def matmul(left, right):
    return jnp.dot(left, right, precision=HIGH)

def layer_norm(x, norm_gain, norm_shift):
    centered = x - lax.optimization_barrier(jnp.mean(x, -1, keepdims=True))
    spread = lax.optimization_barrier(jnp.mean(centered * centered, -1, keepdims=True))
    return centered * lax.rsqrt(spread + EPS) * norm_gain + norm_shift

def bucket_table(length):
    places = jnp.arange(length, dtype=jnp.int32)
    index = lax.optimization_barrier(jnp.sum((places[:, None] >= jnp.asarray(EDGES)[None, :]).astype(jnp.int32), 1))
    return (index[None, :] == jnp.arange(NB, dtype=jnp.int32)[:, None]).astype(jnp.float32)

def relative(offsets_bias, length):
    places = jnp.arange(length, dtype=jnp.int32)
    distance = jnp.maximum(places[:, None] - places[None, :], 0)
    return jnp.take(offsets_bias, distance, axis=1)

def unpack(vec, level):
    first_row = 2 + 5 * level
    bias_rows = 2 * FF // D
    inner_bias = vec[12:12 + bias_rows].reshape(2, FF)[level]
    rel_table = vec[12 + bias_rows:].reshape(2, HEADS, NB)[level]
    return (vec[first_row], vec[first_row + 1], vec[first_row + 2], vec[first_row + 3], vec[first_row + 4], inner_bias, rel_table)

def layer_apply(x, is_live, attn_w, feed_w, vec, level):
    length = x.shape[0]
    gain_one, shift_one, gain_two, shift_two, bias_out, inner_bias, rel_table = unpack(vec, level)
    normed = low(layer_norm(x, gain_one, shift_one))
    mixed = low_back(low(matmul(normed, attn_w[:, :3 * D])))
    query = mixed[:, 0:D].reshape(length, HEADS, HD)
    keys = mixed[:, D:2 * D].reshape(length, HEADS, HD)
    values = mixed[:, 2 * D:3 * D].reshape(length, HEADS, HD)
    offsets_bias = matmul(rel_table, bucket_table(length))
    places = jnp.arange(length, dtype=jnp.int32)
    allowed = (places[:, None] >= places[None, :]) & (is_live[None, :] > 0)
    raw_scores = jnp.einsum('thd,shd->hts', query, keys, precision=HIGH) * HD ** (-0.5) + relative(offsets_bias, length)
    scores = jnp.where(allowed[None], low_back(raw_scores), NEG)
    weights_p = low(jax.nn.softmax(scores, axis=-1))
    attended = jnp.einsum('hts,shd->thd', weights_p, values, precision=HIGH).reshape(length, D)
    attended = low_back(low(attended))
    middle = x + low_back(matmul(attended, attn_w[:, 3 * D:]))
    second = low(layer_norm(middle, gain_two, shift_two))
    hidden_pre = low_back(matmul(second, feed_w[:, :FF]) + inner_bias)
    active = low(jax.nn.gelu(hidden_pre))
    return middle + low_back(matmul(active, feed_w[:, FF:].T) + bias_out)

def shift_pool(x):
    shifted = jnp.concatenate([jnp.zeros((2, D), x.dtype), x[:-2]], 0)
    return shifted.reshape(-1, 3, D).mean(1)

def row_bits(params, row_bytes, is_live):
    tables, attention, feed_forward, vectors = params
    symbols = jnp.arange(V, dtype=jnp.int32)
    one_hot = (row_bytes[:, None] == symbols[None, :]).astype(jnp.float32)
    start = low_back(matmul(one_hot, tables[0]))
    full_out = layer_apply(start, is_live, attention[0], feed_forward[0], vectors, 0)
    short_out = layer_apply(shift_pool(full_out), is_live[::3], attention[1], feed_forward[1], vectors, 1)
    joined = full_out + jnp.repeat(short_out, 3, axis=0)
    final = low(layer_norm(joined, vectors[0], vectors[1]))
    logits = low_back(matmul(final, tables[1].T) * D ** (-0.5))
    logsum = jax.nn.logsumexp(logits, axis=-1)
    target_hot = (jnp.roll(row_bytes, -1)[:, None] == symbols[None, :]).astype(jnp.float32)
    picked = lax.optimization_barrier(jnp.sum(logits * target_hot, -1))
    token_weight = jnp.concatenate([is_live[1:], jnp.zeros((1,), is_live.dtype)]).astype(jnp.float32)
    return jnp.sum(token_weight * (logsum - picked)) / LOG_TWO

def objective(tables, attention, feed_forward, vectors, row_ids, lives, total):
    params = (low(tables), low(attention), low(feed_forward), low(vectors))
    checked = jax.checkpoint(row_bits)

    def accumulate(carry, inputs):
        return (carry + checked(params, inputs[0], inputs[1]), None)
    bits, unused = lax.scan(accumulate, jnp.zeros((), jnp.float32), (row_ids, lives))
    return (bits / total, bits)

def adam_update(weight, moment, square, gradient, decay, rate):
    moment = BETA_ONE * moment + (1.0 - BETA_ONE) * gradient
    square = BETA_TWO * square + (1.0 - BETA_TWO) * gradient * gradient
    fixed_moment = moment / (1.0 - BETA_ONE ** STEP)
    fixed_square = square / (1.0 - BETA_TWO ** STEP)
    local = weight - rate * (fixed_moment / (jnp.sqrt(fixed_square) + ADAM_EPS) + decay * weight)
    return (moment, square, local)

def reference(byte_ids, live_mask, tables, attention, feed_forward, vectors, moment_tables, moment_attention, moment_feed, moment_vectors, square_tables, square_attention, square_feed, square_vectors, outer_tables, outer_attention, outer_feed, outer_vectors, average_tables, average_attention, average_feed, average_vectors):
    weights = (tables, attention, feed_forward, vectors)
    moments = (moment_tables, moment_attention, moment_feed, moment_vectors)
    squares = (square_tables, square_attention, square_feed, square_vectors)
    outers = (outer_tables, outer_attention, outer_feed, outer_vectors)
    averages = (average_tables, average_attention, average_feed, average_vectors)
    decays = (DECAY, DECAY, DECAY, 0.0)
    rates = (RATE_TABLE, RATE, RATE, RATE_TABLE)
    per_replica = byte_ids.shape[0] // N_REP
    new_moments = [[], [], [], []]
    new_squares = [[], [], [], []]
    deltas = [jnp.zeros_like(w) for w in weights]
    losses, counts, norms = ([], [], [])
    for replica in range(N_REP):
        row_ids = byte_ids[replica * per_replica:(replica + 1) * per_replica]
        lives = live_mask[replica * per_replica:(replica + 1) * per_replica]
        total = jnp.sum(lives[:, 1:]).astype(jnp.float32)

        def bound(tab, att, feed, vec):
            return objective(tab, att, feed, vec, row_ids, lives, total)
        value, pull, bits = jax.vjp(bound, *weights, has_aux=True)
        gradients = pull(jnp.ones_like(value))
        squared = sum((jnp.sum(g * g) for g in gradients))
        global_norm = jnp.sqrt(squared)
        clip_scale = jnp.minimum(1.0, CLIP_AT / (global_norm + 1e-06))
        for index in range(4):
            moment, square, local = adam_update(weights[index], moments[index][replica], squares[index][replica], gradients[index] * clip_scale, decays[index], rates[index])
            new_moments[index].append(moment)
            new_squares[index].append(square)
            deltas[index] = deltas[index] + (local - weights[index])
        losses.append(bits)
        counts.append(total)
        norms.append(global_norm)
    new_weights, new_outers, new_averages = ([], [], [])
    for index in range(4):
        delta = deltas[index] / N_REP
        outer_new = OUTER_MOM * outers[index] + delta
        weight_new = weights[index] + OUTER_RATE * (delta + OUTER_MOM * outer_new)
        new_outers.append(outer_new)
        new_weights.append(weight_new)
        new_averages.append(EVAL_KEEP * averages[index] + (1.0 - EVAL_KEEP) * weight_new)
    stacked_m = [jnp.stack(m) for m in new_moments]
    stacked_s = [jnp.stack(s) for s in new_squares]
    return (jnp.stack(losses), jnp.stack(counts), jnp.stack(norms), stacked_m[0], stacked_m[1], stacked_m[2], stacked_m[3], stacked_s[0], stacked_s[1], stacked_s[2], stacked_s[3], new_weights[0], new_weights[1], new_weights[2], new_weights[3], new_outers[0], new_outers[1], new_outers[2], new_outers[3], new_averages[0], new_averages[1], new_averages[2], new_averages[3])
```

```python
import functools
import math

import jax
import jax.numpy as jnp
import numpy as np
from jax import lax
from jax.experimental import pallas as pl
from jax.experimental.pallas import tpu as pltpu
from jax.sharding import PartitionSpec as P

D = 512
HEADS = 8
HD = 64
FF = 2048
V = 256
NB = 32
STEP = 10
VEC = 21
EDGES = (1, 2, 3, 4, 5, 6, 7, 8, 10, 12, 14, 16, 20, 24, 28, 32, 40, 48, 64, 80, 96, 128, 160, 192)
EDGES = EDGES + (256, 320, 384, 512, 640, 768, 1024)
NEG = -1000000000.0
EPS = 1e-05
LOG_TWO = math.log(2.0)
RATE = 0.01
RATE_TABLE = 0.2
BETA_ONE = 0.9
BETA_TWO = 0.95
ADAM_EPS = 1e-08
DECAY = 0.1
CLIP_AT = 0.02
OUTER_RATE = 0.7
OUTER_MOM = 0.9
EVAL_KEEP = 0.9

TILE = 128
BLK = 384
SUB = BLK // TILE
PAIRS = HEADS // 2
PW = 2 * HD
GELU_C = math.sqrt(2.0 / math.pi)
GELU_A = 0.044715

BF = jnp.bfloat16
F32 = jnp.float32
NN = (((1,), (0,)), ((), ()))
NT = (((1,), (1,)), ((), ()))
TN = (((0,), (0,)), ((), ()))


def mm(left, right, dims=NN):
    return lax.dot_general(left, right, dims, preferred_element_type=F32)


def spans(count):
    out = []
    for d in range(count):
        lo, hi = max(TILE * d - (TILE - 1), 0), TILE * d + TILE - 1
        base = sum(e <= lo for e in EDGES)
        out.append((base, [(e, k + 1) for k, e in enumerate(EDGES) if lo < e <= hi]))
    return out


def fold_matrix(count):
    rows = []
    for base, edges in spans(count):
        row = np.zeros(NB, np.float32)
        row[base] += 1
        rows.append(row)
        for _, bucket in edges:
            row = np.zeros(NB, np.float32)
            row[bucket] += 1
            row[bucket - 1] -= 1
            rows.append(row)
    return np.stack(rows)


def tile_distance(d):
    keys = lax.broadcasted_iota(jnp.int32, (TILE, TILE), 0)
    queries = lax.broadcasted_iota(jnp.int32, (TILE, TILE), 1)
    return TILE * d + queries - keys


def build_bias(rel, bias, count):
    for d, (base, edges) in enumerate(spans(count)):
        distance = tile_distance(d)

        def one_head(h, carry, d=d, base=base, edges=edges, distance=distance):
            tile = jnp.full((TILE, TILE), rel[h, base], F32)
            for edge, bucket in edges:
                tile = jnp.where(distance >= edge, rel[h, bucket], tile)
            if d == 0:
                tile = jnp.where(distance < 0, NEG, tile)
            bias[h, d] = tile
            return carry

        lax.fori_loop(0, HEADS, one_head, 0)


def fold_bias(tiles, sums, count):
    at = 0
    for d, (_, edges) in enumerate(spans(count)):
        distance = tile_distance(d)

        def one_head(h, carry, d=d, edges=edges, distance=distance, at=at):
            tile = tiles[h, d]
            sums[h, at : at + 1] = jnp.sum(tile, 0, keepdims=True)
            for n, (edge, _) in enumerate(edges):
                sums[h, at + 1 + n : at + 2 + n] = jnp.sum(
                    jnp.where(distance >= edge, tile, 0.0), 0, keepdims=True
                )
            return carry

        lax.fori_loop(0, HEADS, one_head, 0)
        at += 1 + len(edges)


def fold_rows(count):
    return sum(1 + len(edges) for _, edges in spans(count))


def norm_stats(x):
    centered = x - jnp.mean(x, -1, keepdims=True)
    rstd = lax.rsqrt(jnp.mean(centered * centered, -1, keepdims=True) + EPS)
    return centered * rstd, rstd


def norm_back(dy, xhat, rstd, gain):
    t = dy * gain
    dx = rstd * (
        t - jnp.mean(t, -1, keepdims=True) - xhat * jnp.mean(t * xhat, -1, keepdims=True)
    )
    return dx, jnp.sum(dy * xhat, 0, keepdims=True), jnp.sum(dy, 0, keepdims=True)


def gelu_pair(u):
    square = u * u
    tanh = jnp.tanh(GELU_C * u * (1.0 + GELU_A * square))
    half = 0.5 * (1.0 + tanh)
    slope = half + 0.5 * u * (1.0 - tanh * tanh) * (GELU_C + 3.0 * GELU_C * GELU_A * square)
    return u * half, slope


def split_heads(pair):
    lane = lax.broadcasted_iota(jnp.int32, pair.shape, 1)
    zero = jnp.zeros_like(pair)
    return jnp.concatenate(
        [jnp.where(lane < HD, pair, zero), jnp.where(lane >= HD, pair, zero)], 0
    )


def cell(block, kb, e, qa, nq):
    return block[kb * TILE : (kb + 1) * TILE, (e * nq + qa) * TILE : (e * nq + qa + 1) * TILE]


def softmax_step(keys, values_t, queries, bias, pair, far, diag, nq, nk, state):
    top, total, acc = state
    raw = mm(keys, queries, NT)
    scores = {}
    for e in range(2):
        for qa in range(nq):
            for kb in range(nk):
                if diag and kb > qa:
                    continue
                scores[kb, e, qa] = cell(raw, kb, e, qa, nq) + bias[2 * pair + e, far + qa - kb]
    highest = []
    for e in range(2):
        for qa in range(nq):
            column = [scores[kb, e, qa] for kb in range(nk) if (kb, e, qa) in scores]
            highest.append(jnp.max(functools.reduce(jnp.maximum, column), 0, keepdims=True))
    old_top = top[...]
    new_top = jnp.maximum(old_top, jnp.concatenate(highest, 1))
    alpha = jnp.exp(old_top - new_top)
    sums = []
    columns = []
    for e in range(2):
        for qa in range(nq):
            at = (e * nq + qa) * TILE
            ceiling = new_top[:, at : at + TILE]
            parts, adds = [], None
            for kb in range(nk):
                if (kb, e, qa) not in scores:
                    parts.append(jnp.zeros((TILE, TILE), BF))
                    continue
                p = jnp.exp(scores[kb, e, qa] - ceiling)
                adds = p if adds is None else adds + p
                parts.append(p.astype(BF))
            sums.append(jnp.sum(adds, 0, keepdims=True))
            columns.append(jnp.concatenate(parts, 0))
    top[...] = new_top
    total[...] = alpha * total[...] + jnp.concatenate(sums, 1)
    acc[...] = alpha * acc[...] + mm(values_t, jnp.concatenate(columns, 1))


def softmax_start(state):
    top, total, acc = state
    top[...] = jnp.full(top.shape, NEG, F32)
    total[...] = jnp.zeros(total.shape, F32)
    acc[...] = jnp.zeros(acc.shape, F32)


def softmax_end(state, n):
    top, total, acc = state
    scaled = acc[...] / total[...]
    out = jnp.concatenate([scaled[:HD, :n], scaled[HD:, n:]], 0).astype(BF)
    return out, top[...] + jnp.log(total[...])


def score_back(keys, values, queries, grads, logsum, inner, bias, pair, far, diag, nq, nk, tiles):
    raw = mm(keys, queries, NT)
    d_p = mm(values, grads, NT)
    probs, scores = {}, {}
    for e in range(2):
        for diff in range(-(nk - 1), nq):
            total = None
            if diag and diff < 0:
                continue
            for kb in range(nk):
                qa = kb + diff
                if qa < 0 or qa >= nq:
                    continue
                at = (e * nq + qa) * TILE
                p = jnp.exp(
                    cell(raw, kb, e, qa, nq)
                    + bias[2 * pair + e, far + diff]
                    - logsum[:, at : at + TILE]
                )
                ds = p * (cell(d_p, kb, e, qa, nq) - inner[:, at : at + TILE])
                total = ds if total is None else total + ds
                probs[kb, e, qa] = p.astype(BF)
                scores[kb, e, qa] = ds.astype(BF)
            tiles[2 * pair + e, far + diff] += total

    def whole(parts):
        empty = jnp.zeros((TILE, TILE), BF)
        return jnp.concatenate(
            [
                jnp.concatenate([parts.get((kb, e, qa), empty) for kb in range(nk)], 0)
                for e in range(2)
                for qa in range(nq)
            ],
            1,
        )

    return whole(probs), whole(scores)


def one_hot(column):
    return column == lax.broadcasted_iota(jnp.int32, (column.shape[0], V), 1)


def full_forward_kernel(
    long_blocks,
    aux,
    embed,
    attn,
    feed,
    rows,
    beta,
    rel,
    x1_out,
    middle_out,
    q_out,
    k_out,
    v_out,
    ot_out,
    lse_out,
    act_out,
    slope_out,
    bias,
    k_all,
    vt_all,
    *state,
):
    step = pl.program_id(0)

    @pl.when(step == 0)
    def _():
        build_bias(rel, bias, bias.shape[1])

    hot = one_hot(aux[:, 0:1]).astype(BF)
    x = mm(hot, embed[...])
    xhat, _ = norm_stats(x)
    normed = (xhat * rows[0:1] + rows[1:2]).astype(BF)
    queries = (mm(normed, attn[:, :D]) * HD**-0.5).astype(BF)
    keys = mm(normed, attn[:, D : 2 * D]).astype(BF)
    values = mm(normed, attn[:, 2 * D : 3 * D]).astype(BF)
    for pair in range(PAIRS):
        cols = slice(pair * PW, (pair + 1) * PW)
        q_out[0, pair] = queries[:, cols]
        k_out[0, pair] = keys[:, cols]
        v_out[0, pair] = values[:, cols]
        k_all[step, pair] = keys[:, cols]
        vt_all[step, pair] = values[:, cols].T
    first = jnp.where(step >= long_blocks, long_blocks, 0)

    def one_pair(pair, carry):
        both = split_heads(q_out[0, pair])
        softmax_start(state)

        def earlier(j, inner):
            far = SUB * (step - j)
            softmax_step(
                k_all[j, pair], vt_all[j, pair], both, bias, pair, far, False, SUB, SUB, state
            )
            return inner

        lax.fori_loop(first, step, earlier, 0)
        softmax_step(
            k_all[step, pair], vt_all[step, pair], both, bias, pair, 0, True, SUB, SUB, state
        )
        ot_out[0, pair], lse_out[0, pair] = softmax_end(state, BLK)
        return carry

    lax.fori_loop(0, PAIRS, one_pair, 0)
    attended = ot_out[0].reshape(D, BLK).T
    middle = x + mm(attended, attn[:, 3 * D :])
    middle_out[...] = middle
    xhat, _ = norm_stats(middle)
    second = (xhat * rows[2:3] + rows[3:4]).astype(BF)
    active, slope = gelu_pair(mm(second, feed[:, :FF]) + beta[...])
    active = active.astype(BF)
    act_out[...] = active
    slope_out[...] = slope.astype(BF)
    x1_out[...] = middle + mm(active, feed[:, FF:], NT) + rows[4:5]


def whole_spec(shape):
    return pl.BlockSpec(shape, lambda i: (0,) * len(shape), pipeline_mode=pl.Buffered(1))


def params(mib, **more):
    return pltpu.CompilerParams(vmem_limit_bytes=mib * 2**20, **more)


def state_scratch(n):
    return [pltpu.VMEM((1, 2 * n), F32), pltpu.VMEM((1, 2 * n), F32), pltpu.VMEM((PW, 2 * n), F32)]


def full_forward(aux, embed, attn, feed, rows, beta, rel, long_blocks):
    tokens = aux.shape[0]
    blocks = tokens // BLK
    far = SUB * long_blocks

    def heads(n, width):
        return (
            jax.ShapeDtypeStruct((blocks, PAIRS, n, width), BF),
            pl.BlockSpec((1, PAIRS, n, width), lambda i: (i, 0, 0, 0)),
        )

    def flat(width, kind):
        return (
            jax.ShapeDtypeStruct((tokens, width), kind),
            pl.BlockSpec((BLK, width), lambda i: (i, 0)),
        )

    outs = [flat(D, F32), flat(D, F32)] + [heads(BLK, PW)] * 3 + [heads(PW, BLK)]
    outs.append(
        (
            jax.ShapeDtypeStruct((blocks, PAIRS, 1, 2 * BLK), F32),
            pl.BlockSpec((1, PAIRS, 1, 2 * BLK), lambda i: (i, 0, 0, 0)),
        )
    )
    outs += [flat(FF, BF)] * 2
    return pl.pallas_call(
        functools.partial(full_forward_kernel, long_blocks),
        grid=(blocks,),
        in_specs=[
            pl.BlockSpec((BLK, aux.shape[1]), lambda i: (i, 0)),
            whole_spec(embed.shape),
            whole_spec(attn.shape),
            whole_spec(feed.shape),
            whole_spec(rows.shape),
            whole_spec(beta.shape),
            pl.BlockSpec(memory_space=pltpu.SMEM),
        ],
        out_specs=[spec for _, spec in outs],
        out_shape=[shape for shape, _ in outs],
        scratch_shapes=[
            pltpu.VMEM((HEADS, far, TILE, TILE), F32),
            pltpu.VMEM((blocks, PAIRS, BLK, PW), BF),
            pltpu.VMEM((blocks, PAIRS, PW, BLK), BF),
        ]
        + state_scratch(BLK),
        compiler_params=params(56),
        name="full_forward",
    )(aux, embed, attn, feed, rows, beta, rel)


PAD = 8


def middle_kernel(
    seq,
    x1,
    aux,
    head,
    attn,
    feed,
    rows,
    beta,
    rel,
    scale,
    final,
    dx_out,
    d_attn,
    d_feed,
    d_head,
    row_grads,
    d_beta,
    bits_out,
    sums,
    xp,
    pooled,
    mixed,
    ot,
    lse,
    active_s,
    slope_s,
    middle_s,
    bias,
    tiles,
    d_mixed,
    *state,
):
    n_long = seq // 3
    spots = ((PAD, 0, n_long), (2 * PAD + seq, n_long, TILE))
    build_bias(rel, bias, bias.shape[1])
    tiles[...] = jnp.zeros_like(tiles)
    lanes = D // TILE
    for c in range(lanes):
        xp[c, 0:PAD] = jnp.zeros((PAD, TILE), F32)
        xp[c, PAD + seq : 2 * PAD + seq] = jnp.zeros((PAD, TILE), F32)
        xp[c, PAD : PAD + seq] = x1[0:seq, c * TILE : (c + 1) * TILE]
        xp[c, 2 * PAD + seq :] = x1[seq:, c * TILE : (c + 1) * TILE]
    for start, at, n in spots:
        for c in range(lanes):
            pooled[at : at + n, c * TILE : (c + 1) * TILE] = (
                xp[c, pl.ds(start - 2, n, stride=3)]
                + xp[c, pl.ds(start - 1, n, stride=3)]
                + xp[c, pl.ds(start, n, stride=3)]
            ) / 3.0

    xhat, _ = norm_stats(pooled[...])
    normed = (xhat * rows[0:1] + rows[1:2]).astype(BF)
    for part in range(3):
        value = mm(normed, attn[:, part * D : (part + 1) * D])
        value = (value * HD**-0.5 if part == 0 else value).astype(BF)
        for pair in range(PAIRS):
            mixed[part, pair] = value[:, pair * PW : (pair + 1) * PW]

    def forward_pair(pair, carry):
        for at, n, offset in ((0, n_long, 0), (n_long, TILE, 2 * n_long)):
            top, total, acc = state
            wide = pl.ds(0, 2 * n)
            part = (top.at[:, wide], total.at[:, wide], acc.at[:, wide])
            softmax_start(part)
            values_t = mixed[2, pair, at : at + n].T
            both = split_heads(mixed[0, pair, at : at + n])
            count = n // TILE
            softmax_step(
                mixed[1, pair, at : at + n], values_t, both, bias, pair, 0, True, count, count, part
            )
            ot[pair, :, at : at + n], lse[pair, :, offset : offset + 2 * n] = softmax_end(part, n)
        return carry

    lax.fori_loop(0, PAIRS, forward_pair, 0)
    middle = pooled[...] + mm(ot[...].reshape(D, ot.shape[2]).T, attn[:, 3 * D :])
    middle_s[...] = middle
    xhat, _ = norm_stats(middle)
    second = (xhat * rows[2:3] + rows[3:4]).astype(BF)
    active, slope = gelu_pair(mm(second, feed[:, :FF]) + beta[...])
    active_s[...] = active.astype(BF)
    slope_s[...] = slope.astype(BF)
    short = middle + mm(active_s[...], feed[:, FF:], NT) + rows[4:5]
    for start, at, n in spots:
        for c in range(lanes):
            part = short[at : at + n, c * TILE : (c + 1) * TILE]
            for k in range(3):
                where = pl.ds(start + k, n, stride=3)
                xp[c, where] = xp[c, where] + part

    d_head[...] = jnp.zeros_like(d_head)
    row_grads[...] = jnp.zeros_like(row_grads)

    def loss_block(b, bits):
        start = pl.multiple_of(b * BLK + jnp.where(b * BLK >= seq, 2 * PAD, PAD), PAD)
        joined = jnp.concatenate([xp[c, pl.ds(start, BLK)] for c in range(lanes)], 1)
        xhat, rstd = norm_stats(joined)
        last = (xhat * final[0:1] + final[1:2]).astype(BF)
        logits = mm(last, head[...], NT) * D**-0.5
        info = aux[pl.ds(pl.multiple_of(b * BLK, BLK), BLK), :]
        weight = info[:, 2:3].astype(F32)
        hot = one_hot(info[:, 1:2])
        highest = jnp.max(logits, -1, keepdims=True)
        powers = jnp.exp(logits - highest)
        total = jnp.sum(powers, -1, keepdims=True)
        picked = jnp.sum(jnp.where(hot, logits, 0.0), -1, keepdims=True)
        lost = weight * (highest + jnp.log(total) - picked)
        d_logits = ((powers / total - hot.astype(F32)) * (weight * scale[0, 0])).astype(BF)
        d_head[...] += mm(d_logits, last, TN) * D**-0.5
        d_last = mm(d_logits, head[...]) * D**-0.5
        dx, d_gain, d_shift = norm_back(d_last, xhat, rstd, final[0:1])
        row_grads[0:1] += d_gain
        row_grads[1:2] += d_shift
        for c in range(lanes):
            xp[c, pl.ds(start, BLK)] = dx[:, c * TILE : (c + 1) * TILE]
        return bits + lost

    bits = lax.fori_loop(0, x1.shape[0] // BLK, loss_block, jnp.zeros((BLK, 1), F32))
    bits_out[...] = jnp.sum(bits, 0, keepdims=True) / LOG_TWO

    d_short = jnp.concatenate(
        [
            jnp.concatenate(
                [
                    xp[c, pl.ds(start, n, stride=3)]
                    + xp[c, pl.ds(start + 1, n, stride=3)]
                    + xp[c, pl.ds(start + 2, n, stride=3)]
                    for c in range(lanes)
                ],
                1,
            )
            for start, at, n in spots
        ],
        0,
    )
    d_branch = d_short.astype(BF)
    row_grads[6:7] = jnp.sum(d_branch.astype(F32), 0, keepdims=True)
    d_feed[:, FF:] = mm(d_branch, active_s[...], TN).astype(BF)
    d_pre = (mm(d_branch, feed[:, FF:]) * slope_s[...].astype(F32)).astype(BF)
    d_beta[...] = jnp.sum(d_pre.astype(F32), 0, keepdims=True)
    xhat, rstd = norm_stats(middle_s[...])
    second = (xhat * rows[2:3] + rows[3:4]).astype(BF)
    d_feed[:, :FF] = mm(second, d_pre, TN).astype(BF)
    dx, d_gain, d_shift = norm_back(mm(d_pre, feed[:, :FF], NT), xhat, rstd, rows[2:3])
    row_grads[4:5] = d_gain
    row_grads[5:6] = d_shift
    d_middle = d_short + dx
    d_mix = d_middle.astype(BF)
    ot_all = ot[...].reshape(D, ot.shape[2])
    d_attn[:, 3 * D :] = mm(ot_all, d_mix).astype(BF)
    d_att = mm(d_mix, attn[:, 3 * D :], NT).astype(BF)
    for pair in range(PAIRS):
        mixed[3, pair] = d_att[:, pair * PW : (pair + 1) * PW]

    def backward_pair(pair, carry):
        for at, n, offset in ((0, n_long, 0), (n_long, TILE, 2 * n_long)):
            d_out = mixed[3, pair, at : at + n]
            product = (d_out.astype(F32).T) * ot[pair, :, at : at + n].astype(F32)
            inner = jnp.concatenate(
                [
                    jnp.sum(product[:HD], 0, keepdims=True),
                    jnp.sum(product[HD:], 0, keepdims=True),
                ],
                1,
            )
            queries = split_heads(mixed[0, pair, at : at + n])
            grads = split_heads(d_out)
            keys = mixed[1, pair, at : at + n]
            count = n // TILE
            p, ds = score_back(
                keys,
                mixed[2, pair, at : at + n],
                queries,
                grads,
                lse[pair, :, offset : offset + 2 * n],
                inner,
                bias,
                pair,
                0,
                True,
                count,
                count,
                tiles,
            )
            dq = mm(keys.T, ds)
            dq = jnp.concatenate([dq[:HD, :n], dq[HD:, n:]], 0) * HD**-0.5
            d_mixed[0, pair, at : at + n] = dq.T.astype(BF)
            d_mixed[1, pair, at : at + n] = mm(ds, queries).astype(BF)
            d_mixed[2, pair, at : at + n] = mm(p, grads).astype(BF)
        return carry

    lax.fori_loop(0, PAIRS, backward_pair, 0)
    fold_bias(tiles, sums, tiles.shape[1])
    d_in = jnp.concatenate([d_mixed[part, pair] for part in range(3) for pair in range(PAIRS)], 1)
    xhat, rstd = norm_stats(pooled[...])
    normed = (xhat * rows[0:1] + rows[1:2]).astype(BF)
    d_attn[:, : 3 * D] = mm(normed, d_in, TN).astype(BF)
    dx, d_gain, d_shift = norm_back(mm(d_in, attn[:, : 3 * D], NT), xhat, rstd, rows[0:1])
    row_grads[2:3] = d_gain
    row_grads[3:4] = d_shift
    d_pool = (d_middle + dx) / 3.0
    for start, at, n in spots:
        for c in range(lanes):
            part = d_pool[at : at + n, c * TILE : (c + 1) * TILE]
            for k in range(3):
                where = pl.ds(start - 2 + k, n, stride=3)
                xp[c, where] = xp[c, where] + part
    for c in range(lanes):
        dx_out[0:seq, c * TILE : (c + 1) * TILE] = xp[c, PAD : PAD + seq]
        dx_out[seq:, c * TILE : (c + 1) * TILE] = xp[c, 2 * PAD + seq :]


def middle_stage(x1, aux, head, attn, feed, rows, beta, rel, scale, final, seq):
    tokens = x1.shape[0]
    n_long = seq // 3
    short = n_long + TILE
    far = n_long // TILE
    vm = pl.BlockSpec(memory_space=pltpu.VMEM)
    return pl.pallas_call(
        functools.partial(middle_kernel, seq),
        in_specs=[vm] * 7 + [pl.BlockSpec(memory_space=pltpu.SMEM)] * 2 + [vm],
        out_specs=[vm] * 8,
        out_shape=[
            jax.ShapeDtypeStruct((tokens, D), F32),
            jax.ShapeDtypeStruct((D, 4 * D), BF),
            jax.ShapeDtypeStruct((D, 2 * FF), BF),
            jax.ShapeDtypeStruct((V, D), F32),
            jax.ShapeDtypeStruct((8, D), F32),
            jax.ShapeDtypeStruct((1, FF), F32),
            jax.ShapeDtypeStruct((1, 1), F32),
            jax.ShapeDtypeStruct((HEADS, fold_rows(far), TILE), F32),
        ],
        scratch_shapes=[
            pltpu.VMEM((D // TILE, tokens + 2 * PAD, TILE), F32),
            pltpu.VMEM((short, D), F32),
            pltpu.VMEM((4, PAIRS, short, PW), BF),
            pltpu.VMEM((PAIRS, PW, short), BF),
            pltpu.VMEM((PAIRS, 1, 2 * short), F32),
            pltpu.VMEM((short, FF), BF),
            pltpu.VMEM((short, FF), BF),
            pltpu.VMEM((short, D), F32),
            pltpu.VMEM((HEADS, far, TILE, TILE), F32),
            pltpu.VMEM((HEADS, far, TILE, TILE), F32),
            pltpu.VMEM((3, PAIRS, short, PW), BF),
        ]
        + state_scratch(n_long),
        compiler_params=params(60),
        name="middle_stage",
    )(x1, aux, head, attn, feed, rows, beta, rel, scale, final)


def feed_back_kernel(
    dx, act, slope, middle, feed, rows, dm_out, d_feed, row_grads, d_beta, up, down
):
    step = pl.program_id(0)

    @pl.when(step == 0)
    def _():
        up[...] = jnp.zeros_like(up)
        down[...] = jnp.zeros_like(down)
        row_grads[...] = jnp.zeros_like(row_grads)
        d_beta[...] = jnp.zeros_like(d_beta)

    d_result = dx[...]
    d_branch = d_result.astype(BF)
    row_grads[2:3] += jnp.sum(d_branch.astype(F32), 0, keepdims=True)
    down[...] += mm(d_branch, act[...], TN)
    d_pre = (mm(d_branch, feed[:, FF:]) * slope[...].astype(F32)).astype(BF)
    d_beta[...] += jnp.sum(d_pre.astype(F32), 0, keepdims=True)
    xhat, rstd = norm_stats(middle[...])
    second = (xhat * rows[2:3] + rows[3:4]).astype(BF)
    up[...] += mm(second, d_pre, TN)
    dn, d_gain, d_shift = norm_back(mm(d_pre, feed[:, :FF], NT), xhat, rstd, rows[2:3])
    row_grads[0:1] += d_gain
    row_grads[1:2] += d_shift
    dm_out[...] = d_result + dn

    @pl.when(step == pl.num_programs(0) - 1)
    def _():
        d_feed[:, :FF] = up[...].astype(BF)
        d_feed[:, FF:] = down[...].astype(BF)


def feed_back(dx, act, slope, middle, feed, rows):
    tokens = dx.shape[0]

    def flat(width):
        return pl.BlockSpec((BLK, width), lambda i: (i, 0))

    return pl.pallas_call(
        feed_back_kernel,
        grid=(tokens // BLK,),
        in_specs=[flat(D), flat(FF), flat(FF), flat(D), whole_spec(feed.shape), whole_spec(rows.shape)],
        out_specs=[
            flat(D),
            whole_spec((D, 2 * FF)),
            whole_spec((8, D)),
            whole_spec((1, FF)),
        ],
        out_shape=[
            jax.ShapeDtypeStruct((tokens, D), F32),
            jax.ShapeDtypeStruct((D, 2 * FF), BF),
            jax.ShapeDtypeStruct((8, D), F32),
            jax.ShapeDtypeStruct((1, FF), F32),
        ],
        scratch_shapes=[pltpu.VMEM((D, FF), F32), pltpu.VMEM((D, FF), F32)],
        compiler_params=params(56),
        name="feed_back",
    )(dx, act, slope, middle, feed, rows)


def attention_back_kernel(
    long_blocks,
    dm,
    aux,
    ot,
    lse,
    q_all,
    k_all,
    v_all,
    embed,
    attn,
    rows,
    rel,
    d_attn,
    d_embed,
    row_grads,
    sums,
    bias,
    tiles,
    kt_all,
    dk_all,
    dv_all,
    dq_t,
    d_att,
    inner,
    weights,
    d_mixed,
):
    step = pl.program_id(0)
    blocks = pl.num_programs(0)
    i = blocks - 1 - step

    @pl.when(step == 0)
    def _():
        build_bias(rel, bias, bias.shape[1])
        tiles[...] = jnp.zeros_like(tiles)
        dk_all[...] = jnp.zeros_like(dk_all)
        dv_all[...] = jnp.zeros_like(dv_all)
        weights[...] = jnp.zeros_like(weights)
        d_embed[...] = jnp.zeros_like(d_embed)
        row_grads[...] = jnp.zeros_like(row_grads)

        def turn(n, carry):
            for pair in range(PAIRS):
                kt_all[n, pair] = k_all[n, pair].T
            return carry

        lax.fori_loop(0, blocks, turn, 0)

    d_middle = dm[...]
    d_mix = d_middle.astype(BF)
    weights[:, 3 * D :] += mm(ot[0].reshape(D, BLK), d_mix)
    out = mm(d_mix, attn[:, 3 * D :], NT).astype(BF)
    for pair in range(PAIRS):
        d_att[pair] = out[:, pair * PW : (pair + 1) * PW]
    product = mm(attn[:, 3 * D :], d_mix, NT).astype(BF).astype(F32) * ot[0].reshape(
        D, BLK
    ).astype(F32)
    for pair in range(PAIRS):
        at = pair * PW
        inner[pair] = jnp.concatenate(
            [
                jnp.sum(product[at : at + HD], 0, keepdims=True),
                jnp.sum(product[at + HD : at + PW], 0, keepdims=True),
            ],
            1,
        )
    first = jnp.where(i >= long_blocks, long_blocks, 0)

    def one_pair(pair, carry):
        queries = split_heads(q_all[i, pair])
        grads = split_heads(d_att[pair])
        dq_t[...] = jnp.zeros_like(dq_t)

        def with_block(j, far, diag):
            p, ds = score_back(
                k_all[j, pair],
                v_all[j, pair],
                queries,
                grads,
                lse[0, pair],
                inner[pair],
                bias,
                pair,
                far,
                diag,
                SUB,
                SUB,
                tiles,
            )
            dv_all[j, pair] += mm(p, grads)
            dk_all[j, pair] += mm(ds, queries)
            dq_t[...] += mm(kt_all[j, pair], ds)

        def earlier(j, inside):
            with_block(j, SUB * (i - j), False)
            return inside

        lax.fori_loop(first, i, earlier, 0)
        with_block(i, 0, True)
        total = dq_t[...]
        total = jnp.concatenate([total[:HD, :BLK], total[HD:, BLK:]], 0) * HD**-0.5
        d_mixed[0, pair] = total.T.astype(BF)
        d_mixed[1, pair] = dk_all[i, pair].astype(BF)
        d_mixed[2, pair] = dv_all[i, pair].astype(BF)
        return carry

    lax.fori_loop(0, PAIRS, one_pair, 0)
    d_in = jnp.concatenate([d_mixed[part, pair] for part in range(3) for pair in range(PAIRS)], 1)
    hot = one_hot(aux[:, 0:1]).astype(BF)
    xhat, rstd = norm_stats(mm(hot, embed[...]))
    normed = (xhat * rows[0:1] + rows[1:2]).astype(BF)
    weights[:, : 3 * D] += mm(normed, d_in, TN)
    dx, d_gain, d_shift = norm_back(mm(d_in, attn[:, : 3 * D], NT), xhat, rstd, rows[0:1])
    row_grads[0:1] += d_gain
    row_grads[1:2] += d_shift
    d_embed[...] += mm(hot, (d_middle + dx).astype(BF), TN)

    @pl.when(step == blocks - 1)
    def _():
        d_attn[...] = weights[...].astype(BF)
        fold_bias(tiles, sums, tiles.shape[1])


def attention_back(dm, aux, ot, lse, q, k, v, embed, attn, rows, rel, long_blocks):
    tokens = dm.shape[0]
    blocks = tokens // BLK
    far = SUB * long_blocks

    def turned(shape):
        return pl.BlockSpec(shape, lambda s: (blocks - 1 - s,) + (0,) * (len(shape) - 1))

    return pl.pallas_call(
        functools.partial(attention_back_kernel, long_blocks),
        grid=(blocks,),
        in_specs=[
            turned((BLK, D)),
            turned((BLK, aux.shape[1])),
            turned((1, PAIRS, PW, BLK)),
            turned((1, PAIRS, 1, 2 * BLK)),
            whole_spec(q.shape),
            whole_spec(k.shape),
            whole_spec(v.shape),
            whole_spec(embed.shape),
            whole_spec(attn.shape),
            whole_spec(rows.shape),
            pl.BlockSpec(memory_space=pltpu.SMEM),
        ],
        out_specs=[
            whole_spec((D, 4 * D)),
            whole_spec((V, D)),
            whole_spec((8, D)),
            whole_spec((HEADS, fold_rows(far), TILE)),
        ],
        out_shape=[
            jax.ShapeDtypeStruct((D, 4 * D), BF),
            jax.ShapeDtypeStruct((V, D), F32),
            jax.ShapeDtypeStruct((8, D), F32),
            jax.ShapeDtypeStruct((HEADS, fold_rows(far), TILE), F32),
        ],
        scratch_shapes=[
            pltpu.VMEM((HEADS, far, TILE, TILE), F32),
            pltpu.VMEM((HEADS, far, TILE, TILE), F32),
            pltpu.VMEM((blocks, PAIRS, PW, BLK), BF),
            pltpu.VMEM((blocks, PAIRS, BLK, PW), F32),
            pltpu.VMEM((blocks, PAIRS, BLK, PW), F32),
            pltpu.VMEM((PW, 2 * BLK), F32),
            pltpu.VMEM((PAIRS, BLK, PW), BF),
            pltpu.VMEM((PAIRS, 1, 2 * BLK), F32),
            pltpu.VMEM((D, 4 * D), F32),
            pltpu.VMEM((3, PAIRS, BLK, PW), BF),
        ],
        compiler_params=params(60),
        name="attention_back",
    )(dm, aux, ot, lse, q, k, v, embed, attn, rows, rel)


def adam_update(weight, moment, square, gradient, decay, rate):
    moment = BETA_ONE * moment + (1.0 - BETA_ONE) * gradient
    square = BETA_TWO * square + (1.0 - BETA_TWO) * gradient * gradient
    fixed_moment = moment / (1.0 - BETA_ONE**STEP)
    fixed_square = square / (1.0 - BETA_TWO**STEP)
    delta = -rate * (fixed_moment / (jnp.sqrt(fixed_square) + ADAM_EPS) + decay * weight)
    return (moment, square, delta)


def local_gradients(byte_ids, live_mask, tables, attn_pair, feed_pair, vec, axes):
    seq = byte_ids.shape[1]
    long_blocks = seq // BLK
    weight = jnp.concatenate([live_mask[:, 1:], jnp.zeros_like(live_mask[:, :1])], 1)
    info = jnp.stack([byte_ids, jnp.roll(byte_ids, -1, 1), weight, weight], -1)
    aux = jnp.concatenate([info[0], info[1, :BLK]], 0)
    count = lax.psum(jnp.sum(weight.astype(F32)), axes)
    scale = (1.0 / (count * LOG_TWO)).reshape(1, 1)
    rows = [
        jnp.concatenate([vec[2 + 5 * l : 7 + 5 * l], jnp.zeros((3, D), F32)], 0) for l in range(2)
    ]
    bias_rows = 2 * FF // D
    beta = vec[12 : 12 + bias_rows].reshape(2, 1, FF)
    rel = vec[12 + bias_rows :].reshape(2, HEADS, NB)
    x1, middle, q, k, v, ot, lse, act, slope = full_forward(
        aux, tables[0], attn_pair[0], feed_pair[0], rows[0], beta[0], rel[0], long_blocks
    )
    d_x1, d_attn_1, d_feed_1, d_head, short_rows, d_beta_1, bits, sums_1 = middle_stage(
        x1, aux, tables[1], attn_pair[1], feed_pair[1], rows[1], beta[1], rel[1], scale, vec[0:2], seq
    )
    d_middle, d_feed_0, feed_rows, d_beta_0 = feed_back(
        d_x1, act, slope, middle, feed_pair[0], rows[0]
    )
    d_attn_0, d_embed, attn_rows, sums_0 = attention_back(
        d_middle, aux, ot, lse, q, k, v, tables[0], attn_pair[0], rows[0], rel[0], long_blocks
    )

    def d_rel(sums):
        fold = fold_matrix(long_blocks * SUB if sums is sums_0 else seq // 3 // TILE)
        return jnp.dot(jnp.sum(sums, -1), fold, precision=lax.Precision.HIGHEST).reshape(1, -1)

    d_vec = jnp.concatenate(
        [
            short_rows[0:2],
            attn_rows[0:2],
            feed_rows[0:3],
            short_rows[2:7],
            d_beta_0.reshape(-1, D),
            d_beta_1.reshape(-1, D),
            jnp.concatenate([d_rel(sums_0), d_rel(sums_1)], 1),
        ],
        0,
    )
    grads = (jnp.stack([d_embed, d_head]), (d_attn_0, d_attn_1), (d_feed_0, d_feed_1), d_vec)
    return bits[0, 0], count, grads


def per_device(
    byte_ids,
    live_mask,
    tables,
    attention,
    feed_forward,
    vectors,
    moment_tables,
    moment_attention,
    moment_feed,
    moment_vectors,
    square_tables,
    square_attention,
    square_feed,
    square_vectors,
    outer_tables,
    outer_attention,
    outer_feed,
    outer_vectors,
    average_tables,
    average_attention,
    average_feed,
    average_vectors,
):
    axes = ("wide", "narrow")

    def gather(x, axis):
        return lax.all_gather(x.astype(BF), axes, axis=axis, tiled=True)

    full_tables = gather(tables, 1)
    vec = gather(vectors, 1).astype(F32)
    attn_pair = [gather(attention[l], 0) for l in range(2)]
    feed_pair = [gather(feed_forward[l], 0) for l in range(2)]
    bits, count, grads = local_gradients(
        byte_ids, live_mask, full_tables, attn_pair, feed_pair, vec, axes
    )

    def scatter(x, axis):
        return lax.psum_scatter(x, axes, scatter_dimension=axis, tiled=True).astype(F32)

    raw = (
        scatter(grads[0], 1),
        jnp.stack([scatter(g, 0) for g in grads[1]]),
        jnp.stack([scatter(g, 0) for g in grads[2]]),
        scatter(grads[3], 1),
    )
    squares_local = sum((jnp.sum(g * g) for g in raw))
    norm_squared, loss_total = lax.psum((squares_local, bits), axes)
    gradient_norm = jnp.sqrt(norm_squared)
    factor = jnp.minimum(1.0, CLIP_AT / (gradient_norm + 1e-06))
    weights = (tables, attention, feed_forward, vectors)
    moments = (moment_tables, moment_attention, moment_feed, moment_vectors)
    squares = (square_tables, square_attention, square_feed, square_vectors)
    outers = (outer_tables, outer_attention, outer_feed, outer_vectors)
    averages = (average_tables, average_attention, average_feed, average_vectors)
    decays = (DECAY, DECAY, DECAY, 0.0)
    rates = (RATE_TABLE, RATE, RATE, RATE_TABLE)
    updated = [
        adam_update(
            weights[index],
            moments[index][0],
            squares[index][0],
            raw[index] * factor,
            decays[index],
            rates[index],
        )
        for index in range(4)
    ]
    replicas = lax.axis_size("rep")
    new_weights, new_outers, new_averages = ([], [], [])
    for index in range(4):
        delta = lax.psum(updated[index][2].astype(BF), "rep").astype(F32) / replicas
        outer_new = OUTER_MOM * outers[index] + delta
        weight_new = weights[index] + OUTER_RATE * (delta + OUTER_MOM * outer_new)
        new_outers.append(outer_new)
        new_weights.append(weight_new)
        new_averages.append(EVAL_KEEP * averages[index] + (1.0 - EVAL_KEEP) * weight_new)
    return (
        loss_total.reshape(1),
        count.reshape(1),
        gradient_norm.reshape(1),
        *[u[0][None] for u in updated],
        *[u[1][None] for u in updated],
        *new_weights,
        *new_outers,
        *new_averages,
    )


def solution(mesh):
    rows = P(("rep", "wide", "narrow"), None)
    split = (
        P(None, ("wide", "narrow"), None),
        P(None, ("wide", "narrow"), None),
        P(None, ("wide", "narrow"), None),
        P(None, ("wide", "narrow")),
    )
    own = tuple(P("rep", *spec) for spec in split)
    return jax.shard_map(
        per_device,
        mesh=mesh,
        in_specs=(rows, rows) + split + own + own + split + split,
        out_specs=(P("rep"),) * 3 + own + own + split * 3,
        check_vma=False,
    )
```

```python
import functools
import math

import jax
import jax.numpy as jnp
import numpy as np
from jax import lax
from jax.experimental import pallas as pl
from jax.experimental.pallas import tpu as pltpu
from jax.sharding import PartitionSpec as P

D = 512
HEADS = 8
HD = 64
FF = 2048
V = 256
NB = 32
STEP = 10
VEC = 21
EDGES = (1, 2, 3, 4, 5, 6, 7, 8, 10, 12, 14, 16, 20, 24, 28, 32, 40, 48, 64, 80, 96, 128, 160, 192)
EDGES = EDGES + (256, 320, 384, 512, 640, 768, 1024)
NEG = -1000000000.0
EPS = 1e-05
LOG_TWO = math.log(2.0)
RATE = 0.01
RATE_TABLE = 0.2
BETA_ONE = 0.9
BETA_TWO = 0.95
ADAM_EPS = 1e-08
DECAY = 0.1
CLIP_AT = 0.02
OUTER_RATE = 0.7
OUTER_MOM = 0.9
EVAL_KEEP = 0.9

TILE = 128
BLK = 384
SUB = BLK // TILE
PAIRS = HEADS // 2
PW = 2 * HD
GELU_C = math.sqrt(2.0 / math.pi)
GELU_A = 0.044715

BF = jnp.bfloat16
F32 = jnp.float32
NN = (((1,), (0,)), ((), ()))
NT = (((1,), (1,)), ((), ()))
TN = (((0,), (0,)), ((), ()))


def mm(left, right, dims=NN):
    return lax.dot_general(left, right, dims, preferred_element_type=F32)


def spans(count):
    out = []
    for d in range(count):
        lo, hi = max(TILE * d - (TILE - 1), 0), TILE * d + TILE - 1
        base = sum(e <= lo for e in EDGES)
        out.append((base, [(e, k + 1) for k, e in enumerate(EDGES) if lo < e <= hi]))
    return out


def fold_matrix(count):
    rows = []
    for base, edges in spans(count):
        row = np.zeros(NB, np.float32)
        row[base] += 1
        rows.append(row)
        for _, bucket in edges:
            row = np.zeros(NB, np.float32)
            row[bucket] += 1
            row[bucket - 1] -= 1
            rows.append(row)
    return np.stack(rows)


def tile_distance(d):
    keys = lax.broadcasted_iota(jnp.int32, (TILE, TILE), 0)
    queries = lax.broadcasted_iota(jnp.int32, (TILE, TILE), 1)
    return TILE * d + queries - keys


def build_bias(rel, bias, count):
    for d, (base, edges) in enumerate(spans(count)):
        distance = tile_distance(d)

        def one_head(h, carry, d=d, base=base, edges=edges, distance=distance):
            tile = jnp.full((TILE, TILE), rel[h, base], F32)
            for edge, bucket in edges:
                tile = jnp.where(distance >= edge, rel[h, bucket], tile)
            if d == 0:
                tile = jnp.where(distance < 0, NEG, tile)
            bias[h, d] = tile
            return carry

        lax.fori_loop(0, HEADS, one_head, 0)


def fold_bias(tiles, sums, count):
    at = 0
    for d, (_, edges) in enumerate(spans(count)):
        distance = tile_distance(d)

        def one_head(h, carry, d=d, edges=edges, distance=distance, at=at):
            tile = tiles[h, d]
            sums[h, at : at + 1] = jnp.sum(tile, 0, keepdims=True)
            for n, (edge, _) in enumerate(edges):
                sums[h, at + 1 + n : at + 2 + n] = jnp.sum(
                    jnp.where(distance >= edge, tile, 0.0), 0, keepdims=True
                )
            return carry

        lax.fori_loop(0, HEADS, one_head, 0)
        at += 1 + len(edges)


def fold_rows(count):
    return sum(1 + len(edges) for _, edges in spans(count))


def norm_stats(x):
    centered = x - jnp.mean(x, -1, keepdims=True)
    rstd = lax.rsqrt(jnp.mean(centered * centered, -1, keepdims=True) + EPS)
    return centered * rstd, rstd


def norm_back(dy, xhat, rstd, gain):
    t = dy * gain
    dx = rstd * (
        t - jnp.mean(t, -1, keepdims=True) - xhat * jnp.mean(t * xhat, -1, keepdims=True)
    )
    return dx, jnp.sum(dy * xhat, 0, keepdims=True), jnp.sum(dy, 0, keepdims=True)


def gelu_pair(u):
    square = u * u
    tanh = jnp.tanh(GELU_C * u * (1.0 + GELU_A * square))
    half = 0.5 * (1.0 + tanh)
    slope = half + 0.5 * u * (1.0 - tanh * tanh) * (GELU_C + 3.0 * GELU_C * GELU_A * square)
    return u * half, slope


def split_heads(pair):
    lane = lax.broadcasted_iota(jnp.int32, pair.shape, 1)
    zero = jnp.zeros_like(pair)
    return jnp.concatenate(
        [jnp.where(lane < HD, pair, zero), jnp.where(lane >= HD, pair, zero)], 0
    )


def cell(block, kb, e, qa, nq):
    return block[kb * TILE : (kb + 1) * TILE, (e * nq + qa) * TILE : (e * nq + qa + 1) * TILE]


def softmax_step(keys, values_t, queries, bias, pair, far, diag, nq, nk, state):
    top, total, acc = state
    raw = mm(keys, queries, NT)
    scores = {}
    for e in range(2):
        for qa in range(nq):
            for kb in range(nk):
                if diag and kb > qa:
                    continue
                scores[kb, e, qa] = cell(raw, kb, e, qa, nq) + bias[2 * pair + e, far + qa - kb]
    highest = []
    for e in range(2):
        for qa in range(nq):
            column = [scores[kb, e, qa] for kb in range(nk) if (kb, e, qa) in scores]
            highest.append(jnp.max(functools.reduce(jnp.maximum, column), 0, keepdims=True))
    old_top = top[...]
    new_top = jnp.maximum(old_top, jnp.concatenate(highest, 1))
    alpha = jnp.exp(old_top - new_top)
    sums = []
    columns = []
    for e in range(2):
        for qa in range(nq):
            at = (e * nq + qa) * TILE
            ceiling = new_top[:, at : at + TILE]
            parts, adds = [], None
            for kb in range(nk):
                if (kb, e, qa) not in scores:
                    parts.append(jnp.zeros((TILE, TILE), BF))
                    continue
                p = jnp.exp(scores[kb, e, qa] - ceiling)
                adds = p if adds is None else adds + p
                parts.append(p.astype(BF))
            sums.append(jnp.sum(adds, 0, keepdims=True))
            columns.append(jnp.concatenate(parts, 0))
    top[...] = new_top
    total[...] = alpha * total[...] + jnp.concatenate(sums, 1)
    acc[...] = alpha * acc[...] + mm(values_t, jnp.concatenate(columns, 1))


def softmax_start(state):
    top, total, acc = state
    top[...] = jnp.full(top.shape, NEG, F32)
    total[...] = jnp.zeros(total.shape, F32)
    acc[...] = jnp.zeros(acc.shape, F32)


def softmax_end(state, n):
    top, total, acc = state
    scaled = acc[...] / total[...]
    out = jnp.concatenate([scaled[:HD, :n], scaled[HD:, n:]], 0).astype(BF)
    return out, top[...] + jnp.log(total[...])


def score_back(keys, values, queries, grads, logsum, inner, bias, pair, far, diag, nq, nk, tiles):
    raw = mm(keys, queries, NT)
    d_p = mm(values, grads, NT)
    probs, scores = {}, {}
    for e in range(2):
        for diff in range(-(nk - 1), nq):
            total = None
            if diag and diff < 0:
                continue
            for kb in range(nk):
                qa = kb + diff
                if qa < 0 or qa >= nq:
                    continue
                at = (e * nq + qa) * TILE
                p = jnp.exp(
                    cell(raw, kb, e, qa, nq)
                    + bias[2 * pair + e, far + diff]
                    - logsum[:, at : at + TILE]
                )
                ds = p * (cell(d_p, kb, e, qa, nq) - inner[:, at : at + TILE])
                total = ds if total is None else total + ds
                probs[kb, e, qa] = p.astype(BF)
                scores[kb, e, qa] = ds.astype(BF)
            tiles[2 * pair + e, far + diff] += total

    def whole(parts):
        empty = jnp.zeros((TILE, TILE), BF)
        return jnp.concatenate(
            [
                jnp.concatenate([parts.get((kb, e, qa), empty) for kb in range(nk)], 0)
                for e in range(2)
                for qa in range(nq)
            ],
            1,
        )

    return whole(probs), whole(scores)


def one_hot(column):
    return column == lax.broadcasted_iota(jnp.int32, (column.shape[0], V), 1)


def full_forward_kernel(
    long_blocks,
    aux,
    embed,
    wts,
    rows,
    beta,
    rel,
    x1_out,
    middle_out,
    q_out,
    k_out,
    v_out,
    ot_out,
    lse_out,
    act_out,
    slope_out,
    bias,
    k_all,
    vt_all,
    *state,
):
    step = pl.program_id(0)

    @pl.when(step == 0)
    def _():
        build_bias(rel, bias, bias.shape[1])

    hot = one_hot(aux[:, 0:1]).astype(BF)
    x = mm(hot, embed[...])
    xhat, _ = norm_stats(x)
    normed = (xhat * rows[0:1] + rows[1:2]).astype(BF)
    queries = (mm(normed, wts[0, :, :D]) * HD**-0.5).astype(BF)
    keys = mm(normed, wts[0, :, D : 2 * D]).astype(BF)
    values = mm(normed, wts[1, :, :D]).astype(BF)
    for pair in range(PAIRS):
        cols = slice(pair * PW, (pair + 1) * PW)
        q_out[0, pair] = queries[:, cols]
        k_out[0, pair] = keys[:, cols]
        v_out[0, pair] = values[:, cols]
        k_all[step, pair] = keys[:, cols]
        vt_all[step, pair] = values[:, cols].T
    first = jnp.where(step >= long_blocks, long_blocks, 0)

    def one_pair(pair, carry):
        both = split_heads(q_out[0, pair])
        softmax_start(state)

        def earlier(j, inner):
            far = SUB * (step - j)
            softmax_step(
                k_all[j, pair], vt_all[j, pair], both, bias, pair, far, False, SUB, SUB, state
            )
            return inner

        lax.fori_loop(first, step, earlier, 0)
        softmax_step(
            k_all[step, pair], vt_all[step, pair], both, bias, pair, 0, True, SUB, SUB, state
        )
        ot_out[0, pair], lse_out[0, pair] = softmax_end(state, BLK)
        return carry

    lax.fori_loop(0, PAIRS, one_pair, 0)
    attended = ot_out[0].reshape(D, BLK).T
    middle = x + mm(attended, wts[1, :, D : 2 * D])
    middle_out[...] = middle
    xhat, _ = norm_stats(middle)
    second = (xhat * rows[2:3] + rows[3:4]).astype(BF)
    active, slope = gelu_pair(mm(second, wts[0, :, 2 * D :]) + beta[...])
    active = active.astype(BF)
    act_out[...] = active
    slope_out[...] = slope.astype(BF)
    x1_out[...] = middle + mm(active, wts[1, :, 2 * D :], NT) + rows[4:5]


def whole_spec(shape):
    return pl.BlockSpec(shape, lambda i: (0,) * len(shape), pipeline_mode=pl.Buffered(1))


def params(mib, **more):
    return pltpu.CompilerParams(vmem_limit_bytes=mib * 2**20, **more)


def state_scratch(n):
    return [pltpu.VMEM((1, 2 * n), F32), pltpu.VMEM((1, 2 * n), F32), pltpu.VMEM((PW, 2 * n), F32)]


def full_forward(aux, embed, wts, rows, beta, rel, long_blocks):
    tokens = aux.shape[0]
    blocks = tokens // BLK
    far = SUB * long_blocks

    def heads(n, width):
        return (
            jax.ShapeDtypeStruct((blocks, PAIRS, n, width), BF),
            pl.BlockSpec((1, PAIRS, n, width), lambda i: (i, 0, 0, 0)),
        )

    def flat(width, kind):
        return (
            jax.ShapeDtypeStruct((tokens, width), kind),
            pl.BlockSpec((BLK, width), lambda i: (i, 0)),
        )

    outs = [flat(D, F32), flat(D, F32)] + [heads(BLK, PW)] * 3 + [heads(PW, BLK)]
    outs.append(
        (
            jax.ShapeDtypeStruct((blocks, PAIRS, 1, 2 * BLK), F32),
            pl.BlockSpec((1, PAIRS, 1, 2 * BLK), lambda i: (i, 0, 0, 0)),
        )
    )
    outs += [flat(FF, BF)] * 2
    return pl.pallas_call(
        functools.partial(full_forward_kernel, long_blocks),
        grid=(blocks,),
        in_specs=[
            pl.BlockSpec((BLK, aux.shape[1]), lambda i: (i, 0)),
            whole_spec(embed.shape),
            whole_spec(wts.shape),
            whole_spec(rows.shape),
            whole_spec(beta.shape),
            pl.BlockSpec(memory_space=pltpu.SMEM),
        ],
        out_specs=[spec for _, spec in outs],
        out_shape=[shape for shape, _ in outs],
        scratch_shapes=[
            pltpu.VMEM((HEADS, far, TILE, TILE), F32),
            pltpu.VMEM((blocks, PAIRS, BLK, PW), BF),
            pltpu.VMEM((blocks, PAIRS, PW, BLK), BF),
        ]
        + state_scratch(BLK),
        compiler_params=params(56),
        name="full_forward",
    )(aux, embed, wts, rows, beta, rel)


PAD = 8


def middle_kernel(
    seq,
    x1,
    aux,
    head,
    wts,
    rows,
    beta,
    rel,
    scale,
    final,
    dx_out,
    d_wts,
    d_head,
    row_grads,
    d_beta,
    bits_out,
    sums,
    xp,
    pooled,
    mixed,
    ot,
    lse,
    active_s,
    slope_s,
    middle_s,
    bias,
    tiles,
    d_mixed,
    *state,
):
    n_long = seq // 3
    spots = ((PAD, 0, n_long), (2 * PAD + seq, n_long, TILE))
    build_bias(rel, bias, bias.shape[1])
    tiles[...] = jnp.zeros_like(tiles)
    lanes = D // TILE
    for c in range(lanes):
        xp[c, 0:PAD] = jnp.zeros((PAD, TILE), F32)
        xp[c, PAD + seq : 2 * PAD + seq] = jnp.zeros((PAD, TILE), F32)
        xp[c, PAD : PAD + seq] = x1[0:seq, c * TILE : (c + 1) * TILE]
        xp[c, 2 * PAD + seq :] = x1[seq:, c * TILE : (c + 1) * TILE]
    for start, at, n in spots:
        for c in range(lanes):
            pooled[at : at + n, c * TILE : (c + 1) * TILE] = (
                xp[c, pl.ds(start - 2, n, stride=3)]
                + xp[c, pl.ds(start - 1, n, stride=3)]
                + xp[c, pl.ds(start, n, stride=3)]
            ) / 3.0

    xhat, _ = norm_stats(pooled[...])
    normed = (xhat * rows[0:1] + rows[1:2]).astype(BF)
    for part in range(3):
        half, at = part // 2, part % 2 * D
        value = mm(normed, wts[half, :, at : at + D])
        value = (value * HD**-0.5 if part == 0 else value).astype(BF)
        for pair in range(PAIRS):
            mixed[part, pair] = value[:, pair * PW : (pair + 1) * PW]

    def forward_pair(pair, carry):
        for at, n, offset in ((0, n_long, 0), (n_long, TILE, 2 * n_long)):
            top, total, acc = state
            wide = pl.ds(0, 2 * n)
            part = (top.at[:, wide], total.at[:, wide], acc.at[:, wide])
            softmax_start(part)
            values_t = mixed[2, pair, at : at + n].T
            both = split_heads(mixed[0, pair, at : at + n])
            count = n // TILE
            softmax_step(
                mixed[1, pair, at : at + n], values_t, both, bias, pair, 0, True, count, count, part
            )
            ot[pair, :, at : at + n], lse[pair, :, offset : offset + 2 * n] = softmax_end(part, n)
        return carry

    lax.fori_loop(0, PAIRS, forward_pair, 0)
    middle = pooled[...] + mm(ot[...].reshape(D, ot.shape[2]).T, wts[1, :, D : 2 * D])
    middle_s[...] = middle
    xhat, _ = norm_stats(middle)
    second = (xhat * rows[2:3] + rows[3:4]).astype(BF)
    active, slope = gelu_pair(mm(second, wts[0, :, 2 * D :]) + beta[...])
    active_s[...] = active.astype(BF)
    slope_s[...] = slope.astype(BF)
    short = middle + mm(active_s[...], wts[1, :, 2 * D :], NT) + rows[4:5]
    for start, at, n in spots:
        for c in range(lanes):
            part = short[at : at + n, c * TILE : (c + 1) * TILE]
            for k in range(3):
                where = pl.ds(start + k, n, stride=3)
                xp[c, where] = xp[c, where] + part

    d_head[...] = jnp.zeros_like(d_head)
    row_grads[...] = jnp.zeros_like(row_grads)

    def loss_block(b, bits):
        start = pl.multiple_of(b * BLK + jnp.where(b * BLK >= seq, 2 * PAD, PAD), PAD)
        joined = jnp.concatenate([xp[c, pl.ds(start, BLK)] for c in range(lanes)], 1)
        xhat, rstd = norm_stats(joined)
        last = (xhat * final[0:1] + final[1:2]).astype(BF)
        logits = mm(last, head[...], NT) * D**-0.5
        info = aux[pl.ds(pl.multiple_of(b * BLK, BLK), BLK), :]
        weight = info[:, 2:3].astype(F32)
        hot = one_hot(info[:, 1:2])
        highest = jnp.max(logits, -1, keepdims=True)
        powers = jnp.exp(logits - highest)
        total = jnp.sum(powers, -1, keepdims=True)
        picked = jnp.sum(jnp.where(hot, logits, 0.0), -1, keepdims=True)
        lost = weight * (highest + jnp.log(total) - picked)
        d_logits = ((powers / total - hot.astype(F32)) * (weight * scale[0, 0])).astype(BF)
        d_head[...] += mm(d_logits, last, TN) * D**-0.5
        d_last = mm(d_logits, head[...]) * D**-0.5
        dx, d_gain, d_shift = norm_back(d_last, xhat, rstd, final[0:1])
        row_grads[0:1] += d_gain
        row_grads[1:2] += d_shift
        for c in range(lanes):
            xp[c, pl.ds(start, BLK)] = dx[:, c * TILE : (c + 1) * TILE]
        return bits + lost

    bits = lax.fori_loop(0, x1.shape[0] // BLK, loss_block, jnp.zeros((BLK, 1), F32))
    bits_out[...] = jnp.sum(bits, 0, keepdims=True) / LOG_TWO

    d_short = jnp.concatenate(
        [
            jnp.concatenate(
                [
                    xp[c, pl.ds(start, n, stride=3)]
                    + xp[c, pl.ds(start + 1, n, stride=3)]
                    + xp[c, pl.ds(start + 2, n, stride=3)]
                    for c in range(lanes)
                ],
                1,
            )
            for start, at, n in spots
        ],
        0,
    )
    d_branch = d_short.astype(BF)
    row_grads[6:7] = jnp.sum(d_branch.astype(F32), 0, keepdims=True)
    d_wts[1, :, 2 * D :] = mm(d_branch, active_s[...], TN).astype(BF)
    d_pre = (mm(d_branch, wts[1, :, 2 * D :]) * slope_s[...].astype(F32)).astype(BF)
    d_beta[...] = jnp.sum(d_pre.astype(F32), 0, keepdims=True)
    xhat, rstd = norm_stats(middle_s[...])
    second = (xhat * rows[2:3] + rows[3:4]).astype(BF)
    d_wts[0, :, 2 * D :] = mm(second, d_pre, TN).astype(BF)
    dx, d_gain, d_shift = norm_back(mm(d_pre, wts[0, :, 2 * D :], NT), xhat, rstd, rows[2:3])
    row_grads[4:5] = d_gain
    row_grads[5:6] = d_shift
    d_middle = d_short + dx
    d_mix = d_middle.astype(BF)
    ot_all = ot[...].reshape(D, ot.shape[2])
    d_wts[1, :, D : 2 * D] = mm(ot_all, d_mix).astype(BF)
    d_att = mm(d_mix, wts[1, :, D : 2 * D], NT).astype(BF)
    for pair in range(PAIRS):
        mixed[3, pair] = d_att[:, pair * PW : (pair + 1) * PW]

    def backward_pair(pair, carry):
        for at, n, offset in ((0, n_long, 0), (n_long, TILE, 2 * n_long)):
            d_out = mixed[3, pair, at : at + n]
            product = (d_out.astype(F32).T) * ot[pair, :, at : at + n].astype(F32)
            inner = jnp.concatenate(
                [
                    jnp.sum(product[:HD], 0, keepdims=True),
                    jnp.sum(product[HD:], 0, keepdims=True),
                ],
                1,
            )
            queries = split_heads(mixed[0, pair, at : at + n])
            grads = split_heads(d_out)
            keys = mixed[1, pair, at : at + n]
            count = n // TILE
            p, ds = score_back(
                keys,
                mixed[2, pair, at : at + n],
                queries,
                grads,
                lse[pair, :, offset : offset + 2 * n],
                inner,
                bias,
                pair,
                0,
                True,
                count,
                count,
                tiles,
            )
            dq = mm(keys.T, ds)
            dq = jnp.concatenate([dq[:HD, :n], dq[HD:, n:]], 0) * HD**-0.5
            d_mixed[0, pair, at : at + n] = dq.T.astype(BF)
            d_mixed[1, pair, at : at + n] = mm(ds, queries).astype(BF)
            d_mixed[2, pair, at : at + n] = mm(p, grads).astype(BF)
        return carry

    lax.fori_loop(0, PAIRS, backward_pair, 0)
    fold_bias(tiles, sums, tiles.shape[1])
    d_in = jnp.concatenate([d_mixed[part, pair] for part in range(3) for pair in range(PAIRS)], 1)
    xhat, rstd = norm_stats(pooled[...])
    normed = (xhat * rows[0:1] + rows[1:2]).astype(BF)
    d_wts[0, :, : 2 * D] = mm(normed, d_in[:, : 2 * D], TN).astype(BF)
    d_wts[1, :, :D] = mm(normed, d_in[:, 2 * D :], TN).astype(BF)
    dx, d_gain, d_shift = norm_back(mm(d_in[:, : 2 * D], wts[0, :, : 2 * D], NT) + mm(d_in[:, 2 * D :], wts[1, :, :D], NT), xhat, rstd, rows[0:1])
    row_grads[2:3] = d_gain
    row_grads[3:4] = d_shift
    d_pool = (d_middle + dx) / 3.0
    for start, at, n in spots:
        for c in range(lanes):
            part = d_pool[at : at + n, c * TILE : (c + 1) * TILE]
            for k in range(3):
                where = pl.ds(start - 2 + k, n, stride=3)
                xp[c, where] = xp[c, where] + part
    for c in range(lanes):
        dx_out[0:seq, c * TILE : (c + 1) * TILE] = xp[c, PAD : PAD + seq]
        dx_out[seq:, c * TILE : (c + 1) * TILE] = xp[c, 2 * PAD + seq :]


def middle_stage(x1, aux, head, wts, rows, beta, rel, scale, final, seq):
    tokens = x1.shape[0]
    n_long = seq // 3
    short = n_long + TILE
    far = n_long // TILE
    vm = pl.BlockSpec(memory_space=pltpu.VMEM)
    return pl.pallas_call(
        functools.partial(middle_kernel, seq),
        in_specs=[vm] * 6 + [pl.BlockSpec(memory_space=pltpu.SMEM)] * 2 + [vm],
        out_specs=[vm] * 7,
        out_shape=[
            jax.ShapeDtypeStruct((tokens, D), F32),
            jax.ShapeDtypeStruct((2, D, 2 * D + FF), BF),
            jax.ShapeDtypeStruct((V, D), F32),
            jax.ShapeDtypeStruct((8, D), F32),
            jax.ShapeDtypeStruct((1, FF), F32),
            jax.ShapeDtypeStruct((1, 1), F32),
            jax.ShapeDtypeStruct((HEADS, fold_rows(far), TILE), F32),
        ],
        scratch_shapes=[
            pltpu.VMEM((D // TILE, tokens + 2 * PAD, TILE), F32),
            pltpu.VMEM((short, D), F32),
            pltpu.VMEM((4, PAIRS, short, PW), BF),
            pltpu.VMEM((PAIRS, PW, short), BF),
            pltpu.VMEM((PAIRS, 1, 2 * short), F32),
            pltpu.VMEM((short, FF), BF),
            pltpu.VMEM((short, FF), BF),
            pltpu.VMEM((short, D), F32),
            pltpu.VMEM((HEADS, far, TILE, TILE), F32),
            pltpu.VMEM((HEADS, far, TILE, TILE), F32),
            pltpu.VMEM((3, PAIRS, short, PW), BF),
        ]
        + state_scratch(n_long),
        compiler_params=params(60),
        name="middle_stage",
    )(x1, aux, head, wts, rows, beta, rel, scale, final)


def feed_back_kernel(
    dx, act, slope, middle, wts, rows, dm_out, d_feed, row_grads, d_beta, up, down
):
    step = pl.program_id(0)

    @pl.when(step == 0)
    def _():
        up[...] = jnp.zeros_like(up)
        down[...] = jnp.zeros_like(down)
        row_grads[...] = jnp.zeros_like(row_grads)
        d_beta[...] = jnp.zeros_like(d_beta)

    d_result = dx[...]
    d_branch = d_result.astype(BF)
    row_grads[2:3] += jnp.sum(d_branch.astype(F32), 0, keepdims=True)
    down[...] += mm(d_branch, act[...], TN)
    d_pre = (mm(d_branch, wts[1, :, 2 * D :]) * slope[...].astype(F32)).astype(BF)
    d_beta[...] += jnp.sum(d_pre.astype(F32), 0, keepdims=True)
    xhat, rstd = norm_stats(middle[...])
    second = (xhat * rows[2:3] + rows[3:4]).astype(BF)
    up[...] += mm(second, d_pre, TN)
    dn, d_gain, d_shift = norm_back(mm(d_pre, wts[0, :, 2 * D :], NT), xhat, rstd, rows[2:3])
    row_grads[0:1] += d_gain
    row_grads[1:2] += d_shift
    dm_out[...] = d_result + dn

    @pl.when(step == pl.num_programs(0) - 1)
    def _():
        d_feed[0] = up[...].astype(BF)
        d_feed[1] = down[...].astype(BF)


def feed_back(dx, act, slope, middle, wts, rows):
    tokens = dx.shape[0]

    def flat(width):
        return pl.BlockSpec((BLK, width), lambda i: (i, 0))

    return pl.pallas_call(
        feed_back_kernel,
        grid=(tokens // BLK,),
        in_specs=[flat(D), flat(FF), flat(FF), flat(D), whole_spec(wts.shape), whole_spec(rows.shape)],
        out_specs=[
            flat(D),
            whole_spec((2, D, FF)),
            whole_spec((8, D)),
            whole_spec((1, FF)),
        ],
        out_shape=[
            jax.ShapeDtypeStruct((tokens, D), F32),
            jax.ShapeDtypeStruct((2, D, FF), BF),
            jax.ShapeDtypeStruct((8, D), F32),
            jax.ShapeDtypeStruct((1, FF), F32),
        ],
        scratch_shapes=[pltpu.VMEM((D, FF), F32), pltpu.VMEM((D, FF), F32)],
        compiler_params=params(56),
        name="feed_back",
    )(dx, act, slope, middle, wts, rows)


def attention_back_kernel(
    long_blocks,
    dm,
    aux,
    ot,
    lse,
    q_all,
    k_all,
    v_all,
    embed,
    wts,
    rows,
    rel,
    d_attn,
    d_embed,
    row_grads,
    sums,
    bias,
    tiles,
    kt_all,
    dk_all,
    dv_all,
    dq_t,
    d_att,
    inner,
    weights,
    d_mixed,
):
    step = pl.program_id(0)
    blocks = pl.num_programs(0)
    i = blocks - 1 - step

    @pl.when(step == 0)
    def _():
        build_bias(rel, bias, bias.shape[1])
        tiles[...] = jnp.zeros_like(tiles)
        dk_all[...] = jnp.zeros_like(dk_all)
        dv_all[...] = jnp.zeros_like(dv_all)
        weights[...] = jnp.zeros_like(weights)
        d_embed[...] = jnp.zeros_like(d_embed)
        row_grads[...] = jnp.zeros_like(row_grads)

        def turn(n, carry):
            for pair in range(PAIRS):
                kt_all[n, pair] = k_all[n, pair].T
            return carry

        lax.fori_loop(0, blocks, turn, 0)

    d_middle = dm[...]
    d_mix = d_middle.astype(BF)
    weights[1, :, D:] += mm(ot[0].reshape(D, BLK), d_mix)
    out = mm(d_mix, wts[1, :, D : 2 * D], NT).astype(BF)
    for pair in range(PAIRS):
        d_att[pair] = out[:, pair * PW : (pair + 1) * PW]
    product = mm(wts[1, :, D : 2 * D], d_mix, NT).astype(BF).astype(F32) * ot[0].reshape(
        D, BLK
    ).astype(F32)
    for pair in range(PAIRS):
        at = pair * PW
        inner[pair] = jnp.concatenate(
            [
                jnp.sum(product[at : at + HD], 0, keepdims=True),
                jnp.sum(product[at + HD : at + PW], 0, keepdims=True),
            ],
            1,
        )
    first = jnp.where(i >= long_blocks, long_blocks, 0)

    def one_pair(pair, carry):
        queries = split_heads(q_all[i, pair])
        grads = split_heads(d_att[pair])
        dq_t[...] = jnp.zeros_like(dq_t)

        def with_block(j, far, diag):
            p, ds = score_back(
                k_all[j, pair],
                v_all[j, pair],
                queries,
                grads,
                lse[0, pair],
                inner[pair],
                bias,
                pair,
                far,
                diag,
                SUB,
                SUB,
                tiles,
            )
            dv_all[j, pair] += mm(p, grads)
            dk_all[j, pair] += mm(ds, queries)
            dq_t[...] += mm(kt_all[j, pair], ds)

        def earlier(j, inside):
            with_block(j, SUB * (i - j), False)
            return inside

        lax.fori_loop(first, i, earlier, 0)
        with_block(i, 0, True)
        total = dq_t[...]
        total = jnp.concatenate([total[:HD, :BLK], total[HD:, BLK:]], 0) * HD**-0.5
        d_mixed[0, pair] = total.T.astype(BF)
        d_mixed[1, pair] = dk_all[i, pair].astype(BF)
        d_mixed[2, pair] = dv_all[i, pair].astype(BF)
        return carry

    lax.fori_loop(0, PAIRS, one_pair, 0)
    d_in = jnp.concatenate([d_mixed[part, pair] for part in range(3) for pair in range(PAIRS)], 1)
    hot = one_hot(aux[:, 0:1]).astype(BF)
    xhat, rstd = norm_stats(mm(hot, embed[...]))
    normed = (xhat * rows[0:1] + rows[1:2]).astype(BF)
    weights[0] += mm(normed, d_in[:, : 2 * D], TN)
    weights[1, :, :D] += mm(normed, d_in[:, 2 * D :], TN)
    dx, d_gain, d_shift = norm_back(mm(d_in[:, : 2 * D], wts[0, :, : 2 * D], NT) + mm(d_in[:, 2 * D :], wts[1, :, :D], NT), xhat, rstd, rows[0:1])
    row_grads[0:1] += d_gain
    row_grads[1:2] += d_shift
    d_embed[...] += mm(hot, (d_middle + dx).astype(BF), TN)

    @pl.when(step == blocks - 1)
    def _():
        d_attn[...] = weights[...].astype(BF)
        fold_bias(tiles, sums, tiles.shape[1])


def attention_back(dm, aux, ot, lse, q, k, v, embed, wts, rows, rel, long_blocks):
    tokens = dm.shape[0]
    blocks = tokens // BLK
    far = SUB * long_blocks

    def turned(shape):
        return pl.BlockSpec(shape, lambda s: (blocks - 1 - s,) + (0,) * (len(shape) - 1))

    return pl.pallas_call(
        functools.partial(attention_back_kernel, long_blocks),
        grid=(blocks,),
        in_specs=[
            turned((BLK, D)),
            turned((BLK, aux.shape[1])),
            turned((1, PAIRS, PW, BLK)),
            turned((1, PAIRS, 1, 2 * BLK)),
            whole_spec(q.shape),
            whole_spec(k.shape),
            whole_spec(v.shape),
            whole_spec(embed.shape),
            whole_spec((2, D, 2 * D)),
            whole_spec(rows.shape),
            pl.BlockSpec(memory_space=pltpu.SMEM),
        ],
        out_specs=[
            whole_spec((2, D, 2 * D)),
            whole_spec((V, D)),
            whole_spec((8, D)),
            whole_spec((HEADS, fold_rows(far), TILE)),
        ],
        out_shape=[
            jax.ShapeDtypeStruct((2, D, 2 * D), BF),
            jax.ShapeDtypeStruct((V, D), F32),
            jax.ShapeDtypeStruct((8, D), F32),
            jax.ShapeDtypeStruct((HEADS, fold_rows(far), TILE), F32),
        ],
        scratch_shapes=[
            pltpu.VMEM((HEADS, far, TILE, TILE), F32),
            pltpu.VMEM((HEADS, far, TILE, TILE), F32),
            pltpu.VMEM((blocks, PAIRS, PW, BLK), BF),
            pltpu.VMEM((blocks, PAIRS, BLK, PW), F32),
            pltpu.VMEM((blocks, PAIRS, BLK, PW), F32),
            pltpu.VMEM((PW, 2 * BLK), F32),
            pltpu.VMEM((PAIRS, BLK, PW), BF),
            pltpu.VMEM((PAIRS, 1, 2 * BLK), F32),
            pltpu.VMEM((2, D, 2 * D), F32),
            pltpu.VMEM((3, PAIRS, BLK, PW), BF),
        ],
        compiler_params=params(60),
        name="attention_back",
    )(dm, aux, ot, lse, q, k, v, embed, wts, rows, rel)


MESH = pl.DeviceIdType.MESH
MISC_ROWS = 32
MISC_COLS = D + 128


class Place:
    def __init__(self, wide, narrow):
        self.W, self.N = wide, narrow
        self.slabs = wide * narrow
        self.c = lax.axis_index("rep")
        self.w = lax.axis_index("wide")
        self.n = lax.axis_index("narrow")
        hi, lo = self.n // 2, self.n % 2
        self.a0 = (1 - self.c) * hi + self.c * lo
        self.b0 = (1 - self.c) * lo + self.c * hi
        self.group = self.w // (wide // 2)

    def narrow_of(self, a, b):
        return a * (2 - self.c) + b * (1 + self.c)

    def slab(self, w, a, b):
        return w * self.N + self.narrow_of(a, b)

    def chip(self, w, a, b):
        return {"wide": w, "narrow": self.narrow_of(a, b)}

    def sibling(self):
        return {"rep": 1 - self.c}


def greet(devices):
    barrier = pltpu.get_barrier_semaphore()
    for device in devices:
        pl.semaphore_signal(barrier, inc=1, device_id=device, device_id_type=MESH)
    pl.semaphore_wait(barrier, len(devices))


def slab_form(rows, cols):
    return (rows, cols) if rows % 16 == 0 else (16, rows * cols // 16)


def gather_greetings(at):
    return [
        {"wide": lax.rem(at.w + 1, at.W)},
        {"wide": lax.rem(at.w + at.W - 1, at.W)},
        at.chip(at.w, at.a0, 1 - at.b0),
        at.chip(at.w, 1 - at.a0, at.b0),
        at.sibling(),
    ]


class GatherStream:
    def __init__(self, at, src, out, send, recv, local):
        self.at, self.src, self.out, self.send, self.recv = at, src, out, send, recv
        self.own = at.slab(at.w, at.a0, at.b0)
        self.keep = pltpu.make_async_copy(src, out.at[at.c, self.own], local)

    def copy(self, ref, slab, way, peer):
        return pltpu.make_async_remote_copy(
            src_ref=ref,
            dst_ref=self.out.at[self.at.c, slab],
            send_sem=self.send.at[way, slab],
            recv_sem=self.recv.at[1 if way == 4 else 0, slab],
            device_id=peer,
            device_id_type=MESH,
        )

    def arrived(self, slab, half, kind):
        pltpu.make_async_remote_copy(
            src_ref=self.out.at[half, slab],
            dst_ref=self.out.at[half, slab],
            send_sem=self.send.at[4, slab],
            recv_sem=self.recv.at[kind, slab],
            device_id=self.at.sibling(),
            device_id_type=MESH,
        ).wait_recv()

    def onward(self, w, mine, act, up, down):
        at = self.at
        slab = at.slab(w, at.a0, at.b0)
        ref = self.src if mine else self.out.at[at.c, slab]
        if up:

            @pl.when(at.w < at.W - 1)
            def _():
                act(self.copy(ref, slab, 0, {"wide": jnp.minimum(at.w + 1, at.W - 1)}))

        if down:

            @pl.when(at.w > 0)
            def _():
                act(self.copy(ref, slab, 1, {"wide": jnp.maximum(at.w - 1, 0)}))

        act(self.copy(ref, slab, 2, at.chip(at.w, at.a0, 1 - at.b0)))
        act(self.copy(ref, slab, 3, at.chip(at.w, 1 - at.a0, at.b0)))
        act(self.copy(ref, slab, 4, at.sibling()))

    def across(self, w, act):
        at = self.at
        slab = at.slab(w, at.a0, 1 - at.b0)
        ref = self.out.at[at.c, slab]
        act(self.copy(ref, slab, 3, at.chip(at.w, 1 - at.a0, at.b0)))
        act(self.copy(ref, slab, 4, at.sibling()))

    def last(self, w, act):
        at = self.at
        for b in (at.b0, 1 - at.b0):
            slab = at.slab(w, 1 - at.a0, b)
            act(self.copy(self.out.at[at.c, slab], slab, 4, at.sibling()))

    def both_sides(self, k, body):
        at = self.at

        @pl.when(at.w - k >= 0)
        def _():
            body(jnp.maximum(at.w - k, 0), True)

        @pl.when(at.w + k < at.W)
        def _():
            body(jnp.minimum(at.w + k, at.W - 1), False)

    def start(self):
        self.keep.start()
        self.onward(self.at.w, True, lambda copy: copy.start(), True, True)

    def run_across(self, w):
        self.arrived(self.at.slab(w, self.at.a0, 1 - self.at.b0), self.at.c, 0)
        self.across(w, lambda copy: copy.start())

    def run_last(self, w):
        for b in (self.at.b0, 1 - self.at.b0):
            self.arrived(self.at.slab(w, 1 - self.at.a0, b), self.at.c, 0)
        self.last(w, lambda copy: copy.start())

    def step(self, k):
        at = self.at

        def along(w, below):
            self.arrived(at.slab(w, at.a0, at.b0), at.c, 0)
            self.onward(w, False, lambda copy: copy.start(), below, not below)

        self.both_sides(k, along)
        self.both_sides(k, lambda w, below: self.run_across(w))
        self.both_sides(k, lambda w, below: self.run_last(w))

    def run(self):
        self.run_across(self.at.w)
        self.run_last(self.at.w)

        def body(k, carry):
            self.step(k)
            return carry

        lax.fori_loop(1, self.at.W, body, 0)

    def finish(self):
        at = self.at
        done = lambda copy: copy.wait_send()
        self.keep.wait()
        self.onward(at.w, True, done, True, True)
        self.across(at.w, done)
        self.last(at.w, done)

        def body(k, carry):
            self.both_sides(
                k, lambda w, below: self.onward(w, False, done, below, not below)
            )
            self.both_sides(k, lambda w, below: self.across(w, done))
            self.both_sides(k, lambda w, below: self.last(w, done))
            return carry

        lax.fori_loop(1, at.W, body, 0)

        def from_sibling(slab, carry):
            self.arrived(slab, 1 - at.c, 1)
            return carry

        lax.fori_loop(0, at.slabs, from_sibling, 0)


def gather_sems(slabs):
    return [
        pltpu.SemaphoreType.DMA((5, slabs)),
        pltpu.SemaphoreType.DMA((2, slabs)),
        pltpu.SemaphoreType.DMA,
    ]


def gather_kernel(wide, narrow, count, *refs):
    at = Place(wide, narrow)
    greet(gather_greetings(at))
    streams = [
        GatherStream(at, refs[i], refs[count + i], *refs[2 * count + 3 * i : 2 * count + 3 * i + 3])
        for i in range(count)
    ]
    for stream in streams:
        stream.start()
        stream.run()
    for stream in streams:
        stream.finish()


def gather_all(arrays, wide, narrow, collective_id):
    slabs = wide * narrow
    anywhere = pl.BlockSpec(memory_space=pl.ANY)
    scratch = []
    for _ in arrays:
        scratch += gather_sems(slabs)
    return pl.pallas_call(
        functools.partial(gather_kernel, wide, narrow, len(arrays)),
        in_specs=[anywhere] * len(arrays),
        out_specs=[anywhere] * len(arrays),
        out_shape=[jax.ShapeDtypeStruct((2, slabs) + x.shape, x.dtype) for x in arrays],
        scratch_shapes=scratch,
        compiler_params=params(16, collective_id=collective_id, has_side_effects=True),
        name="gather_all",
    )(*arrays)


class ScatterStream:
    def __init__(self, at, src, out, own, side, first, second, along, fin, sems):
        self.at, self.src, self.out = at, src, out
        self.own, self.side, self.first, self.second, self.along, self.fin = (
            own,
            side,
            first,
            second,
            along,
            fin,
        )
        self.local, self.side_sem, self.first_sem, self.second_sem, self.along_sem, self.fin_sem = sems
        self.levels = (at.W // 2).bit_length() - 1

    def remote(self, src, dst, sems, index, device):
        return pltpu.make_async_remote_copy(
            src_ref=src,
            dst_ref=dst,
            send_sem=sems.at[(0,) + index],
            recv_sem=sems.at[(1,) + index],
            device_id=device,
            device_id_type=MESH,
        )

    def side_copy(self, slab):
        c = self.at.c
        return self.remote(
            self.src.at[1 - c, slab], self.side.at[slab], self.side_sem, (slab,), self.at.sibling()
        )

    def own_copy(self):
        return pltpu.make_async_copy(self.src.at[self.at.c], self.own, self.local)

    def first_copy(self, w, b):
        at = self.at
        slab = at.slab(w, 1 - at.a0, b)
        return self.remote(
            self.own.at[slab],
            self.first.at[2 * w + b],
            self.first_sem,
            (2 * w + b,),
            at.chip(at.w, 1 - at.a0, at.b0),
        )

    def second_copy(self, w):
        at = self.at
        return self.remote(
            self.own.at[at.slab(w, at.a0, 1 - at.b0)],
            self.second.at[w],
            self.second_sem,
            (w,),
            at.chip(at.w, at.a0, 1 - at.b0),
        )

    def along_place(self, level):
        W = self.at.W
        return W - (W >> level), W >> (level + 1)

    def along_copy(self, level, k):
        at = self.at
        unit = 1 << level
        bit = (at.w // unit) % 2
        partner = at.w + unit * (1 - 2 * bit)
        start, _ = self.along_place(level)
        w = k * 2 * unit + partner % (2 * unit)
        return self.remote(
            self.own.at[at.slab(w, at.a0, at.b0)],
            self.along.at[start + k],
            self.along_sem,
            (start + k,),
            {"wide": partner},
        )

    def home(self):
        at = self.at
        return lax.rem(at.w + at.W // 2, at.W)

    def cross_copy(self):
        at = self.at
        return self.remote(
            self.own.at[at.slab(self.home(), at.a0, at.b0)],
            self.fin.at[at.c],
            self.fin_sem,
            (at.c,),
            {"wide": self.home(), "rep": at.group},
        )

    def over_copy(self):
        at = self.at
        return self.remote(
            self.own.at[at.slab(at.w, at.a0, at.b0)],
            self.fin.at[at.c],
            self.fin_sem,
            (at.c,),
            at.sibling(),
        )

    def start(self):
        at = self.at
        self.own_copy().start()
        other = 1 - at.c
        hi, lo = at.n // 2, at.n % 2
        a1 = (1 - other) * hi + other * lo
        b1 = (1 - other) * lo + other * hi
        for a, b in ((1 - a1, 0), (1 - a1, 1), (a1, 1 - b1), (a1, b1)):

            def body(w, carry, a=a, b=b):
                self.side_copy(w * at.N + a * (2 - other) + b * (1 + other)).start()
                return carry

            lax.fori_loop(0, at.W, body, 0)

    def total(self, slab):
        self.side_copy(slab).wait_recv()
        return self.own[slab].astype(F32) + self.side[slab].astype(F32)

    def wait_first(self, w, b):
        self.first_copy(w, b).wait_recv()
        return self.first[2 * w + b].astype(F32)

    def stage_first(self):
        at = self.at
        self.own_copy().wait()

        def body(k, carry):
            w, b = k // 2, k % 2
            slab = at.slab(w, 1 - at.a0, b)
            self.own[slab] = self.total(slab).astype(BF)
            self.first_copy(w, b).start()
            return carry

        lax.fori_loop(0, 2 * at.W, body, 0)

    def stage_second(self):
        at = self.at

        def body(w, carry):
            slab = at.slab(w, at.a0, 1 - at.b0)
            self.own[slab] = (self.total(slab) + self.wait_first(w, 1 - at.b0)).astype(BF)
            self.second_copy(w).start()
            return carry

        lax.fori_loop(0, at.W, body, 0)

    def column(self, w, levels):
        at = self.at
        value = self.total(at.slab(w, at.a0, at.b0)) + self.wait_first(w, at.b0)
        self.second_copy(w).wait_recv()
        value = value + self.second[w].astype(F32)
        for level in range(levels):
            start, _ = self.along_place(level)
            k = w // (2 << level)
            self.along_copy(level, k).wait_recv()
            value = value + self.along[start + k].astype(F32)
        return value

    def stage_along(self):
        at = self.at
        for level in range(self.levels):
            unit = 1 << level
            partner = at.w + unit * (1 - 2 * ((at.w // unit) % 2))

            def body(k, carry, level=level, unit=unit, partner=partner):
                w = k * 2 * unit + partner % (2 * unit)
                self.own[at.slab(w, at.a0, at.b0)] = self.column(w, level).astype(BF)
                self.along_copy(level, k).start()
                return carry

            lax.fori_loop(0, self.along_place(level)[1], body, 0)

    def stage_home(self):
        at = self.at
        away = at.slab(self.home(), at.a0, at.b0)
        self.own[away] = self.column(self.home(), self.levels).astype(BF)
        self.cross_copy().start()
        mine = at.slab(at.w, at.a0, at.b0)
        value = self.column(at.w, self.levels)
        self.own[mine] = value.astype(BF)

        @pl.when(at.c != at.group)
        def _():
            self.over_copy().start()

        self.out[at.c] = value

    def finish(self):
        at = self.at

        @pl.when(at.c == at.group)
        def _():
            self.fin_wait(1 - at.c)
            self.out[1 - at.c] = self.fin[1 - at.c].astype(F32)

        @pl.when(at.c != at.group)
        def _():
            for half in range(2):
                self.fin_wait(half)
                self.out[half] = self.fin[half].astype(F32)
            self.over_copy().wait_send()

        self.cross_copy().wait_send()

        def sides(slab, carry):
            self.side_copy(slab).wait_send()
            return carry

        lax.fori_loop(0, at.slabs, sides, 0)

        def firsts(k, carry):
            self.first_copy(k // 2, k % 2).wait_send()
            return carry

        lax.fori_loop(0, 2 * at.W, firsts, 0)

        def seconds(w, carry):
            self.second_copy(w).wait_send()
            return carry

        lax.fori_loop(0, at.W, seconds, 0)
        for level in range(self.levels):

            def alongs(k, carry, level=level):
                self.along_copy(level, k).wait_send()
                return carry

            lax.fori_loop(0, self.along_place(level)[1], alongs, 0)

    def fin_wait(self, half):
        self.remote(
            self.fin.at[half], self.fin.at[half], self.fin_sem, (half,), self.at.sibling()
        ).wait_recv()


def scatter_scratch(wide, narrow, form):
    slabs = wide * narrow
    sizes = (slabs, slabs, 2 * wide, wide, max(wide - 2, 1), 2)
    dma = pltpu.SemaphoreType.DMA
    return [pltpu.VMEM((size,) + form, BF) for size in sizes] + [dma] + [
        dma((2, size)) for size in sizes[1:]
    ]


def scatter_greetings(at):
    out = [
        at.chip(at.w, at.a0, 1 - at.b0),
        at.chip(at.w, 1 - at.a0, at.b0),
        at.sibling(),
    ]
    for level in range((at.W // 2).bit_length() - 1):
        unit = 1 << level
        out.append({"wide": at.w + unit * (1 - 2 * ((at.w // unit) % 2))})
    out.append({"wide": lax.rem(at.w + at.W // 2, at.W)})
    out.append({"wide": lax.rem(at.w + at.W // 2, at.W), "rep": 1 - at.c})
    return out


def scatter_kernel(wide, narrow, count, *refs):
    at = Place(wide, narrow)
    greet(scatter_greetings(at))
    bits, bits_out = refs[count], refs[2 * count + 1]
    bits_in, bits_sem = refs[2 * count + 2], refs[2 * count + 3]
    rest = refs[2 * count + 4 :]
    streams = []
    for i in range(count):
        part = rest[12 * i : 12 * i + 12]
        streams.append(ScatterStream(at, refs[i], refs[count + 1 + i], *part[:6], part[6:]))
    tiny = pltpu.make_async_remote_copy(
        src_ref=bits,
        dst_ref=bits_in,
        send_sem=bits_sem.at[0],
        recv_sem=bits_sem.at[1],
        device_id=at.sibling(),
        device_id_type=MESH,
    )
    tiny.start()
    for stream in streams:
        stream.start()
    for stream in streams:
        stream.stage_first()
    for stream in streams:
        stream.stage_second()
    for stream in streams:
        stream.stage_along()
    for stream in streams:
        stream.stage_home()
    for stream in streams:
        stream.finish()
    tiny.wait()
    bits_out[...] = jnp.where(at.c == at.group, bits[...] + bits_in[...], 0.0)


def scatter_all(arrays, bits, wide, narrow, collective_id):
    count = len(arrays)
    vm = pl.BlockSpec(memory_space=pltpu.VMEM)
    anywhere = pl.BlockSpec(memory_space=pl.ANY)
    scratch = [pltpu.VMEM(bits.shape, F32), pltpu.SemaphoreType.DMA((2,))]
    for x in arrays:
        scratch += scatter_scratch(wide, narrow, x.shape[2:])
    return pl.pallas_call(
        functools.partial(scatter_kernel, wide, narrow, count),
        in_specs=[anywhere] * count + [vm],
        out_specs=[vm] * (count + 1),
        out_shape=[jax.ShapeDtypeStruct((2,) + x.shape[2:], F32) for x in arrays]
        + [jax.ShapeDtypeStruct(bits.shape, F32)],
        scratch_shapes=scratch,
        compiler_params=params(60, collective_id=collective_id, has_side_effects=True),
        name="scatter_all",
    )(*arrays, bits)


def adam_update(weight, moment, square, gradient, decay, rate):
    moment = BETA_ONE * moment + (1.0 - BETA_ONE) * gradient
    square = BETA_TWO * square + (1.0 - BETA_TWO) * gradient * gradient
    fixed_moment = moment / (1.0 - BETA_ONE**STEP)
    fixed_square = square / (1.0 - BETA_TWO**STEP)
    delta = -rate * (fixed_moment / (jnp.sqrt(fixed_square) + ADAM_EPS) + decay * weight)
    return (moment, square, delta)


def update_partners(wide, narrow):
    out = []
    n, w = lax.axis_index("narrow"), lax.axis_index("wide")
    for axis, here, size in (("narrow", n, narrow), ("wide", w, wide)):
        unit = 1
        while unit < size:
            out.append({axis: here + unit * (1 - 2 * ((here // unit) % 2))})
            unit *= 2
    return out


def update_kernel(wide, narrow, *refs):
    g_misc, g_feed, g_attn, g_short, bits = refs[:5]
    weights, moments, squares, outers, averages = (refs[5 + 4 * k : 9 + 4 * k] for k in range(5))
    scalars = refs[25]
    new_m, new_s, new_w, new_o, new_a = (refs[26 + 4 * k : 30 + 4 * k] for k in range(5))
    sums, arrived, sum_sems = refs[46:49]
    mine, other, delta_sems = refs[49:53], refs[53:57], refs[57]
    partners = update_partners(wide, narrow)
    sibling = {"rep": 1 - lax.axis_index("rep")}
    greet(partners + [sibling])

    squared = jnp.zeros((1, 1), F32)
    for ref in (g_misc, g_feed, g_attn, g_short):
        for half in range(2):
            value = ref[half]
            value = jnp.sum(value * value, 0, keepdims=True)
            squared = squared + jnp.sum(value, 1, keepdims=True)
    row = lax.broadcasted_iota(jnp.int32, (8, 128), 0)
    total = jnp.where(row == 0, squared, jnp.where(row == 1, bits[...], 0.0))
    for k, partner in enumerate(partners):
        sums[k] = total
        copy = pltpu.make_async_remote_copy(
            src_ref=sums.at[k],
            dst_ref=arrived.at[k],
            send_sem=sum_sems.at[0, k],
            recv_sem=sum_sems.at[1, k],
            device_id=partner,
            device_id_type=MESH,
        )
        copy.start()
        copy.wait()
        total = total + arrived[k]
    norm = jnp.sqrt(total[0:1, 0:1])
    scalars[...] = jnp.where(row == 0, norm, total)
    factor = jnp.minimum(1.0, CLIP_AT / (norm + 1e-06))

    table_rows, columns = weights[0].shape[1], weights[3].shape[1]
    wide_cols = slice(D, D + columns)
    pieces = []
    for half in range(2):
        pieces.append((2, 1, half, FF, lambda h: g_short[h, :, 2 * D :], DECAY, RATE))
        pieces.append((1, 1, half, 2 * D, lambda h: g_short[h, :, : 2 * D], DECAY, RATE))
        pieces.append((2, 0, half, FF, lambda h: g_feed[h], DECAY, RATE))
        pieces.append((1, 0, half, 2 * D, lambda h: g_attn[h], DECAY, RATE))
    for layer in range(2):
        pieces.append(
            (0, layer, 0, D, lambda h, layer=layer: g_misc[layer, :table_rows, :D], DECAY, RATE_TABLE)
        )
    for which, layer, half, width, gradient, decay, rate in pieces:
        at = (layer, slice(None), slice(half * width, (half + 1) * width))
        m, s, delta = adam_update(
            weights[which][at],
            moments[which][at],
            squares[which][at],
            gradient(half) * factor,
            decay,
            rate,
        )
        new_m[which][at] = m
        new_s[which][at] = s
        mine[which][at] = delta.astype(mine[which].dtype)
    m, s, delta = adam_update(
        weights[3][...],
        moments[3][...],
        squares[3][...],
        g_misc[0, :VEC, wide_cols] * factor,
        0.0,
        RATE_TABLE,
    )
    new_m[3][...] = m
    new_s[3][...] = s
    mine[3][...] = delta
    copies = [
        pltpu.make_async_remote_copy(
            src_ref=mine[which],
            dst_ref=other[which],
            send_sem=delta_sems.at[0, which],
            recv_sem=delta_sems.at[1, which],
            device_id=sibling,
            device_id_type=MESH,
        )
        for which in range(4)
    ]
    for copy in copies:
        copy.start()
    for which in (2, 1, 0, 3):
        copies[which].wait()
        parts = [()] if which == 3 else [(0,), (1,)]
        for at in parts:
            at = at + (Ellipsis,)
            delta = (mine[which][at].astype(F32) + other[which][at].astype(F32)) * 0.5
            outer = OUTER_MOM * outers[which][at] + delta
            weight = weights[which][at] + OUTER_RATE * (delta + OUTER_MOM * outer)
            new_o[which][at] = outer
            new_w[which][at] = weight
            new_a[which][at] = EVAL_KEEP * averages[which][at] + (1.0 - EVAL_KEEP) * weight


def update(grads, bits, arrays, wide, narrow, collective_id):
    weights = arrays[:4]
    stages = (wide * narrow).bit_length() - 1
    vm = pl.BlockSpec(memory_space=pltpu.VMEM)
    like = [jax.ShapeDtypeStruct(x.shape, F32) for x in weights]
    kinds = [BF if x.shape[-2] % 16 == 0 else F32 for x in weights]
    deltas = [pltpu.VMEM(x.shape, kind) for x, kind in zip(weights, kinds)]
    dma = pltpu.SemaphoreType.DMA
    return pl.pallas_call(
        functools.partial(update_kernel, wide, narrow),
        in_specs=[vm] * 25,
        out_specs=[vm] * 21,
        out_shape=[jax.ShapeDtypeStruct((8, 128), F32)] + like * 5,
        scratch_shapes=[
            pltpu.VMEM((stages, 8, 128), F32),
            pltpu.VMEM((stages, 8, 128), F32),
            dma((2, stages)),
        ]
        + deltas
        + deltas
        + [dma((2, 4))],
        compiler_params=params(60, collective_id=collective_id, has_side_effects=True),
        name="update",
    )(*grads, bits, *arrays)


def local_gradients(byte_ids, live_mask, tables, wts, vec, count):
    seq = byte_ids.shape[1]
    long_blocks = seq // BLK
    weight = jnp.concatenate([live_mask[:, 1:], jnp.zeros_like(live_mask[:, :1])], 1)
    info = jnp.stack([byte_ids, jnp.roll(byte_ids, -1, 1), weight, weight], -1)
    aux = jnp.concatenate([info[0], info[1, :BLK]], 0)
    scale = (1.0 / (count * LOG_TWO)).reshape(1, 1)
    rows = [
        jnp.concatenate([vec[2 + 5 * l : 7 + 5 * l], jnp.zeros((3, D), F32)], 0) for l in range(2)
    ]
    bias_rows = 2 * FF // D
    beta = vec[12 : 12 + bias_rows].reshape(2, 1, FF)
    rel = vec[12 + bias_rows :].reshape(2, HEADS, NB)
    x1, middle, q, k, v, ot, lse, act, slope = full_forward(
        aux, tables[0], wts[0], rows[0], beta[0], rel[0], long_blocks
    )
    d_x1, d_short, d_head, short_rows, d_beta_1, bits, sums_1 = middle_stage(
        x1, aux, tables[1], wts[1], rows[1], beta[1], rel[1], scale, vec[0:2], seq
    )
    d_middle, d_feed, feed_rows, d_beta_0 = feed_back(d_x1, act, slope, middle, wts[0], rows[0])
    d_attn, d_embed, attn_rows, sums_0 = attention_back(
        d_middle, aux, ot, lse, q, k, v, tables[0], wts[0], rows[0], rel[0], long_blocks
    )

    def d_rel(sums, far):
        fold = fold_matrix(far)
        return jnp.dot(jnp.sum(sums, -1), fold, precision=lax.Precision.HIGHEST).reshape(1, -1)

    d_vec = jnp.concatenate(
        [
            short_rows[0:2],
            attn_rows[0:2],
            feed_rows[0:3],
            short_rows[2:7],
            d_beta_0.reshape(-1, D),
            d_beta_1.reshape(-1, D),
            jnp.concatenate([d_rel(sums_0, long_blocks * SUB), d_rel(sums_1, seq // 3 // TILE)], 1),
        ],
        0,
    )
    return bits, (d_embed, d_head), d_feed, d_attn, d_short, d_vec


def pad_to(x, rows, cols):
    return jnp.pad(x, [(0, 0)] * (x.ndim - 2) + [(0, rows - x.shape[-2]), (0, cols - x.shape[-1])])


def per_device(wide, narrow, byte_ids, live_mask, *arrays):
    tables, attention, feed_forward, vectors = arrays[:4]
    slabs = wide * narrow
    core = lax.axis_index("rep")
    group = lax.axis_index("wide") // (wide // 2)
    rows = attention.shape[1]
    form = slab_form(rows, 2 * D + FF)

    axes = ("rep", "wide", "narrow")
    moves = []
    for r in range(2):
        for w in range(wide):
            for n in range(narrow):
                to = (w % 2, r * (wide // 2) + w // 2, n)
                moves.append(((r * wide + w) * narrow + n, (to[0] * wide + to[1]) * narrow + to[2]))
    moved = lax.ppermute(byte_ids + V * live_mask, axes, moves)
    ids, lives = moved % V, moved // V

    def half_of(x, width):
        return lax.dynamic_slice_in_dim(x, core * width, width, 1)

    packed = [
        jnp.concatenate([half_of(attention[l], 2 * D), half_of(feed_forward[l], FF)], 1)
        .astype(BF)
        .reshape(form)
        for l in range(2)
    ]
    own_count = jnp.sum(live_mask[:, 1:])
    digits = jnp.stack([own_count // 64, own_count % 64]).astype(F32).reshape(1, 2)
    side = jnp.concatenate(
        [pad_to(vectors, 24, 128), pad_to(digits, MISC_ROWS - 24, 128)], 0
    )
    misc = jnp.concatenate([pad_to(tables[core], MISC_ROWS, D), side], 1).astype(BF)
    misc_all, *wts = gather_all([misc] + packed, wide, narrow, 1)
    wts = [w.reshape(2, D, 2 * D + FF) for w in wts]
    table_rows = tables.shape[1]
    full_tables = misc_all[:, :, :table_rows, :D].reshape(2, V, D)
    cols = vectors.shape[1]
    vec = misc_all[0, :, :VEC, D : D + cols].astype(F32).transpose(1, 0, 2).reshape(VEC, D)
    tally = misc_all[:, :, 24, D : D + 2].astype(F32)
    counts = jnp.sum(tally[:, :, 0] * 64.0 + tally[:, :, 1], 1)

    bits, d_tables, d_feed, d_attn, d_short, d_vec = local_gradients(
        ids, lives, full_tables, wts, vec, counts[group]
    )

    d_vec = pad_to(d_vec.reshape(VEC, slabs, cols).transpose(1, 0, 2), MISC_ROWS, 128)
    d_misc = jnp.stack(
        [
            jnp.concatenate([pad_to(d.reshape(slabs, table_rows, D), MISC_ROWS, D), extra], -1)
            for d, extra in zip(d_tables, (d_vec, jnp.zeros_like(d_vec)))
        ]
    ).astype(BF)
    parts = [d_misc] + [
        d.reshape((2, slabs) + slab_form(rows, d.shape[-1])) for d in (d_short, d_feed, d_attn)
    ]
    *sums, bits = scatter_all(parts, jnp.broadcast_to(bits, (8, 128)), wide, narrow, 2)
    g_misc, g_short, g_feed, g_attn = sums
    grads = [g_misc] + [g.reshape(2, rows, -1) for g in (g_feed, g_attn, g_short)]
    states = [x[0] if 4 <= k < 12 else x for k, x in enumerate(arrays)]
    scalars, *new = update(grads, bits, states, wide, narrow, 3)
    new = [x[None] if k < 8 else x for k, x in enumerate(new)]
    return (scalars[1, :1], counts[core].reshape(1), scalars[0, :1], *new)


def solution(mesh):
    rows = P(("rep", "wide", "narrow"), None)
    split = (
        P(None, ("wide", "narrow"), None),
        P(None, ("wide", "narrow"), None),
        P(None, ("wide", "narrow"), None),
        P(None, ("wide", "narrow")),
    )
    own = tuple(P("rep", *spec) for spec in split)
    return jax.shard_map(
        functools.partial(per_device, mesh.shape["wide"], mesh.shape["narrow"]),
        mesh=mesh,
        in_specs=(rows, rows) + split + own + own + split + split,
        out_specs=(P("rep"),) * 3 + own + own + split * 3,
        check_vma=False,
    )
```

```python
import functools
import math

import jax
import jax.numpy as jnp
import numpy as np
from jax import lax
from jax.experimental import pallas as pl
from jax.experimental.pallas import tpu as pltpu
from jax.sharding import PartitionSpec as P

D = 512
HEADS = 8
HD = 64
FF = 2048
V = 256
NB = 32
STEP = 10
VEC = 21
EDGES = (1, 2, 3, 4, 5, 6, 7, 8, 10, 12, 14, 16, 20, 24, 28, 32, 40, 48, 64, 80, 96, 128, 160, 192)
EDGES = EDGES + (256, 320, 384, 512, 640, 768, 1024)
NEG = -1000000000.0
EPS = 1e-05
LOG_TWO = math.log(2.0)
RATE = 0.01
RATE_TABLE = 0.2
BETA_ONE = 0.9
BETA_TWO = 0.95
ADAM_EPS = 1e-08
DECAY = 0.1
CLIP_AT = 0.02
OUTER_RATE = 0.7
OUTER_MOM = 0.9
EVAL_KEEP = 0.9

TILE = 128
BLK = 384
SUB = BLK // TILE
PAIRS = HEADS // 2
PW = 2 * HD
GELU_C = math.sqrt(2.0 / math.pi)
GELU_A = 0.044715

BF = jnp.bfloat16
F32 = jnp.float32
NN = (((1,), (0,)), ((), ()))
NT = (((1,), (1,)), ((), ()))
TN = (((0,), (0,)), ((), ()))


def mm(left, right, dims=NN):
    return lax.dot_general(left, right, dims, preferred_element_type=F32)


def spans(count):
    out = []
    for d in range(count):
        lo, hi = max(TILE * d - (TILE - 1), 0), TILE * d + TILE - 1
        base = sum(e <= lo for e in EDGES)
        out.append((base, [(e, k + 1) for k, e in enumerate(EDGES) if lo < e <= hi]))
    return out


def fold_matrix(count):
    rows = []
    for base, edges in spans(count):
        row = np.zeros(NB, np.float32)
        row[base] += 1
        rows.append(row)
        for _, bucket in edges:
            row = np.zeros(NB, np.float32)
            row[bucket] += 1
            row[bucket - 1] -= 1
            rows.append(row)
    return np.stack(rows)


def tile_distance(d):
    keys = lax.broadcasted_iota(jnp.int32, (TILE, TILE), 0)
    queries = lax.broadcasted_iota(jnp.int32, (TILE, TILE), 1)
    return TILE * d + queries - keys


def build_bias(rel, bias, count):
    for d, (base, edges) in enumerate(spans(count)):
        distance = tile_distance(d)

        def one_head(h, carry, d=d, base=base, edges=edges, distance=distance):
            tile = jnp.full((TILE, TILE), rel[h, base], F32)
            for edge, bucket in edges:
                tile = jnp.where(distance >= edge, rel[h, bucket], tile)
            if d == 0:
                tile = jnp.where(distance < 0, NEG, tile)
            bias[h, d] = tile
            return carry

        lax.fori_loop(0, HEADS, one_head, 0)


def fold_bias(tiles, sums, count):
    at = 0
    for d, (_, edges) in enumerate(spans(count)):
        distance = tile_distance(d)

        def one_head(h, carry, d=d, edges=edges, distance=distance, at=at):
            tile = tiles[h, d]
            sums[h, at : at + 1] = jnp.sum(tile, 0, keepdims=True)
            for n, (edge, _) in enumerate(edges):
                sums[h, at + 1 + n : at + 2 + n] = jnp.sum(
                    jnp.where(distance >= edge, tile, 0.0), 0, keepdims=True
                )
            return carry

        lax.fori_loop(0, HEADS, one_head, 0)
        at += 1 + len(edges)


def fold_rows(count):
    return sum(1 + len(edges) for _, edges in spans(count))


def norm_stats(x):
    centered = x - jnp.mean(x, -1, keepdims=True)
    rstd = lax.rsqrt(jnp.mean(centered * centered, -1, keepdims=True) + EPS)
    return centered * rstd, rstd


def norm_back(dy, xhat, rstd, gain):
    t = dy * gain
    dx = rstd * (
        t - jnp.mean(t, -1, keepdims=True) - xhat * jnp.mean(t * xhat, -1, keepdims=True)
    )
    return dx, jnp.sum(dy * xhat, 0, keepdims=True), jnp.sum(dy, 0, keepdims=True)


def gelu_pair(u):
    square = u * u
    tanh = jnp.tanh(GELU_C * u * (1.0 + GELU_A * square))
    half = 0.5 * (1.0 + tanh)
    slope = half + 0.5 * u * (1.0 - tanh * tanh) * (GELU_C + 3.0 * GELU_C * GELU_A * square)
    return u * half, slope


def split_heads(pair):
    lane = lax.broadcasted_iota(jnp.int32, pair.shape, 1)
    zero = jnp.zeros_like(pair)
    return jnp.concatenate(
        [jnp.where(lane < HD, pair, zero), jnp.where(lane >= HD, pair, zero)], 0
    )


def cell(block, kb, e, qa, nq):
    return block[kb * TILE : (kb + 1) * TILE, (e * nq + qa) * TILE : (e * nq + qa + 1) * TILE]


def softmax_step(keys, values_t, queries, bias, pair, far, diag, nq, nk, state):
    top, total, acc = state
    raw = mm(keys, queries, NT)
    scores = {}
    for e in range(2):
        for qa in range(nq):
            for kb in range(nk):
                if diag and kb > qa:
                    continue
                scores[kb, e, qa] = cell(raw, kb, e, qa, nq) + bias[2 * pair + e, far + qa - kb]
    highest = []
    for e in range(2):
        for qa in range(nq):
            column = [scores[kb, e, qa] for kb in range(nk) if (kb, e, qa) in scores]
            highest.append(jnp.max(functools.reduce(jnp.maximum, column), 0, keepdims=True))
    old_top = top[...]
    new_top = jnp.maximum(old_top, jnp.concatenate(highest, 1))
    alpha = jnp.exp(old_top - new_top)
    sums = []
    columns = []
    for e in range(2):
        for qa in range(nq):
            at = (e * nq + qa) * TILE
            ceiling = new_top[:, at : at + TILE]
            parts, adds = [], None
            for kb in range(nk):
                if (kb, e, qa) not in scores:
                    parts.append(jnp.zeros((TILE, TILE), BF))
                    continue
                p = jnp.exp(scores[kb, e, qa] - ceiling)
                adds = p if adds is None else adds + p
                parts.append(p.astype(BF))
            sums.append(jnp.sum(adds, 0, keepdims=True))
            columns.append(jnp.concatenate(parts, 0))
    top[...] = new_top
    total[...] = alpha * total[...] + jnp.concatenate(sums, 1)
    acc[...] = alpha * acc[...] + mm(values_t, jnp.concatenate(columns, 1))


def softmax_start(state):
    top, total, acc = state
    top[...] = jnp.full(top.shape, NEG, F32)
    total[...] = jnp.zeros(total.shape, F32)
    acc[...] = jnp.zeros(acc.shape, F32)


def softmax_end(state, n):
    top, total, acc = state
    scaled = acc[...] / total[...]
    out = jnp.concatenate([scaled[:HD, :n], scaled[HD:, n:]], 0).astype(BF)
    return out, top[...] + jnp.log(total[...])


def score_back(keys, values, queries, grads, logsum, inner, bias, pair, far, diag, nq, nk, tiles):
    raw = mm(keys, queries, NT)
    d_p = mm(values, grads, NT)
    probs, scores = {}, {}
    for e in range(2):
        for diff in range(-(nk - 1), nq):
            total = None
            if diag and diff < 0:
                continue
            for kb in range(nk):
                qa = kb + diff
                if qa < 0 or qa >= nq:
                    continue
                at = (e * nq + qa) * TILE
                p = jnp.exp(
                    cell(raw, kb, e, qa, nq)
                    + bias[2 * pair + e, far + diff]
                    - logsum[:, at : at + TILE]
                )
                ds = p * (cell(d_p, kb, e, qa, nq) - inner[:, at : at + TILE])
                total = ds if total is None else total + ds
                probs[kb, e, qa] = p.astype(BF)
                scores[kb, e, qa] = ds.astype(BF)
            tiles[2 * pair + e, far + diff] += total

    def whole(parts):
        empty = jnp.zeros((TILE, TILE), BF)
        return jnp.concatenate(
            [
                jnp.concatenate([parts.get((kb, e, qa), empty) for kb in range(nk)], 0)
                for e in range(2)
                for qa in range(nq)
            ],
            1,
        )

    return whole(probs), whole(scores)


def one_hot(column):
    return column == lax.broadcasted_iota(jnp.int32, (column.shape[0], V), 1)


def full_forward_kernel(
    long_blocks,
    aux,
    embed,
    wts,
    rows,
    beta,
    rel,
    x1_out,
    middle_out,
    q_out,
    k_out,
    v_out,
    ot_out,
    lse_out,
    act_out,
    slope_out,
    bias,
    k_all,
    vt_all,
    *state,
):
    step = pl.program_id(0)

    @pl.when(step == 0)
    def _():
        build_bias(rel, bias, bias.shape[1])

    hot = one_hot(aux[:, 0:1]).astype(BF)
    x = mm(hot, embed[...])
    xhat, _ = norm_stats(x)
    normed = (xhat * rows[0:1] + rows[1:2]).astype(BF)
    queries = (mm(normed, wts[0, :, :D]) * HD**-0.5).astype(BF)
    keys = mm(normed, wts[0, :, D : 2 * D]).astype(BF)
    values = mm(normed, wts[1, :, :D]).astype(BF)
    for pair in range(PAIRS):
        cols = slice(pair * PW, (pair + 1) * PW)
        q_out[0, pair] = queries[:, cols]
        k_out[0, pair] = keys[:, cols]
        v_out[0, pair] = values[:, cols]
        k_all[step, pair] = keys[:, cols]
        vt_all[step, pair] = values[:, cols].T
    first = jnp.where(step >= long_blocks, long_blocks, 0)

    def one_pair(pair, carry):
        both = split_heads(q_out[0, pair])
        softmax_start(state)

        def earlier(j, inner):
            far = SUB * (step - j)
            softmax_step(
                k_all[j, pair], vt_all[j, pair], both, bias, pair, far, False, SUB, SUB, state
            )
            return inner

        lax.fori_loop(first, step, earlier, 0)
        softmax_step(
            k_all[step, pair], vt_all[step, pair], both, bias, pair, 0, True, SUB, SUB, state
        )
        ot_out[0, pair], lse_out[0, pair] = softmax_end(state, BLK)
        return carry

    lax.fori_loop(0, PAIRS, one_pair, 0)
    attended = ot_out[0].reshape(D, BLK).T
    middle = x + mm(attended, wts[1, :, D : 2 * D])
    middle_out[...] = middle
    xhat, _ = norm_stats(middle)
    second = (xhat * rows[2:3] + rows[3:4]).astype(BF)
    active, slope = gelu_pair(mm(second, wts[0, :, 2 * D :]) + beta[...])
    active = active.astype(BF)
    act_out[...] = active
    slope_out[...] = slope.astype(BF)
    x1_out[...] = middle + mm(active, wts[1, :, 2 * D :], NT) + rows[4:5]


def whole_spec(shape):
    return pl.BlockSpec(shape, lambda i: (0,) * len(shape), pipeline_mode=pl.Buffered(1))


def params(mib, **more):
    return pltpu.CompilerParams(vmem_limit_bytes=mib * 2**20, **more)


def state_scratch(n):
    return [pltpu.VMEM((1, 2 * n), F32), pltpu.VMEM((1, 2 * n), F32), pltpu.VMEM((PW, 2 * n), F32)]


def full_forward(aux, embed, wts, rows, beta, rel, long_blocks):
    tokens = aux.shape[0]
    blocks = tokens // BLK
    far = SUB * long_blocks

    def heads(n, width):
        return (
            jax.ShapeDtypeStruct((blocks, PAIRS, n, width), BF),
            pl.BlockSpec((1, PAIRS, n, width), lambda i: (i, 0, 0, 0)),
        )

    def flat(width, kind):
        return (
            jax.ShapeDtypeStruct((tokens, width), kind),
            pl.BlockSpec((BLK, width), lambda i: (i, 0)),
        )

    outs = [flat(D, F32), flat(D, F32)] + [heads(BLK, PW)] * 3 + [heads(PW, BLK)]
    outs.append(
        (
            jax.ShapeDtypeStruct((blocks, PAIRS, 1, 2 * BLK), F32),
            pl.BlockSpec((1, PAIRS, 1, 2 * BLK), lambda i: (i, 0, 0, 0)),
        )
    )
    outs += [flat(FF, BF)] * 2
    return pl.pallas_call(
        functools.partial(full_forward_kernel, long_blocks),
        grid=(blocks,),
        in_specs=[
            pl.BlockSpec((BLK, aux.shape[1]), lambda i: (i, 0)),
            whole_spec(embed.shape),
            whole_spec(wts.shape),
            whole_spec(rows.shape),
            whole_spec(beta.shape),
            pl.BlockSpec(memory_space=pltpu.SMEM),
        ],
        out_specs=[spec for _, spec in outs],
        out_shape=[shape for shape, _ in outs],
        scratch_shapes=[
            pltpu.VMEM((HEADS, far, TILE, TILE), F32),
            pltpu.VMEM((blocks, PAIRS, BLK, PW), BF),
            pltpu.VMEM((blocks, PAIRS, PW, BLK), BF),
        ]
        + state_scratch(BLK),
        compiler_params=params(56),
        name="full_forward",
    )(aux, embed, wts, rows, beta, rel)


PAD = 8


def middle_kernel(
    seq,
    x1,
    aux,
    head,
    wts,
    rows,
    beta,
    rel,
    scale,
    final,
    dx_out,
    d_attn,
    d_feed,
    d_head,
    row_grads,
    d_beta,
    bits_out,
    sums,
    xp,
    pooled,
    mixed,
    ot,
    lse,
    active_s,
    slope_s,
    middle_s,
    bias,
    tiles,
    d_mixed,
    *state,
):
    n_long = seq // 3
    spots = ((PAD, 0, n_long), (2 * PAD + seq, n_long, TILE))
    build_bias(rel, bias, bias.shape[1])
    tiles[...] = jnp.zeros_like(tiles)
    lanes = D // TILE
    for c in range(lanes):
        xp[c, 0:PAD] = jnp.zeros((PAD, TILE), F32)
        xp[c, PAD + seq : 2 * PAD + seq] = jnp.zeros((PAD, TILE), F32)
        xp[c, PAD : PAD + seq] = x1[0:seq, c * TILE : (c + 1) * TILE]
        xp[c, 2 * PAD + seq :] = x1[seq:, c * TILE : (c + 1) * TILE]
    for start, at, n in spots:
        for c in range(lanes):
            pooled[at : at + n, c * TILE : (c + 1) * TILE] = (
                xp[c, pl.ds(start - 2, n, stride=3)]
                + xp[c, pl.ds(start - 1, n, stride=3)]
                + xp[c, pl.ds(start, n, stride=3)]
            ) / 3.0

    xhat, _ = norm_stats(pooled[...])
    normed = (xhat * rows[0:1] + rows[1:2]).astype(BF)
    for part in range(3):
        half, at = part // 2, part % 2 * D
        value = mm(normed, wts[half, :, at : at + D])
        value = (value * HD**-0.5 if part == 0 else value).astype(BF)
        for pair in range(PAIRS):
            mixed[part, pair] = value[:, pair * PW : (pair + 1) * PW]

    def forward_pair(pair, carry):
        for at, n, offset in ((0, n_long, 0), (n_long, TILE, 2 * n_long)):
            top, total, acc = state
            wide = pl.ds(0, 2 * n)
            part = (top.at[:, wide], total.at[:, wide], acc.at[:, wide])
            softmax_start(part)
            values_t = mixed[2, pair, at : at + n].T
            both = split_heads(mixed[0, pair, at : at + n])
            count = n // TILE
            softmax_step(
                mixed[1, pair, at : at + n], values_t, both, bias, pair, 0, True, count, count, part
            )
            ot[pair, :, at : at + n], lse[pair, :, offset : offset + 2 * n] = softmax_end(part, n)
        return carry

    lax.fori_loop(0, PAIRS, forward_pair, 0)
    middle = pooled[...] + mm(ot[...].reshape(D, ot.shape[2]).T, wts[1, :, D : 2 * D])
    middle_s[...] = middle
    xhat, _ = norm_stats(middle)
    second = (xhat * rows[2:3] + rows[3:4]).astype(BF)
    active, slope = gelu_pair(mm(second, wts[0, :, 2 * D :]) + beta[...])
    active_s[...] = active.astype(BF)
    slope_s[...] = slope.astype(BF)
    short = middle + mm(active_s[...], wts[1, :, 2 * D :], NT) + rows[4:5]
    for start, at, n in spots:
        for c in range(lanes):
            part = short[at : at + n, c * TILE : (c + 1) * TILE]
            for k in range(3):
                where = pl.ds(start + k, n, stride=3)
                xp[c, where] = xp[c, where] + part

    d_head[...] = jnp.zeros_like(d_head)
    row_grads[...] = jnp.zeros_like(row_grads)

    def loss_block(b, bits):
        start = pl.multiple_of(b * BLK + jnp.where(b * BLK >= seq, 2 * PAD, PAD), PAD)
        joined = jnp.concatenate([xp[c, pl.ds(start, BLK)] for c in range(lanes)], 1)
        xhat, rstd = norm_stats(joined)
        last = (xhat * final[0:1] + final[1:2]).astype(BF)
        logits = mm(last, head[...], NT) * D**-0.5
        info = aux[pl.ds(pl.multiple_of(b * BLK, BLK), BLK), :]
        weight = info[:, 2:3].astype(F32)
        hot = one_hot(info[:, 1:2])
        highest = jnp.max(logits, -1, keepdims=True)
        powers = jnp.exp(logits - highest)
        total = jnp.sum(powers, -1, keepdims=True)
        picked = jnp.sum(jnp.where(hot, logits, 0.0), -1, keepdims=True)
        lost = weight * (highest + jnp.log(total) - picked)
        d_logits = ((powers / total - hot.astype(F32)) * (weight * scale[0, 0])).astype(BF)
        d_head[...] += mm(d_logits, last, TN) * D**-0.5
        d_last = mm(d_logits, head[...]) * D**-0.5
        dx, d_gain, d_shift = norm_back(d_last, xhat, rstd, final[0:1])
        row_grads[0:1] += d_gain
        row_grads[1:2] += d_shift
        for c in range(lanes):
            xp[c, pl.ds(start, BLK)] = dx[:, c * TILE : (c + 1) * TILE]
        return bits + lost

    bits = lax.fori_loop(0, x1.shape[0] // BLK, loss_block, jnp.zeros((BLK, 1), F32))
    bits_out[...] = jnp.sum(bits, 0, keepdims=True) / LOG_TWO

    d_short = jnp.concatenate(
        [
            jnp.concatenate(
                [
                    xp[c, pl.ds(start, n, stride=3)]
                    + xp[c, pl.ds(start + 1, n, stride=3)]
                    + xp[c, pl.ds(start + 2, n, stride=3)]
                    for c in range(lanes)
                ],
                1,
            )
            for start, at, n in spots
        ],
        0,
    )
    d_branch = d_short.astype(BF)
    row_grads[6:7] = jnp.sum(d_branch.astype(F32), 0, keepdims=True)
    d_feed[1] = mm(d_branch, active_s[...], TN).astype(BF)
    d_pre = (mm(d_branch, wts[1, :, 2 * D :]) * slope_s[...].astype(F32)).astype(BF)
    d_beta[...] = jnp.sum(d_pre.astype(F32), 0, keepdims=True)
    xhat, rstd = norm_stats(middle_s[...])
    second = (xhat * rows[2:3] + rows[3:4]).astype(BF)
    d_feed[0] = mm(second, d_pre, TN).astype(BF)
    dx, d_gain, d_shift = norm_back(mm(d_pre, wts[0, :, 2 * D :], NT), xhat, rstd, rows[2:3])
    row_grads[4:5] = d_gain
    row_grads[5:6] = d_shift
    d_middle = d_short + dx
    d_mix = d_middle.astype(BF)
    ot_all = ot[...].reshape(D, ot.shape[2])
    d_attn[1, :, D:] = mm(ot_all, d_mix).astype(BF)
    d_att = mm(d_mix, wts[1, :, D : 2 * D], NT).astype(BF)
    for pair in range(PAIRS):
        mixed[3, pair] = d_att[:, pair * PW : (pair + 1) * PW]

    def backward_pair(pair, carry):
        for at, n, offset in ((0, n_long, 0), (n_long, TILE, 2 * n_long)):
            d_out = mixed[3, pair, at : at + n]
            product = (d_out.astype(F32).T) * ot[pair, :, at : at + n].astype(F32)
            inner = jnp.concatenate(
                [
                    jnp.sum(product[:HD], 0, keepdims=True),
                    jnp.sum(product[HD:], 0, keepdims=True),
                ],
                1,
            )
            queries = split_heads(mixed[0, pair, at : at + n])
            grads = split_heads(d_out)
            keys = mixed[1, pair, at : at + n]
            count = n // TILE
            p, ds = score_back(
                keys,
                mixed[2, pair, at : at + n],
                queries,
                grads,
                lse[pair, :, offset : offset + 2 * n],
                inner,
                bias,
                pair,
                0,
                True,
                count,
                count,
                tiles,
            )
            dq = mm(keys.T, ds)
            dq = jnp.concatenate([dq[:HD, :n], dq[HD:, n:]], 0) * HD**-0.5
            d_mixed[0, pair, at : at + n] = dq.T.astype(BF)
            d_mixed[1, pair, at : at + n] = mm(ds, queries).astype(BF)
            d_mixed[2, pair, at : at + n] = mm(p, grads).astype(BF)
        return carry

    lax.fori_loop(0, PAIRS, backward_pair, 0)
    fold_bias(tiles, sums, tiles.shape[1])
    d_in = jnp.concatenate([d_mixed[part, pair] for part in range(3) for pair in range(PAIRS)], 1)
    xhat, rstd = norm_stats(pooled[...])
    normed = (xhat * rows[0:1] + rows[1:2]).astype(BF)
    d_attn[0] = mm(normed, d_in[:, : 2 * D], TN).astype(BF)
    d_attn[1, :, :D] = mm(normed, d_in[:, 2 * D :], TN).astype(BF)
    dx, d_gain, d_shift = norm_back(mm(d_in[:, : 2 * D], wts[0, :, : 2 * D], NT) + mm(d_in[:, 2 * D :], wts[1, :, :D], NT), xhat, rstd, rows[0:1])
    row_grads[2:3] = d_gain
    row_grads[3:4] = d_shift
    d_pool = (d_middle + dx) / 3.0
    for start, at, n in spots:
        for c in range(lanes):
            part = d_pool[at : at + n, c * TILE : (c + 1) * TILE]
            for k in range(3):
                where = pl.ds(start - 2 + k, n, stride=3)
                xp[c, where] = xp[c, where] + part
    for c in range(lanes):
        dx_out[0:seq, c * TILE : (c + 1) * TILE] = xp[c, PAD : PAD + seq]
        dx_out[seq:, c * TILE : (c + 1) * TILE] = xp[c, 2 * PAD + seq :]


def middle_stage(x1, aux, head, wts, rows, beta, rel, scale, final, seq):
    tokens = x1.shape[0]
    n_long = seq // 3
    short = n_long + TILE
    far = n_long // TILE
    vm = pl.BlockSpec(memory_space=pltpu.VMEM)
    return pl.pallas_call(
        functools.partial(middle_kernel, seq),
        in_specs=[vm] * 6 + [pl.BlockSpec(memory_space=pltpu.SMEM)] * 2 + [vm],
        out_specs=[vm] * 8,
        out_shape=[
            jax.ShapeDtypeStruct((tokens, D), F32),
            jax.ShapeDtypeStruct((2, D, 2 * D), BF),
            jax.ShapeDtypeStruct((2, D, FF), BF),
            jax.ShapeDtypeStruct((V, D), F32),
            jax.ShapeDtypeStruct((8, D), F32),
            jax.ShapeDtypeStruct((1, FF), F32),
            jax.ShapeDtypeStruct((1, 1), F32),
            jax.ShapeDtypeStruct((HEADS, fold_rows(far), TILE), F32),
        ],
        scratch_shapes=[
            pltpu.VMEM((D // TILE, tokens + 2 * PAD, TILE), F32),
            pltpu.VMEM((short, D), F32),
            pltpu.VMEM((4, PAIRS, short, PW), BF),
            pltpu.VMEM((PAIRS, PW, short), BF),
            pltpu.VMEM((PAIRS, 1, 2 * short), F32),
            pltpu.VMEM((short, FF), BF),
            pltpu.VMEM((short, FF), BF),
            pltpu.VMEM((short, D), F32),
            pltpu.VMEM((HEADS, far, TILE, TILE), F32),
            pltpu.VMEM((HEADS, far, TILE, TILE), F32),
            pltpu.VMEM((3, PAIRS, short, PW), BF),
        ]
        + state_scratch(n_long),
        compiler_params=params(60),
        name="middle_stage",
    )(x1, aux, head, wts, rows, beta, rel, scale, final)


def feed_back_kernel(
    dx, act, slope, middle, wts, rows, dm_out, d_feed, row_grads, d_beta, up, down
):
    step = pl.program_id(0)

    @pl.when(step == 0)
    def _():
        up[...] = jnp.zeros_like(up)
        down[...] = jnp.zeros_like(down)
        row_grads[...] = jnp.zeros_like(row_grads)
        d_beta[...] = jnp.zeros_like(d_beta)

    d_result = dx[...]
    d_branch = d_result.astype(BF)
    row_grads[2:3] += jnp.sum(d_branch.astype(F32), 0, keepdims=True)
    down[...] += mm(d_branch, act[...], TN)
    d_pre = (mm(d_branch, wts[1, :, 2 * D :]) * slope[...].astype(F32)).astype(BF)
    d_beta[...] += jnp.sum(d_pre.astype(F32), 0, keepdims=True)
    xhat, rstd = norm_stats(middle[...])
    second = (xhat * rows[2:3] + rows[3:4]).astype(BF)
    up[...] += mm(second, d_pre, TN)
    dn, d_gain, d_shift = norm_back(mm(d_pre, wts[0, :, 2 * D :], NT), xhat, rstd, rows[2:3])
    row_grads[0:1] += d_gain
    row_grads[1:2] += d_shift
    dm_out[...] = d_result + dn

    @pl.when(step == pl.num_programs(0) - 1)
    def _():
        d_feed[0] = up[...].astype(BF)
        d_feed[1] = down[...].astype(BF)


def feed_back(dx, act, slope, middle, wts, rows):
    tokens = dx.shape[0]

    def flat(width):
        return pl.BlockSpec((BLK, width), lambda i: (i, 0))

    return pl.pallas_call(
        feed_back_kernel,
        grid=(tokens // BLK,),
        in_specs=[flat(D), flat(FF), flat(FF), flat(D), whole_spec(wts.shape), whole_spec(rows.shape)],
        out_specs=[
            flat(D),
            whole_spec((2, D, FF)),
            whole_spec((8, D)),
            whole_spec((1, FF)),
        ],
        out_shape=[
            jax.ShapeDtypeStruct((tokens, D), F32),
            jax.ShapeDtypeStruct((2, D, FF), BF),
            jax.ShapeDtypeStruct((8, D), F32),
            jax.ShapeDtypeStruct((1, FF), F32),
        ],
        scratch_shapes=[pltpu.VMEM((D, FF), F32), pltpu.VMEM((D, FF), F32)],
        compiler_params=params(56),
        name="feed_back",
    )(dx, act, slope, middle, wts, rows)


def attention_back_kernel(
    long_blocks,
    dm,
    aux,
    ot,
    lse,
    q_all,
    k_all,
    v_all,
    embed,
    wts,
    rows,
    rel,
    d_attn,
    d_embed,
    row_grads,
    sums,
    bias,
    tiles,
    kt_all,
    dk_all,
    dv_all,
    dq_t,
    d_att,
    inner,
    weights,
    d_mixed,
):
    step = pl.program_id(0)
    blocks = pl.num_programs(0)
    i = blocks - 1 - step

    @pl.when(step == 0)
    def _():
        build_bias(rel, bias, bias.shape[1])
        tiles[...] = jnp.zeros_like(tiles)
        dk_all[...] = jnp.zeros_like(dk_all)
        dv_all[...] = jnp.zeros_like(dv_all)
        weights[...] = jnp.zeros_like(weights)
        d_embed[...] = jnp.zeros_like(d_embed)
        row_grads[...] = jnp.zeros_like(row_grads)

        def turn(n, carry):
            for pair in range(PAIRS):
                kt_all[n, pair] = k_all[n, pair].T
            return carry

        lax.fori_loop(0, blocks, turn, 0)

    d_middle = dm[...]
    d_mix = d_middle.astype(BF)
    weights[1, :, D:] += mm(ot[0].reshape(D, BLK), d_mix)
    out = mm(d_mix, wts[1, :, D : 2 * D], NT).astype(BF)
    for pair in range(PAIRS):
        d_att[pair] = out[:, pair * PW : (pair + 1) * PW]
    product = mm(wts[1, :, D : 2 * D], d_mix, NT).astype(BF).astype(F32) * ot[0].reshape(
        D, BLK
    ).astype(F32)
    for pair in range(PAIRS):
        at = pair * PW
        inner[pair] = jnp.concatenate(
            [
                jnp.sum(product[at : at + HD], 0, keepdims=True),
                jnp.sum(product[at + HD : at + PW], 0, keepdims=True),
            ],
            1,
        )
    first = jnp.where(i >= long_blocks, long_blocks, 0)

    def one_pair(pair, carry):
        queries = split_heads(q_all[i, pair])
        grads = split_heads(d_att[pair])
        dq_t[...] = jnp.zeros_like(dq_t)

        def with_block(j, far, diag):
            p, ds = score_back(
                k_all[j, pair],
                v_all[j, pair],
                queries,
                grads,
                lse[0, pair],
                inner[pair],
                bias,
                pair,
                far,
                diag,
                SUB,
                SUB,
                tiles,
            )
            dv_all[j, pair] += mm(p, grads)
            dk_all[j, pair] += mm(ds, queries)
            dq_t[...] += mm(kt_all[j, pair], ds)

        def earlier(j, inside):
            with_block(j, SUB * (i - j), False)
            return inside

        lax.fori_loop(first, i, earlier, 0)
        with_block(i, 0, True)
        total = dq_t[...]
        total = jnp.concatenate([total[:HD, :BLK], total[HD:, BLK:]], 0) * HD**-0.5
        d_mixed[0, pair] = total.T.astype(BF)
        d_mixed[1, pair] = dk_all[i, pair].astype(BF)
        d_mixed[2, pair] = dv_all[i, pair].astype(BF)
        return carry

    lax.fori_loop(0, PAIRS, one_pair, 0)
    d_in = jnp.concatenate([d_mixed[part, pair] for part in range(3) for pair in range(PAIRS)], 1)
    hot = one_hot(aux[:, 0:1]).astype(BF)
    xhat, rstd = norm_stats(mm(hot, embed[...]))
    normed = (xhat * rows[0:1] + rows[1:2]).astype(BF)
    weights[0] += mm(normed, d_in[:, : 2 * D], TN)
    weights[1, :, :D] += mm(normed, d_in[:, 2 * D :], TN)
    dx, d_gain, d_shift = norm_back(mm(d_in[:, : 2 * D], wts[0, :, : 2 * D], NT) + mm(d_in[:, 2 * D :], wts[1, :, :D], NT), xhat, rstd, rows[0:1])
    row_grads[0:1] += d_gain
    row_grads[1:2] += d_shift
    d_embed[...] += mm(hot, (d_middle + dx).astype(BF), TN)

    @pl.when(step == blocks - 1)
    def _():
        d_attn[...] = weights[...].astype(BF)
        fold_bias(tiles, sums, tiles.shape[1])


def attention_back(dm, aux, ot, lse, q, k, v, embed, wts, rows, rel, long_blocks):
    tokens = dm.shape[0]
    blocks = tokens // BLK
    far = SUB * long_blocks

    def turned(shape):
        return pl.BlockSpec(shape, lambda s: (blocks - 1 - s,) + (0,) * (len(shape) - 1))

    return pl.pallas_call(
        functools.partial(attention_back_kernel, long_blocks),
        grid=(blocks,),
        in_specs=[
            turned((BLK, D)),
            turned((BLK, aux.shape[1])),
            turned((1, PAIRS, PW, BLK)),
            turned((1, PAIRS, 1, 2 * BLK)),
            whole_spec(q.shape),
            whole_spec(k.shape),
            whole_spec(v.shape),
            whole_spec(embed.shape),
            whole_spec((2, D, 2 * D)),
            whole_spec(rows.shape),
            pl.BlockSpec(memory_space=pltpu.SMEM),
        ],
        out_specs=[
            whole_spec((2, D, 2 * D)),
            whole_spec((V, D)),
            whole_spec((8, D)),
            whole_spec((HEADS, fold_rows(far), TILE)),
        ],
        out_shape=[
            jax.ShapeDtypeStruct((2, D, 2 * D), BF),
            jax.ShapeDtypeStruct((V, D), F32),
            jax.ShapeDtypeStruct((8, D), F32),
            jax.ShapeDtypeStruct((HEADS, fold_rows(far), TILE), F32),
        ],
        scratch_shapes=[
            pltpu.VMEM((HEADS, far, TILE, TILE), F32),
            pltpu.VMEM((HEADS, far, TILE, TILE), F32),
            pltpu.VMEM((blocks, PAIRS, PW, BLK), BF),
            pltpu.VMEM((blocks, PAIRS, BLK, PW), F32),
            pltpu.VMEM((blocks, PAIRS, BLK, PW), F32),
            pltpu.VMEM((PW, 2 * BLK), F32),
            pltpu.VMEM((PAIRS, BLK, PW), BF),
            pltpu.VMEM((PAIRS, 1, 2 * BLK), F32),
            pltpu.VMEM((2, D, 2 * D), F32),
            pltpu.VMEM((3, PAIRS, BLK, PW), BF),
        ],
        compiler_params=params(60),
        name="attention_back",
    )(dm, aux, ot, lse, q, k, v, embed, wts, rows, rel)


MESH = pl.DeviceIdType.MESH
MISC_ROWS = 32
MISC_COLS = D + 128


class Place:
    def __init__(self, wide, narrow):
        self.W, self.N = wide, narrow
        self.slabs = wide * narrow
        self.c = lax.axis_index("rep")
        self.w = lax.axis_index("wide")
        self.n = lax.axis_index("narrow")
        hi, lo = self.n // 2, self.n % 2
        self.a0 = (1 - self.c) * hi + self.c * lo
        self.b0 = (1 - self.c) * lo + self.c * hi
        self.group = self.w // (wide // 2)

    def narrow_of(self, a, b):
        return a * (2 - self.c) + b * (1 + self.c)

    def slab(self, w, a, b):
        return w * self.N + self.narrow_of(a, b)

    def chip(self, w, a, b):
        return {"wide": w, "narrow": self.narrow_of(a, b)}

    def sibling(self):
        return {"rep": 1 - self.c}


def greet(devices):
    barrier = pltpu.get_barrier_semaphore()
    for device in devices:
        pl.semaphore_signal(barrier, inc=1, device_id=device, device_id_type=MESH)
    pl.semaphore_wait(barrier, len(devices))


def slab_form(rows, cols):
    return (rows, cols) if rows % 16 == 0 else (16, rows * cols // 16)


def gather_greetings(at):
    return [
        {"wide": lax.rem(at.w + 1, at.W)},
        {"wide": lax.rem(at.w + at.W - 1, at.W)},
        at.chip(at.w, at.a0, 1 - at.b0),
        at.chip(at.w, 1 - at.a0, at.b0),
        at.sibling(),
    ]


class GatherStream:
    def __init__(self, at, src, out, send, recv, local):
        self.at, self.src, self.out, self.send, self.recv = at, src, out, send, recv
        self.own = at.slab(at.w, at.a0, at.b0)
        self.keep = pltpu.make_async_copy(src, out.at[at.c, self.own], local)

    def copy(self, ref, slab, way, peer):
        return pltpu.make_async_remote_copy(
            src_ref=ref,
            dst_ref=self.out.at[self.at.c, slab],
            send_sem=self.send.at[way, slab],
            recv_sem=self.recv.at[1 if way == 4 else 0, slab],
            device_id=peer,
            device_id_type=MESH,
        )

    def arrived(self, slab, half, kind):
        pltpu.make_async_remote_copy(
            src_ref=self.out.at[half, slab],
            dst_ref=self.out.at[half, slab],
            send_sem=self.send.at[4, slab],
            recv_sem=self.recv.at[kind, slab],
            device_id=self.at.sibling(),
            device_id_type=MESH,
        ).wait_recv()

    def onward(self, w, mine, act, up, down):
        at = self.at
        slab = at.slab(w, at.a0, at.b0)
        ref = self.src if mine else self.out.at[at.c, slab]
        if up:

            @pl.when(at.w < at.W - 1)
            def _():
                act(self.copy(ref, slab, 0, {"wide": jnp.minimum(at.w + 1, at.W - 1)}))

        if down:

            @pl.when(at.w > 0)
            def _():
                act(self.copy(ref, slab, 1, {"wide": jnp.maximum(at.w - 1, 0)}))

        act(self.copy(ref, slab, 2, at.chip(at.w, at.a0, 1 - at.b0)))
        act(self.copy(ref, slab, 3, at.chip(at.w, 1 - at.a0, at.b0)))
        act(self.copy(ref, slab, 4, at.sibling()))

    def across(self, w, act):
        at = self.at
        slab = at.slab(w, at.a0, 1 - at.b0)
        ref = self.out.at[at.c, slab]
        act(self.copy(ref, slab, 3, at.chip(at.w, 1 - at.a0, at.b0)))
        act(self.copy(ref, slab, 4, at.sibling()))

    def last(self, w, act):
        at = self.at
        for b in (at.b0, 1 - at.b0):
            slab = at.slab(w, 1 - at.a0, b)
            act(self.copy(self.out.at[at.c, slab], slab, 4, at.sibling()))

    def both_sides(self, k, body):
        at = self.at

        @pl.when(at.w - k >= 0)
        def _():
            body(jnp.maximum(at.w - k, 0), True)

        @pl.when(at.w + k < at.W)
        def _():
            body(jnp.minimum(at.w + k, at.W - 1), False)

    def start(self):
        self.keep.start()
        self.onward(self.at.w, True, lambda copy: copy.start(), True, True)

    def from_along(self, k):
        def along(w, below):
            self.arrived(self.at.slab(w, self.at.a0, self.at.b0), self.at.c, 0)
            self.onward(w, False, lambda copy: copy.start(), below, not below)

        self.both_sides(k, along)

    def from_first(self, w):
        self.arrived(self.at.slab(w, self.at.a0, 1 - self.at.b0), self.at.c, 0)
        self.across(w, lambda copy: copy.start())

    def from_second(self, w, b):
        at = self.at
        slab = at.slab(w, 1 - at.a0, b)
        self.arrived(slab, at.c, 0)
        self.copy(self.out.at[at.c, slab], slab, 4, at.sibling()).start()

    def depth(self, d):
        at = self.at
        if 1 <= d < at.W:
            self.from_along(d)
        for k, body in (
            (d - 1, lambda w, below=None: self.from_first(w)),
            (d - 1, lambda w, below=None: self.from_second(w, at.b0)),
            (d - 2, lambda w, below=None: self.from_second(w, 1 - at.b0)),
        ):
            if k == 0:
                body(at.w)
            elif 0 < k < at.W:
                self.both_sides(k, body)

    def depths(self):
        return range(1, self.at.W + 2)

    def finish(self):
        at = self.at
        done = lambda copy: copy.wait_send()
        self.keep.wait()
        self.onward(at.w, True, done, True, True)
        self.across(at.w, done)
        self.last(at.w, done)

        def body(k, carry):
            self.both_sides(
                k, lambda w, below: self.onward(w, False, done, below, not below)
            )
            self.both_sides(k, lambda w, below: self.across(w, done))
            self.both_sides(k, lambda w, below: self.last(w, done))
            return carry

        lax.fori_loop(1, at.W, body, 0)

        def from_sibling(slab, carry):
            self.arrived(slab, 1 - at.c, 1)
            return carry

        lax.fori_loop(0, at.slabs, from_sibling, 0)


def gather_sems(slabs):
    return [
        pltpu.SemaphoreType.DMA((5, slabs)),
        pltpu.SemaphoreType.DMA((2, slabs)),
        pltpu.SemaphoreType.DMA,
    ]


def gather_kernel(wide, narrow, count, *refs):
    at = Place(wide, narrow)
    greet(gather_greetings(at))
    streams = [
        GatherStream(at, refs[i], refs[count + i], *refs[2 * count + 3 * i : 2 * count + 3 * i + 3])
        for i in range(count)
    ]
    for stream in streams:
        stream.start()
    for d in streams[0].depths():
        for stream in streams:
            stream.depth(d)
    for stream in streams:
        stream.finish()


def gather_all(arrays, wide, narrow, collective_id):
    slabs = wide * narrow
    anywhere = pl.BlockSpec(memory_space=pl.ANY)
    scratch = []
    for _ in arrays:
        scratch += gather_sems(slabs)
    return pl.pallas_call(
        functools.partial(gather_kernel, wide, narrow, len(arrays)),
        in_specs=[anywhere] * len(arrays),
        out_specs=[anywhere] * len(arrays),
        out_shape=[jax.ShapeDtypeStruct((2, slabs) + x.shape, x.dtype) for x in arrays],
        scratch_shapes=scratch,
        compiler_params=params(16, collective_id=collective_id, has_side_effects=True),
        name="gather_all",
    )(*arrays)


class ScatterStream:
    def __init__(self, at, src, out, own, side, first, second, along, fin, sems):
        self.at, self.src, self.out = at, src, out
        self.own, self.side, self.first, self.second, self.along, self.fin = (
            own,
            side,
            first,
            second,
            along,
            fin,
        )
        self.local, self.side_sem, self.first_sem, self.second_sem, self.along_sem, self.fin_sem = sems
        self.levels = (at.W // 2).bit_length() - 1

    def remote(self, src, dst, sems, index, device):
        return pltpu.make_async_remote_copy(
            src_ref=src,
            dst_ref=dst,
            send_sem=sems.at[(0,) + index],
            recv_sem=sems.at[(1,) + index],
            device_id=device,
            device_id_type=MESH,
        )

    def side_copy(self, slab):
        c = self.at.c
        return self.remote(
            self.src.at[1 - c, slab], self.side.at[slab], self.side_sem, (slab,), self.at.sibling()
        )

    def own_copy(self):
        return pltpu.make_async_copy(self.src.at[self.at.c], self.own, self.local)

    def first_copy(self, w, b):
        at = self.at
        slab = at.slab(w, 1 - at.a0, b)
        return self.remote(
            self.own.at[slab],
            self.first.at[2 * w + b],
            self.first_sem,
            (2 * w + b,),
            at.chip(at.w, 1 - at.a0, at.b0),
        )

    def second_copy(self, w):
        at = self.at
        return self.remote(
            self.own.at[at.slab(w, at.a0, 1 - at.b0)],
            self.second.at[w],
            self.second_sem,
            (w,),
            at.chip(at.w, at.a0, 1 - at.b0),
        )

    def along_place(self, level):
        W = self.at.W
        return W - (W >> level), W >> (level + 1)

    def along_copy(self, level, k):
        at = self.at
        unit = 1 << level
        bit = (at.w // unit) % 2
        partner = at.w + unit * (1 - 2 * bit)
        start, _ = self.along_place(level)
        w = k * 2 * unit + partner % (2 * unit)
        return self.remote(
            self.own.at[at.slab(w, at.a0, at.b0)],
            self.along.at[start + k],
            self.along_sem,
            (start + k,),
            {"wide": partner},
        )

    def home(self):
        at = self.at
        return lax.rem(at.w + at.W // 2, at.W)

    def cross_copy(self):
        at = self.at
        return self.remote(
            self.own.at[at.slab(self.home(), at.a0, at.b0)],
            self.fin.at[at.c],
            self.fin_sem,
            (at.c,),
            {"wide": self.home(), "rep": at.group},
        )

    def over_copy(self):
        at = self.at
        return self.remote(
            self.own.at[at.slab(at.w, at.a0, at.b0)],
            self.fin.at[at.c],
            self.fin_sem,
            (at.c,),
            at.sibling(),
        )

    def turn(self, k):
        return lax.rem(self.at.w + 1 + k, self.at.W)

    def start(self):
        at = self.at
        self.own_copy().start()
        other = 1 - at.c
        hi, lo = at.n // 2, at.n % 2
        a1 = (1 - other) * hi + other * lo
        b1 = (1 - other) * lo + other * hi
        for a, b in ((1 - a1, 0), (1 - a1, 1), (a1, 1 - b1), (a1, b1)):

            def body(k, carry, a=a, b=b):
                w = self.turn(k)
                self.side_copy(w * at.N + a * (2 - other) + b * (1 + other)).start()
                return carry

            lax.fori_loop(0, at.W, body, 0)

    def total(self, slab):
        self.side_copy(slab).wait_recv()
        return self.own[slab].astype(F32) + self.side[slab].astype(F32)

    def wait_first(self, w, b):
        self.first_copy(w, b).wait_recv()
        return self.first[2 * w + b].astype(F32)

    def stage_first(self):
        at = self.at
        self.own_copy().wait()

        for b in (1 - at.b0, at.b0):

            def body(k, carry, b=b):
                w = self.turn(k)
                slab = at.slab(w, 1 - at.a0, b)
                self.own[slab] = self.total(slab).astype(BF)
                self.first_copy(w, b).start()
                return carry

            lax.fori_loop(0, at.W, body, 0)

    def stage_second(self):
        at = self.at

        def body(k, carry):
            w = self.turn(k)
            slab = at.slab(w, at.a0, 1 - at.b0)
            self.own[slab] = (self.total(slab) + self.wait_first(w, 1 - at.b0)).astype(BF)
            self.second_copy(w).start()
            return carry

        lax.fori_loop(0, at.W, body, 0)

    def column(self, w, levels):
        at = self.at
        value = self.total(at.slab(w, at.a0, at.b0)) + self.wait_first(w, at.b0)
        self.second_copy(w).wait_recv()
        value = value + self.second[w].astype(F32)
        for level in range(levels):
            start, _ = self.along_place(level)
            k = w // (2 << level)
            self.along_copy(level, k).wait_recv()
            value = value + self.along[start + k].astype(F32)
        return value

    def stage_along(self):
        at = self.at
        for level in range(self.levels):
            unit = 1 << level
            partner = at.w + unit * (1 - 2 * ((at.w // unit) % 2))

            def body(k, carry, level=level, unit=unit, partner=partner):
                w = k * 2 * unit + partner % (2 * unit)
                self.own[at.slab(w, at.a0, at.b0)] = self.column(w, level).astype(BF)
                self.along_copy(level, k).start()
                return carry

            lax.fori_loop(0, self.along_place(level)[1], body, 0)

    def stage_home(self):
        at = self.at
        away = at.slab(self.home(), at.a0, at.b0)
        self.own[away] = self.column(self.home(), self.levels).astype(BF)
        self.cross_copy().start()
        mine = at.slab(at.w, at.a0, at.b0)
        value = self.column(at.w, self.levels)
        self.own[mine] = value.astype(BF)

        @pl.when(at.c != at.group)
        def _():
            self.over_copy().start()

        self.put(at.c, value)

    def put(self, half, value):
        for h in range(2):

            @pl.when(half == h)
            def _(h=h):
                self.out[h][...] = value

    def finish(self):
        at = self.at

        @pl.when(at.c == at.group)
        def _():
            self.fin_wait(1 - at.c)
            self.put(1 - at.c, self.fin[1 - at.c].astype(F32))

        @pl.when(at.c != at.group)
        def _():
            for half in range(2):
                self.fin_wait(half)
                self.out[half][...] = self.fin[half].astype(F32)
            self.over_copy().wait_send()

        self.cross_copy().wait_send()

        def sides(slab, carry):
            self.side_copy(slab).wait_send()
            return carry

        lax.fori_loop(0, at.slabs, sides, 0)

        def firsts(k, carry):
            self.first_copy(k // 2, k % 2).wait_send()
            return carry

        lax.fori_loop(0, 2 * at.W, firsts, 0)

        def seconds(w, carry):
            self.second_copy(w).wait_send()
            return carry

        lax.fori_loop(0, at.W, seconds, 0)
        for level in range(self.levels):

            def alongs(k, carry, level=level):
                self.along_copy(level, k).wait_send()
                return carry

            lax.fori_loop(0, self.along_place(level)[1], alongs, 0)

    def fin_wait(self, half):
        self.remote(
            self.fin.at[half], self.fin.at[half], self.fin_sem, (half,), self.at.sibling()
        ).wait_recv()


def scatter_scratch(wide, narrow, form):
    slabs = wide * narrow
    sizes = (slabs, slabs, 2 * wide, wide, max(wide - 2, 1), 2)
    dma = pltpu.SemaphoreType.DMA
    return [pltpu.VMEM((size,) + form, BF) for size in sizes] + [dma] + [
        dma((2, size)) for size in sizes[1:]
    ]


def scatter_greetings(at):
    out = [
        at.chip(at.w, at.a0, 1 - at.b0),
        at.chip(at.w, 1 - at.a0, at.b0),
        at.sibling(),
    ]
    for level in range((at.W // 2).bit_length() - 1):
        unit = 1 << level
        out.append({"wide": at.w + unit * (1 - 2 * ((at.w // unit) % 2))})
    out.append({"wide": lax.rem(at.w + at.W // 2, at.W)})
    out.append({"wide": lax.rem(at.w + at.W // 2, at.W), "rep": 1 - at.c})
    return out


def halves_of(ref, layer, width, natural):
    if natural:
        return [ref.at[layer, :, h * width : (h + 1) * width] for h in range(2)]
    return [ref.at[layer, h] for h in range(2)]


def adam_update(weight, moment, square, gradient, decay, rate):
    moment = BETA_ONE * moment + (1.0 - BETA_ONE) * gradient
    square = BETA_TWO * square + (1.0 - BETA_TWO) * gradient * gradient
    fixed_moment = moment / (1.0 - BETA_ONE**STEP)
    fixed_square = square / (1.0 - BETA_TWO**STEP)
    delta = -rate * (fixed_moment / (jnp.sqrt(fixed_square) + ADAM_EPS) + decay * weight)
    return (moment, square, delta)


DECAYS = (DECAY, DECAY, DECAY, 0.0)
RATES = (RATE_TABLE, RATE, RATE, RATE_TABLE)
SOURCES = ((1, 1), (2, 1), (2, 0), (1, 0))


def sum_partners(at):
    out = []
    for axis, here, size in (("narrow", at.n, at.N), ("wide", at.w, at.W)):
        unit = 1
        while unit < size:
            out.append({axis: here + unit * (1 - 2 * ((here // unit) % 2))})
            unit *= 2
    return out


def reduce_kernel(wide, narrow, natural, *refs):
    at = Place(wide, narrow)
    take = iter(refs)

    def some(n):
        return [next(take) for _ in range(n)]

    parts, bits = some(5), next(take)
    hbm_states = some(12)
    grads, deltas, scalars = some(4), some(4), next(take)
    states, state_sems = some(12), next(take)
    misc_sum, bits_in, bits_sem = some(3)
    sums, arrived, sum_sems = some(3)
    mine, other, delta_sems = some(4), some(4), next(take)
    partners = sum_partners(at)
    greet(scatter_greetings(at) + partners)

    tiny = pltpu.make_async_remote_copy(
        src_ref=bits,
        dst_ref=bits_in,
        send_sem=bits_sem.at[0],
        recv_sem=bits_sem.at[1],
        device_id=at.sibling(),
        device_id_type=MESH,
    )
    tiny.start()
    streams = []
    for i in range(5):
        part = some(12)
        if i == 0:
            out = [misc_sum.at[0], misc_sum.at[1]]
        else:
            which, layer = SOURCES[i - 1]
            out = halves_of(grads[which], layer, 2 * D if which == 1 else FF, natural)
        streams.append(ScatterStream(at, parts[i], out, *part[:6], part[6:]))
    for stream in streams:
        stream.start()
    loads = [
        pltpu.make_async_copy(src, dst, state_sems.at[i])
        for i, (src, dst) in enumerate(zip(hbm_states, states))
    ]
    for load in loads:
        load.start()
    for stream in streams:
        stream.stage_first()
    for stream in streams:
        stream.stage_second()
    for stream in streams:
        stream.stage_along()
    for stream in streams:
        stream.stage_home()
    for stream in streams:
        stream.finish()
    tiny.wait()

    table_rows, columns = grads[0].shape[1], grads[3].shape[1]
    for layer in range(2):
        grads[0][layer] = misc_sum[layer, :table_rows, :D]
    grads[3][...] = misc_sum[0, :VEC, D : D + columns]
    squared = jnp.zeros((1, 1), F32)
    for ref in [misc_sum.at[0], misc_sum.at[1]] + [view for s in streams[1:] for view in s.out]:
        value = ref[...]
        value = jnp.sum(value * value, 0, keepdims=True)
        squared = squared + jnp.sum(value, 1, keepdims=True)
    row = lax.broadcasted_iota(jnp.int32, (8, 128), 0)
    lost = jnp.where(at.c == at.group, bits[...] + bits_in[...], 0.0)
    total = jnp.where(row == 0, squared, jnp.where(row == 1, lost, 0.0))
    for k, partner in enumerate(partners):
        sums[k] = total
        copy = pltpu.make_async_remote_copy(
            src_ref=sums.at[k],
            dst_ref=arrived.at[k],
            send_sem=sum_sems.at[0, k],
            recv_sem=sum_sems.at[1, k],
            device_id=partner,
            device_id_type=MESH,
        )
        copy.start()
        copy.wait()
        total = total + arrived[k]
    norm = jnp.sqrt(total[0:1, 0:1])
    factor = jnp.minimum(1.0, CLIP_AT / (norm + 1e-06))
    scalars[...] = jnp.where(row == 0, norm, jnp.where(row == 2, factor, total))
    for load in loads:
        load.wait()

    copies = [
        pltpu.make_async_remote_copy(
            src_ref=mine[which],
            dst_ref=other[which],
            send_sem=delta_sems.at[0, which],
            recv_sem=delta_sems.at[1, which],
            device_id=at.sibling(),
            device_id_type=MESH,
        )
        for which in range(4)
    ]
    order = (2, 1, 0, 3)
    for which in order:
        refs_of = [states[which], states[4 + which], states[8 + which], grads[which], mine[which]]
        if which in (1, 2):
            width = 2 * D if which == 1 else FF
            views = [[ref.at[l] for ref in refs_of] for l in range(2)]
            if natural:
                views = [
                    [ref.at[l, :, h * width : (h + 1) * width] for ref in refs_of]
                    for l in range(2)
                    for h in range(2)
                ]
        else:
            views = [refs_of]
        for weight, moment, square, gradient, target in views:
            _, _, delta = adam_update(
                weight[...],
                moment[...],
                square[...],
                gradient[...] * factor,
                DECAYS[which],
                RATES[which],
            )
            target[...] = delta.astype(target.dtype)
        copies[which].start()
    for which in order:
        copies[which].wait()
        deltas[which][...] = (mine[which][...].astype(F32) + other[which][...].astype(F32)) * 0.5


def reduce_all(parts, bits, states, wide, narrow, natural, collective_id):
    vm = pl.BlockSpec(memory_space=pltpu.VMEM)
    anywhere = pl.BlockSpec(memory_space=pl.ANY)
    like = [jax.ShapeDtypeStruct(x.shape, F32) for x in states[:4]]
    kinds = [BF if x.shape[-2] % 16 == 0 else F32 for x in states[:4]]
    exchanged = [pltpu.VMEM(x.shape, kind) for x, kind in zip(states[:4], kinds)]
    dma = pltpu.SemaphoreType.DMA
    stages = (wide * narrow).bit_length() - 1
    scratch = [pltpu.VMEM(x.shape, F32) for x in states] + [dma((12,))]
    scratch += [pltpu.VMEM((2,) + parts[0].shape[2:], F32), pltpu.VMEM(bits.shape, F32), dma((2,))]
    scratch += [pltpu.VMEM((stages, 8, 128), F32)] * 2 + [dma((2, stages))]
    scratch += exchanged + exchanged + [dma((2, 4))]
    for x in parts:
        scratch += scatter_scratch(wide, narrow, x.shape[2:])
    return pl.pallas_call(
        functools.partial(reduce_kernel, wide, narrow, natural),
        in_specs=[anywhere] * 5 + [vm] + [anywhere] * 12,
        out_specs=[vm] * 9,
        out_shape=like + like + [jax.ShapeDtypeStruct((8, 128), F32)],
        scratch_shapes=scratch,
        compiler_params=params(60, collective_id=collective_id, has_side_effects=True),
        name="reduce_all",
    )(*parts, bits, *states)


def update_kernel(scalars, *refs):
    grads, deltas, weights, moments, squares, outers, averages = (
        refs[4 * k : 4 * k + 4] for k in range(7)
    )
    new_m, new_s, new_w, new_o, new_a = (refs[28 + 4 * k : 32 + 4 * k] for k in range(5))
    factor = scalars[2:3, 0:1]
    for which in range(4):
        moment, square, _ = adam_update(
            weights[which][...],
            moments[which][...],
            squares[which][...],
            grads[which][...] * factor,
            DECAYS[which],
            RATES[which],
        )
        new_m[which][...] = moment
        new_s[which][...] = square
        delta = deltas[which][...]
        outer = OUTER_MOM * outers[which][...] + delta
        weight = weights[which][...] + OUTER_RATE * (delta + OUTER_MOM * outer)
        new_o[which][...] = outer
        new_w[which][...] = weight
        new_a[which][...] = EVAL_KEEP * averages[which][...] + (1.0 - EVAL_KEEP) * weight


def update(scalars, grads, deltas, arrays):
    weights = arrays[:4]
    rows = weights[1].shape[1]

    def quarter(width):
        return pl.BlockSpec((1, rows, width // 4), lambda i: (i // 4, 0, i % 4))

    specs = [
        pl.BlockSpec((1,) + weights[0].shape[1:], lambda i: (i // 4, 0, 0)),
        quarter(4 * D),
        quarter(2 * FF),
        pl.BlockSpec(weights[3].shape, lambda i: (0, 0)),
    ]
    like = [jax.ShapeDtypeStruct(x.shape, F32) for x in weights]
    return pl.pallas_call(
        update_kernel,
        grid=(8,),
        in_specs=[pl.BlockSpec((8, 128), lambda i: (0, 0))] + specs * 7,
        out_specs=specs * 5,
        out_shape=like * 5,
        compiler_params=params(32),
        name="update",
    )(scalars, *grads, *deltas, *arrays)


def local_gradients(byte_ids, live_mask, tables, wts, vec, count):
    seq = byte_ids.shape[1]
    long_blocks = seq // BLK
    weight = jnp.concatenate([live_mask[:, 1:], jnp.zeros_like(live_mask[:, :1])], 1)
    info = jnp.stack([byte_ids, jnp.roll(byte_ids, -1, 1), weight, weight], -1)
    aux = jnp.concatenate([info[0], info[1, :BLK]], 0)
    scale = (1.0 / (count * LOG_TWO)).reshape(1, 1)
    rows = [
        jnp.concatenate([vec[2 + 5 * l : 7 + 5 * l], jnp.zeros((3, D), F32)], 0) for l in range(2)
    ]
    bias_rows = 2 * FF // D
    beta = vec[12 : 12 + bias_rows].reshape(2, 1, FF)
    rel = vec[12 + bias_rows :].reshape(2, HEADS, NB)
    x1, middle, q, k, v, ot, lse, act, slope = full_forward(
        aux, tables[0], wts[0], rows[0], beta[0], rel[0], long_blocks
    )
    d_x1, d_short_attn, d_short_feed, d_head, short_rows, d_beta_1, bits, sums_1 = middle_stage(
        x1, aux, tables[1], wts[1], rows[1], beta[1], rel[1], scale, vec[0:2], seq
    )
    d_middle, d_feed, feed_rows, d_beta_0 = feed_back(d_x1, act, slope, middle, wts[0], rows[0])
    d_attn, d_embed, attn_rows, sums_0 = attention_back(
        d_middle, aux, ot, lse, q, k, v, tables[0], wts[0], rows[0], rel[0], long_blocks
    )

    def d_rel(sums, far):
        fold = fold_matrix(far)
        return jnp.dot(jnp.sum(sums, -1), fold, precision=lax.Precision.HIGHEST).reshape(1, -1)

    d_vec = jnp.concatenate(
        [
            short_rows[0:2],
            attn_rows[0:2],
            feed_rows[0:3],
            short_rows[2:7],
            d_beta_0.reshape(-1, D),
            d_beta_1.reshape(-1, D),
            jnp.concatenate([d_rel(sums_0, long_blocks * SUB), d_rel(sums_1, seq // 3 // TILE)], 1),
        ],
        0,
    )
    return bits, (d_embed, d_head), (d_short_attn, d_short_feed, d_feed, d_attn), d_vec


def pad_to(x, rows, cols):
    return jnp.pad(x, [(0, 0)] * (x.ndim - 2) + [(0, rows - x.shape[-2]), (0, cols - x.shape[-1])])


def per_device(wide, narrow, byte_ids, live_mask, *arrays):
    tables, attention, feed_forward, vectors = arrays[:4]
    slabs = wide * narrow
    core = lax.axis_index("rep")
    group = lax.axis_index("wide") // (wide // 2)
    rows = attention.shape[1]
    form = slab_form(rows, 2 * D + FF)

    axes = ("rep", "wide", "narrow")
    moves = []
    for r in range(2):
        for w in range(wide):
            for n in range(narrow):
                to = (w % 2, r * (wide // 2) + w // 2, n)
                moves.append(((r * wide + w) * narrow + n, (to[0] * wide + to[1]) * narrow + to[2]))
    moved = lax.ppermute(byte_ids + V * live_mask, axes, moves)
    ids, lives = moved % V, moved // V

    def half_of(x, width):
        return lax.dynamic_slice_in_dim(x, core * width, width, 1)

    packed = [
        jnp.concatenate([half_of(attention[l], 2 * D), half_of(feed_forward[l], FF)], 1)
        .astype(BF)
        .reshape(form)
        for l in range(2)
    ]
    own_count = jnp.sum(live_mask[:, 1:])
    digits = jnp.stack([own_count // 64, own_count % 64]).astype(F32).reshape(1, 2)
    side = jnp.concatenate(
        [pad_to(vectors, 24, 128), pad_to(digits, MISC_ROWS - 24, 128)], 0
    )
    misc = jnp.concatenate([pad_to(tables[core], MISC_ROWS, D), side], 1).astype(BF)
    misc_all, *wts = gather_all([misc] + packed, wide, narrow, 1)
    wts = [w.reshape(2, D, 2 * D + FF) for w in wts]
    table_rows = tables.shape[1]
    full_tables = misc_all[:, :, :table_rows, :D].reshape(2, V, D)
    cols = vectors.shape[1]
    vec = misc_all[0, :, :VEC, D : D + cols].astype(F32).transpose(1, 0, 2).reshape(VEC, D)
    tally = misc_all[:, :, 24, D : D + 2].astype(F32)
    counts = jnp.sum(tally[:, :, 0] * 64.0 + tally[:, :, 1], 1)

    bits, d_tables, d_weights, d_vec = local_gradients(
        ids, lives, full_tables, wts, vec, counts[group]
    )

    d_vec = pad_to(d_vec.reshape(VEC, slabs, cols).transpose(1, 0, 2), MISC_ROWS, 128)
    d_misc = jnp.stack(
        [
            jnp.concatenate([pad_to(d.reshape(slabs, table_rows, D), MISC_ROWS, D), extra], -1)
            for d, extra in zip(d_tables, (d_vec, jnp.zeros_like(d_vec)))
        ]
    ).astype(BF)
    parts = [d_misc] + [
        d.reshape((2, slabs) + slab_form(rows, d.shape[-1])) for d in d_weights
    ]
    arrays = [x[0] if 4 <= k < 12 else x for k, x in enumerate(arrays)]
    natural = rows % 16 == 0

    def formed(k, x):
        if natural or k % 4 not in (1, 2):
            return x
        half = x.shape[-1] // 2
        return x.reshape(2, rows, 2, half).swapaxes(1, 2).reshape((2, 2) + slab_form(rows, half))

    def unformed(k, x):
        if natural or k % 4 not in (1, 2):
            return x
        return x.reshape(2, 2, rows, -1).swapaxes(1, 2).reshape(arrays[k].shape)

    states = [formed(k, x) for k, x in enumerate(arrays[:12])]
    *sums, scalars = reduce_all(
        parts, jnp.broadcast_to(bits, (8, 128)), states, wide, narrow, natural, 2
    )
    grads = [unformed(k, x) for k, x in enumerate(sums[:4])]
    deltas = [unformed(k, x) for k, x in enumerate(sums[4:])]
    new = update(scalars, grads, deltas, arrays)
    new = [x[None] if k < 8 else x for k, x in enumerate(new)]
    return (scalars[1, :1], counts[core].reshape(1), scalars[0, :1], *new)


def solution(mesh):
    rows = P(("rep", "wide", "narrow"), None)
    split = (
        P(None, ("wide", "narrow"), None),
        P(None, ("wide", "narrow"), None),
        P(None, ("wide", "narrow"), None),
        P(None, ("wide", "narrow")),
    )
    own = tuple(P("rep", *spec) for spec in split)
    return jax.shard_map(
        functools.partial(per_device, mesh.shape["wide"], mesh.shape["narrow"]),
        mesh=mesh,
        in_specs=(rows, rows) + split + own + own + split + split,
        out_specs=(P("rep"),) * 3 + own + own + split * 3,
        check_vma=False,
    )
```

```python
import functools
import math

import jax
import jax.numpy as jnp
import numpy as np
from jax import lax
from jax.experimental import pallas as pl
from jax.experimental.pallas import tpu as pltpu
from jax.sharding import PartitionSpec as P

D = 512
HEADS = 8
HD = 64
FF = 2048
V = 256
NB = 32
STEP = 10
VEC = 21
EDGES = (1, 2, 3, 4, 5, 6, 7, 8, 10, 12, 14, 16, 20, 24, 28, 32, 40, 48, 64, 80, 96, 128, 160, 192)
EDGES = EDGES + (256, 320, 384, 512, 640, 768, 1024)
NEG = -1000000000.0
EPS = 1e-05
LOG_TWO = math.log(2.0)
RATE = 0.01
RATE_TABLE = 0.2
BETA_ONE = 0.9
BETA_TWO = 0.95
ADAM_EPS = 1e-08
DECAY = 0.1
CLIP_AT = 0.02
OUTER_RATE = 0.7
OUTER_MOM = 0.9
EVAL_KEEP = 0.9

TILE = 128
VMEM_MIB = 63
BLK = 384
SUB = BLK // TILE
PAIRS = HEADS // 2
PW = 2 * HD
GELU_C = math.sqrt(2.0 / math.pi)
GELU_A = 0.044715

BF = jnp.bfloat16
F32 = jnp.float32
NN = (((1,), (0,)), ((), ()))
NT = (((1,), (1,)), ((), ()))
TN = (((0,), (0,)), ((), ()))


def mm(left, right, dims=NN):
    return lax.dot_general(left, right, dims, preferred_element_type=F32)


def spans(count):
    out = []
    for d in range(count):
        lo, hi = max(TILE * d - (TILE - 1), 0), TILE * d + TILE - 1
        base = sum(e <= lo for e in EDGES)
        out.append((base, [(e, k + 1) for k, e in enumerate(EDGES) if lo < e <= hi]))
    return out


def fold_matrix(count):
    rows = []
    for base, edges in spans(count):
        row = np.zeros(NB, np.float32)
        row[base] += 1
        rows.append(row)
        for _, bucket in edges:
            row = np.zeros(NB, np.float32)
            row[bucket] += 1
            row[bucket - 1] -= 1
            rows.append(row)
    return np.stack(rows)


def tile_distance(d):
    keys = lax.broadcasted_iota(jnp.int32, (TILE, TILE), 0)
    queries = lax.broadcasted_iota(jnp.int32, (TILE, TILE), 1)
    return TILE * d + queries - keys


def build_bias(rel, bias, count):
    for d, (base, edges) in enumerate(spans(count)):
        distance = tile_distance(d)

        def one_head(h, carry, d=d, base=base, edges=edges, distance=distance):
            tile = jnp.full((TILE, TILE), rel[h, base], F32)
            for edge, bucket in edges:
                tile = jnp.where(distance >= edge, rel[h, bucket], tile)
            if d == 0:
                tile = jnp.where(distance < 0, NEG, tile)
            bias[h, d] = tile
            return carry

        lax.fori_loop(0, HEADS, one_head, 0)


def fold_bias(tiles, sums, count):
    at = 0
    for d, (_, edges) in enumerate(spans(count)):
        distance = tile_distance(d)

        def one_head(h, carry, d=d, edges=edges, distance=distance, at=at):
            tile = tiles[h, d]
            sums[h, at : at + 1] = jnp.sum(tile, 0, keepdims=True)
            for n, (edge, _) in enumerate(edges):
                sums[h, at + 1 + n : at + 2 + n] = jnp.sum(
                    jnp.where(distance >= edge, tile, 0.0), 0, keepdims=True
                )
            return carry

        lax.fori_loop(0, HEADS, one_head, 0)
        at += 1 + len(edges)


def fold_rows(count):
    return sum(1 + len(edges) for _, edges in spans(count))


def norm_stats(x):
    centered = x - jnp.mean(x, -1, keepdims=True)
    rstd = lax.rsqrt(jnp.mean(centered * centered, -1, keepdims=True) + EPS)
    return centered * rstd, rstd


def norm_back(dy, xhat, rstd, gain):
    t = dy * gain
    dx = rstd * (
        t - jnp.mean(t, -1, keepdims=True) - xhat * jnp.mean(t * xhat, -1, keepdims=True)
    )
    return dx, jnp.sum(dy * xhat, 0, keepdims=True), jnp.sum(dy, 0, keepdims=True)


def gelu_pair(u):
    square = u * u
    tanh = jnp.tanh(GELU_C * u * (1.0 + GELU_A * square))
    half = 0.5 * (1.0 + tanh)
    slope = half + 0.5 * u * (1.0 - tanh * tanh) * (GELU_C + 3.0 * GELU_C * GELU_A * square)
    return u * half, slope


def split_heads(pair):
    lane = lax.broadcasted_iota(jnp.int32, pair.shape, 1)
    zero = jnp.zeros_like(pair)
    return jnp.concatenate(
        [jnp.where(lane < HD, pair, zero), jnp.where(lane >= HD, pair, zero)], 0
    )


def cell(block, kb, e, qa, nq):
    return block[kb * TILE : (kb + 1) * TILE, (e * nq + qa) * TILE : (e * nq + qa + 1) * TILE]


def softmax_step(keys, values_t, queries, bias, pair, far, diag, nq, nk, state):
    top, total, acc = state
    raw = mm(keys, queries, NT)
    scores = {}
    for e in range(2):
        for qa in range(nq):
            for kb in range(nk):
                if diag and kb > qa:
                    continue
                scores[kb, e, qa] = cell(raw, kb, e, qa, nq) + bias[2 * pair + e, far + qa - kb]
    highest = []
    for e in range(2):
        for qa in range(nq):
            column = [scores[kb, e, qa] for kb in range(nk) if (kb, e, qa) in scores]
            highest.append(jnp.max(functools.reduce(jnp.maximum, column), 0, keepdims=True))
    old_top = top[...]
    new_top = jnp.maximum(old_top, jnp.concatenate(highest, 1))
    alpha = jnp.exp(old_top - new_top)
    sums = []
    columns = []
    for e in range(2):
        for qa in range(nq):
            at = (e * nq + qa) * TILE
            ceiling = new_top[:, at : at + TILE]
            parts, adds = [], None
            for kb in range(nk):
                if (kb, e, qa) not in scores:
                    parts.append(jnp.zeros((TILE, TILE), BF))
                    continue
                p = jnp.exp(scores[kb, e, qa] - ceiling)
                adds = p if adds is None else adds + p
                parts.append(p.astype(BF))
            sums.append(jnp.sum(adds, 0, keepdims=True))
            columns.append(jnp.concatenate(parts, 0))
    top[...] = new_top
    total[...] = alpha * total[...] + jnp.concatenate(sums, 1)
    acc[...] = alpha * acc[...] + mm(values_t, jnp.concatenate(columns, 1))


def softmax_start(state):
    top, total, acc = state
    top[...] = jnp.full(top.shape, NEG, F32)
    total[...] = jnp.zeros(total.shape, F32)
    acc[...] = jnp.zeros(acc.shape, F32)


def softmax_end(state, n):
    top, total, acc = state
    scaled = acc[...] / total[...]
    out = jnp.concatenate([scaled[:HD, :n], scaled[HD:, n:]], 0).astype(BF)
    return out, top[...] + jnp.log(total[...])


def score_back(keys, values, queries, grads, logsum, inner, bias, pair, far, diag, nq, nk, tiles):
    raw = mm(keys, queries, NT)
    d_p = mm(values, grads, NT)
    probs, scores = {}, {}
    for e in range(2):
        for diff in range(-(nk - 1), nq):
            total = None
            if diag and diff < 0:
                continue
            for kb in range(nk):
                qa = kb + diff
                if qa < 0 or qa >= nq:
                    continue
                at = (e * nq + qa) * TILE
                p = jnp.exp(
                    cell(raw, kb, e, qa, nq)
                    + bias[2 * pair + e, far + diff]
                    - logsum[:, at : at + TILE]
                )
                ds = p * (cell(d_p, kb, e, qa, nq) - inner[:, at : at + TILE])
                total = ds if total is None else total + ds
                probs[kb, e, qa] = p.astype(BF)
                scores[kb, e, qa] = ds.astype(BF)
            tiles[2 * pair + e, far + diff] += total

    def whole(parts):
        empty = jnp.zeros((TILE, TILE), BF)
        return jnp.concatenate(
            [
                jnp.concatenate([parts.get((kb, e, qa), empty) for kb in range(nk)], 0)
                for e in range(2)
                for qa in range(nq)
            ],
            1,
        )

    return whole(probs), whole(scores)


def one_hot(column):
    return column == lax.broadcasted_iota(jnp.int32, (column.shape[0], V), 1)


def full_forward_kernel(
    long_blocks,
    wide,
    narrow,
    aux,
    embed,
    wts,
    own_feed,
    own_short,
    rows,
    beta,
    rel,
    x1_out,
    middle_out,
    q_out,
    k_out,
    v_out,
    ot_out,
    lse_out,
    act_out,
    slope_out,
    feed_out,
    short_out,
    bias,
    k_all,
    vt_all,
    middles,
    feed,
    feed_sem,
    *more,
):
    step = pl.program_id(0)
    blocks = pl.num_programs(0) // 2
    state, sems = more[:3], more[3:]
    at = Place(wide, narrow)
    feeds = GatherStream(at, own_feed, feed_out, *sems[0:3])
    shorts = GatherStream(at, own_short, short_out, *sems[3:6])

    def when_at(n, *bodies):
        @pl.when(step == n)
        def _():
            for body in bodies:
                body()

    def hop(stream, first, last=None):
        def body():
            for d in range(first, (last or first) + 1):
                if d < at.W + 2:
                    stream.depth(d)

        return body

    @pl.when(step == 0)
    def _():
        greet(gather_greetings(at))
        feeds.start()
        shorts.start()
        build_bias(rel, bias, bias.shape[1])

    @pl.when(step < blocks)
    def _():
        hot = one_hot(aux[:, 0:1]).astype(BF)
        x = mm(hot, embed[...])
        xhat, _ = norm_stats(x)
        normed = (xhat * rows[0:1] + rows[1:2]).astype(BF)
        queries = (mm(normed, wts[0, :, :D]) * HD**-0.5).astype(BF)
        keys = mm(normed, wts[0, :, D : 2 * D]).astype(BF)
        values = mm(normed, wts[1, :, :D]).astype(BF)
        for pair in range(PAIRS):
            cols = slice(pair * PW, (pair + 1) * PW)
            q_out[0, pair] = queries[:, cols]
            k_out[0, pair] = keys[:, cols]
            v_out[0, pair] = values[:, cols]
            k_all[step, pair] = keys[:, cols]
            vt_all[step, pair] = values[:, cols].T
        middles[step] = x

    when_at(0, hop(feeds, 1))
    when_at(1, hop(feeds, 2))
    when_at(3, hop(shorts, 2))

    @pl.when(step < blocks)
    def _():
        first = jnp.where(step >= long_blocks, long_blocks, 0)

        def one_pair(pair, carry):
            both = split_heads(q_out[0, pair])
            softmax_start(state)

            def earlier(j, inner):
                far = SUB * (step - j)
                softmax_step(
                    k_all[j, pair], vt_all[j, pair], both, bias, pair, far, False, SUB, SUB, state
                )
                return inner

            lax.fori_loop(first, step, earlier, 0)
            softmax_step(
                k_all[step, pair], vt_all[step, pair], both, bias, pair, 0, True, SUB, SUB, state
            )
            ot_out[0, pair], lse_out[0, pair] = softmax_end(state, BLK)
            return carry

        lax.fori_loop(0, PAIRS // 2, one_pair, 0)
        when_at(2, hop(feeds, 4))
        lax.fori_loop(PAIRS // 2, PAIRS, one_pair, 0)
        attended = ot_out[0].reshape(D, BLK).T
        middles[step] = middles[step] + mm(attended, wts[1, :, D : 2 * D])

    when_at(1, hop(feeds, 3))
    when_at(2, hop(feeds, 5, at.W + 1), hop(shorts, 1))
    when_at(3, hop(shorts, 3))

    @pl.when(step == blocks)
    def _():
        feeds.finish()
        load = pltpu.make_async_copy(feed_out, feed, feed_sem)
        load.start()
        load.wait()

    @pl.when(step >= blocks)
    def _():
        block = jnp.maximum(step - blocks, 0)
        middle = middles[block]
        middle_out[...] = middle
        xhat, _ = norm_stats(middle)
        second = (xhat * rows[2:3] + rows[3:4]).astype(BF)
        active, slope = gelu_pair(mm(second, feed_half(feed, 0)) + beta[...])
        active = active.astype(BF)
        act_out[...] = active
        slope_out[...] = slope.astype(BF)
        x1_out[...] = middle + mm(active, feed_half(feed, 1), NT) + rows[4:5]

    when_at(4, hop(shorts, 4))
    when_at(5, hop(shorts, 5, at.W + 1))

    @pl.when(step == 2 * blocks - 1)
    def _():
        shorts.finish()


def feed_half(feed, half):
    value = feed[half]
    return value.reshape(D, FF)


def whole_spec(shape):
    return pl.BlockSpec(shape, lambda i: (0,) * len(shape), pipeline_mode=pl.Buffered(1))


def params(mib, **more):
    return pltpu.CompilerParams(vmem_limit_bytes=mib * 2**20, **more)


def state_scratch(n):
    return [pltpu.VMEM((1, 2 * n), F32), pltpu.VMEM((1, 2 * n), F32), pltpu.VMEM((PW, 2 * n), F32)]


def full_forward(aux, embed, wts, own_feed, own_short, rows, beta, rel, long_blocks, wide, narrow):
    tokens = aux.shape[0]
    blocks = tokens // BLK
    far = SUB * long_blocks
    slabs = wide * narrow

    def early(i):
        return jnp.minimum(i, blocks - 1)

    def late(i):
        return jnp.maximum(i - blocks, 0)

    def heads(n, width):
        return (
            jax.ShapeDtypeStruct((blocks, PAIRS, n, width), BF),
            pl.BlockSpec((1, PAIRS, n, width), lambda i: (early(i), 0, 0, 0)),
        )

    def flat(width, kind):
        return (
            jax.ShapeDtypeStruct((tokens, width), kind),
            pl.BlockSpec((BLK, width), lambda i: (late(i), 0)),
        )

    anywhere = pl.BlockSpec(memory_space=pl.ANY)
    outs = [flat(D, F32), flat(D, F32)] + [heads(BLK, PW)] * 3 + [heads(PW, BLK)]
    outs.append(
        (
            jax.ShapeDtypeStruct((blocks, PAIRS, 1, 2 * BLK), F32),
            pl.BlockSpec((1, PAIRS, 1, 2 * BLK), lambda i: (early(i), 0, 0, 0)),
        )
    )
    outs += [flat(FF, BF)] * 2
    outs += [
        (jax.ShapeDtypeStruct((2, slabs) + own.shape, BF), anywhere) for own in (own_feed, own_short)
    ]
    return pl.pallas_call(
        functools.partial(full_forward_kernel, long_blocks, wide, narrow),
        grid=(2 * blocks,),
        in_specs=[
            pl.BlockSpec((BLK, aux.shape[1]), lambda i: (early(i), 0)),
            whole_spec(embed.shape),
            whole_spec(wts.shape),
            anywhere,
            anywhere,
            whole_spec(rows.shape),
            whole_spec(beta.shape),
            pl.BlockSpec(memory_space=pltpu.SMEM),
        ],
        out_specs=[spec for _, spec in outs],
        out_shape=[shape for shape, _ in outs],
        scratch_shapes=[
            pltpu.VMEM((HEADS, far, TILE, TILE), F32),
            pltpu.VMEM((blocks, PAIRS, BLK, PW), BF),
            pltpu.VMEM((blocks, PAIRS, PW, BLK), BF),
            pltpu.VMEM((blocks, BLK, D), F32),
            pltpu.VMEM((2, slabs) + own_feed.shape, BF),
            pltpu.SemaphoreType.DMA,
        ]
        + state_scratch(BLK)
        + gather_sems(slabs) * 2,
        compiler_params=params(VMEM_MIB, collective_id=4, has_side_effects=True),
        name="full_forward",
    )(aux, embed, wts, own_feed, own_short, rows, beta, rel)


PAD = 8


def middle_kernel(
    seq,
    x1,
    aux,
    head,
    wts,
    rows,
    beta,
    rel,
    scale,
    final,
    dx_out,
    d_attn,
    d_feed,
    d_head,
    row_grads,
    d_beta,
    bits_out,
    sums,
    xp,
    pooled,
    mixed,
    ot,
    lse,
    active_s,
    slope_s,
    middle_s,
    bias,
    tiles,
    d_mixed,
    *state,
):
    n_long = seq // 3
    spots = ((PAD, 0, n_long), (2 * PAD + seq, n_long, TILE))
    build_bias(rel, bias, bias.shape[1])
    tiles[...] = jnp.zeros_like(tiles)
    lanes = D // TILE
    for c in range(lanes):
        xp[c, 0:PAD] = jnp.zeros((PAD, TILE), F32)
        xp[c, PAD + seq : 2 * PAD + seq] = jnp.zeros((PAD, TILE), F32)
        xp[c, PAD : PAD + seq] = x1[0:seq, c * TILE : (c + 1) * TILE]
        xp[c, 2 * PAD + seq :] = x1[seq:, c * TILE : (c + 1) * TILE]
    for start, at, n in spots:
        for c in range(lanes):
            pooled[at : at + n, c * TILE : (c + 1) * TILE] = (
                xp[c, pl.ds(start - 2, n, stride=3)]
                + xp[c, pl.ds(start - 1, n, stride=3)]
                + xp[c, pl.ds(start, n, stride=3)]
            ) / 3.0

    xhat, _ = norm_stats(pooled[...])
    normed = (xhat * rows[0:1] + rows[1:2]).astype(BF)
    for part in range(3):
        half, at = part // 2, part % 2 * D
        value = mm(normed, wts[half, :, at : at + D])
        value = (value * HD**-0.5 if part == 0 else value).astype(BF)
        for pair in range(PAIRS):
            mixed[part, pair] = value[:, pair * PW : (pair + 1) * PW]

    def forward_pair(pair, carry):
        for at, n, offset in ((0, n_long, 0), (n_long, TILE, 2 * n_long)):
            top, total, acc = state
            wide = pl.ds(0, 2 * n)
            part = (top.at[:, wide], total.at[:, wide], acc.at[:, wide])
            softmax_start(part)
            values_t = mixed[2, pair, at : at + n].T
            both = split_heads(mixed[0, pair, at : at + n])
            count = n // TILE
            softmax_step(
                mixed[1, pair, at : at + n], values_t, both, bias, pair, 0, True, count, count, part
            )
            ot[pair, :, at : at + n], lse[pair, :, offset : offset + 2 * n] = softmax_end(part, n)
        return carry

    lax.fori_loop(0, PAIRS, forward_pair, 0)
    middle = pooled[...] + mm(ot[...].reshape(D, ot.shape[2]).T, wts[1, :, D : 2 * D])
    middle_s[...] = middle
    xhat, _ = norm_stats(middle)
    second = (xhat * rows[2:3] + rows[3:4]).astype(BF)
    active, slope = gelu_pair(mm(second, wts[0, :, 2 * D :]) + beta[...])
    active_s[...] = active.astype(BF)
    slope_s[...] = slope.astype(BF)
    short = middle + mm(active_s[...], wts[1, :, 2 * D :], NT) + rows[4:5]
    for start, at, n in spots:
        for c in range(lanes):
            part = short[at : at + n, c * TILE : (c + 1) * TILE]
            for k in range(3):
                where = pl.ds(start + k, n, stride=3)
                xp[c, where] = xp[c, where] + part

    d_head[...] = jnp.zeros_like(d_head)
    row_grads[...] = jnp.zeros_like(row_grads)

    def loss_block(b, bits):
        start = pl.multiple_of(b * BLK + jnp.where(b * BLK >= seq, 2 * PAD, PAD), PAD)
        joined = jnp.concatenate([xp[c, pl.ds(start, BLK)] for c in range(lanes)], 1)
        xhat, rstd = norm_stats(joined)
        last = (xhat * final[0:1] + final[1:2]).astype(BF)
        logits = mm(last, head[...], NT) * D**-0.5
        info = aux[pl.ds(pl.multiple_of(b * BLK, BLK), BLK), :]
        weight = info[:, 2:3].astype(F32)
        hot = one_hot(info[:, 1:2])
        highest = jnp.max(logits, -1, keepdims=True)
        powers = jnp.exp(logits - highest)
        total = jnp.sum(powers, -1, keepdims=True)
        picked = jnp.sum(jnp.where(hot, logits, 0.0), -1, keepdims=True)
        lost = weight * (highest + jnp.log(total) - picked)
        d_logits = ((powers / total - hot.astype(F32)) * (weight * scale[0, 0])).astype(BF)
        d_head[...] += mm(d_logits, last, TN) * D**-0.5
        d_last = mm(d_logits, head[...]) * D**-0.5
        dx, d_gain, d_shift = norm_back(d_last, xhat, rstd, final[0:1])
        row_grads[0:1] += d_gain
        row_grads[1:2] += d_shift
        for c in range(lanes):
            xp[c, pl.ds(start, BLK)] = dx[:, c * TILE : (c + 1) * TILE]
        return bits + lost

    bits = lax.fori_loop(0, x1.shape[0] // BLK, loss_block, jnp.zeros((BLK, 1), F32))
    bits_out[...] = jnp.sum(bits, 0, keepdims=True) / LOG_TWO

    d_short = jnp.concatenate(
        [
            jnp.concatenate(
                [
                    xp[c, pl.ds(start, n, stride=3)]
                    + xp[c, pl.ds(start + 1, n, stride=3)]
                    + xp[c, pl.ds(start + 2, n, stride=3)]
                    for c in range(lanes)
                ],
                1,
            )
            for start, at, n in spots
        ],
        0,
    )
    d_branch = d_short.astype(BF)
    row_grads[6:7] = jnp.sum(d_branch.astype(F32), 0, keepdims=True)
    d_feed[1] = mm(d_branch, active_s[...], TN).astype(BF)
    d_pre = (mm(d_branch, wts[1, :, 2 * D :]) * slope_s[...].astype(F32)).astype(BF)
    d_beta[...] = jnp.sum(d_pre.astype(F32), 0, keepdims=True)
    xhat, rstd = norm_stats(middle_s[...])
    second = (xhat * rows[2:3] + rows[3:4]).astype(BF)
    d_feed[0] = mm(second, d_pre, TN).astype(BF)
    dx, d_gain, d_shift = norm_back(mm(d_pre, wts[0, :, 2 * D :], NT), xhat, rstd, rows[2:3])
    row_grads[4:5] = d_gain
    row_grads[5:6] = d_shift
    d_middle = d_short + dx
    d_mix = d_middle.astype(BF)
    ot_all = ot[...].reshape(D, ot.shape[2])
    d_attn[1, :, D:] = mm(ot_all, d_mix).astype(BF)
    d_att = mm(d_mix, wts[1, :, D : 2 * D], NT).astype(BF)
    for pair in range(PAIRS):
        mixed[3, pair] = d_att[:, pair * PW : (pair + 1) * PW]

    def backward_pair(pair, carry):
        for at, n, offset in ((0, n_long, 0), (n_long, TILE, 2 * n_long)):
            d_out = mixed[3, pair, at : at + n]
            product = (d_out.astype(F32).T) * ot[pair, :, at : at + n].astype(F32)
            inner = jnp.concatenate(
                [
                    jnp.sum(product[:HD], 0, keepdims=True),
                    jnp.sum(product[HD:], 0, keepdims=True),
                ],
                1,
            )
            queries = split_heads(mixed[0, pair, at : at + n])
            grads = split_heads(d_out)
            keys = mixed[1, pair, at : at + n]
            count = n // TILE
            p, ds = score_back(
                keys,
                mixed[2, pair, at : at + n],
                queries,
                grads,
                lse[pair, :, offset : offset + 2 * n],
                inner,
                bias,
                pair,
                0,
                True,
                count,
                count,
                tiles,
            )
            dq = mm(keys.T, ds)
            dq = jnp.concatenate([dq[:HD, :n], dq[HD:, n:]], 0) * HD**-0.5
            d_mixed[0, pair, at : at + n] = dq.T.astype(BF)
            d_mixed[1, pair, at : at + n] = mm(ds, queries).astype(BF)
            d_mixed[2, pair, at : at + n] = mm(p, grads).astype(BF)
        return carry

    lax.fori_loop(0, PAIRS, backward_pair, 0)
    fold_bias(tiles, sums, tiles.shape[1])
    d_in = jnp.concatenate([d_mixed[part, pair] for part in range(3) for pair in range(PAIRS)], 1)
    xhat, rstd = norm_stats(pooled[...])
    normed = (xhat * rows[0:1] + rows[1:2]).astype(BF)
    d_attn[0] = mm(normed, d_in[:, : 2 * D], TN).astype(BF)
    d_attn[1, :, :D] = mm(normed, d_in[:, 2 * D :], TN).astype(BF)
    dx, d_gain, d_shift = norm_back(mm(d_in[:, : 2 * D], wts[0, :, : 2 * D], NT) + mm(d_in[:, 2 * D :], wts[1, :, :D], NT), xhat, rstd, rows[0:1])
    row_grads[2:3] = d_gain
    row_grads[3:4] = d_shift
    d_pool = (d_middle + dx) / 3.0
    for start, at, n in spots:
        for c in range(lanes):
            part = d_pool[at : at + n, c * TILE : (c + 1) * TILE]
            for k in range(3):
                where = pl.ds(start - 2 + k, n, stride=3)
                xp[c, where] = xp[c, where] + part
    for c in range(lanes):
        dx_out[0:seq, c * TILE : (c + 1) * TILE] = xp[c, PAD : PAD + seq]
        dx_out[seq:, c * TILE : (c + 1) * TILE] = xp[c, 2 * PAD + seq :]


def middle_stage(x1, aux, head, wts, rows, beta, rel, scale, final, seq):
    tokens = x1.shape[0]
    n_long = seq // 3
    short = n_long + TILE
    far = n_long // TILE
    vm = pl.BlockSpec(memory_space=pltpu.VMEM)
    return pl.pallas_call(
        functools.partial(middle_kernel, seq),
        in_specs=[vm] * 6 + [pl.BlockSpec(memory_space=pltpu.SMEM)] * 2 + [vm],
        out_specs=[vm] * 8,
        out_shape=[
            jax.ShapeDtypeStruct((tokens, D), F32),
            jax.ShapeDtypeStruct((2, D, 2 * D), BF),
            jax.ShapeDtypeStruct((2, D, FF), BF),
            jax.ShapeDtypeStruct((V, D), F32),
            jax.ShapeDtypeStruct((8, D), F32),
            jax.ShapeDtypeStruct((1, FF), F32),
            jax.ShapeDtypeStruct((1, 1), F32),
            jax.ShapeDtypeStruct((HEADS, fold_rows(far), TILE), F32),
        ],
        scratch_shapes=[
            pltpu.VMEM((D // TILE, tokens + 2 * PAD, TILE), F32),
            pltpu.VMEM((short, D), F32),
            pltpu.VMEM((4, PAIRS, short, PW), BF),
            pltpu.VMEM((PAIRS, PW, short), BF),
            pltpu.VMEM((PAIRS, 1, 2 * short), F32),
            pltpu.VMEM((short, FF), BF),
            pltpu.VMEM((short, FF), BF),
            pltpu.VMEM((short, D), F32),
            pltpu.VMEM((HEADS, far, TILE, TILE), F32),
            pltpu.VMEM((HEADS, far, TILE, TILE), F32),
            pltpu.VMEM((3, PAIRS, short, PW), BF),
        ]
        + state_scratch(n_long),
        compiler_params=params(VMEM_MIB),
        name="middle_stage",
    )(x1, aux, head, wts, rows, beta, rel, scale, final)


def feed_back_kernel(
    wide,
    narrow,
    dx,
    act,
    slope,
    middle,
    wts,
    rows,
    ready,
    dm_out,
    d_feed,
    row_grads,
    d_beta,
    sums_out,
    up,
    down,
    *scratch,
):
    step = pl.program_id(0)
    at = Place(wide, narrow)
    stream = ScatterStream(at, ready, halves_out(sums_out), *scratch[:6], scratch[6:])

    @pl.when(step == 0)
    def _():
        greet(scatter_greetings(at))
        stream.start()
        up[...] = jnp.zeros_like(up)
        down[...] = jnp.zeros_like(down)
        row_grads[...] = jnp.zeros_like(row_grads)
        d_beta[...] = jnp.zeros_like(d_beta)

    d_result = dx[...]
    d_branch = d_result.astype(BF)
    row_grads[2:3] += jnp.sum(d_branch.astype(F32), 0, keepdims=True)
    down[...] += mm(d_branch, act[...], TN)
    d_pre = (mm(d_branch, wts[1]) * slope[...].astype(F32)).astype(BF)
    d_beta[...] += jnp.sum(d_pre.astype(F32), 0, keepdims=True)
    xhat, rstd = norm_stats(middle[...])
    second = (xhat * rows[2:3] + rows[3:4]).astype(BF)
    up[...] += mm(second, d_pre, TN)
    dn, d_gain, d_shift = norm_back(mm(d_pre, wts[0], NT), xhat, rstd, rows[2:3])
    row_grads[0:1] += d_gain
    row_grads[1:2] += d_shift
    dm_out[...] = d_result + dn
    for n, body in enumerate((stream.stage_first, stream.stage_second, stream.stage_along)):
        pl.when(step == n)(body)

    @pl.when(step == pl.num_programs(0) - 1)
    def _():
        stream.stage_home()
        d_feed[0] = up[...].astype(BF)
        d_feed[1] = down[...].astype(BF)
        stream.finish()


def halves_out(ref):
    return [ref.at[0], ref.at[1]]


def feed_back(dx, act, slope, middle, wts, rows, ready, wide, narrow):
    tokens = dx.shape[0]
    form = ready.shape[2:]

    def flat(width):
        return pl.BlockSpec((BLK, width), lambda i: (i, 0))

    return pl.pallas_call(
        functools.partial(feed_back_kernel, wide, narrow),
        grid=(tokens // BLK,),
        in_specs=[flat(D), flat(FF), flat(FF), flat(D), whole_spec(wts.shape), whole_spec(rows.shape)]
        + [pl.BlockSpec(memory_space=pl.ANY)],
        out_specs=[
            flat(D),
            whole_spec((2, D, FF)),
            whole_spec((8, D)),
            whole_spec((1, FF)),
            whole_spec((2,) + form),
        ],
        out_shape=[
            jax.ShapeDtypeStruct((tokens, D), F32),
            jax.ShapeDtypeStruct((2, D, FF), BF),
            jax.ShapeDtypeStruct((8, D), F32),
            jax.ShapeDtypeStruct((1, FF), F32),
            jax.ShapeDtypeStruct((2,) + form, F32),
        ],
        scratch_shapes=[pltpu.VMEM((D, FF), F32), pltpu.VMEM((D, FF), F32)]
        + scatter_scratch(wide, narrow, form),
        compiler_params=params(VMEM_MIB, collective_id=5, has_side_effects=True),
        name="feed_back",
    )(dx, act, slope, middle, wts, rows, ready)


def attention_back_kernel(
    long_blocks,
    wide,
    narrow,
    dm,
    aux,
    ot,
    lse,
    q_all,
    k_all,
    v_all,
    embed,
    wts,
    rows,
    rel,
    ready_a,
    ready_b,
    d_attn,
    d_embed,
    row_grads,
    sums,
    out_a,
    out_b,
    bias,
    tiles,
    kt_all,
    dk_all,
    dv_all,
    dq_t,
    d_att,
    inner,
    weights,
    d_mixed,
    *scratch,
):
    step = pl.program_id(0)
    blocks = pl.num_programs(0)
    i = blocks - 1 - step
    at = Place(wide, narrow)
    one = ScatterStream(at, ready_a, halves_out(out_a), *scratch[:6], scratch[6:12])
    two = ScatterStream(at, ready_b, halves_out(out_b), *scratch[12:18], scratch[18:])

    def when_at(n, *bodies):
        @pl.when(step == n)
        def _():
            for body in bodies:
                body()

    @pl.when(step == 0)
    def _():
        greet(scatter_greetings(at))
        one.start()
        two.start()
        build_bias(rel, bias, bias.shape[1])
        tiles[...] = jnp.zeros_like(tiles)
        dk_all[...] = jnp.zeros_like(dk_all)
        dv_all[...] = jnp.zeros_like(dv_all)
        weights[...] = jnp.zeros_like(weights)
        d_embed[...] = jnp.zeros_like(d_embed)
        row_grads[...] = jnp.zeros_like(row_grads)

        def turn(n, carry):
            for pair in range(PAIRS):
                kt_all[n, pair] = k_all[n, pair].T
            return carry

        lax.fori_loop(0, blocks, turn, 0)

    d_middle = dm[...]
    d_mix = d_middle.astype(BF)
    weights[1, :, D:] += mm(ot[0].reshape(D, BLK), d_mix)
    out = mm(d_mix, wts[1, :, D : 2 * D], NT).astype(BF)
    for pair in range(PAIRS):
        d_att[pair] = out[:, pair * PW : (pair + 1) * PW]
    product = mm(wts[1, :, D : 2 * D], d_mix, NT).astype(BF).astype(F32) * ot[0].reshape(
        D, BLK
    ).astype(F32)
    for pair in range(PAIRS):
        top = pair * PW
        inner[pair] = jnp.concatenate(
            [
                jnp.sum(product[top : top + HD], 0, keepdims=True),
                jnp.sum(product[top + HD : top + PW], 0, keepdims=True),
            ],
            1,
        )
    first = jnp.where(i >= long_blocks, long_blocks, 0)

    def one_pair(pair, carry):
        queries = split_heads(q_all[i, pair])
        grads = split_heads(d_att[pair])
        dq_t[...] = jnp.zeros_like(dq_t)

        def with_block(j, far, diag):
            p, ds = score_back(
                k_all[j, pair],
                v_all[j, pair],
                queries,
                grads,
                lse[0, pair],
                inner[pair],
                bias,
                pair,
                far,
                diag,
                SUB,
                SUB,
                tiles,
            )
            dv_all[j, pair] += mm(p, grads)
            dk_all[j, pair] += mm(ds, queries)
            dq_t[...] += mm(kt_all[j, pair], ds)

        def earlier(j, inside):
            with_block(j, SUB * (i - j), False)
            return inside

        lax.fori_loop(first, i, earlier, 0)
        with_block(i, 0, True)
        total = dq_t[...]
        total = jnp.concatenate([total[:HD, :BLK], total[HD:, BLK:]], 0) * HD**-0.5
        d_mixed[0, pair] = total.T.astype(BF)
        d_mixed[1, pair] = dk_all[i, pair].astype(BF)
        d_mixed[2, pair] = dv_all[i, pair].astype(BF)
        return carry

    when_at(0, one.stage_first)
    lax.fori_loop(0, PAIRS // 2, one_pair, 0)
    when_at(1, two.stage_first)
    when_at(2, two.stage_second)
    when_at(3, one.stage_home, two.stage_along)
    lax.fori_loop(PAIRS // 2, PAIRS, one_pair, 0)
    when_at(1, one.stage_second)
    when_at(2, one.stage_along)
    d_in = jnp.concatenate([d_mixed[part, pair] for part in range(3) for pair in range(PAIRS)], 1)
    hot = one_hot(aux[:, 0:1]).astype(BF)
    xhat, rstd = norm_stats(mm(hot, embed[...]))
    normed = (xhat * rows[0:1] + rows[1:2]).astype(BF)
    weights[0] += mm(normed, d_in[:, : 2 * D], TN)
    weights[1, :, :D] += mm(normed, d_in[:, 2 * D :], TN)
    dx, d_gain, d_shift = norm_back(mm(d_in[:, : 2 * D], wts[0, :, : 2 * D], NT) + mm(d_in[:, 2 * D :], wts[1, :, :D], NT), xhat, rstd, rows[0:1])
    row_grads[0:1] += d_gain
    row_grads[1:2] += d_shift
    d_embed[...] += mm(hot, (d_middle + dx).astype(BF), TN)

    @pl.when(step == blocks - 1)
    def _():
        two.stage_home()
        d_attn[...] = weights[...].astype(BF)
        fold_bias(tiles, sums, tiles.shape[1])
        one.finish()
        two.finish()


def attention_back(
    dm, aux, ot, lse, q, k, v, embed, wts, rows, rel, ready_a, ready_b, long_blocks, wide, narrow
):
    tokens = dm.shape[0]
    blocks = tokens // BLK
    far = SUB * long_blocks

    def turned(shape):
        return pl.BlockSpec(shape, lambda s: (blocks - 1 - s,) + (0,) * (len(shape) - 1))

    return pl.pallas_call(
        functools.partial(attention_back_kernel, long_blocks, wide, narrow),
        grid=(blocks,),
        in_specs=[
            turned((BLK, D)),
            turned((BLK, aux.shape[1])),
            turned((1, PAIRS, PW, BLK)),
            turned((1, PAIRS, 1, 2 * BLK)),
            whole_spec(q.shape),
            whole_spec(k.shape),
            whole_spec(v.shape),
            whole_spec(embed.shape),
            whole_spec((2, D, 2 * D)),
            whole_spec(rows.shape),
            pl.BlockSpec(memory_space=pltpu.SMEM),
            pl.BlockSpec(memory_space=pl.ANY),
            pl.BlockSpec(memory_space=pl.ANY),
        ],
        out_specs=[
            whole_spec((2, D, 2 * D)),
            whole_spec((V, D)),
            whole_spec((8, D)),
            whole_spec((HEADS, fold_rows(far), TILE)),
            whole_spec((2,) + ready_a.shape[2:]),
            whole_spec((2,) + ready_b.shape[2:]),
        ],
        out_shape=[
            jax.ShapeDtypeStruct((2, D, 2 * D), BF),
            jax.ShapeDtypeStruct((V, D), F32),
            jax.ShapeDtypeStruct((8, D), F32),
            jax.ShapeDtypeStruct((HEADS, fold_rows(far), TILE), F32),
            jax.ShapeDtypeStruct((2,) + ready_a.shape[2:], F32),
            jax.ShapeDtypeStruct((2,) + ready_b.shape[2:], F32),
        ],
        scratch_shapes=[
            pltpu.VMEM((HEADS, far, TILE, TILE), F32),
            pltpu.VMEM((HEADS, far, TILE, TILE), F32),
            pltpu.VMEM((blocks, PAIRS, PW, BLK), BF),
            pltpu.VMEM((blocks, PAIRS, BLK, PW), F32),
            pltpu.VMEM((blocks, PAIRS, BLK, PW), F32),
            pltpu.VMEM((PW, 2 * BLK), F32),
            pltpu.VMEM((PAIRS, BLK, PW), BF),
            pltpu.VMEM((PAIRS, 1, 2 * BLK), F32),
            pltpu.VMEM((2, D, 2 * D), F32),
            pltpu.VMEM((3, PAIRS, BLK, PW), BF),
        ]
        + scatter_scratch(wide, narrow, ready_a.shape[2:])
        + scatter_scratch(wide, narrow, ready_b.shape[2:]),
        compiler_params=params(VMEM_MIB, collective_id=6, has_side_effects=True),
        name="attention_back",
    )(dm, aux, ot, lse, q, k, v, embed, wts, rows, rel, ready_a, ready_b)


MESH = pl.DeviceIdType.MESH
MISC_ROWS = 32
MISC_COLS = D + 128


class Place:
    def __init__(self, wide, narrow):
        self.W, self.N = wide, narrow
        self.slabs = wide * narrow
        self.c = lax.axis_index("rep")
        self.w = lax.axis_index("wide")
        self.n = lax.axis_index("narrow")
        hi, lo = self.n // 2, self.n % 2
        self.a0 = (1 - self.c) * hi + self.c * lo
        self.b0 = (1 - self.c) * lo + self.c * hi
        self.group = self.w // (wide // 2)

    def narrow_of(self, a, b):
        return a * (2 - self.c) + b * (1 + self.c)

    def slab(self, w, a, b):
        return w * self.N + self.narrow_of(a, b)

    def chip(self, w, a, b):
        return {"wide": w, "narrow": self.narrow_of(a, b)}

    def sibling(self):
        return {"rep": 1 - self.c}


def greet(devices):
    barrier = pltpu.get_barrier_semaphore()
    for device in devices:
        pl.semaphore_signal(barrier, inc=1, device_id=device, device_id_type=MESH)
    pl.semaphore_wait(barrier, len(devices))


def slab_form(rows, cols):
    return (rows, cols) if rows % 16 == 0 else (16, rows * cols // 16)


def gather_greetings(at):
    return [
        {"wide": lax.rem(at.w + 1, at.W)},
        {"wide": lax.rem(at.w + at.W - 1, at.W)},
        at.chip(at.w, at.a0, 1 - at.b0),
        at.chip(at.w, 1 - at.a0, at.b0),
        at.sibling(),
    ]


class GatherStream:
    def __init__(self, at, src, out, send, recv, local):
        self.at, self.src, self.out, self.send, self.recv = at, src, out, send, recv
        self.own = at.slab(at.w, at.a0, at.b0)
        self.keep = pltpu.make_async_copy(src, out.at[at.c, self.own], local)

    def copy(self, ref, slab, way, peer):
        return pltpu.make_async_remote_copy(
            src_ref=ref,
            dst_ref=self.out.at[self.at.c, slab],
            send_sem=self.send.at[way, slab],
            recv_sem=self.recv.at[1 if way == 4 else 0, slab],
            device_id=peer,
            device_id_type=MESH,
        )

    def arrived(self, slab, half, kind):
        pltpu.make_async_remote_copy(
            src_ref=self.out.at[half, slab],
            dst_ref=self.out.at[half, slab],
            send_sem=self.send.at[4, slab],
            recv_sem=self.recv.at[kind, slab],
            device_id=self.at.sibling(),
            device_id_type=MESH,
        ).wait_recv()

    def onward(self, w, mine, act, up, down):
        at = self.at
        slab = at.slab(w, at.a0, at.b0)
        ref = self.src if mine else self.out.at[at.c, slab]
        if up:

            @pl.when(at.w < at.W - 1)
            def _():
                act(self.copy(ref, slab, 0, {"wide": jnp.minimum(at.w + 1, at.W - 1)}))

        if down:

            @pl.when(at.w > 0)
            def _():
                act(self.copy(ref, slab, 1, {"wide": jnp.maximum(at.w - 1, 0)}))

        act(self.copy(ref, slab, 2, at.chip(at.w, at.a0, 1 - at.b0)))
        act(self.copy(ref, slab, 3, at.chip(at.w, 1 - at.a0, at.b0)))
        act(self.copy(ref, slab, 4, at.sibling()))

    def across(self, w, act):
        at = self.at
        slab = at.slab(w, at.a0, 1 - at.b0)
        ref = self.out.at[at.c, slab]
        act(self.copy(ref, slab, 3, at.chip(at.w, 1 - at.a0, at.b0)))
        act(self.copy(ref, slab, 4, at.sibling()))

    def last(self, w, act):
        at = self.at
        for b in (at.b0, 1 - at.b0):
            slab = at.slab(w, 1 - at.a0, b)
            act(self.copy(self.out.at[at.c, slab], slab, 4, at.sibling()))

    def both_sides(self, k, body):
        at = self.at

        @pl.when(at.w - k >= 0)
        def _():
            body(jnp.maximum(at.w - k, 0), True)

        @pl.when(at.w + k < at.W)
        def _():
            body(jnp.minimum(at.w + k, at.W - 1), False)

    def start(self):
        self.keep.start()
        self.onward(self.at.w, True, lambda copy: copy.start(), True, True)

    def from_along(self, k):
        def along(w, below):
            self.arrived(self.at.slab(w, self.at.a0, self.at.b0), self.at.c, 0)
            self.onward(w, False, lambda copy: copy.start(), below, not below)

        self.both_sides(k, along)

    def from_first(self, w):
        self.arrived(self.at.slab(w, self.at.a0, 1 - self.at.b0), self.at.c, 0)
        self.across(w, lambda copy: copy.start())

    def from_second(self, w, b):
        at = self.at
        slab = at.slab(w, 1 - at.a0, b)
        self.arrived(slab, at.c, 0)
        self.copy(self.out.at[at.c, slab], slab, 4, at.sibling()).start()

    def depth(self, d):
        at = self.at
        if 1 <= d < at.W:
            self.from_along(d)
        for k, body in (
            (d - 1, lambda w, below=None: self.from_first(w)),
            (d - 1, lambda w, below=None: self.from_second(w, at.b0)),
            (d - 2, lambda w, below=None: self.from_second(w, 1 - at.b0)),
        ):
            if k == 0:
                body(at.w)
            elif 0 < k < at.W:
                self.both_sides(k, body)

    def depths(self):
        return range(1, self.at.W + 2)

    def finish(self):
        at = self.at
        done = lambda copy: copy.wait_send()
        self.keep.wait()
        self.onward(at.w, True, done, True, True)
        self.across(at.w, done)
        self.last(at.w, done)

        def body(k, carry):
            self.both_sides(
                k, lambda w, below: self.onward(w, False, done, below, not below)
            )
            self.both_sides(k, lambda w, below: self.across(w, done))
            self.both_sides(k, lambda w, below: self.last(w, done))
            return carry

        lax.fori_loop(1, at.W, body, 0)

        def from_sibling(slab, carry):
            self.arrived(slab, 1 - at.c, 1)
            return carry

        lax.fori_loop(0, at.slabs, from_sibling, 0)


def gather_sems(slabs):
    return [
        pltpu.SemaphoreType.DMA((5, slabs)),
        pltpu.SemaphoreType.DMA((2, slabs)),
        pltpu.SemaphoreType.DMA,
    ]


def gather_kernel(wide, narrow, count, *refs):
    at = Place(wide, narrow)
    greet(gather_greetings(at))
    streams = [
        GatherStream(at, refs[i], refs[count + i], *refs[2 * count + 3 * i : 2 * count + 3 * i + 3])
        for i in range(count)
    ]
    for stream in streams:
        stream.start()
    for d in streams[0].depths():
        for stream in streams:
            stream.depth(d)
    for stream in streams:
        stream.finish()


def gather_all(arrays, wide, narrow, collective_id):
    slabs = wide * narrow
    anywhere = pl.BlockSpec(memory_space=pl.ANY)
    scratch = []
    for _ in arrays:
        scratch += gather_sems(slabs)
    return pl.pallas_call(
        functools.partial(gather_kernel, wide, narrow, len(arrays)),
        in_specs=[anywhere] * len(arrays),
        out_specs=[anywhere] * len(arrays),
        out_shape=[jax.ShapeDtypeStruct((2, slabs) + x.shape, x.dtype) for x in arrays],
        scratch_shapes=scratch,
        compiler_params=params(VMEM_MIB, collective_id=collective_id, has_side_effects=True),
        name="gather_all",
    )(*arrays)


class ScatterStream:
    def __init__(self, at, src, out, own, side, first, second, along, fin, sems):
        self.at, self.src, self.out = at, src, out
        self.own, self.side, self.first, self.second, self.along, self.fin = (
            own,
            side,
            first,
            second,
            along,
            fin,
        )
        self.local, self.side_sem, self.first_sem, self.second_sem, self.along_sem, self.fin_sem = sems
        self.levels = (at.W // 2).bit_length() - 1

    def remote(self, src, dst, sems, index, device):
        return pltpu.make_async_remote_copy(
            src_ref=src,
            dst_ref=dst,
            send_sem=sems.at[(0,) + index],
            recv_sem=sems.at[(1,) + index],
            device_id=device,
            device_id_type=MESH,
        )

    def side_copy(self, slab):
        c = self.at.c
        return self.remote(
            self.src.at[1 - c, slab], self.side.at[slab], self.side_sem, (slab,), self.at.sibling()
        )

    def own_copy(self):
        return pltpu.make_async_copy(self.src.at[self.at.c], self.own, self.local)

    def first_copy(self, w, b):
        at = self.at
        slab = at.slab(w, 1 - at.a0, b)
        return self.remote(
            self.own.at[slab],
            self.first.at[2 * w + b],
            self.first_sem,
            (2 * w + b,),
            at.chip(at.w, 1 - at.a0, at.b0),
        )

    def second_copy(self, w):
        at = self.at
        return self.remote(
            self.own.at[at.slab(w, at.a0, 1 - at.b0)],
            self.second.at[w],
            self.second_sem,
            (w,),
            at.chip(at.w, at.a0, 1 - at.b0),
        )

    def along_place(self, level):
        W = self.at.W
        return W - (W >> level), W >> (level + 1)

    def along_copy(self, level, k):
        at = self.at
        unit = 1 << level
        bit = (at.w // unit) % 2
        partner = at.w + unit * (1 - 2 * bit)
        start, _ = self.along_place(level)
        w = k * 2 * unit + partner % (2 * unit)
        return self.remote(
            self.own.at[at.slab(w, at.a0, at.b0)],
            self.along.at[start + k],
            self.along_sem,
            (start + k,),
            {"wide": partner},
        )

    def home(self):
        at = self.at
        return lax.rem(at.w + at.W // 2, at.W)

    def cross_copy(self):
        at = self.at
        return self.remote(
            self.own.at[at.slab(self.home(), at.a0, at.b0)],
            self.fin.at[at.c],
            self.fin_sem,
            (at.c,),
            {"wide": self.home(), "rep": at.group},
        )

    def over_copy(self):
        at = self.at
        return self.remote(
            self.own.at[at.slab(at.w, at.a0, at.b0)],
            self.fin.at[at.c],
            self.fin_sem,
            (at.c,),
            at.sibling(),
        )

    def turn(self, k):
        return lax.rem(self.at.w + 1 + k, self.at.W)

    def start(self):
        at = self.at
        self.own_copy().start()
        other = 1 - at.c
        hi, lo = at.n // 2, at.n % 2
        a1 = (1 - other) * hi + other * lo
        b1 = (1 - other) * lo + other * hi
        for a, b in ((1 - a1, 0), (1 - a1, 1), (a1, 1 - b1), (a1, b1)):

            def body(k, carry, a=a, b=b):
                w = self.turn(k)
                self.side_copy(w * at.N + a * (2 - other) + b * (1 + other)).start()
                return carry

            lax.fori_loop(0, at.W, body, 0)

    def total(self, slab):
        self.side_copy(slab).wait_recv()
        return self.own[slab].astype(F32) + self.side[slab].astype(F32)

    def wait_first(self, w, b):
        self.first_copy(w, b).wait_recv()
        return self.first[2 * w + b].astype(F32)

    def stage_first(self):
        at = self.at
        self.own_copy().wait()

        for b in (1 - at.b0, at.b0):

            def body(k, carry, b=b):
                w = self.turn(k)
                slab = at.slab(w, 1 - at.a0, b)
                self.own[slab] = self.total(slab).astype(BF)
                self.first_copy(w, b).start()
                return carry

            lax.fori_loop(0, at.W, body, 0)

    def stage_second(self):
        at = self.at

        def body(k, carry):
            w = self.turn(k)
            slab = at.slab(w, at.a0, 1 - at.b0)
            self.own[slab] = (self.total(slab) + self.wait_first(w, 1 - at.b0)).astype(BF)
            self.second_copy(w).start()
            return carry

        lax.fori_loop(0, at.W, body, 0)

    def column(self, w, levels):
        at = self.at
        value = self.total(at.slab(w, at.a0, at.b0)) + self.wait_first(w, at.b0)
        self.second_copy(w).wait_recv()
        value = value + self.second[w].astype(F32)
        for level in range(levels):
            start, _ = self.along_place(level)
            k = w // (2 << level)
            self.along_copy(level, k).wait_recv()
            value = value + self.along[start + k].astype(F32)
        return value

    def stage_along(self):
        at = self.at
        for level in range(self.levels):
            unit = 1 << level
            partner = at.w + unit * (1 - 2 * ((at.w // unit) % 2))

            def body(k, carry, level=level, unit=unit, partner=partner):
                w = k * 2 * unit + partner % (2 * unit)
                self.own[at.slab(w, at.a0, at.b0)] = self.column(w, level).astype(BF)
                self.along_copy(level, k).start()
                return carry

            lax.fori_loop(0, self.along_place(level)[1], body, 0)

    def stage_home(self):
        at = self.at
        away = at.slab(self.home(), at.a0, at.b0)
        self.own[away] = self.column(self.home(), self.levels).astype(BF)
        self.cross_copy().start()
        mine = at.slab(at.w, at.a0, at.b0)
        value = self.column(at.w, self.levels)
        self.own[mine] = value.astype(BF)

        @pl.when(at.c != at.group)
        def _():
            self.over_copy().start()

        self.put(at.c, value)

    def put(self, half, value):
        for h in range(2):

            @pl.when(half == h)
            def _(h=h):
                self.out[h][...] = value

    def finish(self):
        at = self.at

        @pl.when(at.c == at.group)
        def _():
            self.fin_wait(1 - at.c)
            self.put(1 - at.c, self.fin[1 - at.c].astype(F32))

        @pl.when(at.c != at.group)
        def _():
            for half in range(2):
                self.fin_wait(half)
                self.out[half][...] = self.fin[half].astype(F32)
            self.over_copy().wait_send()

        self.cross_copy().wait_send()

        def sides(slab, carry):
            self.side_copy(slab).wait_send()
            return carry

        lax.fori_loop(0, at.slabs, sides, 0)

        def firsts(k, carry):
            self.first_copy(k // 2, k % 2).wait_send()
            return carry

        lax.fori_loop(0, 2 * at.W, firsts, 0)

        def seconds(w, carry):
            self.second_copy(w).wait_send()
            return carry

        lax.fori_loop(0, at.W, seconds, 0)
        for level in range(self.levels):

            def alongs(k, carry, level=level):
                self.along_copy(level, k).wait_send()
                return carry

            lax.fori_loop(0, self.along_place(level)[1], alongs, 0)

    def fin_wait(self, half):
        self.remote(
            self.fin.at[half], self.fin.at[half], self.fin_sem, (half,), self.at.sibling()
        ).wait_recv()


def scatter_scratch(wide, narrow, form):
    slabs = wide * narrow
    sizes = (slabs, slabs, 2 * wide, wide, max(wide - 2, 1), 2)
    dma = pltpu.SemaphoreType.DMA
    return [pltpu.VMEM((size,) + form, BF) for size in sizes] + [dma] + [
        dma((2, size)) for size in sizes[1:]
    ]


def scatter_greetings(at):
    out = [
        at.chip(at.w, at.a0, 1 - at.b0),
        at.chip(at.w, 1 - at.a0, at.b0),
        at.sibling(),
    ]
    for level in range((at.W // 2).bit_length() - 1):
        unit = 1 << level
        out.append({"wide": at.w + unit * (1 - 2 * ((at.w // unit) % 2))})
    out.append({"wide": lax.rem(at.w + at.W // 2, at.W)})
    out.append({"wide": lax.rem(at.w + at.W // 2, at.W), "rep": 1 - at.c})
    return out


def halves_of(ref, layer, width, natural):
    if natural:
        return [ref.at[layer, :, h * width : (h + 1) * width] for h in range(2)]
    return [ref.at[layer, h] for h in range(2)]


def adam_update(weight, moment, square, gradient, decay, rate):
    moment = BETA_ONE * moment + (1.0 - BETA_ONE) * gradient
    square = BETA_TWO * square + (1.0 - BETA_TWO) * gradient * gradient
    fixed_moment = moment / (1.0 - BETA_ONE**STEP)
    fixed_square = square / (1.0 - BETA_TWO**STEP)
    delta = -rate * (fixed_moment / (jnp.sqrt(fixed_square) + ADAM_EPS) + decay * weight)
    return (moment, square, delta)


DECAYS = (DECAY, DECAY, DECAY, 0.0)
RATES = (RATE_TABLE, RATE, RATE, RATE_TABLE)
SUMMED = ((1, 1), (2, 1), (2, 0))


def sum_partners(at):
    out = []
    for axis, here, size in (("narrow", at.n, at.N), ("wide", at.w, at.W)):
        unit = 1
        while unit < size:
            out.append({axis: here + unit * (1 - 2 * ((here // unit) % 2))})
            unit *= 2
    return out


def reduce_kernel(wide, narrow, natural, *refs):
    at = Place(wide, narrow)
    take = iter(refs)

    def some(n):
        return [next(take) for _ in range(n)]

    parts, ready, bits = some(2), some(3), next(take)
    hbm_states = some(12)
    grads, deltas, scalars = some(4), some(4), next(take)
    states, state_sems = some(12), next(take)
    misc_sum, bits_in, bits_sem = some(3)
    sums, arrived, sum_sems = some(3)
    mine, other, delta_sems = some(4), some(4), next(take)
    partners = sum_partners(at)
    greet(scatter_greetings(at) + partners)

    tiny = pltpu.make_async_remote_copy(
        src_ref=bits,
        dst_ref=bits_in,
        send_sem=bits_sem.at[0],
        recv_sem=bits_sem.at[1],
        device_id=at.sibling(),
        device_id_type=MESH,
    )
    tiny.start()
    streams = []
    for i, out in enumerate((halves_out(misc_sum), halves_of(grads[1], 0, 2 * D, natural))):
        part = some(12)
        streams.append(ScatterStream(at, parts[i], out, *part[:6], part[6:]))
    for stream in streams:
        stream.start()
    loads = [
        pltpu.make_async_copy(src, dst, state_sems.at[i])
        for i, (src, dst) in enumerate(zip(hbm_states, states))
    ]
    for load in loads:
        load.start()
    views = list(streams[1].out)
    for (which, layer), source in zip(SUMMED, ready):
        targets = halves_of(grads[which], layer, 2 * D if which == 1 else FF, natural)
        views += targets
        for half in range(2):
            targets[half][...] = source[half]
    for stream in streams:
        stream.stage_first()
    for stream in streams:
        stream.stage_second()
    for stream in streams:
        stream.stage_along()
    for stream in streams:
        stream.stage_home()
    for stream in streams:
        stream.finish()
    tiny.wait()

    table_rows, columns = grads[0].shape[1], grads[3].shape[1]
    for layer in range(2):
        grads[0][layer] = misc_sum[layer, :table_rows, :D]
    grads[3][...] = misc_sum[0, :VEC, D : D + columns]
    squared = jnp.zeros((1, 1), F32)
    for ref in halves_out(misc_sum) + views:
        value = ref[...]
        value = jnp.sum(value * value, 0, keepdims=True)
        squared = squared + jnp.sum(value, 1, keepdims=True)
    row = lax.broadcasted_iota(jnp.int32, (8, 128), 0)
    lost = jnp.where(at.c == at.group, bits[...] + bits_in[...], 0.0)
    total = jnp.where(row == 0, squared, jnp.where(row == 1, lost, 0.0))
    for k, partner in enumerate(partners):
        sums[k] = total
        copy = pltpu.make_async_remote_copy(
            src_ref=sums.at[k],
            dst_ref=arrived.at[k],
            send_sem=sum_sems.at[0, k],
            recv_sem=sum_sems.at[1, k],
            device_id=partner,
            device_id_type=MESH,
        )
        copy.start()
        copy.wait()
        total = total + arrived[k]
    norm = jnp.sqrt(total[0:1, 0:1])
    factor = jnp.minimum(1.0, CLIP_AT / (norm + 1e-06))
    scalars[...] = jnp.where(row == 0, norm, jnp.where(row == 2, factor, total))
    for load in loads:
        load.wait()

    copies = [
        pltpu.make_async_remote_copy(
            src_ref=mine[which],
            dst_ref=other[which],
            send_sem=delta_sems.at[0, which],
            recv_sem=delta_sems.at[1, which],
            device_id=at.sibling(),
            device_id_type=MESH,
        )
        for which in range(4)
    ]
    order = (2, 1, 0, 3)
    for which in order:
        refs_of = [states[which], states[4 + which], states[8 + which], grads[which], mine[which]]
        if which in (1, 2):
            width = 2 * D if which == 1 else FF
            views = [[ref.at[l] for ref in refs_of] for l in range(2)]
            if natural:
                views = [
                    [ref.at[l, :, h * width : (h + 1) * width] for ref in refs_of]
                    for l in range(2)
                    for h in range(2)
                ]
        else:
            views = [refs_of]
        for weight, moment, square, gradient, target in views:
            _, _, delta = adam_update(
                weight[...],
                moment[...],
                square[...],
                gradient[...] * factor,
                DECAYS[which],
                RATES[which],
            )
            target[...] = delta.astype(target.dtype)
        copies[which].start()
    for which in order:
        copies[which].wait()
        deltas[which][...] = (mine[which][...].astype(F32) + other[which][...].astype(F32)) * 0.5


def reduce_all(parts, ready, bits, states, wide, narrow, natural, collective_id):
    vm = pl.BlockSpec(memory_space=pltpu.VMEM)
    anywhere = pl.BlockSpec(memory_space=pl.ANY)
    like = [jax.ShapeDtypeStruct(x.shape, F32) for x in states[:4]]
    kinds = [BF if x.shape[-2] % 16 == 0 else F32 for x in states[:4]]
    exchanged = [pltpu.VMEM(x.shape, kind) for x, kind in zip(states[:4], kinds)]
    dma = pltpu.SemaphoreType.DMA
    stages = (wide * narrow).bit_length() - 1
    scratch = [pltpu.VMEM(x.shape, F32) for x in states] + [dma((12,))]
    scratch += [pltpu.VMEM((2,) + parts[0].shape[2:], F32), pltpu.VMEM(bits.shape, F32), dma((2,))]
    scratch += [pltpu.VMEM((stages, 8, 128), F32)] * 2 + [dma((2, stages))]
    scratch += exchanged + exchanged + [dma((2, 4))]
    for x in parts:
        scratch += scatter_scratch(wide, narrow, x.shape[2:])
    return pl.pallas_call(
        functools.partial(reduce_kernel, wide, narrow, natural),
        in_specs=[anywhere] * 2 + [vm] * 4 + [anywhere] * 12,
        out_specs=[vm] * 9,
        out_shape=like + like + [jax.ShapeDtypeStruct((8, 128), F32)],
        scratch_shapes=scratch,
        compiler_params=params(VMEM_MIB, collective_id=collective_id, has_side_effects=True),
        name="reduce_all",
    )(*parts, *ready, bits, *states)


def update_kernel(scalars, *refs):
    grads, deltas, weights, moments, squares, outers, averages = (
        refs[4 * k : 4 * k + 4] for k in range(7)
    )
    new_m, new_s, new_w, new_o, new_a = (refs[28 + 4 * k : 32 + 4 * k] for k in range(5))
    factor = scalars[2:3, 0:1]
    for which in range(4):
        moment, square, _ = adam_update(
            weights[which][...],
            moments[which][...],
            squares[which][...],
            grads[which][...] * factor,
            DECAYS[which],
            RATES[which],
        )
        new_m[which][...] = moment
        new_s[which][...] = square
        delta = deltas[which][...]
        outer = OUTER_MOM * outers[which][...] + delta
        weight = weights[which][...] + OUTER_RATE * (delta + OUTER_MOM * outer)
        new_o[which][...] = outer
        new_w[which][...] = weight
        new_a[which][...] = EVAL_KEEP * averages[which][...] + (1.0 - EVAL_KEEP) * weight


def update(scalars, grads, deltas, arrays):
    weights = arrays[:4]
    rows = weights[1].shape[1]

    def quarter(width):
        return pl.BlockSpec((1, rows, width // 4), lambda i: (i // 4, 0, i % 4))

    specs = [
        pl.BlockSpec((1,) + weights[0].shape[1:], lambda i: (i // 4, 0, 0)),
        quarter(4 * D),
        quarter(2 * FF),
        pl.BlockSpec(weights[3].shape, lambda i: (0, 0)),
    ]
    like = [jax.ShapeDtypeStruct(x.shape, F32) for x in weights]
    return pl.pallas_call(
        update_kernel,
        grid=(8,),
        in_specs=[pl.BlockSpec((8, 128), lambda i: (0, 0))] + specs * 7,
        out_specs=specs * 5,
        out_shape=like * 5,
        compiler_params=params(VMEM_MIB),
        name="update",
    )(scalars, *grads, *deltas, *arrays)


def local_gradients(byte_ids, live_mask, tables, attn, own_feed, own_short, vec, count, wide, narrow):
    seq = byte_ids.shape[1]
    long_blocks = seq // BLK
    weight = jnp.concatenate([live_mask[:, 1:], jnp.zeros_like(live_mask[:, :1])], 1)
    info = jnp.stack([byte_ids, jnp.roll(byte_ids, -1, 1), weight, weight], -1)
    aux = jnp.concatenate([info[0], info[1, :BLK]], 0)
    scale = (1.0 / (count * LOG_TWO)).reshape(1, 1)
    rows = [
        jnp.concatenate([vec[2 + 5 * l : 7 + 5 * l], jnp.zeros((3, D), F32)], 0) for l in range(2)
    ]
    bias_rows = 2 * FF // D
    beta = vec[12 : 12 + bias_rows].reshape(2, 1, FF)
    rel = vec[12 + bias_rows :].reshape(2, HEADS, NB)
    x1, middle, q, k, v, ot, lse, act, slope, feed, short = full_forward(
        aux, tables[0], attn, own_feed, own_short, rows[0], beta[0], rel[0], long_blocks, wide, narrow
    )
    feed = feed.reshape(2, D, FF)
    short = short.reshape(2, D, 2 * D + FF)
    d_x1, d_short_attn, d_short_feed, d_head, short_rows, d_beta_1, bits, sums_1 = middle_stage(
        x1, aux, tables[1], short, rows[1], beta[1], rel[1], scale, vec[0:2], seq
    )

    def slabs_of(d):
        return d.reshape((2, wide * narrow) + slab_form(D // (wide * narrow), d.shape[-1]))

    d_middle, d_feed, feed_rows, d_beta_0, sum_short_attn = feed_back(
        d_x1, act, slope, middle, feed, rows[0], slabs_of(d_short_attn), wide, narrow
    )
    d_attn, d_embed, attn_rows, sums_0, sum_short_feed, sum_feed = attention_back(
        d_middle,
        aux,
        ot,
        lse,
        q,
        k,
        v,
        tables[0],
        attn,
        rows[0],
        rel[0],
        slabs_of(d_short_feed),
        slabs_of(d_feed),
        long_blocks,
        wide,
        narrow,
    )

    def d_rel(sums, far):
        fold = fold_matrix(far)
        return jnp.dot(jnp.sum(sums, -1), fold, precision=lax.Precision.HIGHEST).reshape(1, -1)

    d_vec = jnp.concatenate(
        [
            short_rows[0:2],
            attn_rows[0:2],
            feed_rows[0:3],
            short_rows[2:7],
            d_beta_0.reshape(-1, D),
            d_beta_1.reshape(-1, D),
            jnp.concatenate([d_rel(sums_0, long_blocks * SUB), d_rel(sums_1, seq // 3 // TILE)], 1),
        ],
        0,
    )
    ready = (sum_short_attn, sum_short_feed, sum_feed)
    return bits, (d_embed, d_head), ready, slabs_of(d_attn), d_vec


def pad_to(x, rows, cols):
    return jnp.pad(x, [(0, 0)] * (x.ndim - 2) + [(0, rows - x.shape[-2]), (0, cols - x.shape[-1])])


def per_device(wide, narrow, byte_ids, live_mask, *arrays):
    tables, attention, feed_forward, vectors = arrays[:4]
    slabs = wide * narrow
    core = lax.axis_index("rep")
    group = lax.axis_index("wide") // (wide // 2)
    rows = attention.shape[1]

    axes = ("rep", "wide", "narrow")
    moves = []
    for r in range(2):
        for w in range(wide):
            for n in range(narrow):
                to = (w % 2, r * (wide // 2) + w // 2, n)
                moves.append(((r * wide + w) * narrow + n, (to[0] * wide + to[1]) * narrow + to[2]))
    moved = lax.ppermute(byte_ids + V * live_mask, axes, moves)
    ids, lives = moved % V, moved // V

    def half_of(x, width):
        return lax.dynamic_slice_in_dim(x, core * width, width, 1)

    def packed(x):
        return x.astype(BF).reshape(slab_form(rows, x.shape[-1]))

    own_attn = packed(half_of(attention[0], 2 * D))
    own_feed = packed(half_of(feed_forward[0], FF))
    own_short = packed(
        jnp.concatenate([half_of(attention[1], 2 * D), half_of(feed_forward[1], FF)], 1)
    )
    own_count = jnp.sum(live_mask[:, 1:])
    digits = jnp.stack([own_count // 64, own_count % 64]).astype(F32).reshape(1, 2)
    side = jnp.concatenate(
        [pad_to(vectors, 24, 128), pad_to(digits, MISC_ROWS - 24, 128)], 0
    )
    misc = jnp.concatenate([pad_to(tables[core], MISC_ROWS, D), side], 1).astype(BF)
    misc_all, attn = gather_all([misc, own_attn], wide, narrow, 1)
    attn = attn.reshape(2, D, 2 * D)
    table_rows = tables.shape[1]
    full_tables = misc_all[:, :, :table_rows, :D].reshape(2, V, D)
    cols = vectors.shape[1]
    vec = misc_all[0, :, :VEC, D : D + cols].astype(F32).transpose(1, 0, 2).reshape(VEC, D)
    tally = misc_all[:, :, 24, D : D + 2].astype(F32)
    counts = jnp.sum(tally[:, :, 0] * 64.0 + tally[:, :, 1], 1)

    bits, d_tables, ready, d_attn, d_vec = local_gradients(
        ids, lives, full_tables, attn, own_feed, own_short, vec, counts[group], wide, narrow
    )

    d_vec = pad_to(d_vec.reshape(VEC, slabs, cols).transpose(1, 0, 2), MISC_ROWS, 128)
    d_misc = jnp.stack(
        [
            jnp.concatenate([pad_to(d.reshape(slabs, table_rows, D), MISC_ROWS, D), extra], -1)
            for d, extra in zip(d_tables, (d_vec, jnp.zeros_like(d_vec)))
        ]
    ).astype(BF)
    arrays = [x[0] if 4 <= k < 12 else x for k, x in enumerate(arrays)]
    natural = rows % 16 == 0

    def formed(k, x):
        if natural or k % 4 not in (1, 2):
            return x
        half = x.shape[-1] // 2
        return x.reshape(2, rows, 2, half).swapaxes(1, 2).reshape((2, 2) + slab_form(rows, half))

    def unformed(k, x):
        if natural or k % 4 not in (1, 2):
            return x
        return x.reshape(2, 2, rows, -1).swapaxes(1, 2).reshape(arrays[k].shape)

    states = [formed(k, x) for k, x in enumerate(arrays[:12])]
    *sums, scalars = reduce_all(
        (d_misc, d_attn),
        ready,
        jnp.broadcast_to(bits, (8, 128)),
        states,
        wide,
        narrow,
        natural,
        2,
    )
    grads = [unformed(k, x) for k, x in enumerate(sums[:4])]
    deltas = [unformed(k, x) for k, x in enumerate(sums[4:])]
    new = update(scalars, grads, deltas, arrays)
    new = [x[None] if k < 8 else x for k, x in enumerate(new)]
    return (scalars[1, :1], counts[core].reshape(1), scalars[0, :1], *new)


def solution(mesh):
    rows = P(("rep", "wide", "narrow"), None)
    split = (
        P(None, ("wide", "narrow"), None),
        P(None, ("wide", "narrow"), None),
        P(None, ("wide", "narrow"), None),
        P(None, ("wide", "narrow")),
    )
    own = tuple(P("rep", *spec) for spec in split)
    return jax.shard_map(
        functools.partial(per_device, mesh.shape["wide"], mesh.shape["narrow"]),
        mesh=mesh,
        in_specs=(rows, rows) + split + own + own + split + split,
        out_specs=(P("rep"),) * 3 + own + own + split * 3,
        check_vma=False,
    )
```

```python
import functools
import math

import jax
import jax.numpy as jnp
import numpy as np
from jax import lax
from jax.experimental import pallas as pl
from jax.experimental.pallas import tpu as pltpu
from jax.sharding import PartitionSpec as P

D = 512
HEADS = 8
HD = 64
FF = 2048
V = 256
NB = 32
STEP = 10
VEC = 21
EDGES = (1, 2, 3, 4, 5, 6, 7, 8, 10, 12, 14, 16, 20, 24, 28, 32, 40, 48, 64, 80, 96, 128, 160, 192)
EDGES = EDGES + (256, 320, 384, 512, 640, 768, 1024)
NEG = -1000000000.0
EPS = 1e-05
LOG_TWO = math.log(2.0)
RATE = 0.01
RATE_TABLE = 0.2
BETA_ONE = 0.9
BETA_TWO = 0.95
ADAM_EPS = 1e-08
DECAY = 0.1
CLIP_AT = 0.02
OUTER_RATE = 0.7
OUTER_MOM = 0.9
EVAL_KEEP = 0.9

TILE = 128
BETA_ROW = 12
REL_ROW = 12 + 2 * FF // D
CHUNKS = FF // D
PARTS = 1
WIDTH = FF // PARTS
VMEM_MIB = 63
BLK = 384
SUB = BLK // TILE
PAIRS = HEADS // 2
PW = 2 * HD
GELU_C = math.sqrt(2.0 / math.pi)
GELU_A = 0.044715

BF = jnp.bfloat16
F32 = jnp.float32
NN = (((1,), (0,)), ((), ()))
NT = (((1,), (1,)), ((), ()))
TN = (((0,), (0,)), ((), ()))


def mm(left, right, dims=NN):
    return lax.dot_general(left, right, dims, preferred_element_type=F32)


def spans(count):
    out = []
    for d in range(count):
        lo, hi = max(TILE * d - (TILE - 1), 0), TILE * d + TILE - 1
        base = sum(e <= lo for e in EDGES)
        out.append((base, [(e, k + 1) for k, e in enumerate(EDGES) if lo < e <= hi]))
    return out


def fold_matrix(count):
    rows = []
    for base, edges in spans(count):
        row = np.zeros(NB, np.float32)
        row[base] += 1
        rows.append(row)
        for _, bucket in edges:
            row = np.zeros(NB, np.float32)
            row[bucket] += 1
            row[bucket - 1] -= 1
            rows.append(row)
    out = np.zeros((HEADS, fold_rows(count), HEADS * NB), jnp.bfloat16)
    for h in range(HEADS):
        out[h, : len(rows), h * NB : (h + 1) * NB] = np.stack(rows)
    return out


def tile_distance(d):
    keys = lax.broadcasted_iota(jnp.int32, (TILE, TILE), 0)
    queries = lax.broadcasted_iota(jnp.int32, (TILE, TILE), 1)
    return TILE * d + queries - keys


def build_bias(rel, level, bias, count):
    for d, (base, edges) in enumerate(spans(count)):
        distance = tile_distance(d)

        def one_head(h, carry, d=d, base=base, edges=edges, distance=distance):
            first = level * HEADS * NB + h * NB
            tile = jnp.full((TILE, TILE), rel[REL_ROW, first + base], F32)
            for edge, bucket in edges:
                tile = jnp.where(distance >= edge, rel[REL_ROW, first + bucket], tile)
            if d == 0:
                tile = jnp.where(distance < 0, NEG, tile)
            bias[h, d] = tile
            return carry

        lax.fori_loop(0, HEADS, one_head, 0)


def fold_bias(tiles, sums, count):
    at = 0
    for d, (_, edges) in enumerate(spans(count)):
        distance = tile_distance(d)

        def one_head(h, carry, d=d, edges=edges, distance=distance, at=at):
            tile = tiles[h, d]
            sums[h, at : at + 1] = jnp.sum(tile, 0, keepdims=True)
            for n, (edge, _) in enumerate(edges):
                sums[h, at + 1 + n : at + 2 + n] = jnp.sum(
                    jnp.where(distance >= edge, tile, 0.0), 0, keepdims=True
                )
            return carry

        lax.fori_loop(0, HEADS, one_head, 0)
        at += 1 + len(edges)


def fold_rows(count):
    return -(-sum(1 + len(edges) for _, edges in spans(count)) // 8) * 8


def rel_row(tiles, sums, fold, count):
    sums[...] = jnp.zeros_like(sums)
    fold_bias(tiles, sums, count)
    whole = sums[...].reshape(-1, TILE)
    high = whole.astype(BF)
    low = (whole - high.astype(F32)).astype(BF)
    matrix = fold[...].reshape(-1, HEADS * NB)
    total = mm(high, matrix, TN) + mm(low, matrix, TN)
    return jnp.sum(total, 0, keepdims=True)


def norm_stats(x):
    centered = x - jnp.mean(x, -1, keepdims=True)
    rstd = lax.rsqrt(jnp.mean(centered * centered, -1, keepdims=True) + EPS)
    return centered * rstd, rstd


def norm_back(dy, xhat, rstd, gain):
    t = dy * gain
    dx = rstd * (
        t - jnp.mean(t, -1, keepdims=True) - xhat * jnp.mean(t * xhat, -1, keepdims=True)
    )
    return dx, jnp.sum(dy * xhat, 0, keepdims=True), jnp.sum(dy, 0, keepdims=True)


def gelu_pair(u):
    square = u * u
    tanh = jnp.tanh(GELU_C * u * (1.0 + GELU_A * square))
    half = 0.5 * (1.0 + tanh)
    slope = half + 0.5 * u * (1.0 - tanh * tanh) * (GELU_C + 3.0 * GELU_C * GELU_A * square)
    return u * half, slope


def split_heads(pair):
    lane = lax.broadcasted_iota(jnp.int32, pair.shape, 1)
    zero = jnp.zeros_like(pair)
    return jnp.concatenate(
        [jnp.where(lane < HD, pair, zero), jnp.where(lane >= HD, pair, zero)], 0
    )


def cell(block, kb, e, qa, nq):
    return block[kb * TILE : (kb + 1) * TILE, (e * nq + qa) * TILE : (e * nq + qa + 1) * TILE]


def softmax_step(keys, values_t, queries, bias, pair, far, diag, nq, nk, state):
    top, total, acc = state
    raw = mm(keys, queries, NT)
    scores = {}
    for e in range(2):
        for qa in range(nq):
            for kb in range(nk):
                if diag and kb > qa:
                    continue
                scores[kb, e, qa] = cell(raw, kb, e, qa, nq) + bias[2 * pair + e, far + qa - kb]
    highest = []
    for e in range(2):
        for qa in range(nq):
            column = [scores[kb, e, qa] for kb in range(nk) if (kb, e, qa) in scores]
            highest.append(jnp.max(functools.reduce(jnp.maximum, column), 0, keepdims=True))
    old_top = top[...]
    new_top = jnp.maximum(old_top, jnp.concatenate(highest, 1))
    alpha = jnp.exp(old_top - new_top)
    sums = []
    columns = []
    for e in range(2):
        for qa in range(nq):
            at = (e * nq + qa) * TILE
            ceiling = new_top[:, at : at + TILE]
            parts, adds = [], None
            for kb in range(nk):
                if (kb, e, qa) not in scores:
                    parts.append(jnp.zeros((TILE, TILE), BF))
                    continue
                p = jnp.exp(scores[kb, e, qa] - ceiling)
                adds = p if adds is None else adds + p
                parts.append(p.astype(BF))
            sums.append(jnp.sum(adds, 0, keepdims=True))
            columns.append(jnp.concatenate(parts, 0))
    top[...] = new_top
    total[...] = alpha * total[...] + jnp.concatenate(sums, 1)
    acc[...] = alpha * acc[...] + mm(values_t, jnp.concatenate(columns, 1))


def softmax_start(state):
    top, total, acc = state
    top[...] = jnp.full(top.shape, NEG, F32)
    total[...] = jnp.zeros(total.shape, F32)
    acc[...] = jnp.zeros(acc.shape, F32)


def softmax_end(state, n):
    top, total, acc = state
    scaled = acc[...] / total[...]
    out = jnp.concatenate([scaled[:HD, :n], scaled[HD:, n:]], 0).astype(BF)
    return out, top[...] + jnp.log(total[...])


def score_back(keys, values, queries, grads, logsum, inner, bias, pair, far, diag, nq, nk, tiles):
    raw = mm(keys, queries, NT)
    d_p = mm(values, grads, NT)
    probs, scores = {}, {}
    for e in range(2):
        for diff in range(-(nk - 1), nq):
            total = None
            if diag and diff < 0:
                continue
            for kb in range(nk):
                qa = kb + diff
                if qa < 0 or qa >= nq:
                    continue
                at = (e * nq + qa) * TILE
                p = jnp.exp(
                    cell(raw, kb, e, qa, nq)
                    + bias[2 * pair + e, far + diff]
                    - logsum[:, at : at + TILE]
                )
                ds = p * (cell(d_p, kb, e, qa, nq) - inner[:, at : at + TILE])
                total = ds if total is None else total + ds
                probs[kb, e, qa] = p.astype(BF)
                scores[kb, e, qa] = ds.astype(BF)
            tiles[2 * pair + e, far + diff] += total

    def whole(parts):
        empty = jnp.zeros((TILE, TILE), BF)
        return jnp.concatenate(
            [
                jnp.concatenate([parts.get((kb, e, qa), empty) for kb in range(nk)], 0)
                for e in range(2)
                for qa in range(nq)
            ],
            1,
        )

    return whole(probs), whole(scores)


def beta_of(vec, level, part):
    row = BETA_ROW + level * CHUNKS + part * WIDTH // D
    return jnp.concatenate([vec[r : r + 1] for r in range(row, row + WIDTH // D)], 1)


def put_beta(rows, start, part, value, add):
    for k in range(WIDTH // D):
        row = start + part * WIDTH // D + k
        piece = value[:, k * D : (k + 1) * D]
        rows[row : row + 1] = rows[row : row + 1] + piece if add else piece


def one_hot(column):
    return column == lax.broadcasted_iota(jnp.int32, (column.shape[0], V), 1)


def full_forward_kernel(
    long_blocks,
    wide,
    narrow,
    natural,
    aux,
    embed,
    wts,
    attn_low,
    feed_low,
    vec,
    rel,
    x1_out,
    middle_out,
    q_out,
    k_out,
    v_out,
    ot_out,
    lse_out,
    act_out,
    slope_out,
    feed_out,
    short_attn_out,
    short_feed_out,
    bias,
    k_all,
    vt_all,
    middles,
    feed,
    feed_sem,
    *more,
):
    step = pl.program_id(0)
    blocks = pl.num_programs(0) // 2
    state, sems = more[:3], more[3:]
    at = Place(wide, narrow)
    sources, targets = [], []
    for low, layer, width, out, count in (
        (feed_low, 0, FF, feed_out, 2),
        (attn_low, 1, 2 * D, short_attn_out, 1),
        (feed_low, 1, FF, short_feed_out, 2),
    ):
        sources += column_parts(view_half(low, layer, at.c, width, natural), count)
        targets += column_parts(out, count)
    feed_a, feed_b, short_attn, short_a, short_b = (
        GatherStream(at, source, out, *sems[GATHER_SEMS * k : GATHER_SEMS * (k + 1)])
        for k, (source, out) in enumerate(zip(sources, targets))
    )
    load = pltpu.make_async_copy(feed_out, feed, feed_sem)

    def when_at(n, *bodies):
        @pl.when(step == n)
        def _():
            for body in bodies:
                body()

    def hop(stream, d):
        return lambda: stream.depth(d)

    events = {
        (0, 3): (hop(feed_a, 1), short_attn.start),
        (1, 0): (hop(feed_a, 2), hop(feed_b, 1)),
        (1, 3): (hop(feed_b, 2), short_a.start),
        (2, 0): (hop(feed_a, 3), hop(short_attn, 1)),
        (2, 1): (hop(feed_b, 3), short_b.start),
        (2, 2): (hop(short_attn, 2), hop(short_a, 1)),
        (3, 0): (hop(short_attn, 3), hop(short_b, 1)),
        (3, 3): (hop(short_a, 2),),
    }

    @pl.when(step == 0)
    def _():
        greet(gather_greetings(at))
        feed_a.start()
        feed_b.start()
        build_bias(rel, 0, bias, bias.shape[1])

    @pl.when(step < blocks)
    def _():
        hot = one_hot(aux[:, 0:1]).astype(BF)
        x = mm(hot, embed[0])
        xhat, _ = norm_stats(x)
        normed = (xhat * vec[2:3] + vec[3:4]).astype(BF)
        queries = (mm(normed, wts[0, :, :D]) * HD**-0.5).astype(BF)
        keys = mm(normed, wts[0, :, D : 2 * D]).astype(BF)
        values = mm(normed, wts[1, :, :D]).astype(BF)
        for pair in range(PAIRS):
            cols = slice(pair * PW, (pair + 1) * PW)
            q_out[0, pair] = queries[:, cols]
            k_out[0, pair] = keys[:, cols]
            v_out[0, pair] = values[:, cols]
            k_all[step, pair] = keys[:, cols]
            vt_all[step, pair] = values[:, cols].T
        middles[step] = x


    @pl.when(step < blocks)
    def _():
        first = jnp.where(step >= long_blocks, long_blocks, 0)

        def one_pair(pair, carry):
            both = split_heads(q_out[0, pair])
            softmax_start(state)

            def earlier(j, inner):
                far = SUB * (step - j)
                softmax_step(
                    k_all[j, pair], vt_all[j, pair], both, bias, pair, far, False, SUB, SUB, state
                )
                return inner

            lax.fori_loop(first, step, earlier, 0)
            softmax_step(
                k_all[step, pair], vt_all[step, pair], both, bias, pair, 0, True, SUB, SUB, state
            )
            ot_out[0, pair], lse_out[0, pair] = softmax_end(state, BLK)
            run_events(events, step, pair)
            return carry

        lax.fori_loop(0, PAIRS, one_pair, 0)
        attended = ot_out[0].reshape(D, BLK).T
        middles[step] = middles[step] + mm(attended, wts[1, :, D : 2 * D])

    @pl.when(step == blocks - 1)
    def _():
        feed_a.finish()
        feed_b.finish()
        load.start()
        load.wait()

    @pl.when(step >= blocks)
    def _():
        block = jnp.maximum(step - blocks, 0)
        middle = middles[block]
        middle_out[...] = middle
        xhat, _ = norm_stats(middle)
        second = (xhat * vec[4:5] + vec[5:6]).astype(BF)
        total = middle + vec[6:7]
        up, down = feed_half(feed, 0), feed_half(feed, 1)
        for c in range(PARTS):
            cols = slice(c * WIDTH, (c + 1) * WIDTH)
            active, slope = gelu_pair(mm(second, up[:, cols]) + beta_of(vec, 0, c))
            active = active.astype(BF)
            act_out[:, cols] = active
            slope_out[:, cols] = slope.astype(BF)
            total = total + mm(active, down[:, cols], NT)
        x1_out[...] = total

    when_at(blocks, hop(short_b, 2), hop(short_a, 3))
    when_at(blocks + 1, hop(short_b, 3))

    @pl.when(step == 2 * blocks - 1)
    def _():
        for stream in (short_attn, short_a, short_b):
            stream.finish()


def run_events(events, step, pair):
    for (s, p), bodies in events.items():

        @pl.when((step == s) & (pair == p))
        def _(bodies=bodies):
            for body in bodies:
                body()


def feed_half(feed, half):
    value = feed[half]
    return value.reshape(D, FF)


def whole_spec(shape):
    return pl.BlockSpec(shape, lambda i: (0,) * len(shape), pipeline_mode=pl.Buffered(1))


def params(mib, **more):
    return pltpu.CompilerParams(vmem_limit_bytes=mib * 2**20, **more)


def state_scratch(n):
    return [pltpu.VMEM((1, 2 * n), F32), pltpu.VMEM((1, 2 * n), F32), pltpu.VMEM((PW, 2 * n), F32)]


def full_forward(aux, tables, wts, attn_low, feed_low, vec, long_blocks, wide, narrow, natural):
    tokens = aux.shape[0]
    blocks = tokens // BLK
    far = SUB * long_blocks
    form = feed_low.shape[1:] if natural else feed_low.shape[2:]
    form = (form[0], FF) if natural else form
    half = (form[0], form[1] * 2 * D // FF)

    def early(i):
        return jnp.minimum(i, blocks - 1)

    def late(i):
        return jnp.maximum(i - blocks, 0)

    def heads(n, width):
        return (
            jax.ShapeDtypeStruct((blocks, PAIRS, n, width), BF),
            pl.BlockSpec((1, PAIRS, n, width), lambda i: (early(i), 0, 0, 0)),
        )

    def flat(width, kind):
        return (
            jax.ShapeDtypeStruct((tokens, width), kind),
            pl.BlockSpec((BLK, width), lambda i: (late(i), 0)),
        )

    anywhere = pl.BlockSpec(memory_space=pl.ANY)
    outs = [flat(D, F32), flat(D, F32)] + [heads(BLK, PW)] * 3 + [heads(PW, BLK)]
    outs.append(
        (
            jax.ShapeDtypeStruct((blocks, PAIRS, 1, 2 * BLK), F32),
            pl.BlockSpec((1, PAIRS, 1, 2 * BLK), lambda i: (early(i), 0, 0, 0)),
        )
    )
    outs += [flat(FF, BF)] * 2
    outs += [
        (jax.ShapeDtypeStruct((2, wide, narrow) + each, BF), anywhere) for each in (form, half, form)
    ]
    return pl.pallas_call(
        functools.partial(full_forward_kernel, long_blocks, wide, narrow, natural),
        grid=(2 * blocks,),
        in_specs=[
            pl.BlockSpec((BLK, aux.shape[1]), lambda i: (early(i), 0)),
            whole_spec((1, V, D)),
            whole_spec(wts.shape),
            anywhere,
            anywhere,
            whole_spec(vec.shape),
            pl.BlockSpec(memory_space=pltpu.SMEM),
        ],
        out_specs=[spec for _, spec in outs],
        out_shape=[shape for shape, _ in outs],
        scratch_shapes=[
            pltpu.VMEM((HEADS, far, TILE, TILE), F32),
            pltpu.VMEM((blocks, PAIRS, BLK, PW), BF),
            pltpu.VMEM((blocks, PAIRS, PW, BLK), BF),
            pltpu.VMEM((blocks, BLK, D), F32),
            pltpu.VMEM((2, wide, narrow) + form, BF),
            pltpu.SemaphoreType.DMA,
        ]
        + state_scratch(BLK)
        + gather_sems(wide, narrow) * 5,
        compiler_params=params(VMEM_MIB, collective_id=4, has_side_effects=True),
        name="full_forward",
    )(aux, tables, wts, attn_low, feed_low, vec, vec)


PAD = 8


def middle_kernel(
    seq,
    x1,
    aux,
    head,
    attn,
    feed,
    vec,
    rel,
    scalars,
    fold,
    dx_out,
    d_attn,
    d_feed,
    d_head,
    row_grads,
    bits_out,
    sums,
    xp,
    pooled,
    mixed,
    ot,
    lse,
    active_s,
    slope_s,
    middle_s,
    bias,
    tiles,
    d_mixed,
    *state,
):
    n_long = seq // 3
    spots = ((PAD, 0, n_long), (2 * PAD + seq, n_long, TILE))
    build_bias(rel, 1, bias, bias.shape[1])
    tiles[...] = jnp.zeros_like(tiles)
    lanes = D // TILE
    for c in range(lanes):
        xp[c, 0:PAD] = jnp.zeros((PAD, TILE), F32)
        xp[c, PAD + seq : 2 * PAD + seq] = jnp.zeros((PAD, TILE), F32)
        xp[c, PAD : PAD + seq] = x1[0:seq, c * TILE : (c + 1) * TILE]
        xp[c, 2 * PAD + seq :] = x1[seq:, c * TILE : (c + 1) * TILE]
    for start, at, n in spots:
        for c in range(lanes):
            pooled[at : at + n, c * TILE : (c + 1) * TILE] = (
                xp[c, pl.ds(start - 2, n, stride=3)]
                + xp[c, pl.ds(start - 1, n, stride=3)]
                + xp[c, pl.ds(start, n, stride=3)]
            ) / 3.0

    xhat, _ = norm_stats(pooled[...])
    normed = (xhat * vec[7:8] + vec[8:9]).astype(BF)
    for part in range(3):
        half, at = part // 2, part % 2 * D
        value = mm(normed, attn[half, :, at : at + D])
        value = (value * HD**-0.5 if part == 0 else value).astype(BF)
        for pair in range(PAIRS):
            mixed[part, pair] = value[:, pair * PW : (pair + 1) * PW]

    def forward_pair(pair, carry):
        for at, n, offset in ((0, n_long, 0), (n_long, TILE, 2 * n_long)):
            top, total, acc = state
            wide = pl.ds(0, 2 * n)
            part = (top.at[:, wide], total.at[:, wide], acc.at[:, wide])
            softmax_start(part)
            values_t = mixed[2, pair, at : at + n].T
            both = split_heads(mixed[0, pair, at : at + n])
            count = n // TILE
            softmax_step(
                mixed[1, pair, at : at + n], values_t, both, bias, pair, 0, True, count, count, part
            )
            ot[pair, :, at : at + n], lse[pair, :, offset : offset + 2 * n] = softmax_end(part, n)
        return carry

    lax.fori_loop(0, PAIRS, forward_pair, 0)
    middle = pooled[...] + mm(ot[...].reshape(D, ot.shape[2]).T, attn[1, :, D:])
    middle_s[...] = middle
    xhat, _ = norm_stats(middle)
    second = (xhat * vec[9:10] + vec[10:11]).astype(BF)
    short = middle + vec[11:12]
    for c in range(PARTS):
        cols = slice(c * WIDTH, (c + 1) * WIDTH)
        active, slope = gelu_pair(mm(second, feed[0, :, cols]) + beta_of(vec, 1, c))
        active_s[:, cols] = active.astype(BF)
        slope_s[:, cols] = slope.astype(BF)
        short = short + mm(active_s[:, cols], feed[1, :, cols], NT)
    for start, at, n in spots:
        for c in range(lanes):
            part = short[at : at + n, c * TILE : (c + 1) * TILE]
            for k in range(3):
                where = pl.ds(start + k, n, stride=3)
                xp[c, where] = xp[c, where] + part

    d_head[...] = jnp.zeros_like(d_head)
    row_grads[...] = jnp.zeros_like(row_grads)

    def loss_block(b, bits):
        start = pl.multiple_of(b * BLK + jnp.where(b * BLK >= seq, 2 * PAD, PAD), PAD)
        joined = jnp.concatenate([xp[c, pl.ds(start, BLK)] for c in range(lanes)], 1)
        xhat, rstd = norm_stats(joined)
        last = (xhat * vec[0:1] + vec[1:2]).astype(BF)
        logits = mm(last, head[1], NT) * D**-0.5
        info = aux[pl.ds(pl.multiple_of(b * BLK, BLK), BLK), :]
        weight = info[:, 2:3]
        hot = one_hot(info[:, 1:2])
        highest = jnp.max(logits, -1, keepdims=True)
        powers = jnp.exp(logits - highest)
        total = jnp.sum(powers, -1, keepdims=True)
        picked = jnp.sum(jnp.where(hot, logits, 0.0), -1, keepdims=True)
        lost = weight * (highest + jnp.log(total) - picked)
        d_logits = ((powers / total - hot.astype(F32)) * (weight * scalars[1:2, 0:1])).astype(BF)
        d_head[...] += mm(d_logits, last, TN) * D**-0.5
        d_last = mm(d_logits, head[1]) * D**-0.5
        dx, d_gain, d_shift = norm_back(d_last, xhat, rstd, vec[0:1])
        row_grads[0:1] += d_gain
        row_grads[1:2] += d_shift
        for c in range(lanes):
            xp[c, pl.ds(start, BLK)] = dx[:, c * TILE : (c + 1) * TILE]
        return bits + lost

    bits = lax.fori_loop(0, x1.shape[0] // BLK, loss_block, jnp.zeros((BLK, 1), F32))
    bits_out[...] = jnp.broadcast_to(jnp.sum(bits, 0, keepdims=True) / LOG_TWO, bits_out.shape)

    d_short = jnp.concatenate(
        [
            jnp.concatenate(
                [
                    xp[c, pl.ds(start, n, stride=3)]
                    + xp[c, pl.ds(start + 1, n, stride=3)]
                    + xp[c, pl.ds(start + 2, n, stride=3)]
                    for c in range(lanes)
                ],
                1,
            )
            for start, at, n in spots
        ],
        0,
    )
    d_branch = d_short.astype(BF)
    row_grads[6:7] = jnp.sum(d_branch.astype(F32), 0, keepdims=True)
    xhat, rstd = norm_stats(middle_s[...])
    second = (xhat * vec[9:10] + vec[10:11]).astype(BF)
    d_second = jnp.zeros(d_short.shape, F32)
    for c in range(PARTS):
        cols = slice(c * WIDTH, (c + 1) * WIDTH)
        d_feed[1, :, cols] = mm(d_branch, active_s[:, cols], TN).astype(BF)
        d_pre = (mm(d_branch, feed[1, :, cols]) * slope_s[:, cols].astype(F32)).astype(BF)
        put_beta(row_grads, 7, c, jnp.sum(d_pre.astype(F32), 0, keepdims=True), False)
        d_feed[0, :, cols] = mm(second, d_pre, TN).astype(BF)
        d_second = d_second + mm(d_pre, feed[0, :, cols], NT)
    dx, d_gain, d_shift = norm_back(d_second, xhat, rstd, vec[9:10])
    row_grads[4:5] = d_gain
    row_grads[5:6] = d_shift
    d_middle = d_short + dx
    d_mix = d_middle.astype(BF)
    ot_all = ot[...].reshape(D, ot.shape[2])
    d_attn[1, :, D:] = mm(ot_all, d_mix).astype(BF)
    d_att = mm(d_mix, attn[1, :, D:], NT).astype(BF)
    for pair in range(PAIRS):
        mixed[3, pair] = d_att[:, pair * PW : (pair + 1) * PW]

    def backward_pair(pair, carry):
        for at, n, offset in ((0, n_long, 0), (n_long, TILE, 2 * n_long)):
            d_out = mixed[3, pair, at : at + n]
            product = (d_out.astype(F32).T) * ot[pair, :, at : at + n].astype(F32)
            inner = jnp.concatenate(
                [
                    jnp.sum(product[:HD], 0, keepdims=True),
                    jnp.sum(product[HD:], 0, keepdims=True),
                ],
                1,
            )
            queries = split_heads(mixed[0, pair, at : at + n])
            grads = split_heads(d_out)
            keys = mixed[1, pair, at : at + n]
            count = n // TILE
            p, ds = score_back(
                keys,
                mixed[2, pair, at : at + n],
                queries,
                grads,
                lse[pair, :, offset : offset + 2 * n],
                inner,
                bias,
                pair,
                0,
                True,
                count,
                count,
                tiles,
            )
            dq = mm(keys.T, ds)
            dq = jnp.concatenate([dq[:HD, :n], dq[HD:, n:]], 0) * HD**-0.5
            d_mixed[0, pair, at : at + n] = dq.T.astype(BF)
            d_mixed[1, pair, at : at + n] = mm(ds, queries).astype(BF)
            d_mixed[2, pair, at : at + n] = mm(p, grads).astype(BF)
        return carry

    lax.fori_loop(0, PAIRS, backward_pair, 0)
    rel = rel_row(tiles, sums, fold, tiles.shape[1])
    row_grads[11:12] = jnp.concatenate([jnp.zeros_like(rel), rel], 1)
    d_in = jnp.concatenate([d_mixed[part, pair] for part in range(3) for pair in range(PAIRS)], 1)
    xhat, rstd = norm_stats(pooled[...])
    normed = (xhat * vec[7:8] + vec[8:9]).astype(BF)
    d_attn[0] = mm(normed, d_in[:, : 2 * D], TN).astype(BF)
    d_attn[1, :, :D] = mm(normed, d_in[:, 2 * D :], TN).astype(BF)
    dx, d_gain, d_shift = norm_back(mm(d_in[:, : 2 * D], attn[0], NT) + mm(d_in[:, 2 * D :], attn[1, :, :D], NT), xhat, rstd, vec[7:8])
    row_grads[2:3] = d_gain
    row_grads[3:4] = d_shift
    d_pool = (d_middle + dx) / 3.0
    for start, at, n in spots:
        for c in range(lanes):
            part = d_pool[at : at + n, c * TILE : (c + 1) * TILE]
            for k in range(3):
                where = pl.ds(start - 2 + k, n, stride=3)
                xp[c, where] = xp[c, where] + part
    for c in range(lanes):
        dx_out[0:seq, c * TILE : (c + 1) * TILE] = xp[c, PAD : PAD + seq]
        dx_out[seq:, c * TILE : (c + 1) * TILE] = xp[c, 2 * PAD + seq :]


def middle_stage(x1, aux, tables, attn, feed, vec, scalars, seq):
    tokens = x1.shape[0]
    n_long = seq // 3
    short = n_long + TILE
    far = n_long // TILE
    fold = fold_matrix(far)
    vm = pl.BlockSpec(memory_space=pltpu.VMEM)
    return pl.pallas_call(
        functools.partial(middle_kernel, seq),
        in_specs=[vm] * 6 + [pl.BlockSpec(memory_space=pltpu.SMEM)] + [vm] * 2,
        out_specs=[vm] * 6,
        out_shape=[
            jax.ShapeDtypeStruct((tokens, D), F32),
            jax.ShapeDtypeStruct((2, D, 2 * D), BF),
            jax.ShapeDtypeStruct((2, D, FF), BF),
            jax.ShapeDtypeStruct((V, D), F32),
            jax.ShapeDtypeStruct((16, D), F32),
            jax.ShapeDtypeStruct((8, 128), F32),
        ],
        scratch_shapes=[
            pltpu.VMEM((HEADS, fold_rows(far), TILE), F32),
            pltpu.VMEM((D // TILE, tokens + 2 * PAD, TILE), F32),
            pltpu.VMEM((short, D), F32),
            pltpu.VMEM((4, PAIRS, short, PW), BF),
            pltpu.VMEM((PAIRS, PW, short), BF),
            pltpu.VMEM((PAIRS, 1, 2 * short), F32),
            pltpu.VMEM((short, FF), BF),
            pltpu.VMEM((short, FF), BF),
            pltpu.VMEM((short, D), F32),
            pltpu.VMEM((HEADS, far, TILE, TILE), F32),
            pltpu.VMEM((HEADS, far, TILE, TILE), F32),
            pltpu.VMEM((3, PAIRS, short, PW), BF),
        ]
        + state_scratch(n_long),
        compiler_params=params(VMEM_MIB),
        name="middle_stage",
    )(x1, aux, tables, attn, feed, vec, vec, scalars, fold)


def feed_back_kernel(
    wide,
    narrow,
    dx,
    act,
    slope,
    middle,
    wts,
    vec,
    ready,
    dm_out,
    d_feed,
    row_grads,
    sums_out,
    up,
    down,
    *scratch,
):
    step = pl.program_id(0)
    at = Place(wide, narrow)
    stream = ScatterStream(at, ready, halves_out(sums_out), *scratch[:5], scratch[5:])

    @pl.when(step == 0)
    def _():
        greet(*scatter_greetings(at))
        stream.start()
        up[...] = jnp.zeros_like(up)
        down[...] = jnp.zeros_like(down)
        row_grads[...] = jnp.zeros_like(row_grads)

    d_result = dx[...]
    d_branch = d_result.astype(BF)
    row_grads[2:3] += jnp.sum(d_branch.astype(F32), 0, keepdims=True)
    xhat, rstd = norm_stats(middle[...])
    second = (xhat * vec[4:5] + vec[5:6]).astype(BF)
    d_second = jnp.zeros(d_result.shape, F32)
    for c in range(PARTS):
        cols = slice(c * WIDTH, (c + 1) * WIDTH)
        down[:, cols] += mm(d_branch, act[:, cols], TN)
        d_pre = (mm(d_branch, wts[1, :, cols]) * slope[:, cols].astype(F32)).astype(BF)
        put_beta(row_grads, 3, c, jnp.sum(d_pre.astype(F32), 0, keepdims=True), True)
        up[:, cols] += mm(second, d_pre, TN)
        d_second = d_second + mm(d_pre, wts[0, :, cols], NT)
    dn, d_gain, d_shift = norm_back(d_second, xhat, rstd, vec[4:5])
    row_grads[0:1] += d_gain
    row_grads[1:2] += d_shift
    dm_out[...] = d_result + dn
    for n, body in enumerate((stream.stage_first, stream.stage_second, stream.stage_home)):
        pl.when(step == n)(body)

    @pl.when(step == pl.num_programs(0) - 1)
    def _():
        d_feed[0] = up[...].astype(BF)
        d_feed[1] = down[...].astype(BF)
        stream.finish()


def halves_out(ref):
    return [ref.at[0], ref.at[1]]


def feed_back(dx, act, slope, middle, wts, vec, ready, wide, narrow):
    tokens = dx.shape[0]
    form = ready.shape[3:]

    def flat(width):
        return pl.BlockSpec((BLK, width), lambda i: (i, 0))

    return pl.pallas_call(
        functools.partial(feed_back_kernel, wide, narrow),
        grid=(tokens // BLK,),
        in_specs=[flat(D), flat(FF), flat(FF), flat(D), whole_spec(wts.shape), whole_spec(vec.shape)]
        + [pl.BlockSpec(memory_space=pl.ANY)],
        out_specs=[
            flat(D),
            whole_spec((2, D, FF)),
            whole_spec((8, D)),
            whole_spec((2,) + form),
        ],
        out_shape=[
            jax.ShapeDtypeStruct((tokens, D), F32),
            jax.ShapeDtypeStruct((2, D, FF), BF),
            jax.ShapeDtypeStruct((8, D), F32),
            jax.ShapeDtypeStruct((2,) + form, F32),
        ],
        scratch_shapes=[pltpu.VMEM((D, FF), F32), pltpu.VMEM((D, FF), F32)]
        + scatter_scratch(wide, narrow, form),
        compiler_params=params(VMEM_MIB, collective_id=5, has_side_effects=True),
        name="feed_back",
    )(dx, act, slope, middle, wts, vec, ready)


def attention_back_kernel(
    long_blocks,
    wide,
    narrow,
    dm,
    aux,
    ot,
    lse,
    q_all,
    k_all,
    v_all,
    embed,
    wts,
    vec,
    rel,
    fold,
    ready_a,
    ready_b,
    d_attn,
    d_embed,
    row_grads,
    out_a,
    out_b,
    sums,
    bias,
    tiles,
    kt_all,
    dk_all,
    dv_all,
    dq_t,
    d_att,
    inner,
    weights,
    d_mixed,
    *scratch,
):
    step = pl.program_id(0)
    blocks = pl.num_programs(0)
    i = blocks - 1 - step
    at = Place(wide, narrow)
    streams = []
    for ready, out in ((ready_a, out_a), (ready_b, out_b)):
        for source, target in zip(column_parts(ready, 2), column_parts(out, 2)):
            part = scratch[SCATTER_REFS * len(streams) : SCATTER_REFS * (len(streams) + 1)]
            streams.append(ScatterStream(at, source, halves_out(target), *part[:5], part[5:]))
    one, two, three, four = streams
    events = {
        (0, 0): (one.stage_first,),
        (0, 2): (two.stage_first,),
        (1, 0): (one.stage_second, three.stage_first),
        (1, 1): (two.stage_second,),
        (1, 2): (one.stage_home, four.stage_first),
        (1, 3): (three.stage_second,),
        (2, 0): (two.stage_home, four.stage_second),
        (2, 2): (three.stage_home,),
        (2, 3): (four.stage_home,),
    }

    @pl.when(step == 0)
    def _():
        greet(*scatter_greetings(at))
        for stream in streams:
            stream.start()
        build_bias(rel, 0, bias, bias.shape[1])
        tiles[...] = jnp.zeros_like(tiles)
        dk_all[...] = jnp.zeros_like(dk_all)
        dv_all[...] = jnp.zeros_like(dv_all)
        weights[...] = jnp.zeros_like(weights)
        d_embed[...] = jnp.zeros_like(d_embed)
        row_grads[...] = jnp.zeros_like(row_grads)

        def turn(n, carry):
            for pair in range(PAIRS):
                kt_all[n, pair] = k_all[n, pair].T
            return carry

        lax.fori_loop(0, blocks, turn, 0)

    d_middle = dm[...]
    d_mix = d_middle.astype(BF)
    weights[1, :, D:] += mm(ot[0].reshape(D, BLK), d_mix)
    out = mm(d_mix, wts[1, :, D : 2 * D], NT).astype(BF)
    for pair in range(PAIRS):
        d_att[pair] = out[:, pair * PW : (pair + 1) * PW]
    product = mm(wts[1, :, D : 2 * D], d_mix, NT).astype(BF).astype(F32) * ot[0].reshape(
        D, BLK
    ).astype(F32)
    for pair in range(PAIRS):
        top = pair * PW
        inner[pair] = jnp.concatenate(
            [
                jnp.sum(product[top : top + HD], 0, keepdims=True),
                jnp.sum(product[top + HD : top + PW], 0, keepdims=True),
            ],
            1,
        )
    first = jnp.where(i >= long_blocks, long_blocks, 0)

    def one_pair(pair, carry):
        queries = split_heads(q_all[i, pair])
        grads = split_heads(d_att[pair])
        dq_t[...] = jnp.zeros_like(dq_t)

        def with_block(j, far, diag):
            p, ds = score_back(
                k_all[j, pair],
                v_all[j, pair],
                queries,
                grads,
                lse[0, pair],
                inner[pair],
                bias,
                pair,
                far,
                diag,
                SUB,
                SUB,
                tiles,
            )
            dv_all[j, pair] += mm(p, grads)
            dk_all[j, pair] += mm(ds, queries)
            dq_t[...] += mm(kt_all[j, pair], ds)

        def earlier(j, inside):
            with_block(j, SUB * (i - j), False)
            return inside

        lax.fori_loop(first, i, earlier, 0)
        with_block(i, 0, True)
        total = dq_t[...]
        total = jnp.concatenate([total[:HD, :BLK], total[HD:, BLK:]], 0) * HD**-0.5
        d_mixed[0, pair] = total.T.astype(BF)
        d_mixed[1, pair] = dk_all[i, pair].astype(BF)
        d_mixed[2, pair] = dv_all[i, pair].astype(BF)
        run_events(events, step, pair)
        return carry

    lax.fori_loop(0, PAIRS, one_pair, 0)
    d_in = jnp.concatenate([d_mixed[part, pair] for part in range(3) for pair in range(PAIRS)], 1)
    hot = one_hot(aux[:, 0:1]).astype(BF)
    xhat, rstd = norm_stats(mm(hot, embed[0]))
    normed = (xhat * vec[2:3] + vec[3:4]).astype(BF)
    weights[0] += mm(normed, d_in[:, : 2 * D], TN)
    weights[1, :, :D] += mm(normed, d_in[:, 2 * D :], TN)
    dx, d_gain, d_shift = norm_back(mm(d_in[:, : 2 * D], wts[0, :, : 2 * D], NT) + mm(d_in[:, 2 * D :], wts[1, :, :D], NT), xhat, rstd, vec[2:3])
    row_grads[0:1] += d_gain
    row_grads[1:2] += d_shift
    d_embed[...] += mm(hot, (d_middle + dx).astype(BF), TN)

    @pl.when(step == blocks - 1)
    def _():
        d_attn[...] = weights[...].astype(BF)
        rel = rel_row(tiles, sums, fold, tiles.shape[1])
        row_grads[2:3] = jnp.concatenate([rel, jnp.zeros_like(rel)], 1)
        for stream in streams:
            stream.finish()


def half_width(x):
    return x.shape[3:-1] + (x.shape[-1] // 2,)


def attention_back(
    dm, aux, ot, lse, q, k, v, tables, wts, vec, ready_a, ready_b, long_blocks, wide, narrow
):
    tokens = dm.shape[0]
    blocks = tokens // BLK
    far = SUB * long_blocks
    fold = fold_matrix(far)

    def turned(shape):
        return pl.BlockSpec(shape, lambda s: (blocks - 1 - s,) + (0,) * (len(shape) - 1))

    return pl.pallas_call(
        functools.partial(attention_back_kernel, long_blocks, wide, narrow),
        grid=(blocks,),
        in_specs=[
            turned((BLK, D)),
            turned((BLK, aux.shape[1])),
            turned((1, PAIRS, PW, BLK)),
            turned((1, PAIRS, 1, 2 * BLK)),
            whole_spec(q.shape),
            whole_spec(k.shape),
            whole_spec(v.shape),
            whole_spec((1, V, D)),
            whole_spec((2, D, 2 * D)),
            whole_spec(vec.shape),
            pl.BlockSpec(memory_space=pltpu.SMEM),
            whole_spec(fold.shape),
            pl.BlockSpec(memory_space=pl.ANY),
            pl.BlockSpec(memory_space=pl.ANY),
        ],
        out_specs=[
            whole_spec((2, D, 2 * D)),
            whole_spec((V, D)),
            whole_spec((8, D)),
            whole_spec((2,) + ready_a.shape[3:]),
            whole_spec((2,) + ready_b.shape[3:]),
        ],
        out_shape=[
            jax.ShapeDtypeStruct((2, D, 2 * D), BF),
            jax.ShapeDtypeStruct((V, D), F32),
            jax.ShapeDtypeStruct((8, D), F32),
            jax.ShapeDtypeStruct((2,) + ready_a.shape[3:], F32),
            jax.ShapeDtypeStruct((2,) + ready_b.shape[3:], F32),
        ],
        scratch_shapes=[
            pltpu.VMEM((HEADS, fold_rows(far), TILE), F32),
            pltpu.VMEM((HEADS, far, TILE, TILE), F32),
            pltpu.VMEM((HEADS, far, TILE, TILE), F32),
            pltpu.VMEM((blocks, PAIRS, PW, BLK), BF),
            pltpu.VMEM((blocks, PAIRS, BLK, PW), F32),
            pltpu.VMEM((blocks, PAIRS, BLK, PW), F32),
            pltpu.VMEM((PW, 2 * BLK), F32),
            pltpu.VMEM((PAIRS, BLK, PW), BF),
            pltpu.VMEM((PAIRS, 1, 2 * BLK), F32),
            pltpu.VMEM((2, D, 2 * D), F32),
            pltpu.VMEM((3, PAIRS, BLK, PW), BF),
        ]
        + scatter_scratch(wide, narrow, half_width(ready_a)) * 2
        + scatter_scratch(wide, narrow, half_width(ready_b)) * 2,
        compiler_params=params(VMEM_MIB, collective_id=6, has_side_effects=True),
        name="attention_back",
    )(dm, aux, ot, lse, q, k, v, tables, wts, vec, vec, fold, ready_a, ready_b)


MESH = pl.DeviceIdType.MESH
MISC_ROWS = 32
SIDE = 128
MISC_COLS = D + SIDE
COUNT_ROW = 24


class Place:
    def __init__(self, wide, narrow):
        self.W, self.N = wide, narrow
        self.c = lax.axis_index("rep")
        self.w = lax.axis_index("wide")
        self.n = lax.axis_index("narrow")
        self.a0, self.b0 = self.digits(self.c)
        self.group = self.w // (wide // 2)

    def digits(self, c):
        hi, lo = self.n // 2, self.n % 2
        return (1 - c) * hi + c * lo, (1 - c) * lo + c * hi

    def narrow_of(self, a, b, c=None):
        c = self.c if c is None else c
        return a * (2 - c) + b * (1 + c)

    def chip(self, w, a, b):
        return {"wide": w, "narrow": self.narrow_of(a, b)}

    def sibling(self):
        return {"rep": 1 - self.c}


def greet(devices, more=()):
    barrier = pltpu.get_barrier_semaphore()
    count = len(devices)
    for device in devices:
        pl.semaphore_signal(barrier, inc=1, device_id=device, device_id_type=MESH)
    for condition, device in more:

        @pl.when(condition)
        def _(device=device):
            pl.semaphore_signal(barrier, inc=1, device_id=device, device_id_type=MESH)

        count = count + condition.astype(jnp.int32)
    pl.semaphore_wait(barrier, count)


def slab_form(rows, cols):
    return (rows, cols) if rows % 16 == 0 else (16, rows * cols // 16)


def gather_greetings(at):
    out = [{"wide": lax.rem(at.w + k, at.W)} for k in range(1, at.W)]
    return out + [
        at.chip(at.w, at.a0, 1 - at.b0),
        at.chip(at.w, 1 - at.a0, at.b0),
        at.sibling(),
    ]


class GatherStream:
    def __init__(self, at, src, out, send_along, send, recv, recv_side, local):
        self.at, self.src, self.out = at, src, out
        self.send_along, self.send, self.recv, self.recv_side = send_along, send, recv, recv_side
        self.n0 = at.narrow_of(at.a0, at.b0)
        self.n1 = at.narrow_of(at.a0, 1 - at.b0)
        self.n2 = at.narrow_of(1 - at.a0, at.b0)
        self.n3 = at.narrow_of(1 - at.a0, 1 - at.b0)
        self.keep = pltpu.make_async_copy(src, out.at[at.c, at.w, self.n0], local)

    def copy(self, ref, w, n, sem, peer):
        return pltpu.make_async_remote_copy(
            src_ref=ref,
            dst_ref=self.out.at[self.at.c, w, n],
            send_sem=sem,
            recv_sem=self.recv.at[w, n],
            device_id=peer,
            device_id_type=MESH,
        )

    def arrived(self, w, n):
        self.copy(
            self.out.at[self.at.c, w, n], w, n, self.send.at[0], self.at.sibling()
        ).wait_recv()

    def other(self, k):
        return lax.rem(self.at.w + k, self.at.W)

    def along(self, k):
        at = self.at
        return self.copy(
            self.src, at.w, self.n0, self.send_along.at[k - 1], {"wide": self.other(k)}
        )

    def neighbours(self, w, mine):
        at = self.at
        ref = self.src if mine else self.out.at[at.c, w, self.n0]
        self.copy(ref, w, self.n0, self.send.at[0], at.chip(at.w, at.a0, 1 - at.b0)).start()
        self.copy(ref, w, self.n0, self.send.at[1], at.chip(at.w, 1 - at.a0, at.b0)).start()

    def side(self, n):
        at = self.at
        return pltpu.make_async_remote_copy(
            src_ref=self.out.at[at.c, :, n],
            dst_ref=self.out.at[at.c, :, n],
            send_sem=self.send.at[2 + n],
            recv_sem=self.recv_side.at[n],
            device_id=at.sibling(),
            device_id_type=MESH,
        )

    def start(self):
        self.keep.start()
        for k in self.order():
            self.along(k).start()
        self.neighbours(self.at.w, True)

    def order(self):
        return sorted(range(1, self.at.W), key=lambda k: -min(k, self.at.W - k))

    def depth(self, d):
        at = self.at
        if d == 1:
            for k in self.order()[::-1]:
                w = self.other(k)
                self.arrived(w, self.n0)
                self.neighbours(w, False)
            self.keep.wait()
            self.side(self.n0).start()
        if d == 2:
            for k in [0] + self.order()[::-1]:
                w = self.other(k)
                self.arrived(w, self.n1)
                ref = self.out.at[at.c, w, self.n1]
                peer = at.chip(at.w, 1 - at.a0, at.b0)
                self.copy(ref, w, self.n1, self.send.at[1], peer).start()
            self.side(self.n1).start()
            for k in range(at.W):
                self.arrived(self.other(k), self.n2)
            self.side(self.n2).start()
        if d == 3:
            for k in range(at.W):
                self.arrived(self.other(k), self.n3)
            self.side(self.n3).start()

    def finish(self):
        at = self.at
        for k in self.order():
            self.along(k).wait_send()
        column = self.out.at[at.c, :, self.n0]
        half = self.out.at[at.c, pl.ds(0, at.W // 2)]
        for sem, ref in ((self.send.at[0], column), (self.send.at[1], half)):
            pltpu.make_async_remote_copy(
                src_ref=ref,
                dst_ref=ref,
                send_sem=sem,
                recv_sem=self.recv.at[0, 0],
                device_id=at.sibling(),
                device_id_type=MESH,
            ).wait_send()
        for n in range(at.N):
            self.side(n).wait_send()
        for n in range(at.N):
            pltpu.make_async_remote_copy(
                src_ref=self.out.at[1 - at.c, :, n],
                dst_ref=self.out.at[1 - at.c, :, n],
                send_sem=self.send.at[2 + n],
                recv_sem=self.recv_side.at[n],
                device_id=at.sibling(),
                device_id_type=MESH,
            ).wait_recv()


GATHER_SEMS = 5


def gather_sems(wide, narrow):
    dma = pltpu.SemaphoreType.DMA
    return [dma((wide,)), dma((2 + narrow,)), dma((wide, narrow)), dma((narrow,)), dma]


class ScatterStream:
    def __init__(self, at, src, out, own, side, first, second, fin, sems):
        self.at, self.src, self.out = at, src, out
        self.own, self.side, self.first, self.second, self.fin = own, side, first, second, fin
        self.local, self.side_sem, self.first_sem, self.second_sem, self.home_sem, self.fin_sem = sems
        self.n0 = at.narrow_of(at.a0, at.b0)
        self.n1 = at.narrow_of(at.a0, 1 - at.b0)

    def remote(self, src, dst, sems, index, device):
        return pltpu.make_async_remote_copy(
            src_ref=src,
            dst_ref=dst,
            send_sem=sems.at[(0,) + index],
            recv_sem=sems.at[(1,) + index],
            device_id=device,
            device_id_type=MESH,
        )

    def side_copy(self, n):
        at = self.at
        return self.remote(
            self.src.at[1 - at.c, :, n], self.side.at[:, n], self.side_sem, (n,), at.sibling()
        )

    def own_copy(self):
        return pltpu.make_async_copy(self.src.at[self.at.c], self.own, self.local)

    def first_copy(self, b):
        at = self.at
        return self.remote(
            self.own.at[:, at.narrow_of(1 - at.a0, b)],
            self.first.at[b],
            self.first_sem,
            (b,),
            at.chip(at.w, 1 - at.a0, at.b0),
        )

    def second_copy(self):
        at = self.at
        return self.remote(
            self.own.at[:, self.n1],
            self.second,
            self.second_sem,
            (),
            at.chip(at.w, at.a0, 1 - at.b0),
        )

    def home_copy(self, w):
        at = self.at
        return pltpu.make_async_remote_copy(
            src_ref=self.own.at[w, self.n0],
            dst_ref=self.fin.at[at.w % (at.W // 2), at.c],
            send_sem=self.home_sem.at[w],
            recv_sem=self.fin_sem.at[at.w % (at.W // 2), at.c],
            device_id={"wide": w, "rep": at.group},
            device_id_type=MESH,
        )

    def elsewhere(self, w):
        return (w != self.at.w) | (self.at.c != self.at.group)

    def start(self):
        at = self.at
        self.own_copy().start()
        other = 1 - at.c
        a1, b1 = at.digits(other)
        for a, b in ((1 - a1, 1 - b1), (1 - a1, b1), (a1, 1 - b1), (a1, b1)):
            self.side_copy(at.narrow_of(a, b, other)).start()

    def stage_first(self):
        at = self.at
        self.own_copy().wait()
        for b in (1 - at.b0, at.b0):
            n = at.narrow_of(1 - at.a0, b)
            self.side_copy(n).wait_recv()

            def body(w, carry, n=n):
                self.own[w, n] = (self.own[w, n].astype(F32) + self.side[w, n].astype(F32)).astype(BF)
                return carry

            lax.fori_loop(0, at.W, body, 0)
            self.first_copy(b).start()

    def stage_second(self):
        at = self.at
        self.side_copy(self.n1).wait_recv()
        self.first_copy(1 - at.b0).wait_recv()

        def body(w, carry):
            value = self.own[w, self.n1].astype(F32) + self.side[w, self.n1].astype(F32)
            self.own[w, self.n1] = (value + self.first[1 - at.b0, w].astype(F32)).astype(BF)
            return carry

        lax.fori_loop(0, at.W, body, 0)
        self.second_copy().start()

    def stage_home(self):
        at = self.at
        n = self.n0
        self.side_copy(n).wait_recv()
        self.first_copy(at.b0).wait_recv()
        self.second_copy().wait_recv()

        def body(k, carry):
            w = lax.rem(at.w + at.W // 2 + k, at.W)
            value = self.own[w, n].astype(F32) + self.side[w, n].astype(F32)
            value = value + self.first[at.b0, w].astype(F32) + self.second[w].astype(F32)
            self.own[w, n] = value.astype(BF)

            @pl.when(self.elsewhere(w))
            def _():
                self.home_copy(w).start()

            @pl.when(jnp.logical_not(self.elsewhere(w)))
            def _():
                self.fin[at.w % (at.W // 2), at.c] = value.astype(BF)

            return carry

        lax.fori_loop(0, at.W, body, 0)

    def finish(self):
        at = self.at
        half = at.W // 2
        for h in range(2):
            total = None
            for k in range(half):

                @pl.when((at.c * half + k != at.w) | (at.c != h))
                def _(k=k, h=h):
                    pltpu.make_async_remote_copy(
                        src_ref=self.fin.at[k, h],
                        dst_ref=self.fin.at[k, h],
                        send_sem=self.home_sem.at[0],
                        recv_sem=self.fin_sem.at[k, h],
                        device_id=at.sibling(),
                        device_id_type=MESH,
                    ).wait_recv()

                value = self.fin[k, h].astype(F32)
                total = value if total is None else total + value
            self.out[h][...] = total
        for n in range(at.N):
            self.side_copy(n).wait_send()
        for b in range(2):
            self.first_copy(b).wait_send()
        self.second_copy().wait_send()

        def homes(w, carry):
            @pl.when(self.elsewhere(w))
            def _():
                self.home_copy(w).wait_send()

            return carry

        lax.fori_loop(0, at.W, homes, 0)


SCATTER_REFS = 11


def scatter_scratch(wide, narrow, form):
    sizes = ((wide, narrow), (wide, narrow), (2, wide), (wide,), (wide // 2, 2))
    dma = pltpu.SemaphoreType.DMA
    buffers = [pltpu.VMEM(size + form, BF) for size in sizes]
    return buffers + [dma, dma((2, narrow)), dma((2, 2)), dma((2,)), dma((wide,)), dma((wide // 2, 2))]


def scatter_greetings(at):
    out = [
        at.chip(at.w, at.a0, 1 - at.b0),
        at.chip(at.w, 1 - at.a0, at.b0),
        at.sibling(),
    ]
    more = []
    for k in range(at.W // 2):
        for h in range(2):
            w = at.c * (at.W // 2) + k
            more.append(((w != at.w) | (at.c != h), {"rep": h, "wide": w}))
    return out, more


def place_columns(slabs, cols):
    feature = lax.broadcasted_iota(jnp.int32, (D, slabs * SIDE), 0)
    column = lax.broadcasted_iota(jnp.int32, (D, slabs * SIDE), 1)
    lane = column % SIDE
    return jnp.where((feature == column // SIDE * cols + lane) & (lane < cols), 1.0, 0.0).astype(BF)


def view_half(ref, layer, half, width, natural):
    if natural:
        return ref.at[layer, :, pl.ds(pl.multiple_of(half * width, width), width)]
    return ref.at[layer, half]


def column_parts(ref, count):
    width = ref.shape[-1] // count
    lead = (slice(None),) * (len(ref.shape) - 1)
    return [ref.at[lead + (slice(k * width, (k + 1) * width),)] for k in range(count)]


def prepare_kernel(wide, narrow, natural, *refs):
    take = iter(refs)

    def some(n):
        return [next(take) for _ in range(n)]

    ids, live, tables, attention, feed, vectors = some(6)
    attn_low, feed_low, attn_out, misc_out, aux, scalars = some(6)
    full_tables, vec = some(2) if natural else (None, None)
    misc, misc_low, packed, moved, move_sems = some(5)
    streams = [some(GATHER_SEMS) for _ in range(2)]
    at = Place(wide, narrow)
    seq = ids.shape[1]
    table_rows, cols = tables.shape[1], vectors.shape[1]

    to_core, to_wide = at.w % 2, at.c * (wide // 2) + at.w // 2
    from_wide = 2 * (at.w % (wide // 2)) + at.c
    leaves = (to_core != at.c) | (to_wide != at.w)
    greet(gather_greetings(at), [(leaves, {"rep": at.group, "wide": from_wide})])
    packed[...] = ids[...] + V * live[...]
    move = pltpu.make_async_remote_copy(
        src_ref=packed,
        dst_ref=moved,
        send_sem=move_sems.at[0],
        recv_sem=move_sems.at[1],
        device_id={"rep": to_core, "wide": to_wide},
        device_id_type=MESH,
    )
    stay = pltpu.make_async_copy(packed, moved, move_sems.at[0])
    pl.when(leaves)(move.start)
    pl.when(jnp.logical_not(leaves))(stay.start)

    position = lax.broadcasted_iota(jnp.int32, live.shape, 1)
    tally = jnp.sum(jnp.where(position > 0, live[...], 0).astype(F32), 1, keepdims=True)
    tally = jnp.sum(tally, 0, keepdims=True)
    high = jnp.floor(tally / 64.0)
    lane = lax.broadcasted_iota(jnp.int32, (1, SIDE), 1)
    misc[...] = jnp.zeros_like(misc)
    misc[0:table_rows, 0:D] = tables[at.c]
    misc[0:VEC, D : D + cols] = vectors[...]
    misc[COUNT_ROW : COUNT_ROW + 1, D:] = jnp.where(
        lane == 0, high, jnp.where(lane == 1, tally - 64.0 * high, 0.0)
    )
    misc_low[...] = misc[...].astype(BF)
    attn_low[...] = attention[...].astype(BF)
    small = GatherStream(at, misc_low, misc_out, *streams[0])
    attn = GatherStream(
        at, view_half(attn_low, 0, at.c, 2 * D, natural), attn_out, *streams[1]
    )
    small.start()
    attn.start()
    feed_low[...] = feed[...].astype(BF)

    pl.when(leaves)(move.wait)
    pl.when(jnp.logical_not(leaves))(stay.wait)
    live_at = lax.broadcasted_iota(jnp.int32, (8, seq), 1)
    row_at = lax.broadcasted_iota(jnp.int32, (8, seq), 0)
    start = 0
    for r, length in ((0, seq), (1, BLK)):
        row = moved[r : r + 1]
        after = jnp.concatenate([row[:, 1:], row[:, :1]], 1)
        weight = jnp.where(live_at[0:1] < seq - 1, after // V, 0)
        info = jnp.where(
            row_at == 0, row % V, jnp.where(row_at == 1, after % V, jnp.where(row_at == 2, weight, 0))
        )
        aux[start : start + length] = info[:, :length].astype(F32).T
        start += length
    for stream, d in (
        (small, 1),
        (attn, 1),
        (small, 2),
        (attn, 2),
        (small, 3),
        (attn, 3),
    ):
        stream.depth(d)
    small.finish()
    attn.finish()

    sides = [
        sum(
            misc_out[h, w, n, :, D:].astype(F32) for w in range(wide) for n in range(narrow)
        )
        for h in range(2)
    ]
    counts = [
        side[COUNT_ROW : COUNT_ROW + 1, 0:1] * 64.0 + side[COUNT_ROW : COUNT_ROW + 1, 1:2]
        for side in sides
    ]
    mine = jnp.where(at.group == 0, counts[0], counts[1])
    line = lax.broadcasted_iota(jnp.int32, (8, 128), 0)
    kept = jnp.where(at.c == 0, counts[0], counts[1])
    scalars[...] = jnp.where(line == 0, kept, jnp.where(line == 1, 1.0 / (mine * LOG_TWO), 0.0))
    if natural:
        for h in range(2):
            for w in range(wide):
                for n in range(narrow):
                    s = w * narrow + n
                    full_tables[h, s * table_rows : (s + 1) * table_rows] = misc_out[
                        h, w, n, :table_rows, :D
                    ]
        blocks = [misc_out[0, w, n, :, D:] for w in range(wide) for n in range(narrow)]
        spread = mm(jnp.concatenate(blocks, 1), place_columns(wide * narrow, cols), NT)
        vec[...] = spread[: vec.shape[0]]


def prepare(ids, live, tables, attention, feed, vectors, wide, narrow, natural):
    vm = pl.BlockSpec(memory_space=pltpu.VMEM)
    anywhere = pl.BlockSpec(memory_space=pl.ANY)
    seq = ids.shape[1]
    half_form = attention.shape[1:] if natural else attention.shape[2:]
    half_form = (half_form[0], 2 * D) if natural else half_form
    misc = (MISC_ROWS, MISC_COLS)
    outs = [
        (attention.shape, BF, vm),
        (feed.shape, BF, vm),
        ((2, wide, narrow) + half_form, BF, anywhere),
        ((2, wide, narrow) + misc, BF, vm),
        ((seq + BLK, 8), F32, vm),
        ((8, 128), F32, vm),
    ]
    if natural:
        outs += [((2, V, D), BF, vm), ((24, D), F32, vm)]
    return pl.pallas_call(
        functools.partial(prepare_kernel, wide, narrow, natural),
        in_specs=[vm] * 6,
        out_specs=[spec for _, _, spec in outs],
        out_shape=[jax.ShapeDtypeStruct(shape, kind) for shape, kind, _ in outs],
        scratch_shapes=[
            pltpu.VMEM(misc, F32),
            pltpu.VMEM(misc, BF),
            pltpu.VMEM(ids.shape, jnp.int32),
            pltpu.VMEM(ids.shape, jnp.int32),
            pltpu.SemaphoreType.DMA((2,)),
        ]
        + gather_sems(wide, narrow) * 2,
        compiler_params=params(VMEM_MIB, collective_id=1, has_side_effects=True),
        name="prepare",
    )(ids, live, tables, attention, feed, vectors)


def halves_of(ref, layer, width, natural):
    if natural:
        return [ref.at[layer, :, h * width : (h + 1) * width] for h in range(2)]
    return [ref.at[layer, h] for h in range(2)]


def adam_update(weight, moment, square, gradient, decay, rate):
    moment = BETA_ONE * moment + (1.0 - BETA_ONE) * gradient
    square = BETA_TWO * square + (1.0 - BETA_TWO) * gradient * gradient
    fixed_moment = moment / (1.0 - BETA_ONE**STEP)
    fixed_square = square / (1.0 - BETA_TWO**STEP)
    delta = -rate * (fixed_moment / (jnp.sqrt(fixed_square) + ADAM_EPS) + decay * weight)
    return (moment, square, delta)


DECAYS = (DECAY, DECAY, DECAY, 0.0)
RATES = (RATE_TABLE, RATE, RATE, RATE_TABLE)
SUMMED = ((1, 1), (2, 1), (2, 0))


def sum_stages(wide, narrow):
    return (narrow - 1) + (wide - 1 if wide <= 4 else wide.bit_length() - 1)


def sum_rounds(at):
    rounds = [[(k, {"narrow": lax.rem(at.n + 1 + k, at.N)}) for k in range(at.N - 1)]]
    slot = at.N - 1
    if at.W <= 4:
        rounds.append(
            [(slot + k, {"wide": lax.rem(at.w + 1 + k, at.W)}) for k in range(at.W - 1)]
        )
    else:
        unit = 1
        while unit < at.W:
            rounds.append([(slot, {"wide": at.w + unit * (1 - 2 * ((at.w // unit) % 2))})])
            slot += 1
            unit *= 2
    return [device for peers in rounds for _, device in peers], rounds


def ordered_sum(at, peers, total, arrived):
    if len(peers) == 1:
        return total + arrived[peers[0][0]]
    size = len(peers) + 1
    here = at.n if "narrow" in peers[0][1] else at.w
    out = None
    for index in range(size):
        value = jnp.where(here == index, total, 0.0)
        for k, (slot, _) in enumerate(peers):
            source = lax.rem(here + size - 1 - k, size)
            value = jnp.where(source == index, arrived[slot], value)
        out = value if out is None else out + value
    return out


def pack_misc(at, d_tables, row_sums, rows, packed, cols):
    short_rows, feed_rows, attn_rows = row_sums
    rows[0:2] = short_rows[0:2]
    rows[2:4] = attn_rows[0:2]
    rows[4:7] = feed_rows[0:3]
    rows[7:12] = short_rows[2:7]
    rows[BETA_ROW : BETA_ROW + CHUNKS] = feed_rows[3 : 3 + CHUNKS]
    rows[BETA_ROW + CHUNKS : REL_ROW] = short_rows[7 : 7 + CHUNKS]
    rows[REL_ROW : REL_ROW + 1] = attn_rows[2:3] + short_rows[11:12]
    rows[VEC:] = jnp.zeros((rows.shape[0] - VEC, D), F32)
    tall = jnp.concatenate([rows[...], jnp.zeros((MISC_ROWS - rows.shape[0], D), F32)], 0).astype(BF)
    spread = mm(tall, place_columns(at.W * at.N, cols)).astype(BF)
    count = V // (at.W * at.N)
    for w in range(at.W):
        for n in range(at.N):
            s = w * at.N + n
            for h in range(2):
                packed[h, w, n, :count, :D] = d_tables[h][s * count : (s + 1) * count].astype(BF)
                packed[h, w, n, count:, :D] = jnp.zeros((MISC_ROWS - count, D), BF)
            packed[0, w, n, :, D:] = spread[:, s * SIDE : (s + 1) * SIDE]
            packed[1, w, n, :, D:] = jnp.zeros((MISC_ROWS, SIDE), BF)


def reduce_kernel(wide, narrow, natural, *refs):
    at = Place(wide, narrow)
    take = iter(refs)

    def some(n):
        return [next(take) for _ in range(n)]

    if natural:
        d_tables, row_sums = some(2), some(3)
    else:
        d_misc = next(take)
    d_attn, ready, bits = next(take), some(3), next(take)
    hbm_states = some(12)
    grads, deltas, scalars = some(4), some(4), next(take)
    states, state_sems = some(12), next(take)
    misc_sum, bits_in, bits_sem = some(3)
    sums, arrived, sum_sems = some(3)
    mine, other, delta_sems = some(4), some(4), next(take)
    if natural:
        misc_rows, d_misc = some(2)
    greetings, rounds = sum_rounds(at)
    devices, more = scatter_greetings(at)
    greet(devices + greetings, more)
    if natural:
        pack_misc(at, d_tables, row_sums, misc_rows, d_misc, grads[3].shape[1])

    tiny = pltpu.make_async_remote_copy(
        src_ref=bits,
        dst_ref=bits_in,
        send_sem=bits_sem.at[0],
        recv_sem=bits_sem.at[1],
        device_id=at.sibling(),
        device_id_type=MESH,
    )
    tiny.start()
    streams = []
    for i, out in enumerate((halves_out(misc_sum), halves_of(grads[1], 0, 2 * D, natural))):
        part = some(SCATTER_REFS)
        streams.append(ScatterStream(at, (d_misc, d_attn)[i], out, *part[:5], part[5:]))
    for stream in streams:
        stream.start()
    loads = [
        pltpu.make_async_copy(src, dst, state_sems.at[i])
        for i, (src, dst) in enumerate(zip(hbm_states, states))
    ]
    for load in loads:
        load.start()
    views = list(streams[1].out)
    for (which, layer), source in zip(SUMMED, ready):
        targets = halves_of(grads[which], layer, 2 * D if which == 1 else FF, natural)
        views += targets
        for half in range(2):
            targets[half][...] = source[half]
    for stream in streams:
        stream.stage_first()
    for stream in streams:
        stream.stage_second()
    for stream in streams:
        stream.stage_home()
    for stream in streams:
        stream.finish()
    tiny.wait()

    table_rows, columns = grads[0].shape[1], grads[3].shape[1]
    for layer in range(2):
        grads[0][layer] = misc_sum[layer, :table_rows, :D]
    grads[3][...] = misc_sum[0, :VEC, D : D + columns]
    squared = jnp.zeros((1, 1), F32)
    for ref in halves_out(misc_sum) + views:
        value = ref[...]
        value = jnp.sum(value * value, 0, keepdims=True)
        squared = squared + jnp.sum(value, 1, keepdims=True)
    row = lax.broadcasted_iota(jnp.int32, (8, 128), 0)
    lost = jnp.where(at.c == at.group, bits[...] + bits_in[...], 0.0)
    total = jnp.where(row == 0, squared, jnp.where(row == 1, lost, 0.0))
    for peers in rounds:
        copies = []
        for k, partner in peers:
            sums[k] = total
            copies.append(
                pltpu.make_async_remote_copy(
                    src_ref=sums.at[k],
                    dst_ref=arrived.at[k],
                    send_sem=sum_sems.at[0, k],
                    recv_sem=sum_sems.at[1, k],
                    device_id=partner,
                    device_id_type=MESH,
                )
            )
        for copy in copies:
            copy.start()
        for copy in copies:
            copy.wait()
        total = ordered_sum(at, peers, total, arrived)
    norm = jnp.sqrt(total[0:1, 0:1])
    factor = jnp.minimum(1.0, CLIP_AT / (norm + 1e-06))
    scalars[...] = jnp.where(row == 0, norm, jnp.where(row == 2, factor, total))
    for load in loads:
        load.wait()

    copies = [
        pltpu.make_async_remote_copy(
            src_ref=mine[which],
            dst_ref=other[which],
            send_sem=delta_sems.at[0, which],
            recv_sem=delta_sems.at[1, which],
            device_id=at.sibling(),
            device_id_type=MESH,
        )
        for which in range(4)
    ]
    order = (2, 1, 0, 3)
    for which in order:
        refs_of = [states[which], states[4 + which], states[8 + which], grads[which], mine[which]]
        if which in (1, 2):
            width = 2 * D if which == 1 else FF
            views = [[ref.at[l] for ref in refs_of] for l in range(2)]
            if natural:
                views = [
                    [ref.at[l, :, h * width : (h + 1) * width] for ref in refs_of]
                    for l in range(2)
                    for h in range(2)
                ]
        else:
            views = [refs_of]
        for weight, moment, square, gradient, target in views:
            _, _, delta = adam_update(
                weight[...],
                moment[...],
                square[...],
                gradient[...] * factor,
                DECAYS[which],
                RATES[which],
            )
            target[...] = delta.astype(target.dtype)
        copies[which].start()
    for which in order:
        copies[which].wait()
        deltas[which][...] = (mine[which][...].astype(F32) + other[which][...].astype(F32)) * 0.5


def reduce_all(small, d_attn, ready, bits, states, wide, narrow, natural, collective_id):
    vm = pl.BlockSpec(memory_space=pltpu.VMEM)
    anywhere = pl.BlockSpec(memory_space=pl.ANY)
    like = [jax.ShapeDtypeStruct(x.shape, F32) for x in states[:4]]
    kinds = [BF if x.shape[-2] % 16 == 0 else F32 for x in states[:4]]
    exchanged = [pltpu.VMEM(x.shape, kind) for x, kind in zip(states[:4], kinds)]
    dma = pltpu.SemaphoreType.DMA
    stages = sum_stages(wide, narrow)
    misc = (MISC_ROWS, MISC_COLS)
    scratch = [pltpu.VMEM(x.shape, F32) for x in states] + [dma((12,))]
    scratch += [pltpu.VMEM((2,) + misc, F32), pltpu.VMEM(bits.shape, F32), dma((2,))]
    scratch += [pltpu.VMEM((stages, 8, 128), F32)] * 2 + [dma((2, stages))]
    scratch += exchanged + exchanged + [dma((2, 4))]
    if natural:
        scratch += [pltpu.VMEM((24, D), F32), pltpu.VMEM((2, wide, narrow) + misc, BF)]
    for form in (misc, d_attn.shape[3:]):
        scratch += scatter_scratch(wide, narrow, form)
    return pl.pallas_call(
        functools.partial(reduce_kernel, wide, narrow, natural),
        in_specs=[vm if natural else anywhere] * len(small)
        + [anywhere]
        + [vm] * 4
        + [anywhere] * 12,
        out_specs=[vm] * 9,
        out_shape=like + like + [jax.ShapeDtypeStruct((8, 128), F32)],
        scratch_shapes=scratch,
        compiler_params=params(VMEM_MIB, collective_id=collective_id, has_side_effects=True),
        name="reduce_all",
    )(*small, d_attn, *ready, bits, *states)


def update_kernel(scalars, *refs):
    grads, deltas, weights, moments, squares, outers, averages = (
        refs[4 * k : 4 * k + 4] for k in range(7)
    )
    new_m, new_s, new_w, new_o, new_a = (refs[28 + 4 * k : 32 + 4 * k] for k in range(5))
    factor = scalars[2:3, 0:1]
    for which in range(4):
        moment, square, _ = adam_update(
            weights[which][...],
            moments[which][...],
            squares[which][...],
            grads[which][...] * factor,
            DECAYS[which],
            RATES[which],
        )
        new_m[which][...] = moment
        new_s[which][...] = square
        delta = deltas[which][...]
        outer = OUTER_MOM * outers[which][...] + delta
        weight = weights[which][...] + OUTER_RATE * (delta + OUTER_MOM * outer)
        new_o[which][...] = outer
        new_w[which][...] = weight
        new_a[which][...] = EVAL_KEEP * averages[which][...] + (1.0 - EVAL_KEEP) * weight


def update(scalars, grads, deltas, arrays):
    weights = arrays[:4]
    rows = weights[1].shape[1]

    def quarter(width):
        return pl.BlockSpec((1, rows, width // 4), lambda i: (i // 4, 0, i % 4))

    specs = [
        pl.BlockSpec((1,) + weights[0].shape[1:], lambda i: (i // 4, 0, 0)),
        quarter(4 * D),
        quarter(2 * FF),
        pl.BlockSpec(weights[3].shape, lambda i: (0, 0)),
    ]
    like = [jax.ShapeDtypeStruct(x.shape, F32) for x in weights]
    return pl.pallas_call(
        update_kernel,
        grid=(8,),
        in_specs=[pl.BlockSpec((8, 128), lambda i: (0, 0))] + specs * 7,
        out_specs=specs * 5,
        out_shape=like * 5,
        compiler_params=params(VMEM_MIB),
        name="update",
    )(scalars, *grads, *deltas, *arrays)


def pad_to(x, rows, cols):
    return jnp.pad(x, [(0, 0)] * (x.ndim - 2) + [(0, rows - x.shape[-2]), (0, cols - x.shape[-1])])


def per_device(wide, narrow, byte_ids, live_mask, *arrays):
    tables, attention, feed_forward, vectors = arrays[:4]
    rows, table_rows, cols = attention.shape[1], tables.shape[1], vectors.shape[1]
    seq = byte_ids.shape[1]
    long_blocks = seq // BLK
    natural = rows % 16 == 0
    place = (2, wide, narrow)

    def formed(k, x):
        if natural or k % 4 not in (1, 2):
            return x
        half = x.shape[-1] // 2
        return x.reshape(2, rows, 2, half).swapaxes(1, 2).reshape((2, 2) + slab_form(rows, half))

    def unformed(k, x):
        if natural or k % 4 not in (1, 2):
            return x
        return x.reshape(2, 2, rows, -1).swapaxes(1, 2).reshape(arrays[k].shape)

    def slabs_of(d):
        return d.reshape(place + slab_form(rows, d.shape[-1]))

    arrays = [x[0] if 4 <= k < 12 else x for k, x in enumerate(arrays)]
    states = [formed(k, x) for k, x in enumerate(arrays[:12])]
    attn_low, feed_low, attn, misc, aux, scalars, *more = prepare(
        byte_ids, live_mask, tables, states[1], states[2], vectors, wide, narrow, natural
    )
    if natural:
        full_tables, vec = more
    else:
        full_tables = misc[:, :, :, :table_rows, :D].reshape(2, V, D)
        side = misc[0, :, :, :VEC, D : D + cols].astype(F32).reshape(-1, VEC, cols)
        vec = pad_to(side.transpose(1, 0, 2).reshape(VEC, D), 24, D)
    attn = attn.reshape(2, D, 2 * D)
    x1, middle, q, k, v, ot, lse, act, slope, feed, short_attn, short_feed = full_forward(
        aux, full_tables, attn, attn_low, feed_low, vec, long_blocks, wide, narrow, natural
    )
    feed = feed.reshape(2, D, FF)
    d_x1, d_short_attn, d_short_feed, d_head, short_rows, bits = middle_stage(
        x1,
        aux,
        full_tables,
        short_attn.reshape(2, D, 2 * D),
        short_feed.reshape(2, D, FF),
        vec,
        scalars,
        seq,
    )
    d_middle, d_feed, feed_rows, sum_short_attn = feed_back(
        d_x1, act, slope, middle, feed, vec, slabs_of(d_short_attn), wide, narrow
    )
    d_attn, d_embed, attn_rows, sum_short_feed, sum_feed = attention_back(
        d_middle,
        aux,
        ot,
        lse,
        q,
        k,
        v,
        full_tables,
        attn,
        vec,
        slabs_of(d_short_feed),
        slabs_of(d_feed),
        long_blocks,
        wide,
        narrow,
    )
    if natural:
        small = (d_embed, d_head, short_rows, feed_rows, attn_rows)
    else:
        d_vec = jnp.concatenate(
            [
                short_rows[0:2],
                attn_rows[0:2],
                feed_rows[0:3],
                short_rows[2:7],
                feed_rows[3 : 3 + CHUNKS],
                short_rows[7 : 7 + CHUNKS],
                attn_rows[2:3] + short_rows[11:12],
            ],
            0,
        )
        side = pad_to(d_vec.reshape(VEC, -1, cols).transpose(1, 0, 2), MISC_ROWS, SIDE)
        halves = [
            jnp.concatenate([pad_to(d.reshape(-1, table_rows, D), MISC_ROWS, D), extra], -1)
            for d, extra in ((d_embed, side), (d_head, jnp.zeros_like(side)))
        ]
        small = (jnp.stack(halves).astype(BF).reshape(place + (MISC_ROWS, MISC_COLS)),)
    *sums, totals = reduce_all(
        small,
        slabs_of(d_attn),
        (sum_short_attn, sum_short_feed, sum_feed),
        bits,
        states,
        wide,
        narrow,
        natural,
        2,
    )
    grads = [unformed(k, x) for k, x in enumerate(sums[:4])]
    deltas = [unformed(k, x) for k, x in enumerate(sums[4:])]
    new = update(totals, grads, deltas, arrays)
    new = [x[None] if k < 8 else x for k, x in enumerate(new)]
    return (totals[1, :1], scalars[0, :1], totals[0, :1], *new)


def solution(mesh):
    rows = P(("rep", "wide", "narrow"), None)
    split = (
        P(None, ("wide", "narrow"), None),
        P(None, ("wide", "narrow"), None),
        P(None, ("wide", "narrow"), None),
        P(None, ("wide", "narrow")),
    )
    own = tuple(P("rep", *spec) for spec in split)
    return jax.shard_map(
        functools.partial(per_device, mesh.shape["wide"], mesh.shape["narrow"]),
        mesh=mesh,
        in_specs=(rows, rows) + split + own + own + split + split,
        out_specs=(P("rep"),) * 3 + own + own + split * 3,
        check_vma=False,
    )
```

```python
import functools
import math

import jax
import jax.numpy as jnp
import numpy as np
from jax import lax
from jax.experimental import pallas as pl
from jax.experimental.pallas import tpu as pltpu
from jax.sharding import PartitionSpec as P

D = 512
HEADS = 8
HD = 64
FF = 2048
V = 256
NB = 32
STEP = 10
VEC = 21
EDGES = (1, 2, 3, 4, 5, 6, 7, 8, 10, 12, 14, 16, 20, 24, 28, 32, 40, 48, 64, 80, 96, 128, 160, 192)
EDGES = EDGES + (256, 320, 384, 512, 640, 768, 1024)
NEG = -1000000000.0
EPS = 1e-05
LOG_TWO = math.log(2.0)
RATE = 0.01
RATE_TABLE = 0.2
BETA_ONE = 0.9
BETA_TWO = 0.95
ADAM_EPS = 1e-08
DECAY = 0.1
CLIP_AT = 0.02
OUTER_RATE = 0.7
OUTER_MOM = 0.9
EVAL_KEEP = 0.9

TILE = 128
TOGETHER = 2
BETA_ROW = 12
REL_ROW = 12 + 2 * FF // D
CHUNKS = FF // D
PARTS = 1
WIDTH = FF // PARTS
VMEM_MIB = 63
BLK = 384
SUB = BLK // TILE
PAIRS = HEADS // 2
PW = 2 * HD
GELU_C = math.sqrt(2.0 / math.pi)
GELU_A = 0.044715

BF = jnp.bfloat16
F32 = jnp.float32
NN = (((1,), (0,)), ((), ()))
NT = (((1,), (1,)), ((), ()))
TN = (((0,), (0,)), ((), ()))


def mm(left, right, dims=NN):
    return lax.dot_general(left, right, dims, preferred_element_type=F32)


def spans(count):
    out = []
    for d in range(count):
        lo, hi = max(TILE * d - (TILE - 1), 0), TILE * d + TILE - 1
        base = sum(e <= lo for e in EDGES)
        out.append((base, [(e, k + 1) for k, e in enumerate(EDGES) if lo < e <= hi]))
    return out


def fold_matrix(count):
    rows = []
    for base, edges in spans(count):
        row = np.zeros(NB, np.float32)
        row[base] += 1
        rows.append(row)
        for _, bucket in edges:
            row = np.zeros(NB, np.float32)
            row[bucket] += 1
            row[bucket - 1] -= 1
            rows.append(row)
    out = np.zeros((HEADS, fold_rows(count), HEADS * NB), jnp.bfloat16)
    for h in range(HEADS):
        out[h, : len(rows), h * NB : (h + 1) * NB] = np.stack(rows)
    return out


def tile_distance(d):
    keys = lax.broadcasted_iota(jnp.int32, (TILE, TILE), 0)
    queries = lax.broadcasted_iota(jnp.int32, (TILE, TILE), 1)
    return TILE * d + queries - keys


def build_bias(rel, level, bias, count):
    for d, (base, edges) in enumerate(spans(count)):
        distance = tile_distance(d)

        def one_head(h, carry, d=d, base=base, edges=edges, distance=distance):
            first = level * HEADS * NB + h * NB
            tile = jnp.full((TILE, TILE), rel[REL_ROW, first + base], F32)
            for edge, bucket in edges:
                tile = jnp.where(distance >= edge, rel[REL_ROW, first + bucket], tile)
            if d == 0:
                tile = jnp.where(distance < 0, NEG, tile)
            bias[h, d] = tile
            return carry

        lax.fori_loop(0, HEADS, one_head, 0)


def fold_bias(tiles, sums, count):
    at = 0
    for d, (_, edges) in enumerate(spans(count)):
        distance = tile_distance(d)

        def one_head(h, carry, d=d, edges=edges, distance=distance, at=at):
            tile = tiles[h, d]
            sums[h, at : at + 1] = jnp.sum(tile, 0, keepdims=True)
            for n, (edge, _) in enumerate(edges):
                sums[h, at + 1 + n : at + 2 + n] = jnp.sum(
                    jnp.where(distance >= edge, tile, 0.0), 0, keepdims=True
                )
            return carry

        lax.fori_loop(0, HEADS, one_head, 0)
        at += 1 + len(edges)


def fold_rows(count):
    return -(-sum(1 + len(edges) for _, edges in spans(count)) // 8) * 8


def rel_row(tiles, sums, fold, count):
    sums[...] = jnp.zeros_like(sums)
    fold_bias(tiles, sums, count)
    whole = sums[...].reshape(-1, TILE)
    high = whole.astype(BF)
    low = (whole - high.astype(F32)).astype(BF)
    matrix = fold[...].reshape(-1, HEADS * NB)
    total = mm(high, matrix, TN) + mm(low, matrix, TN)
    return jnp.sum(total, 0, keepdims=True)


def norm_stats(x):
    centered = x - jnp.mean(x, -1, keepdims=True)
    rstd = lax.rsqrt(jnp.mean(centered * centered, -1, keepdims=True) + EPS)
    return centered * rstd, rstd


def norm_back(dy, xhat, rstd, gain):
    t = dy * gain
    dx = rstd * (
        t - jnp.mean(t, -1, keepdims=True) - xhat * jnp.mean(t * xhat, -1, keepdims=True)
    )
    return dx, jnp.sum(dy * xhat, 0, keepdims=True), jnp.sum(dy, 0, keepdims=True)


def gelu_pair(u):
    square = u * u
    tanh = jnp.tanh(GELU_C * u * (1.0 + GELU_A * square))
    half = 0.5 * (1.0 + tanh)
    slope = half + 0.5 * u * (1.0 - tanh * tanh) * (GELU_C + 3.0 * GELU_C * GELU_A * square)
    return u * half, slope


def split_heads(pair):
    lane = lax.broadcasted_iota(jnp.int32, (TILE, pair.shape[1]), 1)
    parts = []
    for qa in range(pair.shape[0] // TILE):
        rows = pair[qa * TILE : (qa + 1) * TILE]
        zero = jnp.zeros_like(rows)
        parts += [jnp.where(lane < HD, rows, zero), jnp.where(lane >= HD, rows, zero)]
    return jnp.concatenate(parts, 0)


def interleave(low, high):
    parts = []
    for at in range(0, low.shape[1], TILE):
        parts += [low[:, at : at + TILE], high[:, at : at + TILE]]
    return jnp.concatenate(parts, 1)


def merge_heads(both):
    parts = []
    for at in range(0, both.shape[1], 2 * TILE):
        parts.append(
            jnp.concatenate([both[:HD, at : at + TILE], both[HD:, at + TILE : at + 2 * TILE]], 0)
        )
    return jnp.concatenate(parts, 1)


def tile_products(keys, queries, diag, nq, nk):
    out = {}
    rows = [queries] if not diag else [queries[2 * TILE * kb :] for kb in range(nk)]
    if not diag:
        full = mm(keys, queries, NT)
    for kb in range(nk):
        line = slice(kb * TILE, (kb + 1) * TILE)
        first = kb if diag else 0
        block = mm(keys[line], rows[kb], NT) if diag else full[line]
        for qa in range(first, nq):
            for e in range(2):
                at = (2 * (qa - first) + e) * TILE
                out[kb, e, qa] = block[:, at : at + TILE]
    return out


def by_queries(left, tiles, diag, nq, nk):
    if not diag:
        return mm(left, whole_tiles(tiles, range(nk), range(nq)))
    return jnp.concatenate(
        [
            mm(left[:, : (qa + 1) * TILE], whole_tiles(tiles, range(qa + 1), (qa,)))
            for qa in range(nq)
        ],
        1,
    )


def by_keys(tiles, right, diag, nq, nk):
    if not diag:
        return mm(whole_tiles(tiles, range(nk), range(nq)), right)
    return jnp.concatenate(
        [
            mm(whole_tiles(tiles, (kb,), range(kb, nq)), right[2 * TILE * kb :])
            for kb in range(nk)
        ],
        0,
    )


def whole_tiles(tiles, key_tiles, query_tiles):
    return jnp.concatenate(
        [
            jnp.concatenate([tiles[kb, e, qa] for kb in key_tiles], 0)
            for qa in query_tiles
            for e in range(2)
        ],
        1,
    )


def column_of(qa, e):
    at = (2 * qa + e) * TILE
    return slice(at, at + TILE)


def softmax_step(keys, values_t, queries, bias, pair, far, diag, nq, nk, state):
    top, total, acc = state
    raw = tile_products(keys, queries, diag, nq, nk)
    scores = {
        (kb, e, qa): tile + bias[2 * pair + e, far + qa - kb] for (kb, e, qa), tile in raw.items()
    }
    order = [(qa, e) for qa in range(nq) for e in range(2)]
    highest = []
    for qa, e in order:
        column = [scores[kb, e, qa] for kb in range(nk) if (kb, e, qa) in scores]
        highest.append(jnp.max(functools.reduce(jnp.maximum, column), 0, keepdims=True))
    old_top = top[...]
    new_top = jnp.maximum(old_top, jnp.concatenate(highest, 1))
    alpha = jnp.exp(old_top - new_top)
    sums, probs = [], {}
    for qa, e in order:
        ceiling = new_top[:, column_of(qa, e)]
        adds = None
        for kb in range(nk):
            if (kb, e, qa) in scores:
                p = jnp.exp(scores[kb, e, qa] - ceiling)
                adds = p if adds is None else adds + p
                probs[kb, e, qa] = p.astype(BF)
        sums.append(jnp.sum(adds, 0, keepdims=True))
    top[...] = new_top
    total[...] = alpha * total[...] + jnp.concatenate(sums, 1)
    acc[...] = alpha * acc[...] + by_queries(values_t, probs, diag, nq, nk)


def softmax_start(state):
    top, total, acc = state
    top[...] = jnp.full(top.shape, NEG, F32)
    total[...] = jnp.zeros(total.shape, F32)
    acc[...] = jnp.zeros(acc.shape, F32)


def softmax_end(state):
    top, total, acc = state
    return merge_heads(acc[...] / total[...]).astype(BF), top[...] + jnp.log(total[...])


def score_back(
    keys, values, keys_t, queries, grads, logsum, inner, bias, pair, far, diag, nq, nk, tiles
):
    raw = tile_products(keys, queries, diag, nq, nk)
    d_p = tile_products(values, grads, diag, nq, nk)
    probs, scores = {}, {}
    for e in range(2):
        for diff in range(0 if diag else -(nk - 1), nq):
            total = None
            for kb in range(nk):
                qa = kb + diff
                if qa < 0 or qa >= nq:
                    continue
                cols = column_of(qa, e)
                p = jnp.exp(raw[kb, e, qa] + bias[2 * pair + e, far + diff] - logsum[:, cols])
                ds = p * (d_p[kb, e, qa] - inner[:, cols])
                total = ds if total is None else total + ds
                probs[kb, e, qa] = p.astype(BF)
                scores[kb, e, qa] = ds.astype(BF)
            tiles[2 * pair + e, far + diff] += total
    return (
        by_keys(probs, grads, diag, nq, nk),
        by_keys(scores, queries, diag, nq, nk),
        by_queries(keys_t, scores, diag, nq, nk),
    )


def beta_of(vec, level, part, width):
    row = BETA_ROW + level * CHUNKS + part * width // D
    return jnp.concatenate([vec[r : r + 1] for r in range(row, row + width // D)], 1)


def put_beta(rows, start, part, value, add):
    for k in range(WIDTH // D):
        row = start + part * WIDTH // D + k
        piece = value[:, k * D : (k + 1) * D]
        rows[row : row + 1] = rows[row : row + 1] + piece if add else piece


def one_hot(column):
    return column == lax.broadcasted_iota(jnp.int32, (column.shape[0], V), 1)


def full_forward_kernel(
    long_blocks,
    wide,
    narrow,
    natural,
    aux,
    embed,
    wts,
    attn_low,
    feed_low,
    vec,
    rel,
    x1_out,
    middle_out,
    q_out,
    k_out,
    v_out,
    ot_out,
    lse_out,
    act_out,
    slope_out,
    feed_out,
    short_attn_out,
    short_feed_out,
    bias,
    k_all,
    vt_all,
    middles,
    seconds,
    feed,
    feed_sem,
    *more,
):
    step = pl.program_id(0)
    blocks = pl.num_programs(0) // 3
    states = [more[3 * k : 3 * k + 3] for k in range(TOGETHER)]
    sems = more[3 * TOGETHER :]
    at = Place(wide, narrow)
    sources, targets = [], []
    for low, layer, width, out, count in (
        (feed_low, 0, FF, feed_out, 2),
        (attn_low, 1, 2 * D, short_attn_out, 1),
        (feed_low, 1, FF, short_feed_out, 2),
    ):
        sources += column_parts(view_half(low, layer, at.c, width, natural), count)
        targets += column_parts(out, count)
    feed_a, feed_b, short_attn, short_a, short_b = (
        GatherStream(at, source, out, *sems[GATHER_SEMS * k : GATHER_SEMS * (k + 1)])
        for k, (source, out) in enumerate(zip(sources, targets))
    )
    loads = [
        pltpu.make_async_copy(source, target, feed_sem.at[k])
        for k, (source, target) in enumerate(zip(column_parts(feed_out, 2), column_parts(feed, 2)))
    ]

    def hop(stream, d):
        return lambda: stream.depth(d)

    events = {
        (0, 1): (hop(feed_a, 1),),
        (1, 0): (hop(feed_a, 2), hop(feed_b, 1)),
        (1, 1): (hop(feed_a, 3),),
        (2, "dense"): (hop(feed_b, 2), hop(short_attn, 1)),
        (2, 0): (hop(short_a, 1),),
        (2, 1): (hop(feed_b, 3), hop(short_attn, 2)),
        (3, "dense"): (hop(short_b, 1),),
        (3, 1): (hop(short_a, 2), hop(short_attn, 3)),
        (6, "end"): (hop(short_b, 2), hop(short_a, 3)),
        (9, "end"): (hop(short_b, 3),),
    }

    @pl.when(step == 0)
    def _():
        greet(gather_greetings(at))
        for stream in (feed_a, feed_b):
            stream.start()
        for stream in (short_attn, short_a, short_b):
            stream.start()
        build_bias(rel, 0, bias, bias.shape[1])

    @pl.when(step < blocks)
    def _():
        hot = one_hot(aux[:, 0:1]).astype(BF)
        x = mm(hot, embed[0])
        xhat, _ = norm_stats(x)
        normed = (xhat * vec[2:3] + vec[3:4]).astype(BF)
        queries = (mm(normed, wts[0, :, :D]) * HD**-0.5).astype(BF)
        keys = mm(normed, wts[0, :, D : 2 * D]).astype(BF)
        values = mm(normed, wts[1, :, :D]).astype(BF)
        for pair in range(PAIRS):
            cols = slice(pair * PW, (pair + 1) * PW)
            q_out[0, pair] = queries[:, cols]
            k_out[0, pair] = keys[:, cols]
            v_out[0, pair] = values[:, cols]
            k_all[step, pair] = keys[:, cols]
            vt_all[step, pair] = values[:, cols].T
        middles[step] = x
        run_events(events, step, "dense")


    @pl.when(step < blocks)
    def _():
        first = jnp.where(step >= long_blocks, long_blocks, 0)

        def two_pairs(turn, carry):
            pairs = [turn * TOGETHER + k for k in range(TOGETHER)]
            both = [split_heads(q_out[0, pair]) for pair in pairs]
            for state in states:
                softmax_start(state)

            def with_block(j, far, diag):
                for pair, queries, state in zip(pairs, both, states):
                    softmax_step(
                        k_all[j, pair], vt_all[j, pair], queries, bias, pair, far, diag, SUB, SUB, state
                    )

            def earlier(j, inner):
                with_block(j, SUB * (step - j), False)
                return inner

            lax.fori_loop(first, step, earlier, 0)
            with_block(step, 0, True)
            for pair, state in zip(pairs, states):
                ot_out[0, pair], lse_out[0, pair] = softmax_end(state)
            run_events(events, step, turn)
            return carry

        lax.fori_loop(0, PAIRS // TOGETHER, two_pairs, 0)
        attended = ot_out[0].reshape(D, BLK).T
        middles[step] = middles[step] + mm(attended, wts[1, :, D : 2 * D])

    for k, stream in enumerate((feed_a, feed_b)):
        due = (k + 1) * blocks if natural else blocks

        @pl.when(step == due - 1)
        def _(k=k, stream=stream):
            stream.finish()
            loads[k].start()

        @pl.when(step == due)
        def _(k=k):
            loads[k].wait()

    def weight_half(half, cols):
        if natural:
            return feed[half, :, :, :, cols].reshape(D, cols.stop - cols.start)
        return feed[half].reshape(D, FF)[:, cols]

    def half_feed(block, k):
        width = FF // 2
        cols = slice(k * width, (k + 1) * width)
        up = weight_half(0, cols)
        active, slope = gelu_pair(mm(seconds[block], up) + beta_of(vec, 0, k, width))
        active = active.astype(BF)
        act_out[...] = active
        slope_out[...] = slope.astype(BF)
        return mm(active, weight_half(1, cols), NT)

    @pl.when((step >= blocks) & (step < 2 * blocks))
    def _():
        block = lax.rem(step, blocks)
        middle = middles[block]
        middle_out[...] = middle
        xhat, _ = norm_stats(middle)
        seconds[block] = (xhat * vec[4:5] + vec[5:6]).astype(BF)
        middles[block] = middle + vec[6:7] + half_feed(block, 0)

    @pl.when(step >= 2 * blocks)
    def _():
        block = lax.rem(step, blocks)
        x1_out[...] = middles[block] + half_feed(block, 1)

    run_events(events, step, "end")

    @pl.when(step == 3 * blocks - 1)
    def _():
        for stream in (short_attn, short_a, short_b):
            stream.finish()


def run_events(events, step, point):
    for (s, p), bodies in events.items():
        if isinstance(point, str) or isinstance(p, str):
            if point is not p and point != p:
                continue
            due = step == s
        else:
            due = (step == s) & (point == p)

        @pl.when(due)
        def _(bodies=bodies):
            for body in bodies:
                body()


def whole_spec(shape):
    return pl.BlockSpec(shape, lambda i: (0,) * len(shape), pipeline_mode=pl.Buffered(1))


def params(mib, **more):
    return pltpu.CompilerParams(vmem_limit_bytes=mib * 2**20, **more)


def state_scratch(n):
    return [pltpu.VMEM((1, 2 * n), F32), pltpu.VMEM((1, 2 * n), F32), pltpu.VMEM((PW, 2 * n), F32)]


def full_forward(aux, tables, wts, attn_low, feed_low, vec, long_blocks, wide, narrow, natural):
    tokens = aux.shape[0]
    blocks = tokens // BLK
    far = SUB * long_blocks
    form = feed_low.shape[1:] if natural else feed_low.shape[2:]
    form = (form[0], FF) if natural else form
    half = (form[0], form[1] * 2 * D // FF)

    def early(i):
        return jnp.minimum(i, blocks - 1)

    def late(i, phase):
        return jnp.clip(i - phase * blocks, 0, blocks - 1)

    def heads(n, width):
        return (
            jax.ShapeDtypeStruct((blocks, PAIRS, n, width), BF),
            pl.BlockSpec((1, PAIRS, n, width), lambda i: (early(i), 0, 0, 0)),
        )

    def flat(phase):
        return (
            jax.ShapeDtypeStruct((tokens, D), F32),
            pl.BlockSpec((BLK, D), lambda i: (late(i, phase), 0)),
        )

    def hidden():
        return (
            jax.ShapeDtypeStruct((tokens, FF), BF),
            pl.BlockSpec(
                (BLK, FF // 2),
                lambda i: (
                    lax.rem(jnp.maximum(i - blocks, 0), blocks),
                    jnp.maximum(i - blocks, 0) // blocks,
                ),
            ),
        )

    anywhere = pl.BlockSpec(memory_space=pl.ANY)
    outs = [flat(2), flat(1)] + [heads(BLK, PW)] * 3 + [heads(PW, BLK)]
    outs.append(
        (
            jax.ShapeDtypeStruct((blocks, PAIRS, 1, 2 * BLK), F32),
            pl.BlockSpec((1, PAIRS, 1, 2 * BLK), lambda i: (early(i), 0, 0, 0)),
        )
    )
    outs += [hidden(), hidden()]
    outs += [
        (jax.ShapeDtypeStruct((2, wide, narrow) + each, BF), anywhere) for each in (form, half, form)
    ]
    return pl.pallas_call(
        functools.partial(full_forward_kernel, long_blocks, wide, narrow, natural),
        grid=(3 * blocks,),
        in_specs=[
            pl.BlockSpec((BLK, aux.shape[1]), lambda i: (early(i), 0)),
            whole_spec((1, V, D)),
            whole_spec(wts.shape),
            anywhere,
            anywhere,
            whole_spec(vec.shape),
            pl.BlockSpec(memory_space=pltpu.SMEM),
        ],
        out_specs=[spec for _, spec in outs],
        out_shape=[shape for shape, _ in outs],
        scratch_shapes=[
            pltpu.VMEM((HEADS, far, TILE, TILE), F32),
            pltpu.VMEM((blocks, PAIRS, BLK, PW), BF),
            pltpu.VMEM((blocks, PAIRS, PW, BLK), BF),
            pltpu.VMEM((blocks, BLK, D), F32),
            pltpu.VMEM((blocks, BLK, D), BF),
            pltpu.VMEM((2, wide, narrow) + form, BF),
            pltpu.SemaphoreType.DMA((2,)),
        ]
        + state_scratch(BLK) * TOGETHER
        + gather_sems(wide, narrow) * 5,
        compiler_params=params(VMEM_MIB, collective_id=4, has_side_effects=True),
        name="full_forward",
    )(aux, tables, wts, attn_low, feed_low, vec, vec)


PAD = 8


def middle_kernel(
    seq,
    x1,
    aux,
    head,
    attn,
    feed_in,
    vec,
    rel,
    scalars,
    fold,
    dx_out,
    d_attn,
    d_feed_out,
    d_head,
    row_grads,
    bits_out,
    sums,
    xp,
    pooled,
    mixed,
    ot,
    lse,
    active_s,
    slope_s,
    middle_s,
    bias,
    tiles,
    d_mixed,
    feed,
    d_feed,
    sems,
    *state,
):
    n_long = seq // 3
    spots = ((PAD, 0, n_long), (2 * PAD + seq, n_long, TILE))
    lanes = D // TILE
    def plane_copies(array, out):
        copies = []
        for c in range(lanes):
            for k, (first, start, count) in enumerate(
                ((0, PAD, seq), (seq, 2 * PAD + seq, array.shape[0] - seq))
            ):
                ends = (array.at[first : first + count, c * TILE : (c + 1) * TILE],)
                ends += (xp.at[c, start : start + count],)
                ends = ends[::-1] if out else ends
                copies.append(pltpu.make_async_copy(*ends, sems.at[2 * c + k]))
        return copies

    loads = plane_copies(x1, False)
    load_feed = pltpu.make_async_copy(feed_in, feed, sems.at[2 * lanes])
    store_feed = pltpu.make_async_copy(d_feed, d_feed_out, sems.at[2 * lanes + 1])
    for load in loads:
        load.start()
    load_feed.start()
    build_bias(rel, 1, bias, bias.shape[1])
    tiles[...] = jnp.zeros_like(tiles)
    for c in range(lanes):
        xp[c, 0:PAD] = jnp.zeros((PAD, TILE), F32)
        xp[c, PAD + seq : 2 * PAD + seq] = jnp.zeros((PAD, TILE), F32)
    for load in loads:
        load.wait()
    for start, at, n in spots:
        for c in range(lanes):
            pooled[at : at + n, c * TILE : (c + 1) * TILE] = (
                xp[c, pl.ds(start - 2, n, stride=3)]
                + xp[c, pl.ds(start - 1, n, stride=3)]
                + xp[c, pl.ds(start, n, stride=3)]
            ) / 3.0

    xhat, _ = norm_stats(pooled[...])
    normed = (xhat * vec[7:8] + vec[8:9]).astype(BF)
    for part in range(3):
        half, at = part // 2, part % 2 * D
        value = mm(normed, attn[half, :, at : at + D])
        value = (value * HD**-0.5 if part == 0 else value).astype(BF)
        for pair in range(PAIRS):
            mixed[part, pair] = value[:, pair * PW : (pair + 1) * PW]

    def forward_pair(pair, carry):
        for at, n, offset in ((0, n_long, 0), (n_long, TILE, 2 * n_long)):
            top, total, acc = state
            wide = pl.ds(0, 2 * n)
            part = (top.at[:, wide], total.at[:, wide], acc.at[:, wide])
            softmax_start(part)
            values_t = mixed[2, pair, at : at + n].T
            both = split_heads(mixed[0, pair, at : at + n])
            count = n // TILE
            softmax_step(
                mixed[1, pair, at : at + n], values_t, both, bias, pair, 0, True, count, count, part
            )
            ot[pair, :, at : at + n], lse[pair, :, offset : offset + 2 * n] = softmax_end(part)
        return carry

    lax.fori_loop(0, PAIRS, forward_pair, 0, unroll=2)
    middle = pooled[...] + mm(ot[...].reshape(D, ot.shape[2]).T, attn[1, :, D:])
    middle_s[...] = middle
    xhat, _ = norm_stats(middle)
    second = (xhat * vec[9:10] + vec[10:11]).astype(BF)
    short = middle + vec[11:12]
    load_feed.wait()
    for c in range(PARTS):
        cols = slice(c * WIDTH, (c + 1) * WIDTH)
        active, slope = gelu_pair(mm(second, feed[0, :, cols]) + beta_of(vec, 1, c, WIDTH))
        active_s[:, cols] = active.astype(BF)
        slope_s[:, cols] = slope.astype(BF)
        short = short + mm(active_s[:, cols], feed[1, :, cols], NT)
    for start, at, n in spots:
        for c in range(lanes):
            part = short[at : at + n, c * TILE : (c + 1) * TILE]
            for k in range(3):
                where = pl.ds(start + k, n, stride=3)
                xp[c, where] = xp[c, where] + part

    d_head[...] = jnp.zeros_like(d_head)
    row_grads[...] = jnp.zeros_like(row_grads)

    def loss_block(b, bits):
        start = pl.multiple_of(b * BLK + jnp.where(b * BLK >= seq, 2 * PAD, PAD), PAD)
        joined = jnp.concatenate([xp[c, pl.ds(start, BLK)] for c in range(lanes)], 1)
        xhat, rstd = norm_stats(joined)
        last = (xhat * vec[0:1] + vec[1:2]).astype(BF)
        logits = mm(last, head[1], NT) * D**-0.5
        info = aux[pl.ds(pl.multiple_of(b * BLK, BLK), BLK), :]
        weight = info[:, 2:3]
        hot = one_hot(info[:, 1:2])
        highest = jnp.max(logits, -1, keepdims=True)
        powers = jnp.exp(logits - highest)
        total = jnp.sum(powers, -1, keepdims=True)
        picked = jnp.sum(jnp.where(hot, logits, 0.0), -1, keepdims=True)
        lost = weight * (highest + jnp.log(total) - picked)
        d_logits = ((powers / total - hot.astype(F32)) * (weight * scalars[1:2, 0:1])).astype(BF)
        d_head[...] += mm(d_logits, last, TN) * D**-0.5
        d_last = mm(d_logits, head[1]) * D**-0.5
        dx, d_gain, d_shift = norm_back(d_last, xhat, rstd, vec[0:1])
        row_grads[0:1] += d_gain
        row_grads[1:2] += d_shift
        for c in range(lanes):
            xp[c, pl.ds(start, BLK)] = dx[:, c * TILE : (c + 1) * TILE]
        return bits + lost

    bits = lax.fori_loop(0, x1.shape[0] // BLK, loss_block, jnp.zeros((BLK, 1), F32), unroll=2)
    bits_out[...] = jnp.broadcast_to(jnp.sum(bits, 0, keepdims=True) / LOG_TWO, bits_out.shape)

    d_short = jnp.concatenate(
        [
            jnp.concatenate(
                [
                    xp[c, pl.ds(start, n, stride=3)]
                    + xp[c, pl.ds(start + 1, n, stride=3)]
                    + xp[c, pl.ds(start + 2, n, stride=3)]
                    for c in range(lanes)
                ],
                1,
            )
            for start, at, n in spots
        ],
        0,
    )
    d_branch = d_short.astype(BF)
    row_grads[6:7] = jnp.sum(d_branch.astype(F32), 0, keepdims=True)
    xhat, rstd = norm_stats(middle_s[...])
    second = (xhat * vec[9:10] + vec[10:11]).astype(BF)
    d_second = jnp.zeros(d_short.shape, F32)
    for c in range(PARTS):
        cols = slice(c * WIDTH, (c + 1) * WIDTH)
        d_feed[1, :, cols] = mm(d_branch, active_s[:, cols], TN).astype(BF)
        d_pre = (mm(d_branch, feed[1, :, cols]) * slope_s[:, cols].astype(F32)).astype(BF)
        put_beta(row_grads, 7, c, jnp.sum(d_pre.astype(F32), 0, keepdims=True), False)
        d_feed[0, :, cols] = mm(second, d_pre, TN).astype(BF)
        d_second = d_second + mm(d_pre, feed[0, :, cols], NT)
    store_feed.start()
    dx, d_gain, d_shift = norm_back(d_second, xhat, rstd, vec[9:10])
    row_grads[4:5] = d_gain
    row_grads[5:6] = d_shift
    d_middle = d_short + dx
    d_mix = d_middle.astype(BF)
    ot_all = ot[...].reshape(D, ot.shape[2])
    d_attn[1, :, D:] = mm(ot_all, d_mix).astype(BF)
    d_att = mm(d_mix, attn[1, :, D:], NT).astype(BF)
    for pair in range(PAIRS):
        mixed[3, pair] = d_att[:, pair * PW : (pair + 1) * PW]

    def backward_pair(pair, carry):
        for at, n, offset in ((0, n_long, 0), (n_long, TILE, 2 * n_long)):
            d_out = mixed[3, pair, at : at + n]
            product = (d_out.astype(F32).T) * ot[pair, :, at : at + n].astype(F32)
            inner = interleave(
                jnp.sum(product[:HD], 0, keepdims=True), jnp.sum(product[HD:], 0, keepdims=True)
            )
            queries = split_heads(mixed[0, pair, at : at + n])
            grads = split_heads(d_out)
            keys = mixed[1, pair, at : at + n]
            count = n // TILE
            dv, dk, dq = score_back(
                keys,
                mixed[2, pair, at : at + n],
                keys.T,
                queries,
                grads,
                lse[pair, :, offset : offset + 2 * n],
                inner,
                bias,
                pair,
                0,
                True,
                count,
                count,
                tiles,
            )
            d_mixed[0, pair, at : at + n] = (merge_heads(dq) * HD**-0.5).T.astype(BF)
            d_mixed[1, pair, at : at + n] = dk.astype(BF)
            d_mixed[2, pair, at : at + n] = dv.astype(BF)
        return carry

    lax.fori_loop(0, PAIRS, backward_pair, 0, unroll=2)
    rel = rel_row(tiles, sums, fold, tiles.shape[1])
    row_grads[11:12] = jnp.concatenate([jnp.zeros_like(rel), rel], 1)
    d_in = jnp.concatenate([d_mixed[part, pair] for part in range(3) for pair in range(PAIRS)], 1)
    xhat, rstd = norm_stats(pooled[...])
    normed = (xhat * vec[7:8] + vec[8:9]).astype(BF)
    d_attn[0] = mm(normed, d_in[:, : 2 * D], TN).astype(BF)
    d_attn[1, :, :D] = mm(normed, d_in[:, 2 * D :], TN).astype(BF)
    dx, d_gain, d_shift = norm_back(mm(d_in[:, : 2 * D], attn[0], NT) + mm(d_in[:, 2 * D :], attn[1, :, :D], NT), xhat, rstd, vec[7:8])
    row_grads[2:3] = d_gain
    row_grads[3:4] = d_shift
    d_pool = (d_middle + dx) / 3.0
    for start, at, n in spots:
        for c in range(lanes):
            part = d_pool[at : at + n, c * TILE : (c + 1) * TILE]
            for k in range(3):
                where = pl.ds(start - 2 + k, n, stride=3)
                xp[c, where] = xp[c, where] + part
    stores = plane_copies(dx_out, True)
    for store in stores:
        store.start()
    for store in stores:
        store.wait()
    store_feed.wait()


def middle_stage(x1, aux, tables, attn, feed, vec, scalars, seq):
    tokens = x1.shape[0]
    n_long = seq // 3
    short = n_long + TILE
    far = n_long // TILE
    fold = fold_matrix(far)
    vm = pl.BlockSpec(memory_space=pltpu.VMEM)
    anywhere = pl.BlockSpec(memory_space=pl.ANY)
    return pl.pallas_call(
        functools.partial(middle_kernel, seq),
        in_specs=[anywhere, vm, vm, vm, anywhere, vm, pl.BlockSpec(memory_space=pltpu.SMEM), vm, vm],
        out_specs=[anywhere, vm, anywhere, vm, vm, vm],
        out_shape=[
            jax.ShapeDtypeStruct((tokens, D), F32),
            jax.ShapeDtypeStruct((2, D, 2 * D), BF),
            jax.ShapeDtypeStruct((2, D, FF), BF),
            jax.ShapeDtypeStruct((V, D), F32),
            jax.ShapeDtypeStruct((16, D), F32),
            jax.ShapeDtypeStruct((8, 128), F32),
        ],
        scratch_shapes=[
            pltpu.VMEM((HEADS, fold_rows(far), TILE), F32),
            pltpu.VMEM((D // TILE, tokens + 2 * PAD, TILE), F32),
            pltpu.VMEM((short, D), F32),
            pltpu.VMEM((4, PAIRS, short, PW), BF),
            pltpu.VMEM((PAIRS, PW, short), BF),
            pltpu.VMEM((PAIRS, 1, 2 * short), F32),
            pltpu.VMEM((short, FF), BF),
            pltpu.VMEM((short, FF), BF),
            pltpu.VMEM((short, D), F32),
            pltpu.VMEM((HEADS, far, TILE, TILE), F32),
            pltpu.VMEM((HEADS, far, TILE, TILE), F32),
            pltpu.VMEM((3, PAIRS, short, PW), BF),
            pltpu.VMEM((2, D, FF), BF),
            pltpu.VMEM((2, D, FF), BF),
            pltpu.SemaphoreType.DMA((2 * (D // TILE) + 2,)),
        ]
        + state_scratch(n_long),
        compiler_params=params(VMEM_MIB),
        name="middle_stage",
    )(x1, aux, tables, attn, feed, vec, vec, scalars, fold)


def feed_back_kernel(
    wide,
    narrow,
    dx,
    act,
    slope,
    middle,
    wts,
    vec,
    ready,
    dm_out,
    d_feed,
    row_grads,
    sums_out,
    up,
    down,
    *scratch,
):
    step = pl.program_id(0)
    at = Place(wide, narrow)
    streams = []
    for source, target in zip(column_parts(ready, 2), column_parts(sums_out, 2)):
        part = scratch[SCATTER_REFS * len(streams) : SCATTER_REFS * (len(streams) + 1)]
        streams.append(ScatterStream(at, source, halves_out(target), *part[:5], part[5:]))
    one, two = streams
    events = {
        (0, "dense"): (one.stage_first,),
        (0, "end"): (two.stage_first,),
        (1, "dense"): (one.stage_second,),
        (1, "end"): (two.stage_second,),
        (2, "dense"): (one.stage_home,),
        (2, "end"): (two.stage_home,),
    }

    @pl.when(step == 0)
    def _():
        greet(*scatter_greetings(at))
        one.start()
        two.start()
        up[...] = jnp.zeros_like(up)
        down[...] = jnp.zeros_like(down)
        row_grads[...] = jnp.zeros_like(row_grads)

    d_result = dx[...]
    d_branch = d_result.astype(BF)
    row_grads[2:3] += jnp.sum(d_branch.astype(F32), 0, keepdims=True)
    xhat, rstd = norm_stats(middle[...])
    second = (xhat * vec[4:5] + vec[5:6]).astype(BF)
    run_events(events, step, "dense")
    d_second = jnp.zeros(d_result.shape, F32)
    for c in range(PARTS):
        cols = slice(c * WIDTH, (c + 1) * WIDTH)
        down[:, cols] += mm(d_branch, act[:, cols], TN)
        d_pre = (mm(d_branch, wts[1, :, cols]) * slope[:, cols].astype(F32)).astype(BF)
        put_beta(row_grads, 3, c, jnp.sum(d_pre.astype(F32), 0, keepdims=True), True)
        up[:, cols] += mm(second, d_pre, TN)
        d_second = d_second + mm(d_pre, wts[0, :, cols], NT)
    dn, d_gain, d_shift = norm_back(d_second, xhat, rstd, vec[4:5])
    row_grads[0:1] += d_gain
    row_grads[1:2] += d_shift
    dm_out[...] = d_result + dn
    run_events(events, step, "end")

    @pl.when(step == pl.num_programs(0) - 1)
    def _():
        d_feed[0] = up[...].astype(BF)
        d_feed[1] = down[...].astype(BF)
        one.finish()
        two.finish()


def halves_out(ref):
    return [ref.at[0], ref.at[1]]


def feed_back(dx, act, slope, middle, wts, vec, ready, wide, narrow):
    tokens = dx.shape[0]
    form = ready.shape[3:]

    def flat(width):
        return pl.BlockSpec((BLK, width), lambda i: (i, 0))

    return pl.pallas_call(
        functools.partial(feed_back_kernel, wide, narrow),
        grid=(tokens // BLK,),
        in_specs=[flat(D), flat(FF), flat(FF), flat(D), whole_spec(wts.shape), whole_spec(vec.shape)]
        + [pl.BlockSpec(memory_space=pl.ANY)],
        out_specs=[
            flat(D),
            whole_spec((2, D, FF)),
            whole_spec((8, D)),
            whole_spec((2,) + form),
        ],
        out_shape=[
            jax.ShapeDtypeStruct((tokens, D), F32),
            jax.ShapeDtypeStruct((2, D, FF), BF),
            jax.ShapeDtypeStruct((8, D), F32),
            jax.ShapeDtypeStruct((2,) + form, F32),
        ],
        scratch_shapes=[pltpu.VMEM((D, FF), F32), pltpu.VMEM((D, FF), F32)]
        + scatter_scratch(wide, narrow, half_width(ready)) * 2,
        compiler_params=params(VMEM_MIB, collective_id=5, has_side_effects=True),
        name="feed_back",
    )(dx, act, slope, middle, wts, vec, ready)


def attention_back_kernel(
    long_blocks,
    wide,
    narrow,
    dm,
    aux,
    ot,
    lse,
    q_all,
    k_all,
    v_all,
    embed,
    wts,
    vec,
    rel,
    fold,
    ready_a,
    ready_b,
    d_attn,
    d_embed,
    row_grads,
    out_a,
    out_b,
    sums,
    bias,
    tiles,
    kt_all,
    dk_all,
    dv_all,
    dq_t,
    d_att,
    inner,
    weights,
    d_mixed,
    *scratch,
):
    step = pl.program_id(0)
    blocks = pl.num_programs(0)
    i = blocks - 1 - step
    at = Place(wide, narrow)
    streams = []
    for ready, out in ((ready_a, out_a), (ready_b, out_b)):
        for source, target in zip(column_parts(ready, 2), column_parts(out, 2)):
            part = scratch[SCATTER_REFS * len(streams) : SCATTER_REFS * (len(streams) + 1)]
            streams.append(ScatterStream(at, source, halves_out(target), *part[:5], part[5:]))
    one, two, three, four = streams
    events = {
        (0, 0): (one.stage_first,),
        (0, 1): (two.stage_first,),
        (0, "end"): (three.stage_first,),
        (1, "dense"): (four.stage_first,),
        (1, 0): (one.stage_second,),
        (1, 1): (two.stage_second,),
        (1, "end"): (one.stage_home,),
        (2, 0): (three.stage_second, two.stage_home),
        (2, 1): (four.stage_second,),
        (2, "end"): (three.stage_home,),
        (3, 1): (four.stage_home,),
    }

    @pl.when(step == 0)
    def _():
        greet(*scatter_greetings(at))
        for stream in streams:
            stream.start()
        build_bias(rel, 0, bias, bias.shape[1])
        tiles[...] = jnp.zeros_like(tiles)
        dk_all[...] = jnp.zeros_like(dk_all)
        dv_all[...] = jnp.zeros_like(dv_all)
        weights[...] = jnp.zeros_like(weights)
        d_embed[...] = jnp.zeros_like(d_embed)
        row_grads[...] = jnp.zeros_like(row_grads)

        def turn(n, carry):
            for pair in range(PAIRS):
                kt_all[n, pair] = k_all[n, pair].T
            return carry

        lax.fori_loop(0, blocks, turn, 0)

    d_middle = dm[...]
    d_mix = d_middle.astype(BF)
    weights[1, :, D:] += mm(ot[0].reshape(D, BLK), d_mix)
    out = mm(d_mix, wts[1, :, D : 2 * D], NT).astype(BF)
    for pair in range(PAIRS):
        d_att[pair] = out[:, pair * PW : (pair + 1) * PW]
    product = mm(wts[1, :, D : 2 * D], d_mix, NT).astype(BF).astype(F32) * ot[0].reshape(
        D, BLK
    ).astype(F32)
    for pair in range(PAIRS):
        top = pair * PW
        inner[pair] = interleave(
            jnp.sum(product[top : top + HD], 0, keepdims=True),
            jnp.sum(product[top + HD : top + PW], 0, keepdims=True),
        )
    run_events(events, step, "dense")
    first = jnp.where(i >= long_blocks, long_blocks, 0)

    def two_pairs(turn, carry):
        pairs = [turn * TOGETHER + k for k in range(TOGETHER)]
        queries = [split_heads(q_all[i, pair]) for pair in pairs]
        grads = [split_heads(d_att[pair]) for pair in pairs]
        dq_t[...] = jnp.zeros_like(dq_t)

        def with_block(j, far, diag):
            for k, pair in enumerate(pairs):
                dv, dk, dq = score_back(
                    k_all[j, pair],
                    v_all[j, pair],
                    kt_all[j, pair],
                    queries[k],
                    grads[k],
                    lse[0, pair],
                    inner[pair],
                    bias,
                    pair,
                    far,
                    diag,
                    SUB,
                    SUB,
                    tiles,
                )
                dv_all[j, pair] += dv
                dk_all[j, pair] += dk
                dq_t[k] += dq

        def earlier(j, inside):
            with_block(j, SUB * (i - j), False)
            return inside

        lax.fori_loop(first, i, earlier, 0)
        with_block(i, 0, True)
        for k, pair in enumerate(pairs):
            d_mixed[0, pair] = (merge_heads(dq_t[k]) * HD**-0.5).T.astype(BF)
            d_mixed[1, pair] = dk_all[i, pair].astype(BF)
            d_mixed[2, pair] = dv_all[i, pair].astype(BF)
        run_events(events, step, turn)
        return carry

    lax.fori_loop(0, PAIRS // TOGETHER, two_pairs, 0)
    d_in = jnp.concatenate([d_mixed[part, pair] for part in range(3) for pair in range(PAIRS)], 1)
    hot = one_hot(aux[:, 0:1]).astype(BF)
    xhat, rstd = norm_stats(mm(hot, embed[0]))
    normed = (xhat * vec[2:3] + vec[3:4]).astype(BF)
    weights[0] += mm(normed, d_in[:, : 2 * D], TN)
    weights[1, :, :D] += mm(normed, d_in[:, 2 * D :], TN)
    dx, d_gain, d_shift = norm_back(mm(d_in[:, : 2 * D], wts[0, :, : 2 * D], NT) + mm(d_in[:, 2 * D :], wts[1, :, :D], NT), xhat, rstd, vec[2:3])
    row_grads[0:1] += d_gain
    row_grads[1:2] += d_shift
    d_embed[...] += mm(hot, (d_middle + dx).astype(BF), TN)

    run_events(events, step, "end")

    @pl.when(step == blocks - 1)
    def _():
        d_attn[...] = weights[...].astype(BF)
        rel = rel_row(tiles, sums, fold, tiles.shape[1])
        row_grads[2:3] = jnp.concatenate([rel, jnp.zeros_like(rel)], 1)
        for stream in streams:
            stream.finish()


def half_width(x):
    return x.shape[3:-1] + (x.shape[-1] // 2,)


def attention_back(
    dm, aux, ot, lse, q, k, v, tables, wts, vec, ready_a, ready_b, long_blocks, wide, narrow
):
    tokens = dm.shape[0]
    blocks = tokens // BLK
    far = SUB * long_blocks
    fold = fold_matrix(far)

    def turned(shape):
        return pl.BlockSpec(shape, lambda s: (blocks - 1 - s,) + (0,) * (len(shape) - 1))

    return pl.pallas_call(
        functools.partial(attention_back_kernel, long_blocks, wide, narrow),
        grid=(blocks,),
        in_specs=[
            turned((BLK, D)),
            turned((BLK, aux.shape[1])),
            turned((1, PAIRS, PW, BLK)),
            turned((1, PAIRS, 1, 2 * BLK)),
            whole_spec(q.shape),
            whole_spec(k.shape),
            whole_spec(v.shape),
            whole_spec((1, V, D)),
            whole_spec((2, D, 2 * D)),
            whole_spec(vec.shape),
            pl.BlockSpec(memory_space=pltpu.SMEM),
            whole_spec(fold.shape),
            pl.BlockSpec(memory_space=pl.ANY),
            pl.BlockSpec(memory_space=pl.ANY),
        ],
        out_specs=[
            whole_spec((2, D, 2 * D)),
            whole_spec((V, D)),
            whole_spec((8, D)),
            whole_spec((2,) + ready_a.shape[3:]),
            whole_spec((2,) + ready_b.shape[3:]),
        ],
        out_shape=[
            jax.ShapeDtypeStruct((2, D, 2 * D), BF),
            jax.ShapeDtypeStruct((V, D), F32),
            jax.ShapeDtypeStruct((8, D), F32),
            jax.ShapeDtypeStruct((2,) + ready_a.shape[3:], F32),
            jax.ShapeDtypeStruct((2,) + ready_b.shape[3:], F32),
        ],
        scratch_shapes=[
            pltpu.VMEM((HEADS, fold_rows(far), TILE), F32),
            pltpu.VMEM((HEADS, far, TILE, TILE), F32),
            pltpu.VMEM((HEADS, far, TILE, TILE), F32),
            pltpu.VMEM((blocks, PAIRS, PW, BLK), BF),
            pltpu.VMEM((blocks, PAIRS, BLK, PW), F32),
            pltpu.VMEM((blocks, PAIRS, BLK, PW), F32),
            pltpu.VMEM((TOGETHER, PW, 2 * BLK), F32),
            pltpu.VMEM((PAIRS, BLK, PW), BF),
            pltpu.VMEM((PAIRS, 1, 2 * BLK), F32),
            pltpu.VMEM((2, D, 2 * D), F32),
            pltpu.VMEM((3, PAIRS, BLK, PW), BF),
        ]
        + scatter_scratch(wide, narrow, half_width(ready_a)) * 2
        + scatter_scratch(wide, narrow, half_width(ready_b)) * 2,
        compiler_params=params(VMEM_MIB, collective_id=6, has_side_effects=True),
        name="attention_back",
    )(dm, aux, ot, lse, q, k, v, tables, wts, vec, vec, fold, ready_a, ready_b)


MESH = pl.DeviceIdType.MESH
MISC_ROWS = 32
SIDE = 128
MISC_COLS = D + SIDE
COUNT_ROW = 24


class Place:
    def __init__(self, wide, narrow):
        self.W, self.N = wide, narrow
        self.c = lax.axis_index("rep")
        self.w = lax.axis_index("wide")
        self.n = lax.axis_index("narrow")
        self.a0, self.b0 = self.digits(self.c)
        self.group = self.w // (wide // 2)

    def digits(self, c):
        hi, lo = self.n // 2, self.n % 2
        return (1 - c) * hi + c * lo, (1 - c) * lo + c * hi

    def narrow_of(self, a, b, c=None):
        c = self.c if c is None else c
        return a * (2 - c) + b * (1 + c)

    def chip(self, w, a, b):
        return {"wide": w, "narrow": self.narrow_of(a, b)}

    def sibling(self):
        return {"rep": 1 - self.c}


def greet(devices, more=()):
    barrier = pltpu.get_barrier_semaphore()
    count = len(devices)
    for device in devices:
        pl.semaphore_signal(barrier, inc=1, device_id=device, device_id_type=MESH)
    for condition, device in more:

        @pl.when(condition)
        def _(device=device):
            pl.semaphore_signal(barrier, inc=1, device_id=device, device_id_type=MESH)

        count = count + condition.astype(jnp.int32)
    pl.semaphore_wait(barrier, count)


def slab_form(rows, cols):
    return (rows, cols) if rows % 16 == 0 else (16, rows * cols // 16)


def gather_greetings(at):
    out = [{"wide": lax.rem(at.w + k, at.W)} for k in range(1, at.W)]
    return out + [
        at.chip(at.w, at.a0, 1 - at.b0),
        at.chip(at.w, 1 - at.a0, at.b0),
        at.sibling(),
    ]


class GatherStream:
    def __init__(self, at, src, out, send_along, send, recv, recv_side, local):
        self.at, self.src, self.out = at, src, out
        self.send_along, self.send, self.recv, self.recv_side = send_along, send, recv, recv_side
        self.n0 = at.narrow_of(at.a0, at.b0)
        self.n1 = at.narrow_of(at.a0, 1 - at.b0)
        self.n2 = at.narrow_of(1 - at.a0, at.b0)
        self.n3 = at.narrow_of(1 - at.a0, 1 - at.b0)
        self.local = local

    @property
    def keep(self):
        at = self.at
        return pltpu.make_async_copy(self.src, self.out.at[at.c, at.w, self.n0], self.local)

    def copy(self, ref, w, n, sem, peer):
        return pltpu.make_async_remote_copy(
            src_ref=ref,
            dst_ref=self.out.at[self.at.c, w, n],
            send_sem=sem,
            recv_sem=self.recv.at[w, n],
            device_id=peer,
            device_id_type=MESH,
        )

    def arrived(self, w, n):
        self.copy(
            self.out.at[self.at.c, w, n], w, n, self.send.at[0], self.at.sibling()
        ).wait_recv()

    def other(self, k):
        return lax.rem(self.at.w + k, self.at.W)

    def along(self, k):
        at = self.at
        return self.copy(
            self.src, at.w, self.n0, self.send_along.at[k - 1], {"wide": self.other(k)}
        )

    def neighbours(self, w, mine):
        at = self.at
        ref = self.src if mine else self.out.at[at.c, w, self.n0]
        self.copy(ref, w, self.n0, self.send.at[0], at.chip(at.w, at.a0, 1 - at.b0)).start()
        self.copy(ref, w, self.n0, self.send.at[1], at.chip(at.w, 1 - at.a0, at.b0)).start()

    def side(self, n):
        at = self.at
        return pltpu.make_async_remote_copy(
            src_ref=self.out.at[at.c, :, n],
            dst_ref=self.out.at[at.c, :, n],
            send_sem=self.send.at[2 + n],
            recv_sem=self.recv_side.at[n],
            device_id=at.sibling(),
            device_id_type=MESH,
        )

    def start(self):
        self.start_along()
        self.neighbours(self.at.w, True)

    def start_along(self):
        self.keep.start()
        for k in self.order():
            self.along(k).start()

    def finish_along(self):
        self.keep.wait()
        for k in self.order():
            self.along(k).wait_send()
            self.arrived(self.other(k), self.n0)

    def start_across(self):
        at = self.at
        for k in range(at.W):
            self.neighbours(self.other(k), False)
        self.side(self.n0).start()

    def order(self):
        return sorted(range(1, self.at.W), key=lambda k: -min(k, self.at.W - k))

    def depth(self, d):
        at = self.at
        if d == 1:
            for k in self.order()[::-1]:
                w = self.other(k)
                self.arrived(w, self.n0)
                self.neighbours(w, False)
            self.keep.wait()
            self.side(self.n0).start()
        if d == 2:
            for k in [0] + self.order()[::-1]:
                w = self.other(k)
                self.arrived(w, self.n1)
                ref = self.out.at[at.c, w, self.n1]
                peer = at.chip(at.w, 1 - at.a0, at.b0)
                self.copy(ref, w, self.n1, self.send.at[1], peer).start()
            self.side(self.n1).start()
            for k in range(at.W):
                self.arrived(self.other(k), self.n2)
            self.side(self.n2).start()
        if d == 3:
            for k in range(at.W):
                self.arrived(self.other(k), self.n3)
            self.side(self.n3).start()

    def finish(self, along=True):
        at = self.at
        for k in self.order() if along else ():
            self.along(k).wait_send()
        column = self.out.at[at.c, :, self.n0]
        half = self.out.at[at.c, pl.ds(0, at.W // 2)]
        for sem, ref in ((self.send.at[0], column), (self.send.at[1], half)):
            pltpu.make_async_remote_copy(
                src_ref=ref,
                dst_ref=ref,
                send_sem=sem,
                recv_sem=self.recv.at[0, 0],
                device_id=at.sibling(),
                device_id_type=MESH,
            ).wait_send()
        for n in range(at.N):
            self.side(n).wait_send()
        for n in range(at.N):
            pltpu.make_async_remote_copy(
                src_ref=self.out.at[1 - at.c, :, n],
                dst_ref=self.out.at[1 - at.c, :, n],
                send_sem=self.send.at[2 + n],
                recv_sem=self.recv_side.at[n],
                device_id=at.sibling(),
                device_id_type=MESH,
            ).wait_recv()


GATHER_SEMS = 5


def gather_sems(wide, narrow):
    dma = pltpu.SemaphoreType.DMA
    return [dma((wide,)), dma((2 + narrow,)), dma((wide, narrow)), dma((narrow,)), dma]


class ScatterStream:
    def __init__(self, at, src, out, own, side, first, second, fin, sems):
        self.at, self.src, self.out = at, src, out
        self.own, self.side, self.first, self.second, self.fin = own, side, first, second, fin
        self.local, self.side_sem, self.first_sem, self.second_sem, self.home_sem, self.fin_sem = sems
        self.n0 = at.narrow_of(at.a0, at.b0)
        self.n1 = at.narrow_of(at.a0, 1 - at.b0)

    def remote(self, src, dst, sems, index, device):
        return pltpu.make_async_remote_copy(
            src_ref=src,
            dst_ref=dst,
            send_sem=sems.at[(0,) + index],
            recv_sem=sems.at[(1,) + index],
            device_id=device,
            device_id_type=MESH,
        )

    def side_copy(self, n):
        at = self.at
        return self.remote(
            self.src.at[1 - at.c, :, n], self.side.at[:, n], self.side_sem, (n,), at.sibling()
        )

    def own_copy(self):
        return pltpu.make_async_copy(self.src.at[self.at.c], self.own, self.local)

    def first_copy(self, b):
        at = self.at
        return self.remote(
            self.own.at[:, at.narrow_of(1 - at.a0, b)],
            self.first.at[b],
            self.first_sem,
            (b,),
            at.chip(at.w, 1 - at.a0, at.b0),
        )

    def second_copy(self):
        at = self.at
        return self.remote(
            self.own.at[:, self.n1],
            self.second,
            self.second_sem,
            (),
            at.chip(at.w, at.a0, 1 - at.b0),
        )

    def home_copy(self, w):
        at = self.at
        return pltpu.make_async_remote_copy(
            src_ref=self.own.at[w, self.n0],
            dst_ref=self.fin.at[at.w % (at.W // 2), at.c],
            send_sem=self.home_sem.at[w],
            recv_sem=self.fin_sem.at[at.w % (at.W // 2), at.c],
            device_id={"wide": w, "rep": at.group},
            device_id_type=MESH,
        )

    def elsewhere(self, w):
        return (w != self.at.w) | (self.at.c != self.at.group)

    def start(self):
        at = self.at
        self.own_copy().start()
        other = 1 - at.c
        a1, b1 = at.digits(other)
        for a, b in ((1 - a1, 1 - b1), (1 - a1, b1), (a1, 1 - b1), (a1, b1)):
            self.side_copy(at.narrow_of(a, b, other)).start()

    def stage_first(self):
        at = self.at
        self.own_copy().wait()
        for b in (1 - at.b0, at.b0):
            n = at.narrow_of(1 - at.a0, b)
            self.side_copy(n).wait_recv()

            def body(w, carry, n=n):
                self.own[w, n] = (self.own[w, n].astype(F32) + self.side[w, n].astype(F32)).astype(BF)
                return carry

            lax.fori_loop(0, at.W, body, 0)
            self.first_copy(b).start()

    def stage_second(self):
        at = self.at
        self.side_copy(self.n1).wait_recv()
        self.first_copy(1 - at.b0).wait_recv()

        def body(w, carry):
            value = self.own[w, self.n1].astype(F32) + self.side[w, self.n1].astype(F32)
            self.own[w, self.n1] = (value + self.first[1 - at.b0, w].astype(F32)).astype(BF)
            return carry

        lax.fori_loop(0, at.W, body, 0)
        self.second_copy().start()

    def stage_home(self):
        at = self.at
        n = self.n0
        self.side_copy(n).wait_recv()
        self.first_copy(at.b0).wait_recv()
        self.second_copy().wait_recv()

        def body(k, carry):
            w = lax.rem(at.w + at.W // 2 + k, at.W)
            value = self.own[w, n].astype(F32) + self.side[w, n].astype(F32)
            value = value + self.first[at.b0, w].astype(F32) + self.second[w].astype(F32)
            self.own[w, n] = value.astype(BF)

            @pl.when(self.elsewhere(w))
            def _():
                self.home_copy(w).start()

            @pl.when(jnp.logical_not(self.elsewhere(w)))
            def _():
                self.fin[at.w % (at.W // 2), at.c] = value.astype(BF)

            return carry

        lax.fori_loop(0, at.W, body, 0)

    def finish(self):
        at = self.at
        half = at.W // 2
        for h in range(2):
            total = None
            for k in range(half):

                @pl.when((at.c * half + k != at.w) | (at.c != h))
                def _(k=k, h=h):
                    pltpu.make_async_remote_copy(
                        src_ref=self.fin.at[k, h],
                        dst_ref=self.fin.at[k, h],
                        send_sem=self.home_sem.at[0],
                        recv_sem=self.fin_sem.at[k, h],
                        device_id=at.sibling(),
                        device_id_type=MESH,
                    ).wait_recv()

                value = self.fin[k, h].astype(F32)
                total = value if total is None else total + value
            self.out[h][...] = total
        for n in range(at.N):
            self.side_copy(n).wait_send()
        for b in range(2):
            self.first_copy(b).wait_send()
        self.second_copy().wait_send()

        def homes(w, carry):
            @pl.when(self.elsewhere(w))
            def _():
                self.home_copy(w).wait_send()

            return carry

        lax.fori_loop(0, at.W, homes, 0)


SCATTER_REFS = 11


def scatter_scratch(wide, narrow, form):
    sizes = ((wide, narrow), (wide, narrow), (2, wide), (wide,), (wide // 2, 2))
    dma = pltpu.SemaphoreType.DMA
    buffers = [pltpu.VMEM(size + form, BF) for size in sizes]
    return buffers + [dma, dma((2, narrow)), dma((2, 2)), dma((2,)), dma((wide,)), dma((wide // 2, 2))]


def scatter_greetings(at):
    out = [
        at.chip(at.w, at.a0, 1 - at.b0),
        at.chip(at.w, 1 - at.a0, at.b0),
        at.sibling(),
    ]
    more = []
    for k in range(at.W // 2):
        for h in range(2):
            w = at.c * (at.W // 2) + k
            more.append(((w != at.w) | (at.c != h), {"rep": h, "wide": w}))
    return out, more


def place_columns(slabs, cols):
    feature = lax.broadcasted_iota(jnp.int32, (D, slabs * SIDE), 0)
    column = lax.broadcasted_iota(jnp.int32, (D, slabs * SIDE), 1)
    lane = column % SIDE
    return jnp.where((feature == column // SIDE * cols + lane) & (lane < cols), 1.0, 0.0).astype(BF)


def view_half(ref, layer, half, width, natural):
    if natural:
        return ref.at[layer, :, pl.ds(pl.multiple_of(half * width, width), width)]
    return ref.at[layer, half]


def column_parts(ref, count):
    width = ref.shape[-1] // count
    lead = (slice(None),) * (len(ref.shape) - 1)
    return [ref.at[lead + (slice(k * width, (k + 1) * width),)] for k in range(count)]


def prepare_kernel(wide, narrow, natural, *refs):
    take = iter(refs)

    def some(n):
        return [next(take) for _ in range(n)]

    ids, live, tables, attention, feed, vectors = some(6)
    attn_low, feed_low, attn_out, misc_out, aux, scalars = some(6)
    full_tables, vec = some(2) if natural else (None, None)
    misc, misc_low, packed, moved, move_sems = some(5)
    streams = [some(GATHER_SEMS) for _ in range(2)]
    at = Place(wide, narrow)
    seq = ids.shape[1]
    table_rows, cols = tables.shape[1], vectors.shape[1]

    to_core, to_wide = at.w % 2, at.c * (wide // 2) + at.w // 2
    from_wide = 2 * (at.w % (wide // 2)) + at.c
    leaves = (to_core != at.c) | (to_wide != at.w)
    greet(gather_greetings(at), [(leaves, {"rep": at.group, "wide": from_wide})])
    packed[...] = ids[...] + V * live[...]
    move = pltpu.make_async_remote_copy(
        src_ref=packed,
        dst_ref=moved,
        send_sem=move_sems.at[0],
        recv_sem=move_sems.at[1],
        device_id={"rep": to_core, "wide": to_wide},
        device_id_type=MESH,
    )
    stay = pltpu.make_async_copy(packed, moved, move_sems.at[0])
    pl.when(leaves)(move.start)
    pl.when(jnp.logical_not(leaves))(stay.start)

    position = lax.broadcasted_iota(jnp.int32, live.shape, 1)
    tally = jnp.sum(jnp.where(position > 0, live[...], 0).astype(F32), 1, keepdims=True)
    tally = jnp.sum(tally, 0, keepdims=True)
    high = jnp.floor(tally / 64.0)
    lane = lax.broadcasted_iota(jnp.int32, (1, SIDE), 1)
    misc[...] = jnp.zeros_like(misc)
    misc[0:table_rows, 0:D] = tables[at.c]
    misc[0:VEC, D : D + cols] = vectors[...]
    misc[COUNT_ROW : COUNT_ROW + 1, D:] = jnp.where(
        lane == 0, high, jnp.where(lane == 1, tally - 64.0 * high, 0.0)
    )
    misc_low[...] = misc[...].astype(BF)
    attn_low[...] = attention[...].astype(BF)
    small = GatherStream(at, misc_low, misc_out, *streams[0])
    attn = GatherStream(
        at, view_half(attn_low, 0, at.c, 2 * D, natural), attn_out, *streams[1]
    )
    small.start()
    attn.start()
    feed_low[...] = feed[...].astype(BF)

    pl.when(leaves)(move.wait)
    pl.when(jnp.logical_not(leaves))(stay.wait)
    live_at = lax.broadcasted_iota(jnp.int32, (8, seq), 1)
    row_at = lax.broadcasted_iota(jnp.int32, (8, seq), 0)
    start = 0
    for r, length in ((0, seq), (1, BLK)):
        row = moved[r : r + 1]
        after = jnp.concatenate([row[:, 1:], row[:, :1]], 1)
        weight = jnp.where(live_at[0:1] < seq - 1, after // V, 0)
        info = jnp.where(
            row_at == 0, row % V, jnp.where(row_at == 1, after % V, jnp.where(row_at == 2, weight, 0))
        )
        aux[start : start + length] = info[:, :length].astype(F32).T
        start += length
    for stream, d in (
        (small, 1),
        (attn, 1),
        (small, 2),
        (attn, 2),
        (small, 3),
    ):
        stream.depth(d)
    small.finish()
    sides = [
        sum(
            misc_out[h, w, n, :, D:].astype(F32) for w in range(wide) for n in range(narrow)
        )
        for h in range(2)
    ]
    counts = [
        side[COUNT_ROW : COUNT_ROW + 1, 0:1] * 64.0 + side[COUNT_ROW : COUNT_ROW + 1, 1:2]
        for side in sides
    ]
    mine = jnp.where(at.group == 0, counts[0], counts[1])
    line = lax.broadcasted_iota(jnp.int32, (8, 128), 0)
    kept = jnp.where(at.c == 0, counts[0], counts[1])
    scalars[...] = jnp.where(line == 0, kept, jnp.where(line == 1, 1.0 / (mine * LOG_TWO), 0.0))
    if natural:
        for h in range(2):
            for w in range(wide):
                for n in range(narrow):
                    s = w * narrow + n
                    full_tables[h, s * table_rows : (s + 1) * table_rows] = misc_out[
                        h, w, n, :table_rows, :D
                    ]
        blocks = [misc_out[0, w, n, :, D:] for w in range(wide) for n in range(narrow)]
        spread = mm(jnp.concatenate(blocks, 1), place_columns(wide * narrow, cols), NT)
        vec[...] = spread[: vec.shape[0]]
    attn.depth(3)
    attn.finish()


def prepare(ids, live, tables, attention, feed, vectors, wide, narrow, natural):
    vm = pl.BlockSpec(memory_space=pltpu.VMEM)
    anywhere = pl.BlockSpec(memory_space=pl.ANY)
    seq = ids.shape[1]
    half_form = attention.shape[1:] if natural else attention.shape[2:]
    half_form = (half_form[0], 2 * D) if natural else half_form
    misc = (MISC_ROWS, MISC_COLS)
    outs = [
        (attention.shape, BF, vm),
        (feed.shape, BF, vm),
        ((2, wide, narrow) + half_form, BF, anywhere),
        ((2, wide, narrow) + misc, BF, vm),
        ((seq + BLK, 8), F32, vm),
        ((8, 128), F32, vm),
    ]
    if natural:
        outs += [((2, V, D), BF, vm), ((24, D), F32, vm)]
    return pl.pallas_call(
        functools.partial(prepare_kernel, wide, narrow, natural),
        in_specs=[vm] * 6,
        out_specs=[spec for _, _, spec in outs],
        out_shape=[jax.ShapeDtypeStruct(shape, kind) for shape, kind, _ in outs],
        scratch_shapes=[
            pltpu.VMEM(misc, F32),
            pltpu.VMEM(misc, BF),
            pltpu.VMEM(ids.shape, jnp.int32),
            pltpu.VMEM(ids.shape, jnp.int32),
            pltpu.SemaphoreType.DMA((2,)),
        ]
        + gather_sems(wide, narrow) * 2,
        compiler_params=params(VMEM_MIB, collective_id=1, has_side_effects=True),
        name="prepare",
    )(ids, live, tables, attention, feed, vectors)


def halves_of(ref, layer, width, natural):
    if natural:
        return [ref.at[layer, :, h * width : (h + 1) * width] for h in range(2)]
    return [ref.at[layer, h] for h in range(2)]


def adam_update(weight, moment, square, gradient, decay, rate):
    moment = BETA_ONE * moment + (1.0 - BETA_ONE) * gradient
    square = BETA_TWO * square + (1.0 - BETA_TWO) * gradient * gradient
    fixed_moment = moment / (1.0 - BETA_ONE**STEP)
    fixed_square = square / (1.0 - BETA_TWO**STEP)
    delta = -rate * (fixed_moment / (jnp.sqrt(fixed_square) + ADAM_EPS) + decay * weight)
    return (moment, square, delta)


DECAYS = (DECAY, DECAY, DECAY, 0.0)
RATES = (RATE_TABLE, RATE, RATE, RATE_TABLE)
SUMMED = ((1, 1), (2, 1), (2, 0))


def sum_stages(wide, narrow):
    return (narrow - 1) + (wide - 1 if wide <= 4 else wide.bit_length() - 1)


def sum_rounds(at):
    rounds = [[(k, {"narrow": lax.rem(at.n + 1 + k, at.N)}) for k in range(at.N - 1)]]
    slot = at.N - 1
    if at.W <= 4:
        rounds.append(
            [(slot + k, {"wide": lax.rem(at.w + 1 + k, at.W)}) for k in range(at.W - 1)]
        )
    else:
        unit = 1
        while unit < at.W:
            rounds.append([(slot, {"wide": at.w + unit * (1 - 2 * ((at.w // unit) % 2))})])
            slot += 1
            unit *= 2
    return [device for peers in rounds for _, device in peers], rounds


def ordered_sum(at, peers, total, arrived):
    if len(peers) == 1:
        return total + arrived[peers[0][0]]
    size = len(peers) + 1
    here = at.n if "narrow" in peers[0][1] else at.w
    out = None
    for index in range(size):
        value = jnp.where(here == index, total, 0.0)
        for k, (slot, _) in enumerate(peers):
            source = lax.rem(here + size - 1 - k, size)
            value = jnp.where(source == index, arrived[slot], value)
        out = value if out is None else out + value
    return out


def pack_misc(at, d_tables, row_sums, rows, packed, cols):
    short_rows, feed_rows, attn_rows = row_sums
    rows[0:2] = short_rows[0:2]
    rows[2:4] = attn_rows[0:2]
    rows[4:7] = feed_rows[0:3]
    rows[7:12] = short_rows[2:7]
    rows[BETA_ROW : BETA_ROW + CHUNKS] = feed_rows[3 : 3 + CHUNKS]
    rows[BETA_ROW + CHUNKS : REL_ROW] = short_rows[7 : 7 + CHUNKS]
    rows[REL_ROW : REL_ROW + 1] = attn_rows[2:3] + short_rows[11:12]
    rows[VEC:] = jnp.zeros((rows.shape[0] - VEC, D), F32)
    tall = jnp.concatenate([rows[...], jnp.zeros((MISC_ROWS - rows.shape[0], D), F32)], 0).astype(BF)
    spread = mm(tall, place_columns(at.W * at.N, cols)).astype(BF)
    count = V // (at.W * at.N)
    for w in range(at.W):
        for n in range(at.N):
            s = w * at.N + n
            for h in range(2):
                packed[h, w, n, :count, :D] = d_tables[h][s * count : (s + 1) * count].astype(BF)
                packed[h, w, n, count:, :D] = jnp.zeros((MISC_ROWS - count, D), BF)
            packed[0, w, n, :, D:] = spread[:, s * SIDE : (s + 1) * SIDE]
            packed[1, w, n, :, D:] = jnp.zeros((MISC_ROWS, SIDE), BF)


def reduce_kernel(wide, narrow, natural, *refs):
    at = Place(wide, narrow)
    take = iter(refs)

    def some(n):
        return [next(take) for _ in range(n)]

    if natural:
        d_tables, row_sums = some(2), some(3)
    else:
        d_misc = next(take)
    d_attn, ready, bits = next(take), some(3), next(take)
    hbm_states = some(12)
    grads, deltas, scalars = some(4), some(4), next(take)
    states, state_sems = some(12), next(take)
    misc_sum, bits_in, bits_sem = some(3)
    sums, arrived, sum_sems = some(3)
    mine, other, delta_sems = some(4), some(4), next(take)
    if natural:
        misc_rows, d_misc = some(2)
    greetings, rounds = sum_rounds(at)
    devices, more = scatter_greetings(at)
    greet(devices + greetings, more)

    tiny = pltpu.make_async_remote_copy(
        src_ref=bits,
        dst_ref=bits_in,
        send_sem=bits_sem.at[0],
        recv_sem=bits_sem.at[1],
        device_id=at.sibling(),
        device_id_type=MESH,
    )
    tiny.start()
    attn_views = halves_of(grads[1], 0, 2 * D, natural)
    attn_outs = list(zip(*(column_parts(view, 2) for view in attn_views)))
    streams = []
    for source, out in list(zip(column_parts(d_attn, 2), attn_outs)) + [(d_misc, halves_out(misc_sum))]:
        part = some(SCATTER_REFS)
        streams.append(ScatterStream(at, source, out, *part[:5], part[5:]))
    one, two, small = streams
    one.start()
    two.start()
    if natural:
        pack_misc(at, d_tables, row_sums, misc_rows, d_misc, grads[3].shape[1])
    small.start()
    loads = [
        pltpu.make_async_copy(src, dst, state_sems.at[i])
        for i, (src, dst) in enumerate(zip(hbm_states, states))
    ]
    for load in loads:
        load.start()
    one.stage_first()
    views = attn_views
    for (which, layer), source in zip(SUMMED, ready):
        targets = halves_of(grads[which], layer, 2 * D if which == 1 else FF, natural)
        views += targets
        for half in range(2):
            targets[half][...] = source[half]
    two.stage_first()
    small.stage_first()
    one.stage_second()
    two.stage_second()
    one.stage_home()
    small.stage_second()
    two.stage_home()
    small.stage_home()
    for stream in streams:
        stream.finish()
    tiny.wait()

    table_rows, columns = grads[0].shape[1], grads[3].shape[1]
    for layer in range(2):
        grads[0][layer] = misc_sum[layer, :table_rows, :D]
    grads[3][...] = misc_sum[0, :VEC, D : D + columns]
    squared = jnp.zeros((1, 1), F32)
    for ref in halves_out(misc_sum) + views:
        value = ref[...]
        value = jnp.sum(value * value, 0, keepdims=True)
        squared = squared + jnp.sum(value, 1, keepdims=True)
    row = lax.broadcasted_iota(jnp.int32, (8, 128), 0)
    lost = jnp.where(at.c == at.group, bits[...] + bits_in[...], 0.0)
    total = jnp.where(row == 0, squared, jnp.where(row == 1, lost, 0.0))
    for peers in rounds:
        copies = []
        for k, partner in peers:
            sums[k] = total
            copies.append(
                pltpu.make_async_remote_copy(
                    src_ref=sums.at[k],
                    dst_ref=arrived.at[k],
                    send_sem=sum_sems.at[0, k],
                    recv_sem=sum_sems.at[1, k],
                    device_id=partner,
                    device_id_type=MESH,
                )
            )
        for copy in copies:
            copy.start()
        for copy in copies:
            copy.wait()
        total = ordered_sum(at, peers, total, arrived)
    norm = jnp.sqrt(total[0:1, 0:1])
    factor = jnp.minimum(1.0, CLIP_AT / (norm + 1e-06))
    scalars[...] = jnp.where(row == 0, norm, jnp.where(row == 2, factor, total))
    for load in loads:
        load.wait()

    copies = [
        pltpu.make_async_remote_copy(
            src_ref=mine[which],
            dst_ref=other[which],
            send_sem=delta_sems.at[0, which],
            recv_sem=delta_sems.at[1, which],
            device_id=at.sibling(),
            device_id_type=MESH,
        )
        for which in range(4)
    ]
    order = (2, 1, 0, 3)
    for which in order:
        refs_of = [states[which], states[4 + which], states[8 + which], grads[which], mine[which]]
        if which in (1, 2):
            width = 2 * D if which == 1 else FF
            views = [[ref.at[l] for ref in refs_of] for l in range(2)]
            if natural:
                views = [
                    [ref.at[l, :, h * width : (h + 1) * width] for ref in refs_of]
                    for l in range(2)
                    for h in range(2)
                ]
        else:
            views = [refs_of]
        for weight, moment, square, gradient, target in views:
            _, _, delta = adam_update(
                weight[...],
                moment[...],
                square[...],
                gradient[...] * factor,
                DECAYS[which],
                RATES[which],
            )
            target[...] = delta.astype(target.dtype)
        copies[which].start()
    for which in order:
        copies[which].wait()
        deltas[which][...] = (mine[which][...].astype(F32) + other[which][...].astype(F32)) * 0.5


def reduce_all(small, d_attn, ready, bits, states, wide, narrow, natural, collective_id):
    vm = pl.BlockSpec(memory_space=pltpu.VMEM)
    anywhere = pl.BlockSpec(memory_space=pl.ANY)
    like = [jax.ShapeDtypeStruct(x.shape, F32) for x in states[:4]]
    kinds = [BF if x.shape[-2] % 16 == 0 else F32 for x in states[:4]]
    exchanged = [pltpu.VMEM(x.shape, kind) for x, kind in zip(states[:4], kinds)]
    dma = pltpu.SemaphoreType.DMA
    stages = sum_stages(wide, narrow)
    misc = (MISC_ROWS, MISC_COLS)
    scratch = [pltpu.VMEM(x.shape, F32) for x in states] + [dma((12,))]
    scratch += [pltpu.VMEM((2,) + misc, F32), pltpu.VMEM(bits.shape, F32), dma((2,))]
    scratch += [pltpu.VMEM((stages, 8, 128), F32)] * 2 + [dma((2, stages))]
    scratch += exchanged + exchanged + [dma((2, 4))]
    if natural:
        scratch += [pltpu.VMEM((24, D), F32), pltpu.VMEM((2, wide, narrow) + misc, BF)]
    for form in (half_width(d_attn), half_width(d_attn), misc):
        scratch += scatter_scratch(wide, narrow, form)
    return pl.pallas_call(
        functools.partial(reduce_kernel, wide, narrow, natural),
        in_specs=[vm if natural else anywhere] * len(small)
        + [anywhere]
        + [vm] * 4
        + [anywhere] * 12,
        out_specs=[vm] * 9,
        out_shape=like + like + [jax.ShapeDtypeStruct((8, 128), F32)],
        scratch_shapes=scratch,
        compiler_params=params(VMEM_MIB, collective_id=collective_id, has_side_effects=True),
        name="reduce_all",
    )(*small, d_attn, *ready, bits, *states)


def update_kernel(scalars, totals, counted, *refs):
    grads, deltas, weights, moments, squares, outers, averages = (
        refs[4 * k : 4 * k + 4] for k in range(7)
    )
    new_m, new_s, new_w, new_o, new_a = (refs[28 + 4 * k : 32 + 4 * k] for k in range(5))
    factor = scalars[2:3, 0:1]
    loss, count, norm = refs[48:]
    loss[0] = totals[1, 0]
    count[0] = counted[0, 0]
    norm[0] = totals[0, 0]
    for which in range(4):
        moment, square, _ = adam_update(
            weights[which][...],
            moments[which][...],
            squares[which][...],
            grads[which][...] * factor,
            DECAYS[which],
            RATES[which],
        )
        put_moment(new_m[which], moment)
        put_moment(new_s[which], square)
        delta = deltas[which][...]
        outer = OUTER_MOM * outers[which][...] + delta
        weight = weights[which][...] + OUTER_RATE * (delta + OUTER_MOM * outer)
        new_o[which][...] = outer
        new_w[which][...] = weight
        new_a[which][...] = EVAL_KEEP * averages[which][...] + (1.0 - EVAL_KEEP) * weight


def put_moment(ref, value):
    if len(ref.shape) == 3 and value.ndim == 2:
        for r in range(value.shape[0]):
            ref[r] = value[r : r + 1]
    else:
        ref[...] = value


def update(totals, counted, grads, deltas, arrays):
    weights = arrays[:4]
    rows = weights[1].shape[1]

    def quarter(width):
        return pl.BlockSpec((1, rows, width // 4), lambda i: (i // 4, 0, i % 4))

    specs = [
        pl.BlockSpec((1,) + weights[0].shape[1:], lambda i: (i // 4, 0, 0)),
        quarter(4 * D),
        quarter(2 * FF),
        pl.BlockSpec(weights[3].shape, lambda i: (0, 0)),
    ]
    like = [jax.ShapeDtypeStruct(x.shape, F32) for x in weights]
    vec_rows, cols = weights[3].shape
    lined = (vec_rows, 1, cols)
    own_specs = specs[:3] + [pl.BlockSpec(lined, lambda i: (0, 0, 0))]
    own_like = like[:3] + [jax.ShapeDtypeStruct(lined, F32)]
    scalar = pl.BlockSpec(memory_space=pltpu.SMEM)
    *new, loss, count, norm = pl.pallas_call(
        update_kernel,
        grid=(8,),
        in_specs=[pl.BlockSpec((8, 128), lambda i: (0, 0)), scalar, scalar] + specs * 7,
        out_specs=own_specs * 2 + specs * 3 + [scalar] * 3,
        out_shape=own_like * 2 + like * 3 + [jax.ShapeDtypeStruct((1,), F32)] * 3,
        compiler_params=params(VMEM_MIB),
        name="update",
    )(totals, totals, counted, *grads, *deltas, *arrays)
    for k in (3, 7):
        new[k] = new[k].transpose(1, 0, 2)
    new = [x[None] if k < 8 and k % 4 != 3 else x for k, x in enumerate(new)]
    return (loss, count, norm, *new)


def pad_to(x, rows, cols):
    return jnp.pad(x, [(0, 0)] * (x.ndim - 2) + [(0, rows - x.shape[-2]), (0, cols - x.shape[-1])])


def per_device(wide, narrow, byte_ids, live_mask, *arrays):
    tables, attention, feed_forward, vectors = arrays[:4]
    rows, table_rows, cols = attention.shape[1], tables.shape[1], vectors.shape[1]
    seq = byte_ids.shape[1]
    long_blocks = seq // BLK
    natural = rows % 16 == 0
    place = (2, wide, narrow)

    def formed(k, x):
        if natural or k % 4 not in (1, 2):
            return x
        half = x.shape[-1] // 2
        return x.reshape(2, rows, 2, half).swapaxes(1, 2).reshape((2, 2) + slab_form(rows, half))

    def unformed(k, x):
        if natural or k % 4 not in (1, 2):
            return x
        return x.reshape(2, 2, rows, -1).swapaxes(1, 2).reshape(arrays[k].shape)

    def slabs_of(d):
        return d.reshape(place + slab_form(rows, d.shape[-1]))

    arrays = [x[0] if 4 <= k < 12 else x for k, x in enumerate(arrays)]
    states = [formed(k, x) for k, x in enumerate(arrays[:12])]
    attn_low, feed_low, attn, misc, aux, scalars, *more = prepare(
        byte_ids, live_mask, tables, states[1], states[2], vectors, wide, narrow, natural
    )
    if natural:
        full_tables, vec = more
    else:
        full_tables = misc[:, :, :, :table_rows, :D].reshape(2, V, D)
        side = misc[0, :, :, :VEC, D : D + cols].astype(F32).reshape(-1, VEC, cols)
        vec = pad_to(side.transpose(1, 0, 2).reshape(VEC, D), 24, D)
    attn = attn.reshape(2, D, 2 * D)
    x1, middle, q, k, v, ot, lse, act, slope, feed, short_attn, short_feed = full_forward(
        aux, full_tables, attn, attn_low, feed_low, vec, long_blocks, wide, narrow, natural
    )
    feed = feed.reshape(2, D, FF)
    d_x1, d_short_attn, d_short_feed, d_head, short_rows, bits = middle_stage(
        x1,
        aux,
        full_tables,
        short_attn.reshape(2, D, 2 * D),
        short_feed.reshape(2, D, FF),
        vec,
        scalars,
        seq,
    )
    d_middle, d_feed, feed_rows, sum_short_attn = feed_back(
        d_x1, act, slope, middle, feed, vec, slabs_of(d_short_attn), wide, narrow
    )
    d_attn, d_embed, attn_rows, sum_short_feed, sum_feed = attention_back(
        d_middle,
        aux,
        ot,
        lse,
        q,
        k,
        v,
        full_tables,
        attn,
        vec,
        slabs_of(d_short_feed),
        slabs_of(d_feed),
        long_blocks,
        wide,
        narrow,
    )
    if natural:
        small = (d_embed, d_head, short_rows, feed_rows, attn_rows)
    else:
        d_vec = jnp.concatenate(
            [
                short_rows[0:2],
                attn_rows[0:2],
                feed_rows[0:3],
                short_rows[2:7],
                feed_rows[3 : 3 + CHUNKS],
                short_rows[7 : 7 + CHUNKS],
                attn_rows[2:3] + short_rows[11:12],
            ],
            0,
        )
        side = pad_to(d_vec.reshape(VEC, -1, cols).transpose(1, 0, 2), MISC_ROWS, SIDE)
        halves = [
            jnp.concatenate([pad_to(d.reshape(-1, table_rows, D), MISC_ROWS, D), extra], -1)
            for d, extra in ((d_embed, side), (d_head, jnp.zeros_like(side)))
        ]
        small = (jnp.stack(halves).astype(BF).reshape(place + (MISC_ROWS, MISC_COLS)),)
    *sums, totals = reduce_all(
        small,
        slabs_of(d_attn),
        (sum_short_attn, sum_short_feed, sum_feed),
        bits,
        states,
        wide,
        narrow,
        natural,
        2,
    )
    grads = [unformed(k, x) for k, x in enumerate(sums[:4])]
    deltas = [unformed(k, x) for k, x in enumerate(sums[4:])]
    return update(totals, scalars, grads, deltas, arrays)


def solution(mesh):
    rows = P(("rep", "wide", "narrow"), None)
    split = (
        P(None, ("wide", "narrow"), None),
        P(None, ("wide", "narrow"), None),
        P(None, ("wide", "narrow"), None),
        P(None, ("wide", "narrow")),
    )
    own = tuple(P("rep", *spec) for spec in split)
    return jax.shard_map(
        functools.partial(per_device, mesh.shape["wide"], mesh.shape["narrow"]),
        mesh=mesh,
        in_specs=(rows, rows) + split + own + own + split + split,
        out_specs=(P("rep"),) * 3 + own + own + split * 3,
        check_vma=False,
    )
```

```python
import functools
import math

import jax
import jax.numpy as jnp
import numpy as np
from jax import lax
from jax.experimental import pallas as pl
from jax.experimental.pallas import tpu as pltpu
from jax.sharding import PartitionSpec as P

D = 512
HEADS = 8
HD = 64
FF = 2048
V = 256
NB = 32
STEP = 10
VEC = 21
EDGES = (1, 2, 3, 4, 5, 6, 7, 8, 10, 12, 14, 16, 20, 24, 28, 32, 40, 48, 64, 80, 96, 128, 160, 192)
EDGES = EDGES + (256, 320, 384, 512, 640, 768, 1024)
NEG = -1000000000.0
EPS = 1e-05
LOG_TWO = math.log(2.0)
RATE = 0.01
RATE_TABLE = 0.2
BETA_ONE = 0.9
BETA_TWO = 0.95
ADAM_EPS = 1e-08
DECAY = 0.1
CLIP_AT = 0.02
OUTER_RATE = 0.7
OUTER_MOM = 0.9
EVAL_KEEP = 0.9

TILE = 128
TOGETHER = 2
BETA_ROW = 12
REL_ROW = 12 + 2 * FF // D
CHUNKS = FF // D
PARTS = 1
WIDTH = FF // PARTS
VMEM_MIB = 63
BLK = 384
SUB = BLK // TILE
PAIRS = HEADS // 2
PW = 2 * HD
GELU_C = math.sqrt(2.0 / math.pi)
GELU_A = 0.044715

BF = jnp.bfloat16
F32 = jnp.float32
NN = (((1,), (0,)), ((), ()))
NT = (((1,), (1,)), ((), ()))
TN = (((0,), (0,)), ((), ()))


def mm(left, right, dims=NN):
    return lax.dot_general(left, right, dims, preferred_element_type=F32)


def spans(count):
    out = []
    for d in range(count):
        lo, hi = max(TILE * d - (TILE - 1), 0), TILE * d + TILE - 1
        base = sum(e <= lo for e in EDGES)
        out.append((base, [(e, k + 1) for k, e in enumerate(EDGES) if lo < e <= hi]))
    return out


def fold_matrix(count):
    rows = []
    for base, edges in spans(count):
        row = np.zeros(NB, np.float32)
        row[base] += 1
        rows.append(row)
        for _, bucket in edges:
            row = np.zeros(NB, np.float32)
            row[bucket] += 1
            row[bucket - 1] -= 1
            rows.append(row)
    out = np.zeros((HEADS, fold_rows(count), HEADS * NB), jnp.bfloat16)
    for h in range(HEADS):
        out[h, : len(rows), h * NB : (h + 1) * NB] = np.stack(rows)
    return out


def tile_distance(d):
    keys = lax.broadcasted_iota(jnp.int32, (TILE, TILE), 0)
    queries = lax.broadcasted_iota(jnp.int32, (TILE, TILE), 1)
    return TILE * d + queries - keys


def build_bias(rel, level, bias, count):
    for d, (base, edges) in enumerate(spans(count)):
        distance = tile_distance(d)

        def one_head(h, carry, d=d, base=base, edges=edges, distance=distance):
            first = level * HEADS * NB + h * NB
            tile = jnp.full((TILE, TILE), rel[REL_ROW, first + base], F32)
            for edge, bucket in edges:
                tile = jnp.where(distance >= edge, rel[REL_ROW, first + bucket], tile)
            if d == 0:
                tile = jnp.where(distance < 0, NEG, tile)
            bias[h, d] = tile
            return carry

        lax.fori_loop(0, HEADS, one_head, 0)


def fold_bias(tiles, sums, count):
    at = 0
    for d, (_, edges) in enumerate(spans(count)):
        distance = tile_distance(d)

        def one_head(h, carry, d=d, edges=edges, distance=distance, at=at):
            tile = tiles[h, d]
            sums[h, at : at + 1] = jnp.sum(tile, 0, keepdims=True)
            for n, (edge, _) in enumerate(edges):
                sums[h, at + 1 + n : at + 2 + n] = jnp.sum(
                    jnp.where(distance >= edge, tile, 0.0), 0, keepdims=True
                )
            return carry

        lax.fori_loop(0, HEADS, one_head, 0)
        at += 1 + len(edges)


def fold_rows(count):
    return -(-sum(1 + len(edges) for _, edges in spans(count)) // 8) * 8


def rel_row(tiles, sums, fold, count):
    sums[...] = jnp.zeros_like(sums)
    fold_bias(tiles, sums, count)
    whole = sums[...].reshape(-1, TILE)
    high = whole.astype(BF)
    low = (whole - high.astype(F32)).astype(BF)
    matrix = fold[...].reshape(-1, HEADS * NB)
    total = mm(high, matrix, TN) + mm(low, matrix, TN)
    return jnp.sum(total, 0, keepdims=True)


def norm_stats(x):
    centered = x - jnp.mean(x, -1, keepdims=True)
    rstd = lax.rsqrt(jnp.mean(centered * centered, -1, keepdims=True) + EPS)
    return centered * rstd, rstd


def norm_back(dy, xhat, rstd, gain):
    t = dy * gain
    dx = rstd * (
        t - jnp.mean(t, -1, keepdims=True) - xhat * jnp.mean(t * xhat, -1, keepdims=True)
    )
    return dx, jnp.sum(dy * xhat, 0, keepdims=True), jnp.sum(dy, 0, keepdims=True)


def gelu_pair(u):
    square = u * u
    tanh = jnp.tanh(GELU_C * u * (1.0 + GELU_A * square))
    half = 0.5 * (1.0 + tanh)
    slope = half + 0.5 * u * (1.0 - tanh * tanh) * (GELU_C + 3.0 * GELU_C * GELU_A * square)
    return u * half, slope


def split_heads(pair):
    lane = lax.broadcasted_iota(jnp.int32, (TILE, pair.shape[1]), 1)
    parts = []
    for qa in range(pair.shape[0] // TILE):
        rows = pair[qa * TILE : (qa + 1) * TILE]
        zero = jnp.zeros_like(rows)
        parts += [jnp.where(lane < HD, rows, zero), jnp.where(lane >= HD, rows, zero)]
    return jnp.concatenate(parts, 0)


def interleave(low, high):
    parts = []
    for at in range(0, low.shape[1], TILE):
        parts += [low[:, at : at + TILE], high[:, at : at + TILE]]
    return jnp.concatenate(parts, 1)


def merge_heads(both):
    parts = []
    for at in range(0, both.shape[1], 2 * TILE):
        parts.append(
            jnp.concatenate([both[:HD, at : at + TILE], both[HD:, at + TILE : at + 2 * TILE]], 0)
        )
    return jnp.concatenate(parts, 1)


def tile_products(keys, queries, diag, nq, nk):
    out = {}
    rows = [queries] if not diag else [queries[2 * TILE * kb :] for kb in range(nk)]
    if not diag:
        full = mm(keys, queries, NT)
    for kb in range(nk):
        line = slice(kb * TILE, (kb + 1) * TILE)
        first = kb if diag else 0
        block = mm(keys[line], rows[kb], NT) if diag else full[line]
        for qa in range(first, nq):
            for e in range(2):
                at = (2 * (qa - first) + e) * TILE
                out[kb, e, qa] = block[:, at : at + TILE]
    return out


def by_queries(left, tiles, diag, nq, nk):
    if not diag:
        return mm(left, whole_tiles(tiles, range(nk), range(nq)))
    return jnp.concatenate(
        [
            mm(left[:, : (qa + 1) * TILE], whole_tiles(tiles, range(qa + 1), (qa,)))
            for qa in range(nq)
        ],
        1,
    )


def by_keys(tiles, right, diag, nq, nk):
    if not diag:
        return mm(whole_tiles(tiles, range(nk), range(nq)), right)
    return jnp.concatenate(
        [
            mm(whole_tiles(tiles, (kb,), range(kb, nq)), right[2 * TILE * kb :])
            for kb in range(nk)
        ],
        0,
    )


def whole_tiles(tiles, key_tiles, query_tiles):
    return jnp.concatenate(
        [
            jnp.concatenate([tiles[kb, e, qa] for kb in key_tiles], 0)
            for qa in query_tiles
            for e in range(2)
        ],
        1,
    )


def column_of(qa, e):
    at = (2 * qa + e) * TILE
    return slice(at, at + TILE)


def softmax_step(keys, values_t, queries, bias, pair, far, diag, nq, nk, state):
    top, total, acc = state
    raw = tile_products(keys, queries, diag, nq, nk)
    scores = {
        (kb, e, qa): tile + bias[2 * pair + e, far + qa - kb] for (kb, e, qa), tile in raw.items()
    }
    order = [(qa, e) for qa in range(nq) for e in range(2)]
    highest = []
    for qa, e in order:
        column = [scores[kb, e, qa] for kb in range(nk) if (kb, e, qa) in scores]
        highest.append(jnp.max(functools.reduce(jnp.maximum, column), 0, keepdims=True))
    old_top = top[...]
    new_top = jnp.maximum(old_top, jnp.concatenate(highest, 1))
    alpha = jnp.exp(old_top - new_top)
    sums, probs = [], {}
    for qa, e in order:
        ceiling = new_top[:, column_of(qa, e)]
        adds = None
        for kb in range(nk):
            if (kb, e, qa) in scores:
                p = jnp.exp(scores[kb, e, qa] - ceiling)
                adds = p if adds is None else adds + p
                probs[kb, e, qa] = p.astype(BF)
        sums.append(jnp.sum(adds, 0, keepdims=True))
    top[...] = new_top
    total[...] = alpha * total[...] + jnp.concatenate(sums, 1)
    acc[...] = alpha * acc[...] + by_queries(values_t, probs, diag, nq, nk)


def softmax_start(state):
    top, total, acc = state
    top[...] = jnp.full(top.shape, NEG, F32)
    total[...] = jnp.zeros(total.shape, F32)
    acc[...] = jnp.zeros(acc.shape, F32)


def softmax_end(state):
    top, total, acc = state
    return merge_heads(acc[...] / total[...]).astype(BF), top[...] + jnp.log(total[...])


def score_back(
    keys, values, keys_t, queries, grads, logsum, inner, bias, pair, far, diag, nq, nk, tiles
):
    raw = tile_products(keys, queries, diag, nq, nk)
    d_p = tile_products(values, grads, diag, nq, nk)
    probs, scores = {}, {}
    for e in range(2):
        for diff in range(0 if diag else -(nk - 1), nq):
            total = None
            for kb in range(nk):
                qa = kb + diff
                if qa < 0 or qa >= nq:
                    continue
                cols = column_of(qa, e)
                p = jnp.exp(raw[kb, e, qa] + bias[2 * pair + e, far + diff] - logsum[:, cols])
                ds = p * (d_p[kb, e, qa] - inner[:, cols])
                total = ds if total is None else total + ds
                probs[kb, e, qa] = p.astype(BF)
                scores[kb, e, qa] = ds.astype(BF)
            tiles[2 * pair + e, far + diff] += total
    return (
        by_keys(probs, grads, diag, nq, nk),
        by_keys(scores, queries, diag, nq, nk),
        by_queries(keys_t, scores, diag, nq, nk),
    )


def beta_of(vec, level, part, width):
    row = BETA_ROW + level * CHUNKS + part * width // D
    return jnp.concatenate([vec[r : r + 1] for r in range(row, row + width // D)], 1)


def put_beta(rows, start, part, value, add):
    for k in range(WIDTH // D):
        row = start + part * WIDTH // D + k
        piece = value[:, k * D : (k + 1) * D]
        rows[row : row + 1] = rows[row : row + 1] + piece if add else piece


def one_hot(column):
    return column == lax.broadcasted_iota(jnp.int32, (column.shape[0], V), 1)


def full_forward_kernel(
    long_blocks,
    wide,
    narrow,
    natural,
    aux,
    embed,
    wts,
    attn_low,
    feed_low,
    vec,
    rel,
    x1_out,
    middle_out,
    q_out,
    k_out,
    v_out,
    ot_out,
    lse_out,
    act_out,
    slope_out,
    feed_out,
    short_attn_out,
    short_feed_out,
    bias,
    k_all,
    vt_all,
    middles,
    seconds,
    feed,
    feed_sem,
    *more,
):
    step = pl.program_id(0)
    blocks = pl.num_programs(0) // 3
    states = [more[3 * k : 3 * k + 3] for k in range(TOGETHER)]
    sems = more[3 * TOGETHER :]
    at = Place(wide, narrow)
    sources, targets = [], []
    for low, layer, width, out, count in (
        (feed_low, 0, FF, feed_out, 2),
        (attn_low, 1, 2 * D, short_attn_out, 1),
        (feed_low, 1, FF, short_feed_out, 2),
    ):
        sources += column_parts(view_half(low, layer, at.c, width, natural), count)
        targets += column_parts(out, count)
    feed_a, feed_b, short_attn, short_a, short_b = (
        HostedStream(
            at, source, out, *sems[GATHER_SEMS * k : GATHER_SEMS * (k + 1)]
        )
        for k, (source, out) in enumerate(zip(sources, targets))
    )
    loads = [
        pltpu.make_async_copy(source, target, feed_sem.at[k])
        for k, (source, target) in enumerate(zip(column_parts(feed_out, 2), column_parts(feed, 2)))
    ]

    def hop(stream, d):
        return lambda: stream.depth(d)

    events = {
        (1, 0): (hop(feed_a, 1),),
        (2, "dense"): (hop(feed_b, 1), hop(feed_a, 2)),
        (2, 0): (hop(short_attn, 1),),
        (2, 1): (hop(feed_a, 3), hop(feed_b, 2)),
        (3, "dense"): (hop(short_a, 1),),
        (3, 1): (hop(short_attn, 2),),
        (4, "end"): (hop(short_b, 1), hop(feed_b, 3)),
        (5, "end"): (hop(short_a, 2),),
        (6, "end"): (hop(short_attn, 3),),
        (8, "end"): (hop(short_b, 2),),
        (9, "end"): (hop(short_a, 3),),
        (10, "end"): (hop(short_b, 3),),
    }


    @pl.when(step == 0)
    def _():
        greet(gather_greetings(at))()
        for stream in (feed_a, feed_b, short_attn, short_a, short_b):
            stream.start()
        build_bias(rel, 0, bias, bias.shape[1])

    @pl.when(step < blocks)
    def _():
        hot = one_hot(aux[:, 0:1]).astype(BF)
        x = mm(hot, embed[0])
        xhat, _ = norm_stats(x)
        normed = (xhat * vec[2:3] + vec[3:4]).astype(BF)
        queries = (mm(normed, wts[0, :, :D]) * HD**-0.5).astype(BF)
        keys = mm(normed, wts[0, :, D : 2 * D]).astype(BF)
        values = mm(normed, wts[1, :, :D]).astype(BF)
        for pair in range(PAIRS):
            cols = slice(pair * PW, (pair + 1) * PW)
            q_out[0, pair] = queries[:, cols]
            k_out[0, pair] = keys[:, cols]
            v_out[0, pair] = values[:, cols]
            k_all[step, pair] = keys[:, cols]
            vt_all[step, pair] = values[:, cols].T
        middles[step] = x
        run_events(events, step, "dense")


    @pl.when(step < blocks)
    def _():
        first = jnp.where(step >= long_blocks, long_blocks, 0)

        def two_pairs(turn, carry):
            pairs = [turn * TOGETHER + k for k in range(TOGETHER)]
            both = [split_heads(q_out[0, pair]) for pair in pairs]
            for state in states:
                softmax_start(state)

            def with_block(j, far, diag):
                for pair, queries, state in zip(pairs, both, states):
                    softmax_step(
                        k_all[j, pair], vt_all[j, pair], queries, bias, pair, far, diag, SUB, SUB, state
                    )

            def earlier(j, inner):
                with_block(j, SUB * (step - j), False)
                return inner

            lax.fori_loop(first, step, earlier, 0)
            with_block(step, 0, True)
            for pair, state in zip(pairs, states):
                ot_out[0, pair], lse_out[0, pair] = softmax_end(state)
            run_events(events, step, turn)
            return carry

        lax.fori_loop(0, PAIRS // TOGETHER, two_pairs, 0)
        attended = ot_out[0].reshape(D, BLK).T
        middles[step] = middles[step] + mm(attended, wts[1, :, D : 2 * D])

    for k, stream in enumerate((feed_a, feed_b)):
        due = (k + 1) * blocks if natural else blocks

        @pl.when(step == due - 1)
        def _(k=k, stream=stream):
            stream.finish()
            loads[k].start()

        @pl.when(step == due)
        def _(k=k):
            loads[k].wait()

    def weight_half(half, cols):
        if natural:
            return feed[half, :, :, :, cols].reshape(D, cols.stop - cols.start)
        return feed[half].reshape(D, FF)[:, cols]

    def half_feed(block, k):
        width = FF // 2
        cols = slice(k * width, (k + 1) * width)
        up = weight_half(0, cols)
        active, slope = gelu_pair(mm(seconds[block], up) + beta_of(vec, 0, k, width))
        active = active.astype(BF)
        act_out[...] = active
        slope_out[...] = slope.astype(BF)
        return mm(active, weight_half(1, cols), NT)

    @pl.when((step >= blocks) & (step < 2 * blocks))
    def _():
        block = lax.rem(step, blocks)
        middle = middles[block]
        middle_out[...] = middle
        xhat, _ = norm_stats(middle)
        seconds[block] = (xhat * vec[4:5] + vec[5:6]).astype(BF)
        middles[block] = middle + vec[6:7] + half_feed(block, 0)

    @pl.when(step >= 2 * blocks)
    def _():
        block = lax.rem(step, blocks)
        x1_out[...] = middles[block] + half_feed(block, 1)

    run_events(events, step, "end")

    @pl.when(step == 3 * blocks - 1)
    def _():
        for stream in (short_attn, short_a, short_b):
            stream.finish()


def run_events(events, step, point):
    for (s, p), bodies in events.items():
        if isinstance(point, str) or isinstance(p, str):
            if point is not p and point != p:
                continue
            due = step == s
        else:
            due = (step == s) & (point == p)

        @pl.when(due)
        def _(bodies=bodies):
            for body in bodies:
                body()


def whole_spec(shape):
    return pl.BlockSpec(shape, lambda i: (0,) * len(shape), pipeline_mode=pl.Buffered(1))


def params(mib, **more):
    return pltpu.CompilerParams(vmem_limit_bytes=mib * 2**20, **more)


def state_scratch(n):
    return [pltpu.VMEM((1, 2 * n), F32), pltpu.VMEM((1, 2 * n), F32), pltpu.VMEM((PW, 2 * n), F32)]


def full_forward(aux, tables, wts, attn_low, feed_low, vec, long_blocks, wide, narrow, natural):
    tokens = aux.shape[0]
    blocks = tokens // BLK
    far = SUB * long_blocks
    form = feed_low.shape[1:] if natural else feed_low.shape[2:]
    form = (form[0], FF) if natural else form
    half = (form[0], form[1] * 2 * D // FF)

    def early(i):
        return jnp.minimum(i, blocks - 1)

    def late(i, phase):
        return jnp.clip(i - phase * blocks, 0, blocks - 1)

    def heads(n, width):
        return (
            jax.ShapeDtypeStruct((blocks, PAIRS, n, width), BF),
            pl.BlockSpec((1, PAIRS, n, width), lambda i: (early(i), 0, 0, 0)),
        )

    def flat(phase):
        return (
            jax.ShapeDtypeStruct((tokens, D), F32),
            pl.BlockSpec((BLK, D), lambda i: (late(i, phase), 0)),
        )

    def hidden():
        return (
            jax.ShapeDtypeStruct((tokens, FF), BF),
            pl.BlockSpec(
                (BLK, FF // 2),
                lambda i: (
                    lax.rem(jnp.maximum(i - blocks, 0), blocks),
                    jnp.maximum(i - blocks, 0) // blocks,
                ),
            ),
        )

    anywhere = pl.BlockSpec(memory_space=pl.ANY)
    outs = [flat(2), flat(1)] + [heads(BLK, PW)] * 3 + [heads(PW, BLK)]
    outs.append(
        (
            jax.ShapeDtypeStruct((blocks, PAIRS, 1, 2 * BLK), F32),
            pl.BlockSpec((1, PAIRS, 1, 2 * BLK), lambda i: (early(i), 0, 0, 0)),
        )
    )
    outs += [hidden(), hidden()]
    outs += [
        (jax.ShapeDtypeStruct((2, wide, narrow) + each, BF), anywhere) for each in (form, half, form)
    ]
    return pl.pallas_call(
        functools.partial(full_forward_kernel, long_blocks, wide, narrow, natural),
        grid=(3 * blocks,),
        in_specs=[
            pl.BlockSpec((BLK, aux.shape[1]), lambda i: (early(i), 0)),
            whole_spec((1, V, D)),
            whole_spec(wts.shape),
            anywhere,
            anywhere,
            whole_spec(vec.shape),
            pl.BlockSpec(memory_space=pltpu.SMEM),
        ],
        out_specs=[spec for _, spec in outs],
        out_shape=[shape for shape, _ in outs],
        scratch_shapes=[
            pltpu.VMEM((HEADS, far, TILE, TILE), F32),
            pltpu.VMEM((blocks, PAIRS, BLK, PW), BF),
            pltpu.VMEM((blocks, PAIRS, PW, BLK), BF),
            pltpu.VMEM((blocks, BLK, D), F32),
            pltpu.VMEM((blocks, BLK, D), BF),
            pltpu.VMEM((2, wide, narrow) + form, BF),
            pltpu.SemaphoreType.DMA((2,)),
        ]
        + state_scratch(BLK) * TOGETHER
        + gather_sems(wide, narrow) * 5,
        compiler_params=params(VMEM_MIB, collective_id=4, has_side_effects=True),
        name="full_forward",
    )(aux, tables, wts, attn_low, feed_low, vec, vec)


PAD = 8


def middle_kernel(
    seq,
    x1,
    aux,
    head,
    attn,
    feed_in,
    vec,
    rel,
    scalars,
    fold,
    dx_out,
    d_attn,
    d_feed_out,
    d_head,
    row_grads,
    bits_out,
    sums,
    xp,
    pooled,
    mixed,
    ot,
    lse,
    active_s,
    slope_s,
    middle_s,
    bias,
    tiles,
    d_mixed,
    feed,
    d_feed,
    sems,
    *state,
):
    n_long = seq // 3
    spots = ((PAD, 0, n_long), (2 * PAD + seq, n_long, TILE))
    lanes = D // TILE
    def plane_copies(array, out):
        copies = []
        for c in range(lanes):
            for k, (first, start, count) in enumerate(
                ((0, PAD, seq), (seq, 2 * PAD + seq, array.shape[0] - seq))
            ):
                ends = (array.at[first : first + count, c * TILE : (c + 1) * TILE],)
                ends += (xp.at[c, start : start + count],)
                ends = ends[::-1] if out else ends
                copies.append(pltpu.make_async_copy(*ends, sems.at[2 * c + k]))
        return copies

    loads = plane_copies(x1, False)
    load_feed = pltpu.make_async_copy(feed_in, feed, sems.at[2 * lanes])
    store_feed = pltpu.make_async_copy(d_feed, d_feed_out, sems.at[2 * lanes + 1])
    for load in loads:
        load.start()
    load_feed.start()
    build_bias(rel, 1, bias, bias.shape[1])
    tiles[...] = jnp.zeros_like(tiles)
    for c in range(lanes):
        xp[c, 0:PAD] = jnp.zeros((PAD, TILE), F32)
        xp[c, PAD + seq : 2 * PAD + seq] = jnp.zeros((PAD, TILE), F32)
    for load in loads:
        load.wait()
    for start, at, n in spots:
        for c in range(lanes):
            pooled[at : at + n, c * TILE : (c + 1) * TILE] = (
                xp[c, pl.ds(start - 2, n, stride=3)]
                + xp[c, pl.ds(start - 1, n, stride=3)]
                + xp[c, pl.ds(start, n, stride=3)]
            ) / 3.0

    xhat, _ = norm_stats(pooled[...])
    normed = (xhat * vec[7:8] + vec[8:9]).astype(BF)
    for part in range(3):
        half, at = part // 2, part % 2 * D
        value = mm(normed, attn[half, :, at : at + D])
        value = (value * HD**-0.5 if part == 0 else value).astype(BF)
        for pair in range(PAIRS):
            mixed[part, pair] = value[:, pair * PW : (pair + 1) * PW]

    def forward_pair(pair, carry):
        for at, n, offset in ((0, n_long, 0), (n_long, TILE, 2 * n_long)):
            top, total, acc = state
            wide = pl.ds(0, 2 * n)
            part = (top.at[:, wide], total.at[:, wide], acc.at[:, wide])
            softmax_start(part)
            values_t = mixed[2, pair, at : at + n].T
            both = split_heads(mixed[0, pair, at : at + n])
            count = n // TILE
            softmax_step(
                mixed[1, pair, at : at + n], values_t, both, bias, pair, 0, True, count, count, part
            )
            ot[pair, :, at : at + n], lse[pair, :, offset : offset + 2 * n] = softmax_end(part)
        return carry

    lax.fori_loop(0, PAIRS, forward_pair, 0, unroll=4)
    middle = pooled[...] + mm(ot[...].reshape(D, ot.shape[2]).T, attn[1, :, D:])
    middle_s[...] = middle
    xhat, _ = norm_stats(middle)
    second = (xhat * vec[9:10] + vec[10:11]).astype(BF)
    short = middle + vec[11:12]
    load_feed.wait()
    for c in range(PARTS):
        cols = slice(c * WIDTH, (c + 1) * WIDTH)
        active, slope = gelu_pair(mm(second, feed[0, :, cols]) + beta_of(vec, 1, c, WIDTH))
        active_s[:, cols] = active.astype(BF)
        slope_s[:, cols] = slope.astype(BF)
        short = short + mm(active_s[:, cols], feed[1, :, cols], NT)
    for start, at, n in spots:
        for c in range(lanes):
            part = short[at : at + n, c * TILE : (c + 1) * TILE]
            for k in range(3):
                where = pl.ds(start + k, n, stride=3)
                xp[c, where] = xp[c, where] + part

    d_head[...] = jnp.zeros_like(d_head)
    row_grads[...] = jnp.zeros_like(row_grads)

    def loss_block(b, bits):
        start = pl.multiple_of(b * BLK + jnp.where(b * BLK >= seq, 2 * PAD, PAD), PAD)
        joined = jnp.concatenate([xp[c, pl.ds(start, BLK)] for c in range(lanes)], 1)
        xhat, rstd = norm_stats(joined)
        last = (xhat * vec[0:1] + vec[1:2]).astype(BF)
        logits = mm(last, head[1], NT) * D**-0.5
        info = aux[pl.ds(pl.multiple_of(b * BLK, BLK), BLK), :]
        weight = info[:, 2:3]
        hot = one_hot(info[:, 1:2])
        highest = jnp.max(logits, -1, keepdims=True)
        powers = jnp.exp(logits - highest)
        total = jnp.sum(powers, -1, keepdims=True)
        picked = jnp.sum(jnp.where(hot, logits, 0.0), -1, keepdims=True)
        lost = weight * (highest + jnp.log(total) - picked)
        d_logits = ((powers / total - hot.astype(F32)) * (weight * scalars[1:2, 0:1])).astype(BF)
        d_head[...] += mm(d_logits, last, TN) * D**-0.5
        d_last = mm(d_logits, head[1]) * D**-0.5
        dx, d_gain, d_shift = norm_back(d_last, xhat, rstd, vec[0:1])
        row_grads[0:1] += d_gain
        row_grads[1:2] += d_shift
        for c in range(lanes):
            xp[c, pl.ds(start, BLK)] = dx[:, c * TILE : (c + 1) * TILE]
        return bits + lost

    bits = lax.fori_loop(0, x1.shape[0] // BLK, loss_block, jnp.zeros((BLK, 1), F32), unroll=4)
    bits_out[...] = jnp.broadcast_to(jnp.sum(bits, 0, keepdims=True) / LOG_TWO, bits_out.shape)

    d_short = jnp.concatenate(
        [
            jnp.concatenate(
                [
                    xp[c, pl.ds(start, n, stride=3)]
                    + xp[c, pl.ds(start + 1, n, stride=3)]
                    + xp[c, pl.ds(start + 2, n, stride=3)]
                    for c in range(lanes)
                ],
                1,
            )
            for start, at, n in spots
        ],
        0,
    )
    d_branch = d_short.astype(BF)
    row_grads[6:7] = jnp.sum(d_branch.astype(F32), 0, keepdims=True)
    xhat, rstd = norm_stats(middle_s[...])
    second = (xhat * vec[9:10] + vec[10:11]).astype(BF)
    d_second = jnp.zeros(d_short.shape, F32)
    for c in range(PARTS):
        cols = slice(c * WIDTH, (c + 1) * WIDTH)
        d_feed[1, :, cols] = mm(d_branch, active_s[:, cols], TN).astype(BF)
        d_pre = (mm(d_branch, feed[1, :, cols]) * slope_s[:, cols].astype(F32)).astype(BF)
        put_beta(row_grads, 7, c, jnp.sum(d_pre.astype(F32), 0, keepdims=True), False)
        d_feed[0, :, cols] = mm(second, d_pre, TN).astype(BF)
        d_second = d_second + mm(d_pre, feed[0, :, cols], NT)
    store_feed.start()
    dx, d_gain, d_shift = norm_back(d_second, xhat, rstd, vec[9:10])
    row_grads[4:5] = d_gain
    row_grads[5:6] = d_shift
    d_middle = d_short + dx
    d_mix = d_middle.astype(BF)
    ot_all = ot[...].reshape(D, ot.shape[2])
    d_attn[1, :, D:] = mm(ot_all, d_mix).astype(BF)
    d_att = mm(d_mix, attn[1, :, D:], NT).astype(BF)
    for pair in range(PAIRS):
        mixed[3, pair] = d_att[:, pair * PW : (pair + 1) * PW]

    def backward_pair(pair, carry):
        for at, n, offset in ((0, n_long, 0), (n_long, TILE, 2 * n_long)):
            d_out = mixed[3, pair, at : at + n]
            product = (d_out.astype(F32).T) * ot[pair, :, at : at + n].astype(F32)
            inner = interleave(
                jnp.sum(product[:HD], 0, keepdims=True), jnp.sum(product[HD:], 0, keepdims=True)
            )
            queries = split_heads(mixed[0, pair, at : at + n])
            grads = split_heads(d_out)
            keys = mixed[1, pair, at : at + n]
            count = n // TILE
            dv, dk, dq = score_back(
                keys,
                mixed[2, pair, at : at + n],
                keys.T,
                queries,
                grads,
                lse[pair, :, offset : offset + 2 * n],
                inner,
                bias,
                pair,
                0,
                True,
                count,
                count,
                tiles,
            )
            d_mixed[0, pair, at : at + n] = (merge_heads(dq) * HD**-0.5).T.astype(BF)
            d_mixed[1, pair, at : at + n] = dk.astype(BF)
            d_mixed[2, pair, at : at + n] = dv.astype(BF)
        return carry

    lax.fori_loop(0, PAIRS, backward_pair, 0, unroll=4)
    rel = rel_row(tiles, sums, fold, tiles.shape[1])
    row_grads[11:12] = jnp.concatenate([jnp.zeros_like(rel), rel], 1)
    d_in = jnp.concatenate([d_mixed[part, pair] for part in range(3) for pair in range(PAIRS)], 1)
    xhat, rstd = norm_stats(pooled[...])
    normed = (xhat * vec[7:8] + vec[8:9]).astype(BF)
    d_attn[0] = mm(normed, d_in[:, : 2 * D], TN).astype(BF)
    d_attn[1, :, :D] = mm(normed, d_in[:, 2 * D :], TN).astype(BF)
    dx, d_gain, d_shift = norm_back(mm(d_in[:, : 2 * D], attn[0], NT) + mm(d_in[:, 2 * D :], attn[1, :, :D], NT), xhat, rstd, vec[7:8])
    row_grads[2:3] = d_gain
    row_grads[3:4] = d_shift
    d_pool = (d_middle + dx) / 3.0
    for start, at, n in spots:
        for c in range(lanes):
            part = d_pool[at : at + n, c * TILE : (c + 1) * TILE]
            for k in range(3):
                where = pl.ds(start - 2 + k, n, stride=3)
                xp[c, where] = xp[c, where] + part
    stores = plane_copies(dx_out, True)
    for store in stores:
        store.start()
    for store in stores:
        store.wait()
    store_feed.wait()


def middle_stage(x1, aux, tables, attn, feed, vec, scalars, seq):
    tokens = x1.shape[0]
    n_long = seq // 3
    short = n_long + TILE
    far = n_long // TILE
    fold = fold_matrix(far)
    vm = pl.BlockSpec(memory_space=pltpu.VMEM)
    anywhere = pl.BlockSpec(memory_space=pl.ANY)
    return pl.pallas_call(
        functools.partial(middle_kernel, seq),
        in_specs=[anywhere, vm, vm, vm, anywhere, vm, pl.BlockSpec(memory_space=pltpu.SMEM), vm, vm],
        out_specs=[anywhere, vm, anywhere, vm, vm, vm],
        out_shape=[
            jax.ShapeDtypeStruct((tokens, D), F32),
            jax.ShapeDtypeStruct((2, D, 2 * D), BF),
            jax.ShapeDtypeStruct((2, D, FF), BF),
            jax.ShapeDtypeStruct((V, D), F32),
            jax.ShapeDtypeStruct((16, D), F32),
            jax.ShapeDtypeStruct((8, 128), F32),
        ],
        scratch_shapes=[
            pltpu.VMEM((HEADS, fold_rows(far), TILE), F32),
            pltpu.VMEM((D // TILE, tokens + 2 * PAD, TILE), F32),
            pltpu.VMEM((short, D), F32),
            pltpu.VMEM((4, PAIRS, short, PW), BF),
            pltpu.VMEM((PAIRS, PW, short), BF),
            pltpu.VMEM((PAIRS, 1, 2 * short), F32),
            pltpu.VMEM((short, FF), BF),
            pltpu.VMEM((short, FF), BF),
            pltpu.VMEM((short, D), F32),
            pltpu.VMEM((HEADS, far, TILE, TILE), F32),
            pltpu.VMEM((HEADS, far, TILE, TILE), F32),
            pltpu.VMEM((3, PAIRS, short, PW), BF),
            pltpu.VMEM((2, D, FF), BF),
            pltpu.VMEM((2, D, FF), BF),
            pltpu.SemaphoreType.DMA((2 * (D // TILE) + 2,)),
        ]
        + state_scratch(n_long),
        compiler_params=params(VMEM_MIB),
        name="middle_stage",
    )(x1, aux, tables, attn, feed, vec, vec, scalars, fold)


def feed_back_kernel(
    wide,
    narrow,
    dx,
    act,
    slope,
    middle,
    wts,
    vec,
    ready,
    dm_out,
    d_feed,
    row_grads,
    sums_out,
    up,
    down,
    *scratch,
):
    step = pl.program_id(0)
    at = Place(wide, narrow)
    streams = []
    for source, target in zip(column_parts(ready, 2), column_parts(sums_out, 2)):
        part = scratch[SCATTER_REFS * len(streams) : SCATTER_REFS * (len(streams) + 1)]
        streams.append(ScatterStream(at, source, halves_out(target), *part[:5], part[5:]))
    one, two = streams
    events = {
        (0, "dense"): (one.stage_first,),
        (0, "end"): (two.stage_first,),
        (1, "dense"): (one.stage_second,),
        (1, "end"): (two.stage_second,),
        (2, "dense"): (one.stage_home,),
        (2, "end"): (two.stage_home,),
    }

    @pl.when(step == 0)
    def _():
        all_here = greet(*scatter_greetings(at))
        up[...] = jnp.zeros_like(up)
        down[...] = jnp.zeros_like(down)
        all_here()
        one.start()
        two.start()
        row_grads[...] = jnp.zeros_like(row_grads)

    d_result = dx[...]
    d_branch = d_result.astype(BF)
    row_grads[2:3] += jnp.sum(d_branch.astype(F32), 0, keepdims=True)
    xhat, rstd = norm_stats(middle[...])
    second = (xhat * vec[4:5] + vec[5:6]).astype(BF)
    run_events(events, step, "dense")
    d_second = jnp.zeros(d_result.shape, F32)
    for c in range(PARTS):
        cols = slice(c * WIDTH, (c + 1) * WIDTH)
        down[:, cols] += mm(d_branch, act[:, cols], TN)
        d_pre = (mm(d_branch, wts[1, :, cols]) * slope[:, cols].astype(F32)).astype(BF)
        put_beta(row_grads, 3, c, jnp.sum(d_pre.astype(F32), 0, keepdims=True), True)
        up[:, cols] += mm(second, d_pre, TN)
        d_second = d_second + mm(d_pre, wts[0, :, cols], NT)
    dn, d_gain, d_shift = norm_back(d_second, xhat, rstd, vec[4:5])
    row_grads[0:1] += d_gain
    row_grads[1:2] += d_shift
    dm_out[...] = d_result + dn
    run_events(events, step, "end")

    @pl.when(step == pl.num_programs(0) - 1)
    def _():
        d_feed[0] = up[...].astype(BF)
        d_feed[1] = down[...].astype(BF)
        one.finish()
        two.finish()


def halves_out(ref):
    return [ref.at[0], ref.at[1]]


def feed_back(dx, act, slope, middle, wts, vec, ready, wide, narrow):
    tokens = dx.shape[0]
    form = ready.shape[3:]

    def flat(width):
        return pl.BlockSpec((BLK, width), lambda i: (i, 0))

    return pl.pallas_call(
        functools.partial(feed_back_kernel, wide, narrow),
        grid=(tokens // BLK,),
        in_specs=[flat(D), flat(FF), flat(FF), flat(D), whole_spec(wts.shape), whole_spec(vec.shape)]
        + [pl.BlockSpec(memory_space=pl.ANY)],
        out_specs=[
            flat(D),
            whole_spec((2, D, FF)),
            whole_spec((8, D)),
            whole_spec((2,) + form),
        ],
        out_shape=[
            jax.ShapeDtypeStruct((tokens, D), F32),
            jax.ShapeDtypeStruct((2, D, FF), BF),
            jax.ShapeDtypeStruct((8, D), F32),
            jax.ShapeDtypeStruct((2,) + form, F32),
        ],
        scratch_shapes=[pltpu.VMEM((D, FF), F32), pltpu.VMEM((D, FF), F32)]
        + scatter_scratch(wide, narrow, half_width(ready)) * 2,
        compiler_params=params(VMEM_MIB, collective_id=5, has_side_effects=True),
        name="feed_back",
    )(dx, act, slope, middle, wts, vec, ready)


def attention_back_kernel(
    long_blocks,
    wide,
    narrow,
    dm,
    aux,
    ot,
    lse,
    q_all,
    k_all,
    v_all,
    embed,
    wts,
    vec,
    rel,
    fold,
    ready_a,
    ready_b,
    d_attn,
    d_embed,
    row_grads,
    out_a,
    out_b,
    sums,
    bias,
    tiles,
    kt_all,
    dk_all,
    dv_all,
    dq_t,
    d_att,
    inner,
    weights,
    d_mixed,
    *scratch,
):
    step = pl.program_id(0)
    blocks = pl.num_programs(0)
    i = blocks - 1 - step
    at = Place(wide, narrow)
    streams = []
    for ready, out in ((ready_a, out_a), (ready_b, out_b)):
        for source, target in zip(column_parts(ready, 2), column_parts(out, 2)):
            part = scratch[SCATTER_REFS * len(streams) : SCATTER_REFS * (len(streams) + 1)]
            streams.append(ScatterStream(at, source, halves_out(target), *part[:5], part[5:]))
    one, two, three, four = streams
    events = {
        (0, 0): (one.stage_first,),
        (0, 1): (two.stage_first,),
        (0, "end"): (three.stage_first,),
        (1, "dense"): (four.stage_first,),
        (1, 0): (one.stage_second,),
        (1, 1): (two.stage_second,),
        (1, "end"): (one.stage_home,),
        (2, 0): (three.stage_second, two.stage_home),
        (2, 1): (four.stage_second,),
        (2, "end"): (three.stage_home,),
        (3, 1): (four.stage_home,),
    }

    @pl.when(step == 0)
    def _():
        all_here = greet(*scatter_greetings(at))
        build_bias(rel, 0, bias, bias.shape[1])
        all_here()
        for stream in streams:
            stream.start()
        tiles[...] = jnp.zeros_like(tiles)
        dk_all[...] = jnp.zeros_like(dk_all)
        dv_all[...] = jnp.zeros_like(dv_all)
        weights[...] = jnp.zeros_like(weights)
        d_embed[...] = jnp.zeros_like(d_embed)
        row_grads[...] = jnp.zeros_like(row_grads)

        def turn(n, carry):
            for pair in range(PAIRS):
                kt_all[n, pair] = k_all[n, pair].T
            return carry

        lax.fori_loop(0, blocks, turn, 0)

    d_middle = dm[...]
    d_mix = d_middle.astype(BF)
    weights[1, :, D:] += mm(ot[0].reshape(D, BLK), d_mix)
    out = mm(d_mix, wts[1, :, D : 2 * D], NT).astype(BF)
    for pair in range(PAIRS):
        d_att[pair] = out[:, pair * PW : (pair + 1) * PW]
    product = mm(wts[1, :, D : 2 * D], d_mix, NT).astype(BF).astype(F32) * ot[0].reshape(
        D, BLK
    ).astype(F32)
    for pair in range(PAIRS):
        top = pair * PW
        inner[pair] = interleave(
            jnp.sum(product[top : top + HD], 0, keepdims=True),
            jnp.sum(product[top + HD : top + PW], 0, keepdims=True),
        )
    run_events(events, step, "dense")
    first = jnp.where(i >= long_blocks, long_blocks, 0)

    def two_pairs(turn, carry):
        pairs = [turn * TOGETHER + k for k in range(TOGETHER)]
        queries = [split_heads(q_all[i, pair]) for pair in pairs]
        grads = [split_heads(d_att[pair]) for pair in pairs]
        dq_t[...] = jnp.zeros_like(dq_t)

        def with_block(j, far, diag):
            for k, pair in enumerate(pairs):
                dv, dk, dq = score_back(
                    k_all[j, pair],
                    v_all[j, pair],
                    kt_all[j, pair],
                    queries[k],
                    grads[k],
                    lse[0, pair],
                    inner[pair],
                    bias,
                    pair,
                    far,
                    diag,
                    SUB,
                    SUB,
                    tiles,
                )
                dv_all[j, pair] += dv
                dk_all[j, pair] += dk
                dq_t[k] += dq

        def earlier(j, inside):
            with_block(j, SUB * (i - j), False)
            return inside

        lax.fori_loop(first, i, earlier, 0)
        with_block(i, 0, True)
        for k, pair in enumerate(pairs):
            d_mixed[0, pair] = (merge_heads(dq_t[k]) * HD**-0.5).T.astype(BF)
            d_mixed[1, pair] = dk_all[i, pair].astype(BF)
            d_mixed[2, pair] = dv_all[i, pair].astype(BF)
        run_events(events, step, turn)
        return carry

    lax.fori_loop(0, PAIRS // TOGETHER, two_pairs, 0)
    d_in = jnp.concatenate([d_mixed[part, pair] for part in range(3) for pair in range(PAIRS)], 1)
    hot = one_hot(aux[:, 0:1]).astype(BF)
    xhat, rstd = norm_stats(mm(hot, embed[0]))
    normed = (xhat * vec[2:3] + vec[3:4]).astype(BF)
    weights[0] += mm(normed, d_in[:, : 2 * D], TN)
    weights[1, :, :D] += mm(normed, d_in[:, 2 * D :], TN)
    dx, d_gain, d_shift = norm_back(mm(d_in[:, : 2 * D], wts[0, :, : 2 * D], NT) + mm(d_in[:, 2 * D :], wts[1, :, :D], NT), xhat, rstd, vec[2:3])
    row_grads[0:1] += d_gain
    row_grads[1:2] += d_shift
    d_embed[...] += mm(hot, (d_middle + dx).astype(BF), TN)

    run_events(events, step, "end")

    @pl.when(step == blocks - 1)
    def _():
        d_attn[...] = weights[...].astype(BF)
        rel = rel_row(tiles, sums, fold, tiles.shape[1])
        row_grads[2:3] = jnp.concatenate([rel, jnp.zeros_like(rel)], 1)
        for stream in streams:
            stream.finish()


def half_width(x):
    return x.shape[3:-1] + (x.shape[-1] // 2,)


def attention_back(
    dm, aux, ot, lse, q, k, v, tables, wts, vec, ready_a, ready_b, long_blocks, wide, narrow
):
    tokens = dm.shape[0]
    blocks = tokens // BLK
    far = SUB * long_blocks
    fold = fold_matrix(far)

    def turned(shape):
        return pl.BlockSpec(shape, lambda s: (blocks - 1 - s,) + (0,) * (len(shape) - 1))

    return pl.pallas_call(
        functools.partial(attention_back_kernel, long_blocks, wide, narrow),
        grid=(blocks,),
        in_specs=[
            turned((BLK, D)),
            turned((BLK, aux.shape[1])),
            turned((1, PAIRS, PW, BLK)),
            turned((1, PAIRS, 1, 2 * BLK)),
            whole_spec(q.shape),
            whole_spec(k.shape),
            whole_spec(v.shape),
            whole_spec((1, V, D)),
            whole_spec((2, D, 2 * D)),
            whole_spec(vec.shape),
            pl.BlockSpec(memory_space=pltpu.SMEM),
            whole_spec(fold.shape),
            pl.BlockSpec(memory_space=pl.ANY),
            pl.BlockSpec(memory_space=pl.ANY),
        ],
        out_specs=[
            whole_spec((2, D, 2 * D)),
            whole_spec((V, D)),
            whole_spec((8, D)),
            whole_spec((2,) + ready_a.shape[3:]),
            whole_spec((2,) + ready_b.shape[3:]),
        ],
        out_shape=[
            jax.ShapeDtypeStruct((2, D, 2 * D), BF),
            jax.ShapeDtypeStruct((V, D), F32),
            jax.ShapeDtypeStruct((8, D), F32),
            jax.ShapeDtypeStruct((2,) + ready_a.shape[3:], F32),
            jax.ShapeDtypeStruct((2,) + ready_b.shape[3:], F32),
        ],
        scratch_shapes=[
            pltpu.VMEM((HEADS, fold_rows(far), TILE), F32),
            pltpu.VMEM((HEADS, far, TILE, TILE), F32),
            pltpu.VMEM((HEADS, far, TILE, TILE), F32),
            pltpu.VMEM((blocks, PAIRS, PW, BLK), BF),
            pltpu.VMEM((blocks, PAIRS, BLK, PW), F32),
            pltpu.VMEM((blocks, PAIRS, BLK, PW), F32),
            pltpu.VMEM((TOGETHER, PW, 2 * BLK), F32),
            pltpu.VMEM((PAIRS, BLK, PW), BF),
            pltpu.VMEM((PAIRS, 1, 2 * BLK), F32),
            pltpu.VMEM((2, D, 2 * D), F32),
            pltpu.VMEM((3, PAIRS, BLK, PW), BF),
        ]
        + scatter_scratch(wide, narrow, half_width(ready_a)) * 2
        + scatter_scratch(wide, narrow, half_width(ready_b)) * 2,
        compiler_params=params(VMEM_MIB, collective_id=6, has_side_effects=True),
        name="attention_back",
    )(dm, aux, ot, lse, q, k, v, tables, wts, vec, vec, fold, ready_a, ready_b)


MESH = pl.DeviceIdType.MESH
MISC_ROWS = 32
SIDE = 128
MISC_COLS = D + SIDE
COUNT_ROW = 24


class Place:
    def __init__(self, wide, narrow):
        self.W, self.N = wide, narrow
        self.c = lax.axis_index("rep")
        self.w = lax.axis_index("wide")
        self.n = lax.axis_index("narrow")
        self.a0, self.b0 = self.digits(self.c)
        self.group = self.w // (wide // 2)

    def digits(self, c):
        hi, lo = self.n // 2, self.n % 2
        return (1 - c) * hi + c * lo, (1 - c) * lo + c * hi

    def narrow_of(self, a, b, c=None):
        c = self.c if c is None else c
        return a * (2 - c) + b * (1 + c)

    def chip(self, w, a, b):
        return {"wide": w, "narrow": self.narrow_of(a, b)}

    def sibling(self):
        return {"rep": 1 - self.c}


def greet(devices, more=()):
    barrier = pltpu.get_barrier_semaphore()
    count = len(devices)
    for device in devices:
        pl.semaphore_signal(barrier, inc=1, device_id=device, device_id_type=MESH)
    for condition, device in more:

        @pl.when(condition)
        def _(device=device):
            pl.semaphore_signal(barrier, inc=1, device_id=device, device_id_type=MESH)

        count = count + condition.astype(jnp.int32)
    return lambda: pl.semaphore_wait(barrier, count)


def slab_form(rows, cols):
    return (rows, cols) if rows % 16 == 0 else (16, rows * cols // 16)


def gather_greetings(at):
    out = [{"wide": lax.rem(at.w + k, at.W)} for k in range(1, at.W)]
    return out + [
        at.chip(at.w, at.a0, 1 - at.b0),
        at.chip(at.w, 1 - at.a0, at.b0),
        at.sibling(),
    ]


class GatherStream:
    def __init__(self, at, src, out, send_along, send, recv, recv_side, local):
        self.at, self.src, self.out = at, src, out
        self.send_along, self.send, self.recv, self.recv_side = send_along, send, recv, recv_side
        self.n0 = at.narrow_of(at.a0, at.b0)
        self.n1 = at.narrow_of(at.a0, 1 - at.b0)
        self.n2 = at.narrow_of(1 - at.a0, at.b0)
        self.n3 = at.narrow_of(1 - at.a0, 1 - at.b0)
        self.local = local

    @property
    def keep(self):
        at = self.at
        return pltpu.make_async_copy(self.src, self.out.at[at.c, at.w, self.n0], self.local)

    def copy(self, ref, w, n, sem, peer):
        return pltpu.make_async_remote_copy(
            src_ref=ref,
            dst_ref=self.out.at[self.at.c, w, n],
            send_sem=sem,
            recv_sem=self.recv.at[w, n],
            device_id=peer,
            device_id_type=MESH,
        )

    def arrived(self, w, n):
        self.copy(
            self.out.at[self.at.c, w, n], w, n, self.send.at[0], self.at.sibling()
        ).wait_recv()

    def other(self, k):
        return lax.rem(self.at.w + k, self.at.W)

    def along(self, k):
        at = self.at
        return self.copy(
            self.src, at.w, self.n0, self.send_along.at[k - 1], {"wide": self.other(k)}
        )

    def neighbours(self, w, mine):
        at = self.at
        ref = self.src if mine else self.out.at[at.c, w, self.n0]
        self.copy(ref, w, self.n0, self.send.at[0], at.chip(at.w, at.a0, 1 - at.b0)).start()
        self.copy(ref, w, self.n0, self.send.at[1], at.chip(at.w, 1 - at.a0, at.b0)).start()

    def side(self, n):
        at = self.at
        return pltpu.make_async_remote_copy(
            src_ref=self.out.at[at.c, :, n],
            dst_ref=self.out.at[at.c, :, n],
            send_sem=self.send.at[2 + n],
            recv_sem=self.recv_side.at[n],
            device_id=at.sibling(),
            device_id_type=MESH,
        )

    def start(self):
        self.start_along()
        self.neighbours(self.at.w, True)

    def start_along(self):
        self.keep.start()
        for k in self.order():
            self.along(k).start()

    def finish_along(self):
        self.keep.wait()
        for k in self.order():
            self.along(k).wait_send()
            self.arrived(self.other(k), self.n0)

    def start_across(self):
        at = self.at
        for k in range(at.W):
            self.neighbours(self.other(k), False)
        self.side(self.n0).start()

    def order(self):
        return sorted(range(1, self.at.W), key=lambda k: -min(k, self.at.W - k))

    def depth(self, d):
        at = self.at
        if d == 1:
            for k in self.order()[::-1]:
                w = self.other(k)
                self.arrived(w, self.n0)
                self.neighbours(w, False)
            self.keep.wait()
            self.side(self.n0).start()
        if d == 2:
            for k in [0] + self.order()[::-1]:
                w = self.other(k)
                self.arrived(w, self.n1)
                ref = self.out.at[at.c, w, self.n1]
                peer = at.chip(at.w, 1 - at.a0, at.b0)
                self.copy(ref, w, self.n1, self.send.at[1], peer).start()
            self.side(self.n1).start()
            for k in range(at.W):
                self.arrived(self.other(k), self.n2)
            self.side(self.n2).start()
        if d == 3:
            for k in range(at.W):
                self.arrived(self.other(k), self.n3)
            self.side(self.n3).start()

    def finish(self, along=True):
        at = self.at
        for k in self.order() if along else ():
            self.along(k).wait_send()
        column = self.out.at[at.c, :, self.n0]
        half = self.out.at[at.c, pl.ds(0, at.W // 2)]
        for sem, ref in ((self.send.at[0], column), (self.send.at[1], half)):
            pltpu.make_async_remote_copy(
                src_ref=ref,
                dst_ref=ref,
                send_sem=sem,
                recv_sem=self.recv.at[0, 0],
                device_id=at.sibling(),
                device_id_type=MESH,
            ).wait_send()
        for n in range(at.N):
            self.side(n).wait_send()
        for n in range(at.N):
            pltpu.make_async_remote_copy(
                src_ref=self.out.at[1 - at.c, :, n],
                dst_ref=self.out.at[1 - at.c, :, n],
                send_sem=self.send.at[2 + n],
                recv_sem=self.recv_side.at[n],
                device_id=at.sibling(),
                device_id_type=MESH,
            ).wait_recv()


class HostedStream(GatherStream):
    def column(self, half, n, count=None):
        return self.out.at[half, :, n] if count is None else self.out.at[half, pl.ds(0, count), n]

    def all_of(self, ref, send, recv):
        return pltpu.make_async_remote_copy(
            src_ref=ref,
            dst_ref=ref,
            send_sem=send,
            recv_sem=recv,
            device_id=self.at.sibling(),
            device_id_type=MESH,
        )

    def copy(self, ref, w, n, sem, peer):
        return pltpu.make_async_remote_copy(
            src_ref=ref,
            dst_ref=self.out.at[self.at.c, w, n],
            send_sem=sem,
            recv_sem=self.recv.at[0, n],
            device_id=peer,
            device_id_type=MESH,
        )

    def along(self, k):
        at = self.at
        return self.copy(self.src, at.w, self.n0, self.send_along.at[0], {"wide": self.other(k)})

    def second(self):
        at = self.at
        ref = self.column(at.c, self.n1)
        return pltpu.make_async_remote_copy(
            src_ref=ref,
            dst_ref=ref,
            send_sem=self.send_along.at[1],
            recv_sem=self.recv.at[0, self.n1],
            device_id=at.chip(at.w, 1 - at.a0, at.b0),
            device_id_type=MESH,
        )

    def arrived_all(self, n, count=None):
        self.all_of(self.column(self.at.c, n, count), self.send.at[0], self.recv.at[0, n]).wait_recv()

    def side(self, n):
        at = self.at
        ref = self.column(at.c, n)
        return pltpu.make_async_remote_copy(
            src_ref=ref,
            dst_ref=ref,
            send_sem=self.send.at[2],
            recv_sem=self.recv_side.at[0],
            device_id=at.sibling(),
            device_id_type=MESH,
        )

    def depth(self, d):
        at = self.at
        if d == 1:
            self.arrived_all(self.n0, at.W - 1)
            for k in self.order()[::-1]:
                self.neighbours(self.other(k), False)
            self.keep.wait()
            self.side(self.n0).start()
        if d == 2:
            self.arrived_all(self.n1)
            self.second().start()
            self.side(self.n1).start()
            self.arrived_all(self.n2)
            self.side(self.n2).start()
        if d == 3:
            self.arrived_all(self.n3)
            self.side(self.n3).start()

    def finish(self):
        at = self.at
        far = self.column(at.c, self.n0, at.W - 1)
        self.all_of(far, self.send_along.at[0], self.recv.at[0, 0]).wait_send()
        for k in range(2):
            self.all_of(
                self.column(at.c, self.n0), self.send.at[k], self.recv.at[0, 0]
            ).wait_send()
        self.second().wait_send()
        self.all_of(self.out.at[at.c], self.send.at[2], self.recv.at[0, 0]).wait_send()
        self.all_of(self.out.at[1 - at.c], self.send.at[2], self.recv_side.at[0]).wait_recv()


GATHER_SEMS = 5


def gather_sems(wide, narrow):
    dma = pltpu.SemaphoreType.DMA
    return [dma((wide,)), dma((2 + narrow,)), dma((wide, narrow)), dma((narrow,)), dma]


class ScatterStream:
    def __init__(self, at, src, out, own, side, first, second, fin, sems):
        self.at, self.src, self.out = at, src, out
        self.own, self.side, self.first, self.second, self.fin = own, side, first, second, fin
        self.local, self.side_sem, self.first_sem, self.second_sem, self.home_sem, self.fin_sem = sems
        self.n0 = at.narrow_of(at.a0, at.b0)
        self.n1 = at.narrow_of(at.a0, 1 - at.b0)

    def remote(self, src, dst, sems, index, device):
        return pltpu.make_async_remote_copy(
            src_ref=src,
            dst_ref=dst,
            send_sem=sems.at[(0,) + index],
            recv_sem=sems.at[(1,) + index],
            device_id=device,
            device_id_type=MESH,
        )

    def side_copy(self, n):
        at = self.at
        return self.remote(
            self.src.at[1 - at.c, :, n], self.side.at[:, n], self.side_sem, (n,), at.sibling()
        )

    def own_copy(self):
        return pltpu.make_async_copy(self.src.at[self.at.c], self.own, self.local)

    def first_copy(self, b):
        at = self.at
        return self.remote(
            self.own.at[:, at.narrow_of(1 - at.a0, b)],
            self.first.at[b],
            self.first_sem,
            (b,),
            at.chip(at.w, 1 - at.a0, at.b0),
        )

    def second_copy(self):
        at = self.at
        return self.remote(
            self.own.at[:, self.n1],
            self.second,
            self.second_sem,
            (),
            at.chip(at.w, at.a0, 1 - at.b0),
        )

    def home_copy(self, w):
        at = self.at
        return pltpu.make_async_remote_copy(
            src_ref=self.own.at[w, self.n0],
            dst_ref=self.fin.at[at.w % (at.W // 2), at.c],
            send_sem=self.home_sem.at[w],
            recv_sem=self.fin_sem.at[at.w % (at.W // 2), at.c],
            device_id={"wide": w, "rep": at.group},
            device_id_type=MESH,
        )

    def elsewhere(self, w):
        return (w != self.at.w) | (self.at.c != self.at.group)

    def start(self):
        at = self.at
        self.own_copy().start()
        other = 1 - at.c
        a1, b1 = at.digits(other)
        for a, b in ((1 - a1, 1 - b1), (1 - a1, b1), (a1, 1 - b1), (a1, b1)):
            self.side_copy(at.narrow_of(a, b, other)).start()

    def stage_first(self):
        at = self.at
        self.own_copy().wait()
        for b in (1 - at.b0, at.b0):
            n = at.narrow_of(1 - at.a0, b)
            self.side_copy(n).wait_recv()

            def body(w, carry, n=n):
                self.own[w, n] = (self.own[w, n].astype(F32) + self.side[w, n].astype(F32)).astype(BF)
                return carry

            lax.fori_loop(0, at.W, body, 0)
            self.first_copy(b).start()

    def stage_second(self):
        at = self.at
        self.side_copy(self.n1).wait_recv()
        self.first_copy(1 - at.b0).wait_recv()

        def body(w, carry):
            value = self.own[w, self.n1].astype(F32) + self.side[w, self.n1].astype(F32)
            self.own[w, self.n1] = (value + self.first[1 - at.b0, w].astype(F32)).astype(BF)
            return carry

        lax.fori_loop(0, at.W, body, 0)
        self.second_copy().start()

    def stage_home(self):
        at = self.at
        n = self.n0
        self.side_copy(n).wait_recv()
        self.first_copy(at.b0).wait_recv()
        self.second_copy().wait_recv()

        def body(k, carry):
            w = lax.rem(at.w + at.W // 2 + k, at.W)
            value = self.own[w, n].astype(F32) + self.side[w, n].astype(F32)
            value = value + self.first[at.b0, w].astype(F32) + self.second[w].astype(F32)
            self.own[w, n] = value.astype(BF)

            @pl.when(self.elsewhere(w))
            def _():
                self.home_copy(w).start()

            @pl.when(jnp.logical_not(self.elsewhere(w)))
            def _():
                self.fin[at.w % (at.W // 2), at.c] = value.astype(BF)

            return carry

        lax.fori_loop(0, at.W, body, 0)

    def finish(self):
        at = self.at
        half = at.W // 2
        for h in range(2):
            total = None
            for k in range(half):

                @pl.when((at.c * half + k != at.w) | (at.c != h))
                def _(k=k, h=h):
                    pltpu.make_async_remote_copy(
                        src_ref=self.fin.at[k, h],
                        dst_ref=self.fin.at[k, h],
                        send_sem=self.home_sem.at[0],
                        recv_sem=self.fin_sem.at[k, h],
                        device_id=at.sibling(),
                        device_id_type=MESH,
                    ).wait_recv()

                value = self.fin[k, h].astype(F32)
                total = value if total is None else total + value
            self.out[h][...] = total
        for n in range(at.N):
            self.side_copy(n).wait_send()
        for b in range(2):
            self.first_copy(b).wait_send()
        self.second_copy().wait_send()

        def homes(w, carry):
            @pl.when(self.elsewhere(w))
            def _():
                self.home_copy(w).wait_send()

            return carry

        lax.fori_loop(0, at.W, homes, 0)


SCATTER_REFS = 11


def scatter_scratch(wide, narrow, form):
    sizes = ((wide, narrow), (wide, narrow), (2, wide), (wide,), (wide // 2, 2))
    dma = pltpu.SemaphoreType.DMA
    buffers = [pltpu.VMEM(size + form, BF) for size in sizes]
    return buffers + [dma, dma((2, narrow)), dma((2, 2)), dma((2,)), dma((wide,)), dma((wide // 2, 2))]


def scatter_greetings(at):
    out = [
        at.chip(at.w, at.a0, 1 - at.b0),
        at.chip(at.w, 1 - at.a0, at.b0),
        at.sibling(),
    ]
    more = []
    for k in range(at.W // 2):
        for h in range(2):
            w = at.c * (at.W // 2) + k
            more.append(((w != at.w) | (at.c != h), {"rep": h, "wide": w}))
    return out, more


def place_columns(slabs, cols):
    feature = lax.broadcasted_iota(jnp.int32, (D, slabs * SIDE), 0)
    column = lax.broadcasted_iota(jnp.int32, (D, slabs * SIDE), 1)
    lane = column % SIDE
    return jnp.where((feature == column // SIDE * cols + lane) & (lane < cols), 1.0, 0.0).astype(BF)


def view_half(ref, layer, half, width, natural):
    if natural:
        return ref.at[layer, :, pl.ds(pl.multiple_of(half * width, width), width)]
    return ref.at[layer, half]


def column_parts(ref, count):
    width = ref.shape[-1] // count
    lead = (slice(None),) * (len(ref.shape) - 1)
    return [ref.at[lead + (slice(k * width, (k + 1) * width),)] for k in range(count)]


def prepare_kernel(wide, narrow, natural, *refs):
    take = iter(refs)

    def some(n):
        return [next(take) for _ in range(n)]

    ids, live, tables, attention, feed, vectors = some(6)
    attn_low, feed_low, attn_out, misc_out, aux, scalars = some(6)
    full_tables, vec = some(2) if natural else (None, None)
    misc, misc_low, packed, moved, move_sems = some(5)
    streams = [some(GATHER_SEMS) for _ in range(2)]
    at = Place(wide, narrow)
    seq = ids.shape[1]
    table_rows, cols = tables.shape[1], vectors.shape[1]

    to_core, to_wide = at.w % 2, at.c * (wide // 2) + at.w // 2
    from_wide = 2 * (at.w % (wide // 2)) + at.c
    leaves = (to_core != at.c) | (to_wide != at.w)
    greet(gather_greetings(at), [(leaves, {"rep": at.group, "wide": from_wide})])()
    packed[...] = ids[...] + V * live[...]
    move = pltpu.make_async_remote_copy(
        src_ref=packed,
        dst_ref=moved,
        send_sem=move_sems.at[0],
        recv_sem=move_sems.at[1],
        device_id={"rep": to_core, "wide": to_wide},
        device_id_type=MESH,
    )
    stay = pltpu.make_async_copy(packed, moved, move_sems.at[0])
    pl.when(leaves)(move.start)
    pl.when(jnp.logical_not(leaves))(stay.start)

    position = lax.broadcasted_iota(jnp.int32, live.shape, 1)
    tally = jnp.sum(jnp.where(position > 0, live[...], 0).astype(F32), 1, keepdims=True)
    tally = jnp.sum(tally, 0, keepdims=True)
    high = jnp.floor(tally / 64.0)
    lane = lax.broadcasted_iota(jnp.int32, (1, SIDE), 1)
    misc[...] = jnp.zeros_like(misc)
    misc[0:table_rows, 0:D] = tables[at.c]
    misc[0:VEC, D : D + cols] = vectors[...]
    misc[COUNT_ROW : COUNT_ROW + 1, D:] = jnp.where(
        lane == 0, high, jnp.where(lane == 1, tally - 64.0 * high, 0.0)
    )
    misc_low[...] = misc[...].astype(BF)
    attn_low[...] = attention[...].astype(BF)
    small = GatherStream(at, misc_low, misc_out, *streams[0])
    attn = GatherStream(
        at, view_half(attn_low, 0, at.c, 2 * D, natural), attn_out, *streams[1]
    )
    small.start()
    attn.start()
    feed_low[...] = feed[...].astype(BF)

    pl.when(leaves)(move.wait)
    pl.when(jnp.logical_not(leaves))(stay.wait)
    live_at = lax.broadcasted_iota(jnp.int32, (8, seq), 1)
    row_at = lax.broadcasted_iota(jnp.int32, (8, seq), 0)
    start = 0
    for r, length in ((0, seq), (1, BLK)):
        row = moved[r : r + 1]
        after = jnp.concatenate([row[:, 1:], row[:, :1]], 1)
        weight = jnp.where(live_at[0:1] < seq - 1, after // V, 0)
        info = jnp.where(
            row_at == 0, row % V, jnp.where(row_at == 1, after % V, jnp.where(row_at == 2, weight, 0))
        )
        aux[start : start + length] = info[:, :length].astype(F32).T
        start += length
    for stream, d in (
        (small, 1),
        (attn, 1),
        (small, 2),
        (attn, 2),
        (small, 3),
    ):
        stream.depth(d)
    small.finish()
    sides = [
        sum(
            misc_out[h, w, n, :, D:].astype(F32) for w in range(wide) for n in range(narrow)
        )
        for h in range(2)
    ]
    counts = [
        side[COUNT_ROW : COUNT_ROW + 1, 0:1] * 64.0 + side[COUNT_ROW : COUNT_ROW + 1, 1:2]
        for side in sides
    ]
    mine = jnp.where(at.group == 0, counts[0], counts[1])
    line = lax.broadcasted_iota(jnp.int32, (8, 128), 0)
    kept = jnp.where(at.c == 0, counts[0], counts[1])
    scalars[...] = jnp.where(line == 0, kept, jnp.where(line == 1, 1.0 / (mine * LOG_TWO), 0.0))
    if natural:
        for h in range(2):
            for w in range(wide):
                for n in range(narrow):
                    s = w * narrow + n
                    full_tables[h, s * table_rows : (s + 1) * table_rows] = misc_out[
                        h, w, n, :table_rows, :D
                    ]
        blocks = [misc_out[0, w, n, :, D:] for w in range(wide) for n in range(narrow)]
        spread = mm(jnp.concatenate(blocks, 1), place_columns(wide * narrow, cols), NT)
        vec[...] = spread[: vec.shape[0]]
    attn.depth(3)
    attn.finish()


def prepare(ids, live, tables, attention, feed, vectors, wide, narrow, natural):
    vm = pl.BlockSpec(memory_space=pltpu.VMEM)
    anywhere = pl.BlockSpec(memory_space=pl.ANY)
    seq = ids.shape[1]
    half_form = attention.shape[1:] if natural else attention.shape[2:]
    half_form = (half_form[0], 2 * D) if natural else half_form
    misc = (MISC_ROWS, MISC_COLS)
    outs = [
        (attention.shape, BF, vm),
        (feed.shape, BF, vm),
        ((2, wide, narrow) + half_form, BF, anywhere),
        ((2, wide, narrow) + misc, BF, vm),
        ((seq + BLK, 8), F32, vm),
        ((8, 128), F32, vm),
    ]
    if natural:
        outs += [((2, V, D), BF, vm), ((24, D), F32, vm)]
    return pl.pallas_call(
        functools.partial(prepare_kernel, wide, narrow, natural),
        in_specs=[vm] * 6,
        out_specs=[spec for _, _, spec in outs],
        out_shape=[jax.ShapeDtypeStruct(shape, kind) for shape, kind, _ in outs],
        scratch_shapes=[
            pltpu.VMEM(misc, F32),
            pltpu.VMEM(misc, BF),
            pltpu.VMEM(ids.shape, jnp.int32),
            pltpu.VMEM(ids.shape, jnp.int32),
            pltpu.SemaphoreType.DMA((2,)),
        ]
        + gather_sems(wide, narrow) * 2,
        compiler_params=params(VMEM_MIB, collective_id=1, has_side_effects=True),
        name="prepare",
    )(ids, live, tables, attention, feed, vectors)


def halves_of(ref, layer, width, natural):
    if natural:
        return [ref.at[layer, :, h * width : (h + 1) * width] for h in range(2)]
    return [ref.at[layer, h] for h in range(2)]


def adam_update(weight, moment, square, gradient, decay, rate):
    moment = BETA_ONE * moment + (1.0 - BETA_ONE) * gradient
    square = BETA_TWO * square + (1.0 - BETA_TWO) * gradient * gradient
    fixed_moment = moment / (1.0 - BETA_ONE**STEP)
    fixed_square = square / (1.0 - BETA_TWO**STEP)
    delta = -rate * (fixed_moment / (jnp.sqrt(fixed_square) + ADAM_EPS) + decay * weight)
    return (moment, square, delta)


DECAYS = (DECAY, DECAY, DECAY, 0.0)
RATES = (RATE_TABLE, RATE, RATE, RATE_TABLE)
SUMMED = ((1, 1), (2, 1), (2, 0))


def sum_stages(wide, narrow):
    if wide * narrow <= 16:
        return wide * narrow - 1
    return narrow - 1 + wide.bit_length() - 1


def sum_rounds(at):
    W, N = at.W, at.N
    if W * N <= 16:
        peers = []
        for k in range(1, W * N):
            device = {"wide": lax.rem(at.w + k // N, W), "narrow": lax.rem(at.n + k % N, N)}
            peers.append((k - 1, device))
        rounds = [peers]
    else:
        rounds = [[(k, {"narrow": lax.rem(at.n + 1 + k, N)}) for k in range(N - 1)]]
        slot, unit = N - 1, 1
        while unit < W:
            rounds.append([(slot, {"wide": at.w + unit * (1 - 2 * ((at.w // unit) % 2))})])
            slot += 1
            unit *= 2
    return [device for peers in rounds for _, device in peers], rounds


def ordered_sum(at, peers, total, arrived):
    if len(peers) == 1:
        return total + arrived[peers[0][0]]
    whole = len(peers) + 1 == at.W * at.N
    values = [(at.w * at.N + at.n if whole else at.n, total)]
    for slot, _ in peers:
        k = slot + 1
        if whole:
            source = lax.rem(at.w + at.W - k // at.N, at.W) * at.N
            source = source + lax.rem(at.n + at.N - k % at.N, at.N)
        else:
            source = lax.rem(at.n + at.N - k, at.N)
        values.append((source, arrived[slot]))
    out = None
    for index in range(len(values)):
        value = jnp.zeros_like(total)
        for source, piece in values:
            value = jnp.where(source == index, piece, value)
        out = value if out is None else out + value
    return out


def pack_misc(at, d_tables, row_sums, rows, packed, cols):
    short_rows, feed_rows, attn_rows = row_sums
    rows[0:2] = short_rows[0:2]
    rows[2:4] = attn_rows[0:2]
    rows[4:7] = feed_rows[0:3]
    rows[7:12] = short_rows[2:7]
    rows[BETA_ROW : BETA_ROW + CHUNKS] = feed_rows[3 : 3 + CHUNKS]
    rows[BETA_ROW + CHUNKS : REL_ROW] = short_rows[7 : 7 + CHUNKS]
    rows[REL_ROW : REL_ROW + 1] = attn_rows[2:3] + short_rows[11:12]
    rows[VEC:] = jnp.zeros((rows.shape[0] - VEC, D), F32)
    tall = jnp.concatenate([rows[...], jnp.zeros((MISC_ROWS - rows.shape[0], D), F32)], 0).astype(BF)
    spread = mm(tall, place_columns(at.W * at.N, cols)).astype(BF)
    count = V // (at.W * at.N)
    for w in range(at.W):
        for n in range(at.N):
            s = w * at.N + n
            for h in range(2):
                packed[h, w, n, :count, :D] = d_tables[h][s * count : (s + 1) * count].astype(BF)
                packed[h, w, n, count:, :D] = jnp.zeros((MISC_ROWS - count, D), BF)
            packed[0, w, n, :, D:] = spread[:, s * SIDE : (s + 1) * SIDE]
            packed[1, w, n, :, D:] = jnp.zeros((MISC_ROWS, SIDE), BF)


def reduce_kernel(wide, narrow, natural, *refs):
    at = Place(wide, narrow)
    take = iter(refs)

    def some(n):
        return [next(take) for _ in range(n)]

    if natural:
        d_tables, row_sums = some(2), some(3)
    else:
        d_misc = next(take)
    d_attn, ready, bits = next(take), some(3), next(take)
    hbm_states = some(12)
    grads, deltas, scalars = some(4), some(4), next(take)
    states, state_sems = some(12), next(take)
    misc_sum, bits_in, bits_sem = some(3)
    sums, arrived, sum_sems = some(3)
    mine, other, delta_sems = some(4), some(4), next(take)
    if natural:
        misc_rows, d_misc = some(2)
    greetings, rounds = sum_rounds(at)
    devices, more = scatter_greetings(at)
    all_here = greet(devices + greetings, more)

    tiny = pltpu.make_async_remote_copy(
        src_ref=bits,
        dst_ref=bits_in,
        send_sem=bits_sem.at[0],
        recv_sem=bits_sem.at[1],
        device_id=at.sibling(),
        device_id_type=MESH,
    )
    attn_views = halves_of(grads[1], 0, 2 * D, natural)
    attn_outs = list(zip(*(column_parts(view, 2) for view in attn_views)))
    streams = []
    for source, out in list(zip(column_parts(d_attn, 2), attn_outs)) + [(d_misc, halves_out(misc_sum))]:
        part = some(SCATTER_REFS)
        streams.append(ScatterStream(at, source, out, *part[:5], part[5:]))
    one, two, small = streams
    all_here()
    one.start()
    two.start()
    tiny.start()
    if natural:
        pack_misc(at, d_tables, row_sums, misc_rows, d_misc, grads[3].shape[1])
    small.start()
    loads = [
        pltpu.make_async_copy(src, dst, state_sems.at[i])
        for i, (src, dst) in enumerate(zip(hbm_states, states))
    ]
    for load in loads:
        load.start()
    one.stage_first()
    views = attn_views
    for (which, layer), source in zip(SUMMED, ready):
        targets = halves_of(grads[which], layer, 2 * D if which == 1 else FF, natural)
        views += targets
        for half in range(2):
            targets[half][...] = source[half]
    two.stage_first()
    small.stage_first()
    one.stage_second()
    two.stage_second()
    one.stage_home()
    small.stage_second()
    two.stage_home()
    small.stage_home()
    for stream in streams:
        stream.finish()
    tiny.wait()

    table_rows, columns = grads[0].shape[1], grads[3].shape[1]
    for layer in range(2):
        grads[0][layer] = misc_sum[layer, :table_rows, :D]
    grads[3][...] = misc_sum[0, :VEC, D : D + columns]
    squared = jnp.zeros((1, 1), F32)
    for ref in halves_out(misc_sum) + views:
        value = ref[...]
        value = jnp.sum(value * value, 0, keepdims=True)
        squared = squared + jnp.sum(value, 1, keepdims=True)
    row = lax.broadcasted_iota(jnp.int32, (8, 128), 0)
    lost = jnp.where(at.c == at.group, bits[...] + bits_in[...], 0.0)
    total = jnp.where(row == 0, squared, jnp.where(row == 1, lost, 0.0))
    for peers in rounds:
        copies = []
        for k, partner in peers:
            sums[k] = total
            copies.append(
                pltpu.make_async_remote_copy(
                    src_ref=sums.at[k],
                    dst_ref=arrived.at[k],
                    send_sem=sum_sems.at[0, k],
                    recv_sem=sum_sems.at[1, k],
                    device_id=partner,
                    device_id_type=MESH,
                )
            )
        for copy in copies:
            copy.start()
        for copy in copies:
            copy.wait()
        total = ordered_sum(at, peers, total, arrived)
    norm = jnp.sqrt(total[0:1, 0:1])
    factor = jnp.minimum(1.0, CLIP_AT / (norm + 1e-06))
    scalars[...] = jnp.where(row == 0, norm, jnp.where(row == 2, factor, total))
    for load in loads:
        load.wait()

    copies = [
        pltpu.make_async_remote_copy(
            src_ref=mine[which],
            dst_ref=other[which],
            send_sem=delta_sems.at[0, which],
            recv_sem=delta_sems.at[1, which],
            device_id=at.sibling(),
            device_id_type=MESH,
        )
        for which in range(4)
    ]
    order = (2, 1, 0, 3)
    for which in order:
        refs_of = [states[which], states[4 + which], states[8 + which], grads[which], mine[which]]
        if which in (1, 2):
            width = 2 * D if which == 1 else FF
            views = [[ref.at[l] for ref in refs_of] for l in range(2)]
            if natural:
                views = [
                    [ref.at[l, :, h * width : (h + 1) * width] for ref in refs_of]
                    for l in range(2)
                    for h in range(2)
                ]
        else:
            views = [refs_of]
        for weight, moment, square, gradient, target in views:
            _, _, delta = adam_update(
                weight[...],
                moment[...],
                square[...],
                gradient[...] * factor,
                DECAYS[which],
                RATES[which],
            )
            target[...] = delta.astype(target.dtype)
        copies[which].start()
    for which in order:
        copies[which].wait()
        deltas[which][...] = (mine[which][...].astype(F32) + other[which][...].astype(F32)) * 0.5


def reduce_all(small, d_attn, ready, bits, states, wide, narrow, natural, collective_id):
    vm = pl.BlockSpec(memory_space=pltpu.VMEM)
    anywhere = pl.BlockSpec(memory_space=pl.ANY)
    like = [jax.ShapeDtypeStruct(x.shape, F32) for x in states[:4]]
    kinds = [BF if x.shape[-2] % 16 == 0 else F32 for x in states[:4]]
    exchanged = [pltpu.VMEM(x.shape, kind) for x, kind in zip(states[:4], kinds)]
    dma = pltpu.SemaphoreType.DMA
    stages = sum_stages(wide, narrow)
    misc = (MISC_ROWS, MISC_COLS)
    scratch = [pltpu.VMEM(x.shape, F32) for x in states] + [dma((12,))]
    scratch += [pltpu.VMEM((2,) + misc, F32), pltpu.VMEM(bits.shape, F32), dma((2,))]
    scratch += [pltpu.VMEM((stages, 8, 128), F32)] * 2 + [dma((2, stages))]
    scratch += exchanged + exchanged + [dma((2, 4))]
    if natural:
        scratch += [pltpu.VMEM((24, D), F32), pltpu.VMEM((2, wide, narrow) + misc, BF)]
    for form in (half_width(d_attn), half_width(d_attn), misc):
        scratch += scatter_scratch(wide, narrow, form)
    return pl.pallas_call(
        functools.partial(reduce_kernel, wide, narrow, natural),
        in_specs=[vm if natural else anywhere] * len(small)
        + [anywhere]
        + [vm] * 4
        + [anywhere] * 12,
        out_specs=[vm] * 9,
        out_shape=like + like + [jax.ShapeDtypeStruct((8, 128), F32)],
        scratch_shapes=scratch,
        compiler_params=params(VMEM_MIB, collective_id=collective_id, has_side_effects=True),
        name="reduce_all",
    )(*small, d_attn, *ready, bits, *states)


def update_kernel(scalars, totals, counted, *refs):
    grads, deltas, weights, moments, squares, outers, averages = (
        refs[4 * k : 4 * k + 4] for k in range(7)
    )
    new_m, new_s, new_w, new_o, new_a = (refs[28 + 4 * k : 32 + 4 * k] for k in range(5))
    factor = scalars[2:3, 0:1]
    loss, count, norm = refs[48:]
    loss[0] = totals[1, 0]
    count[0] = counted[0, 0]
    norm[0] = totals[0, 0]
    for which in range(4):
        moment, square, _ = adam_update(
            weights[which][...],
            moments[which][...],
            squares[which][...],
            grads[which][...] * factor,
            DECAYS[which],
            RATES[which],
        )
        put_moment(new_m[which], moment)
        put_moment(new_s[which], square)
        delta = deltas[which][...]
        outer = OUTER_MOM * outers[which][...] + delta
        weight = weights[which][...] + OUTER_RATE * (delta + OUTER_MOM * outer)
        new_o[which][...] = outer
        new_w[which][...] = weight
        new_a[which][...] = EVAL_KEEP * averages[which][...] + (1.0 - EVAL_KEEP) * weight


def put_moment(ref, value):
    if len(ref.shape) == 3 and value.ndim == 2:
        for r in range(value.shape[0]):
            ref[r] = value[r : r + 1]
    else:
        ref[...] = value


def update(totals, counted, grads, deltas, arrays):
    weights = arrays[:4]
    rows = weights[1].shape[1]

    def quarter(width):
        return pl.BlockSpec((1, rows, width // 4), lambda i: (i // 4, 0, i % 4))

    specs = [
        pl.BlockSpec((1,) + weights[0].shape[1:], lambda i: (i // 4, 0, 0)),
        quarter(4 * D),
        quarter(2 * FF),
        pl.BlockSpec(weights[3].shape, lambda i: (0, 0)),
    ]
    like = [jax.ShapeDtypeStruct(x.shape, F32) for x in weights]
    vec_rows, cols = weights[3].shape
    lined = (vec_rows, 1, cols)
    own_specs = specs[:3] + [pl.BlockSpec(lined, lambda i: (0, 0, 0))]
    own_like = like[:3] + [jax.ShapeDtypeStruct(lined, F32)]
    scalar = pl.BlockSpec(memory_space=pltpu.SMEM)
    *new, loss, count, norm = pl.pallas_call(
        update_kernel,
        grid=(8,),
        in_specs=[pl.BlockSpec((8, 128), lambda i: (0, 0)), scalar, scalar] + specs * 7,
        out_specs=own_specs * 2 + specs * 3 + [scalar] * 3,
        out_shape=own_like * 2 + like * 3 + [jax.ShapeDtypeStruct((1,), F32)] * 3,
        compiler_params=params(VMEM_MIB),
        name="update",
    )(totals, totals, counted, *grads, *deltas, *arrays)
    for k in (3, 7):
        new[k] = new[k].transpose(1, 0, 2)
    new = [x[None] if k < 8 and k % 4 != 3 else x for k, x in enumerate(new)]
    return (loss, count, norm, *new)


def pad_to(x, rows, cols):
    return jnp.pad(x, [(0, 0)] * (x.ndim - 2) + [(0, rows - x.shape[-2]), (0, cols - x.shape[-1])])


def per_device(wide, narrow, byte_ids, live_mask, *arrays):
    tables, attention, feed_forward, vectors = arrays[:4]
    rows, table_rows, cols = attention.shape[1], tables.shape[1], vectors.shape[1]
    seq = byte_ids.shape[1]
    long_blocks = seq // BLK
    natural = rows % 16 == 0
    place = (2, wide, narrow)

    def formed(k, x):
        if natural or k % 4 not in (1, 2):
            return x
        half = x.shape[-1] // 2
        return x.reshape(2, rows, 2, half).swapaxes(1, 2).reshape((2, 2) + slab_form(rows, half))

    def unformed(k, x):
        if natural or k % 4 not in (1, 2):
            return x
        return x.reshape(2, 2, rows, -1).swapaxes(1, 2).reshape(arrays[k].shape)

    def slabs_of(d):
        return d.reshape(place + slab_form(rows, d.shape[-1]))

    arrays = [x[0] if 4 <= k < 12 else x for k, x in enumerate(arrays)]
    states = [formed(k, x) for k, x in enumerate(arrays[:12])]
    attn_low, feed_low, attn, misc, aux, scalars, *more = prepare(
        byte_ids, live_mask, tables, states[1], states[2], vectors, wide, narrow, natural
    )
    if natural:
        full_tables, vec = more
    else:
        full_tables = misc[:, :, :, :table_rows, :D].reshape(2, V, D)
        side = misc[0, :, :, :VEC, D : D + cols].astype(F32).reshape(-1, VEC, cols)
        vec = pad_to(side.transpose(1, 0, 2).reshape(VEC, D), 24, D)
    attn = attn.reshape(2, D, 2 * D)
    x1, middle, q, k, v, ot, lse, act, slope, feed, short_attn, short_feed = full_forward(
        aux, full_tables, attn, attn_low, feed_low, vec, long_blocks, wide, narrow, natural
    )
    feed = feed.reshape(2, D, FF)
    d_x1, d_short_attn, d_short_feed, d_head, short_rows, bits = middle_stage(
        x1,
        aux,
        full_tables,
        short_attn.reshape(2, D, 2 * D),
        short_feed.reshape(2, D, FF),
        vec,
        scalars,
        seq,
    )
    d_middle, d_feed, feed_rows, sum_short_attn = feed_back(
        d_x1, act, slope, middle, feed, vec, slabs_of(d_short_attn), wide, narrow
    )
    d_attn, d_embed, attn_rows, sum_short_feed, sum_feed = attention_back(
        d_middle,
        aux,
        ot,
        lse,
        q,
        k,
        v,
        full_tables,
        attn,
        vec,
        slabs_of(d_short_feed),
        slabs_of(d_feed),
        long_blocks,
        wide,
        narrow,
    )
    if natural:
        small = (d_embed, d_head, short_rows, feed_rows, attn_rows)
    else:
        d_vec = jnp.concatenate(
            [
                short_rows[0:2],
                attn_rows[0:2],
                feed_rows[0:3],
                short_rows[2:7],
                feed_rows[3 : 3 + CHUNKS],
                short_rows[7 : 7 + CHUNKS],
                attn_rows[2:3] + short_rows[11:12],
            ],
            0,
        )
        side = pad_to(d_vec.reshape(VEC, -1, cols).transpose(1, 0, 2), MISC_ROWS, SIDE)
        halves = [
            jnp.concatenate([pad_to(d.reshape(-1, table_rows, D), MISC_ROWS, D), extra], -1)
            for d, extra in ((d_embed, side), (d_head, jnp.zeros_like(side)))
        ]
        small = (jnp.stack(halves).astype(BF).reshape(place + (MISC_ROWS, MISC_COLS)),)
    *sums, totals = reduce_all(
        small,
        slabs_of(d_attn),
        (sum_short_attn, sum_short_feed, sum_feed),
        bits,
        states,
        wide,
        narrow,
        natural,
        2,
    )
    grads = [unformed(k, x) for k, x in enumerate(sums[:4])]
    deltas = [unformed(k, x) for k, x in enumerate(sums[4:])]
    return update(totals, scalars, grads, deltas, arrays)


def solution(mesh):
    rows = P(("rep", "wide", "narrow"), None)
    split = (
        P(None, ("wide", "narrow"), None),
        P(None, ("wide", "narrow"), None),
        P(None, ("wide", "narrow"), None),
        P(None, ("wide", "narrow")),
    )
    own = tuple(P("rep", *spec) for spec in split)
    return jax.shard_map(
        functools.partial(per_device, mesh.shape["wide"], mesh.shape["narrow"]),
        mesh=mesh,
        in_specs=(rows, rows) + split + own + own + split + split,
        out_specs=(P("rep"),) * 3 + own + own + split * 3,
        check_vma=False,
    )
```

```python
import functools
import math

import jax
import jax.numpy as jnp
import numpy as np
from jax import lax
from jax.experimental import pallas as pl
from jax.experimental.pallas import tpu as pltpu
from jax.sharding import PartitionSpec as P

D = 512
HEADS = 8
HD = 64
FF = 2048
V = 256
NB = 32
STEP = 10
VEC = 21
EDGES = (1, 2, 3, 4, 5, 6, 7, 8, 10, 12, 14, 16, 20, 24, 28, 32, 40, 48, 64, 80, 96, 128, 160, 192)
EDGES = EDGES + (256, 320, 384, 512, 640, 768, 1024)
NEG = -1000000000.0
EPS = 1e-05
LOG_TWO = math.log(2.0)
RATE = 0.01
RATE_TABLE = 0.2
BETA_ONE = 0.9
BETA_TWO = 0.95
ADAM_EPS = 1e-08
DECAY = 0.1
CLIP_AT = 0.02
OUTER_RATE = 0.7
OUTER_MOM = 0.9
EVAL_KEEP = 0.9

TILE = 128
TOGETHER = 2
BETA_ROW = 12
REL_ROW = 12 + 2 * FF // D
CHUNKS = FF // D
PARTS = 1
WIDTH = FF // PARTS
VMEM_MIB = 63
BLK = 384
SUB = BLK // TILE
PAIRS = HEADS // 2
PW = 2 * HD
GELU_C = math.sqrt(2.0 / math.pi)
GELU_A = 0.044715

BF = jnp.bfloat16
F32 = jnp.float32
NN = (((1,), (0,)), ((), ()))
NT = (((1,), (1,)), ((), ()))
TN = (((0,), (0,)), ((), ()))


def mm(left, right, dims=NN):
    return lax.dot_general(left, right, dims, preferred_element_type=F32)


def spans(count):
    out = []
    for d in range(count):
        lo, hi = max(TILE * d - (TILE - 1), 0), TILE * d + TILE - 1
        base = sum(e <= lo for e in EDGES)
        out.append((base, [(e, k + 1) for k, e in enumerate(EDGES) if lo < e <= hi]))
    return out


def fold_matrix(count):
    rows = []
    for base, edges in spans(count):
        row = np.zeros(NB, np.float32)
        row[base] += 1
        rows.append(row)
        for _, bucket in edges:
            row = np.zeros(NB, np.float32)
            row[bucket] += 1
            row[bucket - 1] -= 1
            rows.append(row)
    out = np.zeros((HEADS, fold_rows(count), HEADS * NB), jnp.bfloat16)
    for h in range(HEADS):
        out[h, : len(rows), h * NB : (h + 1) * NB] = np.stack(rows)
    return out


def tile_distance(d):
    keys = lax.broadcasted_iota(jnp.int32, (TILE, TILE), 0)
    queries = lax.broadcasted_iota(jnp.int32, (TILE, TILE), 1)
    return TILE * d + queries - keys


def build_bias(rel, level, bias, count):
    for d, (base, edges) in enumerate(spans(count)):
        distance = tile_distance(d)

        def one_head(h, carry, d=d, base=base, edges=edges, distance=distance):
            first = level * HEADS * NB + h * NB
            tile = jnp.full((TILE, TILE), rel[REL_ROW, first + base], F32)
            for edge, bucket in edges:
                tile = jnp.where(distance >= edge, rel[REL_ROW, first + bucket], tile)
            if d == 0:
                tile = jnp.where(distance < 0, NEG, tile)
            bias[h, d] = tile
            return carry

        lax.fori_loop(0, HEADS, one_head, 0)


def fold_bias(tiles, sums, count):
    at = 0
    for d, (_, edges) in enumerate(spans(count)):
        distance = tile_distance(d)

        def one_head(h, carry, d=d, edges=edges, distance=distance, at=at):
            tile = tiles[h, d]
            sums[h, at : at + 1] = jnp.sum(tile, 0, keepdims=True)
            for n, (edge, _) in enumerate(edges):
                sums[h, at + 1 + n : at + 2 + n] = jnp.sum(
                    jnp.where(distance >= edge, tile, 0.0), 0, keepdims=True
                )
            return carry

        lax.fori_loop(0, HEADS, one_head, 0)
        at += 1 + len(edges)


def fold_rows(count):
    return -(-sum(1 + len(edges) for _, edges in spans(count)) // 8) * 8


def rel_row(tiles, sums, fold, count):
    sums[...] = jnp.zeros_like(sums)
    fold_bias(tiles, sums, count)
    whole = sums[...].reshape(-1, TILE)
    high = whole.astype(BF)
    low = (whole - high.astype(F32)).astype(BF)
    matrix = fold[...].reshape(-1, HEADS * NB)
    total = mm(high, matrix, TN) + mm(low, matrix, TN)
    return jnp.sum(total, 0, keepdims=True)


def norm_stats(x):
    centered = x - jnp.mean(x, -1, keepdims=True)
    rstd = lax.rsqrt(jnp.mean(centered * centered, -1, keepdims=True) + EPS)
    return centered * rstd, rstd


def norm_back(dy, xhat, rstd, gain):
    t = dy * gain
    dx = rstd * (
        t - jnp.mean(t, -1, keepdims=True) - xhat * jnp.mean(t * xhat, -1, keepdims=True)
    )
    return dx, jnp.sum(dy * xhat, 0, keepdims=True), jnp.sum(dy, 0, keepdims=True)


def gelu_pair(u):
    square = u * u
    tanh = jnp.tanh(GELU_C * u * (1.0 + GELU_A * square))
    half = 0.5 * (1.0 + tanh)
    slope = half + 0.5 * u * (1.0 - tanh * tanh) * (GELU_C + 3.0 * GELU_C * GELU_A * square)
    return u * half, slope


def split_heads(pair):
    lane = lax.broadcasted_iota(jnp.int32, (TILE, pair.shape[1]), 1)
    parts = []
    for qa in range(pair.shape[0] // TILE):
        rows = pair[qa * TILE : (qa + 1) * TILE]
        zero = jnp.zeros_like(rows)
        parts += [jnp.where(lane < HD, rows, zero), jnp.where(lane >= HD, rows, zero)]
    return jnp.concatenate(parts, 0)


def interleave(low, high):
    parts = []
    for at in range(0, low.shape[1], TILE):
        parts += [low[:, at : at + TILE], high[:, at : at + TILE]]
    return jnp.concatenate(parts, 1)


def merge_heads(both):
    parts = []
    for at in range(0, both.shape[1], 2 * TILE):
        parts.append(
            jnp.concatenate([both[:HD, at : at + TILE], both[HD:, at + TILE : at + 2 * TILE]], 0)
        )
    return jnp.concatenate(parts, 1)


def tile_products(keys, queries, diag, nq, nk):
    out = {}
    rows = [queries] if not diag else [queries[2 * TILE * kb :] for kb in range(nk)]
    if not diag:
        full = mm(keys, queries, NT)
    for kb in range(nk):
        line = slice(kb * TILE, (kb + 1) * TILE)
        first = kb if diag else 0
        block = mm(keys[line], rows[kb], NT) if diag else full[line]
        for qa in range(first, nq):
            for e in range(2):
                at = (2 * (qa - first) + e) * TILE
                out[kb, e, qa] = block[:, at : at + TILE]
    return out


def by_queries(left, tiles, diag, nq, nk):
    if not diag:
        return mm(left, whole_tiles(tiles, range(nk), range(nq)))
    return jnp.concatenate(
        [
            mm(left[:, : (qa + 1) * TILE], whole_tiles(tiles, range(qa + 1), (qa,)))
            for qa in range(nq)
        ],
        1,
    )


def by_keys(tiles, right, diag, nq, nk):
    if not diag:
        return mm(whole_tiles(tiles, range(nk), range(nq)), right)
    return jnp.concatenate(
        [
            mm(whole_tiles(tiles, (kb,), range(kb, nq)), right[2 * TILE * kb :])
            for kb in range(nk)
        ],
        0,
    )


def whole_tiles(tiles, key_tiles, query_tiles):
    return jnp.concatenate(
        [
            jnp.concatenate([tiles[kb, e, qa] for kb in key_tiles], 0)
            for qa in query_tiles
            for e in range(2)
        ],
        1,
    )


def column_of(qa, e):
    at = (2 * qa + e) * TILE
    return slice(at, at + TILE)


def softmax_step(keys, values_t, queries, bias, pair, far, diag, nq, nk, state):
    top, total, acc = state
    raw = tile_products(keys, queries, diag, nq, nk)
    scores = {
        (kb, e, qa): tile + bias[2 * pair + e, far + qa - kb] for (kb, e, qa), tile in raw.items()
    }
    order = [(qa, e) for qa in range(nq) for e in range(2)]
    highest = []
    for qa, e in order:
        column = [scores[kb, e, qa] for kb in range(nk) if (kb, e, qa) in scores]
        highest.append(jnp.max(functools.reduce(jnp.maximum, column), 0, keepdims=True))
    old_top = top[...]
    new_top = jnp.maximum(old_top, jnp.concatenate(highest, 1))
    alpha = jnp.exp(old_top - new_top)
    sums, probs = [], {}
    for qa, e in order:
        ceiling = new_top[:, column_of(qa, e)]
        adds = None
        for kb in range(nk):
            if (kb, e, qa) in scores:
                p = jnp.exp(scores[kb, e, qa] - ceiling)
                adds = p if adds is None else adds + p
                probs[kb, e, qa] = p.astype(BF)
        sums.append(jnp.sum(adds, 0, keepdims=True))
    top[...] = new_top
    total[...] = alpha * total[...] + jnp.concatenate(sums, 1)
    acc[...] = alpha * acc[...] + by_queries(values_t, probs, diag, nq, nk)


def softmax_start(state):
    top, total, acc = state
    top[...] = jnp.full(top.shape, NEG, F32)
    total[...] = jnp.zeros(total.shape, F32)
    acc[...] = jnp.zeros(acc.shape, F32)


def softmax_end(state):
    top, total, acc = state
    return merge_heads(acc[...] / total[...]).astype(BF), top[...] + jnp.log(total[...])


def score_back(
    keys, values, keys_t, queries, grads, logsum, inner, bias, pair, far, diag, nq, nk, tiles
):
    raw = tile_products(keys, queries, diag, nq, nk)
    d_p = tile_products(values, grads, diag, nq, nk)
    probs, scores = {}, {}
    for e in range(2):
        for diff in range(0 if diag else -(nk - 1), nq):
            total = None
            for kb in range(nk):
                qa = kb + diff
                if qa < 0 or qa >= nq:
                    continue
                cols = column_of(qa, e)
                p = jnp.exp(raw[kb, e, qa] + bias[2 * pair + e, far + diff] - logsum[:, cols])
                ds = p * (d_p[kb, e, qa] - inner[:, cols])
                total = ds if total is None else total + ds
                probs[kb, e, qa] = p.astype(BF)
                scores[kb, e, qa] = ds.astype(BF)
            tiles[2 * pair + e, far + diff] += total
    return (
        by_keys(probs, grads, diag, nq, nk),
        by_keys(scores, queries, diag, nq, nk),
        by_queries(keys_t, scores, diag, nq, nk),
    )


def beta_of(vec, level, part, width):
    row = BETA_ROW + level * CHUNKS + part * width // D
    return jnp.concatenate([vec[r : r + 1] for r in range(row, row + width // D)], 1)


def put_beta(rows, start, part, value, add):
    for k in range(WIDTH // D):
        row = start + part * WIDTH // D + k
        piece = value[:, k * D : (k + 1) * D]
        rows[row : row + 1] = rows[row : row + 1] + piece if add else piece


def one_hot(column):
    return column == lax.broadcasted_iota(jnp.int32, (column.shape[0], V), 1)


def full_forward_kernel(
    long_blocks,
    wide,
    narrow,
    natural,
    aux,
    embed,
    wts,
    attn_low,
    feed_low,
    vec,
    rel,
    x1_out,
    middle_out,
    q_out,
    k_out,
    v_out,
    ot_out,
    lse_out,
    act_out,
    slope_out,
    feed_out,
    short_attn_out,
    short_feed_out,
    bias,
    k_all,
    vt_all,
    middles,
    seconds,
    feed,
    feed_sem,
    *more,
):
    step = pl.program_id(0)
    blocks = pl.num_programs(0) // 3
    states = [more[3 * k : 3 * k + 3] for k in range(TOGETHER)]
    sems = more[3 * TOGETHER :]
    at = Place(wide, narrow)
    sources, targets = [], []
    for low, layer, width, out, count in (
        (feed_low, 0, FF, feed_out, 2),
        (attn_low, 1, 2 * D, short_attn_out, 1),
        (feed_low, 1, FF, short_feed_out, 2),
    ):
        sources += column_parts(view_half(low, layer, at.c, width, natural), count)
        targets += column_parts(out, count)
    feed_a, feed_b, short_attn, short_a, short_b = (
        HostedStream(
            at, source, out, *sems[GATHER_SEMS * k : GATHER_SEMS * (k + 1)]
        )
        for k, (source, out) in enumerate(zip(sources, targets))
    )
    loads = [
        pltpu.make_async_copy(source, target, feed_sem.at[k])
        for k, (source, target) in enumerate(zip(column_parts(feed_out, 2), column_parts(feed, 2)))
    ]

    def hop(stream, d):
        return lambda: stream.depth(d)

    events = {
        (1, 0): (hop(feed_a, 1),),
        (2, "dense"): (hop(feed_b, 1), hop(feed_a, 2)),
        (2, 0): (hop(short_attn, 1),),
        (2, 1): (hop(feed_a, 3), hop(feed_b, 2)),
        (3, "dense"): (hop(short_a, 1),),
        (3, 1): (hop(short_attn, 2),),
        (4, "end"): (hop(short_b, 1), hop(feed_b, 3)),
        (5, "end"): (hop(short_a, 2),),
        (6, "end"): (hop(short_attn, 3),),
        (8, "end"): (hop(short_b, 2),),
        (9, "end"): (hop(short_a, 3),),
        (10, "end"): (hop(short_b, 3),),
    }


    @pl.when(step == 0)
    def _():
        greet(gather_greetings(at))()
        for stream in (feed_a, feed_b, short_attn, short_a, short_b):
            stream.start()
        build_bias(rel, 0, bias, bias.shape[1])

    @pl.when(step < blocks)
    def _():
        hot = one_hot(aux[:, 0:1]).astype(BF)
        x = mm(hot, embed[0])
        xhat, _ = norm_stats(x)
        normed = (xhat * vec[2:3] + vec[3:4]).astype(BF)
        queries = (mm(normed, wts[0, :, :D]) * HD**-0.5).astype(BF)
        keys = mm(normed, wts[0, :, D : 2 * D]).astype(BF)
        values = mm(normed, wts[1, :, :D]).astype(BF)
        for pair in range(PAIRS):
            cols = slice(pair * PW, (pair + 1) * PW)
            q_out[0, pair] = queries[:, cols]
            k_out[0, pair] = keys[:, cols]
            v_out[0, pair] = values[:, cols]
            k_all[step, pair] = keys[:, cols]
            vt_all[step, pair] = values[:, cols].T
        middles[step] = x
        run_events(events, step, "dense")


    @pl.when(step < blocks)
    def _():
        first = jnp.where(step >= long_blocks, long_blocks, 0)

        def two_pairs(turn, carry):
            pairs = [turn * TOGETHER + k for k in range(TOGETHER)]
            both = [split_heads(q_out[0, pair]) for pair in pairs]
            for state in states:
                softmax_start(state)

            def with_block(j, far, diag):
                for pair, queries, state in zip(pairs, both, states):
                    softmax_step(
                        k_all[j, pair], vt_all[j, pair], queries, bias, pair, far, diag, SUB, SUB, state
                    )

            def earlier(j, inner):
                with_block(j, SUB * (step - j), False)
                return inner

            lax.fori_loop(first, step, earlier, 0)
            with_block(step, 0, True)
            for pair, state in zip(pairs, states):
                ot_out[0, pair], lse_out[0, pair] = softmax_end(state)
            run_events(events, step, turn)
            return carry

        lax.fori_loop(0, PAIRS // TOGETHER, two_pairs, 0)
        attended = ot_out[0].reshape(D, BLK).T
        middles[step] = middles[step] + mm(attended, wts[1, :, D : 2 * D])

    for k, stream in enumerate((feed_a, feed_b)):
        due = (k + 1) * blocks if natural else blocks

        @pl.when(step == due - 1)
        def _(k=k, stream=stream):
            stream.finish()
            loads[k].start()

        @pl.when(step == due)
        def _(k=k):
            loads[k].wait()

    def weight_half(half, cols):
        if natural:
            return feed[half, :, :, :, cols].reshape(D, cols.stop - cols.start)
        return feed[half].reshape(D, FF)[:, cols]

    def half_feed(block, k):
        width = FF // 2
        cols = slice(k * width, (k + 1) * width)
        up = weight_half(0, cols)
        active, slope = gelu_pair(mm(seconds[block], up) + beta_of(vec, 0, k, width))
        active = active.astype(BF)
        act_out[...] = active
        slope_out[...] = slope.astype(BF)
        return mm(active, weight_half(1, cols), NT)

    @pl.when((step >= blocks) & (step < 2 * blocks))
    def _():
        block = lax.rem(step, blocks)
        middle = middles[block]
        middle_out[...] = middle
        xhat, _ = norm_stats(middle)
        seconds[block] = (xhat * vec[4:5] + vec[5:6]).astype(BF)
        middles[block] = middle + vec[6:7] + half_feed(block, 0)

    @pl.when(step >= 2 * blocks)
    def _():
        block = lax.rem(step, blocks)
        x1_out[...] = middles[block] + half_feed(block, 1)

    run_events(events, step, "end")

    @pl.when(step == 3 * blocks - 1)
    def _():
        for stream in (short_attn, short_a, short_b):
            stream.finish()


def run_events(events, step, point):
    for (s, p), bodies in events.items():
        if isinstance(point, str) or isinstance(p, str):
            if point is not p and point != p:
                continue
            due = step == s
        else:
            due = (step == s) & (point == p)

        @pl.when(due)
        def _(bodies=bodies):
            for body in bodies:
                body()


def whole_spec(shape):
    return pl.BlockSpec(shape, lambda i: (0,) * len(shape), pipeline_mode=pl.Buffered(1))


def params(mib, **more):
    return pltpu.CompilerParams(vmem_limit_bytes=mib * 2**20, **more)


def state_scratch(n):
    return [pltpu.VMEM((1, 2 * n), F32), pltpu.VMEM((1, 2 * n), F32), pltpu.VMEM((PW, 2 * n), F32)]


def full_forward(aux, tables, wts, attn_low, feed_low, vec, long_blocks, wide, narrow, natural):
    tokens = aux.shape[0]
    blocks = tokens // BLK
    far = SUB * long_blocks
    form = feed_low.shape[1:] if natural else feed_low.shape[2:]
    form = (form[0], FF) if natural else form
    half = (form[0], form[1] * 2 * D // FF)

    def early(i):
        return jnp.minimum(i, blocks - 1)

    def late(i, phase):
        return jnp.clip(i - phase * blocks, 0, blocks - 1)

    def heads(n, width):
        return (
            jax.ShapeDtypeStruct((blocks, PAIRS, n, width), BF),
            pl.BlockSpec((1, PAIRS, n, width), lambda i: (early(i), 0, 0, 0)),
        )

    def flat(phase):
        return (
            jax.ShapeDtypeStruct((tokens, D), F32),
            pl.BlockSpec((BLK, D), lambda i: (late(i, phase), 0)),
        )

    def hidden():
        return (
            jax.ShapeDtypeStruct((tokens, FF), BF),
            pl.BlockSpec(
                (BLK, FF // 2),
                lambda i: (
                    lax.rem(jnp.maximum(i - blocks, 0), blocks),
                    jnp.maximum(i - blocks, 0) // blocks,
                ),
            ),
        )

    anywhere = pl.BlockSpec(memory_space=pl.ANY)
    outs = [flat(2), flat(1)] + [heads(BLK, PW)] * 3 + [heads(PW, BLK)]
    outs.append(
        (
            jax.ShapeDtypeStruct((blocks, PAIRS, 1, 2 * BLK), F32),
            pl.BlockSpec((1, PAIRS, 1, 2 * BLK), lambda i: (early(i), 0, 0, 0)),
        )
    )
    outs += [hidden(), hidden()]
    outs += [
        (jax.ShapeDtypeStruct((2, wide, narrow) + each, BF), anywhere) for each in (form, half, form)
    ]
    return pl.pallas_call(
        functools.partial(full_forward_kernel, long_blocks, wide, narrow, natural),
        grid=(3 * blocks,),
        in_specs=[
            pl.BlockSpec((BLK, aux.shape[1]), lambda i: (early(i), 0)),
            whole_spec((1, V, D)),
            whole_spec(wts.shape),
            anywhere,
            anywhere,
            whole_spec(vec.shape),
            pl.BlockSpec(memory_space=pltpu.SMEM),
        ],
        out_specs=[spec for _, spec in outs],
        out_shape=[shape for shape, _ in outs],
        scratch_shapes=[
            pltpu.VMEM((HEADS, far, TILE, TILE), F32),
            pltpu.VMEM((blocks, PAIRS, BLK, PW), BF),
            pltpu.VMEM((blocks, PAIRS, PW, BLK), BF),
            pltpu.VMEM((blocks, BLK, D), F32),
            pltpu.VMEM((blocks, BLK, D), BF),
            pltpu.VMEM((2, wide, narrow) + form, BF),
            pltpu.SemaphoreType.DMA((2,)),
        ]
        + state_scratch(BLK) * TOGETHER
        + gather_sems(wide, narrow) * 5,
        compiler_params=params(VMEM_MIB, collective_id=4, has_side_effects=True),
        name="full_forward",
    )(aux, tables, wts, attn_low, feed_low, vec, vec)


PAD = 8


def middle_kernel(
    seq,
    x1,
    aux,
    head,
    attn,
    feed_in,
    vec,
    rel,
    scalars,
    fold,
    dx_out,
    d_attn,
    d_feed_out,
    d_head,
    row_grads,
    bits_out,
    sums,
    xp,
    pooled,
    mixed,
    ot,
    lse,
    active_s,
    slope_s,
    middle_s,
    bias,
    tiles,
    d_mixed,
    feed,
    d_feed,
    sems,
    *state,
):
    n_long = seq // 3
    spots = ((PAD, 0, n_long), (2 * PAD + seq, n_long, TILE))
    lanes = D // TILE
    def plane_copies(array, out):
        copies = []
        for c in range(lanes):
            for k, (first, start, count) in enumerate(
                ((0, PAD, seq), (seq, 2 * PAD + seq, array.shape[0] - seq))
            ):
                ends = (array.at[first : first + count, c * TILE : (c + 1) * TILE],)
                ends += (xp.at[c, start : start + count],)
                ends = ends[::-1] if out else ends
                copies.append(pltpu.make_async_copy(*ends, sems.at[2 * c + k]))
        return copies

    loads = plane_copies(x1, False)
    load_feed = pltpu.make_async_copy(feed_in, feed, sems.at[2 * lanes])
    store_feed = pltpu.make_async_copy(d_feed, d_feed_out, sems.at[2 * lanes + 1])
    for load in loads:
        load.start()
    load_feed.start()
    build_bias(rel, 1, bias, bias.shape[1])
    tiles[...] = jnp.zeros_like(tiles)
    for c in range(lanes):
        xp[c, 0:PAD] = jnp.zeros((PAD, TILE), F32)
        xp[c, PAD + seq : 2 * PAD + seq] = jnp.zeros((PAD, TILE), F32)
    for load in loads:
        load.wait()
    for start, at, n in spots:
        for c in range(lanes):
            pooled[at : at + n, c * TILE : (c + 1) * TILE] = (
                xp[c, pl.ds(start - 2, n, stride=3)]
                + xp[c, pl.ds(start - 1, n, stride=3)]
                + xp[c, pl.ds(start, n, stride=3)]
            ) / 3.0

    xhat, _ = norm_stats(pooled[...])
    normed = (xhat * vec[7:8] + vec[8:9]).astype(BF)
    for part in range(3):
        half, at = part // 2, part % 2 * D
        value = mm(normed, attn[half, :, at : at + D])
        value = (value * HD**-0.5 if part == 0 else value).astype(BF)
        for pair in range(PAIRS):
            mixed[part, pair] = value[:, pair * PW : (pair + 1) * PW]

    def forward_pair(pair, carry):
        for at, n, offset in ((0, n_long, 0), (n_long, TILE, 2 * n_long)):
            top, total, acc = state
            wide = pl.ds(0, 2 * n)
            part = (top.at[:, wide], total.at[:, wide], acc.at[:, wide])
            softmax_start(part)
            values_t = mixed[2, pair, at : at + n].T
            both = split_heads(mixed[0, pair, at : at + n])
            count = n // TILE
            softmax_step(
                mixed[1, pair, at : at + n], values_t, both, bias, pair, 0, True, count, count, part
            )
            ot[pair, :, at : at + n], lse[pair, :, offset : offset + 2 * n] = softmax_end(part)
        return carry

    lax.fori_loop(0, PAIRS, forward_pair, 0, unroll=4)
    middle = pooled[...] + mm(ot[...].reshape(D, ot.shape[2]).T, attn[1, :, D:])
    middle_s[...] = middle
    xhat, _ = norm_stats(middle)
    second = (xhat * vec[9:10] + vec[10:11]).astype(BF)
    short = middle + vec[11:12]
    load_feed.wait()
    for c in range(PARTS):
        cols = slice(c * WIDTH, (c + 1) * WIDTH)
        active, slope = gelu_pair(mm(second, feed[0, :, cols]) + beta_of(vec, 1, c, WIDTH))
        active_s[:, cols] = active.astype(BF)
        slope_s[:, cols] = slope.astype(BF)
        short = short + mm(active_s[:, cols], feed[1, :, cols], NT)
    for start, at, n in spots:
        for c in range(lanes):
            part = short[at : at + n, c * TILE : (c + 1) * TILE]
            for k in range(3):
                where = pl.ds(start + k, n, stride=3)
                xp[c, where] = xp[c, where] + part

    d_head[...] = jnp.zeros_like(d_head)
    row_grads[...] = jnp.zeros_like(row_grads)

    def loss_block(b, bits):
        start = pl.multiple_of(b * BLK + jnp.where(b * BLK >= seq, 2 * PAD, PAD), PAD)
        joined = jnp.concatenate([xp[c, pl.ds(start, BLK)] for c in range(lanes)], 1)
        xhat, rstd = norm_stats(joined)
        last = (xhat * vec[0:1] + vec[1:2]).astype(BF)
        logits = mm(last, head[1], NT) * D**-0.5
        info = aux[pl.ds(pl.multiple_of(b * BLK, BLK), BLK), :]
        weight = info[:, 2:3]
        hot = one_hot(info[:, 1:2])
        highest = jnp.max(logits, -1, keepdims=True)
        powers = jnp.exp(logits - highest)
        total = jnp.sum(powers, -1, keepdims=True)
        picked = jnp.sum(jnp.where(hot, logits, 0.0), -1, keepdims=True)
        lost = weight * (highest + jnp.log(total) - picked)
        d_logits = ((powers / total - hot.astype(F32)) * (weight * scalars[1:2, 0:1])).astype(BF)
        d_head[...] += mm(d_logits, last, TN) * D**-0.5
        d_last = mm(d_logits, head[1]) * D**-0.5
        dx, d_gain, d_shift = norm_back(d_last, xhat, rstd, vec[0:1])
        row_grads[0:1] += d_gain
        row_grads[1:2] += d_shift
        for c in range(lanes):
            xp[c, pl.ds(start, BLK)] = dx[:, c * TILE : (c + 1) * TILE]
        return bits + lost

    bits = lax.fori_loop(0, x1.shape[0] // BLK, loss_block, jnp.zeros((BLK, 1), F32), unroll=4)
    bits_out[...] = jnp.broadcast_to(jnp.sum(bits, 0, keepdims=True) / LOG_TWO, bits_out.shape)

    d_short = jnp.concatenate(
        [
            jnp.concatenate(
                [
                    xp[c, pl.ds(start, n, stride=3)]
                    + xp[c, pl.ds(start + 1, n, stride=3)]
                    + xp[c, pl.ds(start + 2, n, stride=3)]
                    for c in range(lanes)
                ],
                1,
            )
            for start, at, n in spots
        ],
        0,
    )
    d_branch = d_short.astype(BF)
    row_grads[6:7] = jnp.sum(d_branch.astype(F32), 0, keepdims=True)
    xhat, rstd = norm_stats(middle_s[...])
    second = (xhat * vec[9:10] + vec[10:11]).astype(BF)
    d_second = jnp.zeros(d_short.shape, F32)
    for c in range(PARTS):
        cols = slice(c * WIDTH, (c + 1) * WIDTH)
        d_feed[1, :, cols] = mm(d_branch, active_s[:, cols], TN).astype(BF)
        d_pre = (mm(d_branch, feed[1, :, cols]) * slope_s[:, cols].astype(F32)).astype(BF)
        put_beta(row_grads, 7, c, jnp.sum(d_pre.astype(F32), 0, keepdims=True), False)
        d_feed[0, :, cols] = mm(second, d_pre, TN).astype(BF)
        d_second = d_second + mm(d_pre, feed[0, :, cols], NT)
    store_feed.start()
    dx, d_gain, d_shift = norm_back(d_second, xhat, rstd, vec[9:10])
    row_grads[4:5] = d_gain
    row_grads[5:6] = d_shift
    d_middle = d_short + dx
    d_mix = d_middle.astype(BF)
    ot_all = ot[...].reshape(D, ot.shape[2])
    d_attn[1, :, D:] = mm(ot_all, d_mix).astype(BF)
    d_att = mm(d_mix, attn[1, :, D:], NT).astype(BF)
    for pair in range(PAIRS):
        mixed[3, pair] = d_att[:, pair * PW : (pair + 1) * PW]

    def backward_pair(pair, carry):
        for at, n, offset in ((0, n_long, 0), (n_long, TILE, 2 * n_long)):
            d_out = mixed[3, pair, at : at + n]
            product = (d_out.astype(F32).T) * ot[pair, :, at : at + n].astype(F32)
            inner = interleave(
                jnp.sum(product[:HD], 0, keepdims=True), jnp.sum(product[HD:], 0, keepdims=True)
            )
            queries = split_heads(mixed[0, pair, at : at + n])
            grads = split_heads(d_out)
            keys = mixed[1, pair, at : at + n]
            count = n // TILE
            dv, dk, dq = score_back(
                keys,
                mixed[2, pair, at : at + n],
                keys.T,
                queries,
                grads,
                lse[pair, :, offset : offset + 2 * n],
                inner,
                bias,
                pair,
                0,
                True,
                count,
                count,
                tiles,
            )
            d_mixed[0, pair, at : at + n] = (merge_heads(dq) * HD**-0.5).T.astype(BF)
            d_mixed[1, pair, at : at + n] = dk.astype(BF)
            d_mixed[2, pair, at : at + n] = dv.astype(BF)
        return carry

    lax.fori_loop(0, PAIRS, backward_pair, 0, unroll=4)
    rel = rel_row(tiles, sums, fold, tiles.shape[1])
    row_grads[11:12] = jnp.concatenate([jnp.zeros_like(rel), rel], 1)
    d_in = jnp.concatenate([d_mixed[part, pair] for part in range(3) for pair in range(PAIRS)], 1)
    xhat, rstd = norm_stats(pooled[...])
    normed = (xhat * vec[7:8] + vec[8:9]).astype(BF)
    d_attn[0] = mm(normed, d_in[:, : 2 * D], TN).astype(BF)
    d_attn[1, :, :D] = mm(normed, d_in[:, 2 * D :], TN).astype(BF)
    dx, d_gain, d_shift = norm_back(mm(d_in[:, : 2 * D], attn[0], NT) + mm(d_in[:, 2 * D :], attn[1, :, :D], NT), xhat, rstd, vec[7:8])
    row_grads[2:3] = d_gain
    row_grads[3:4] = d_shift
    d_pool = (d_middle + dx) / 3.0
    for start, at, n in spots:
        for c in range(lanes):
            part = d_pool[at : at + n, c * TILE : (c + 1) * TILE]
            for k in range(3):
                where = pl.ds(start - 2 + k, n, stride=3)
                xp[c, where] = xp[c, where] + part
    stores = plane_copies(dx_out, True)
    for store in stores:
        store.start()
    for store in stores:
        store.wait()
    store_feed.wait()


def middle_stage(x1, aux, tables, attn, feed, vec, scalars, seq):
    tokens = x1.shape[0]
    n_long = seq // 3
    short = n_long + TILE
    far = n_long // TILE
    fold = fold_matrix(far)
    vm = pl.BlockSpec(memory_space=pltpu.VMEM)
    anywhere = pl.BlockSpec(memory_space=pl.ANY)
    return pl.pallas_call(
        functools.partial(middle_kernel, seq),
        in_specs=[anywhere, vm, vm, vm, anywhere, vm, pl.BlockSpec(memory_space=pltpu.SMEM), vm, vm],
        out_specs=[anywhere, vm, anywhere, vm, vm, vm],
        out_shape=[
            jax.ShapeDtypeStruct((tokens, D), F32),
            jax.ShapeDtypeStruct((2, D, 2 * D), BF),
            jax.ShapeDtypeStruct((2, D, FF), BF),
            jax.ShapeDtypeStruct((V, D), F32),
            jax.ShapeDtypeStruct((16, D), F32),
            jax.ShapeDtypeStruct((8, 128), F32),
        ],
        scratch_shapes=[
            pltpu.VMEM((HEADS, fold_rows(far), TILE), F32),
            pltpu.VMEM((D // TILE, tokens + 2 * PAD, TILE), F32),
            pltpu.VMEM((short, D), F32),
            pltpu.VMEM((4, PAIRS, short, PW), BF),
            pltpu.VMEM((PAIRS, PW, short), BF),
            pltpu.VMEM((PAIRS, 1, 2 * short), F32),
            pltpu.VMEM((short, FF), BF),
            pltpu.VMEM((short, FF), BF),
            pltpu.VMEM((short, D), F32),
            pltpu.VMEM((HEADS, far, TILE, TILE), F32),
            pltpu.VMEM((HEADS, far, TILE, TILE), F32),
            pltpu.VMEM((3, PAIRS, short, PW), BF),
            pltpu.VMEM((2, D, FF), BF),
            pltpu.VMEM((2, D, FF), BF),
            pltpu.SemaphoreType.DMA((2 * (D // TILE) + 2,)),
        ]
        + state_scratch(n_long),
        compiler_params=params(VMEM_MIB),
        name="middle_stage",
    )(x1, aux, tables, attn, feed, vec, vec, scalars, fold)


def feed_back_kernel(
    wide,
    narrow,
    dx,
    act,
    slope,
    middle,
    wts_in,
    vec,
    ready,
    dm_out,
    d_feed,
    row_grads,
    sums_out,
    wts,
    load_sem,
    up,
    down,
    *scratch,
):
    step = pl.program_id(0)
    at = Place(wide, narrow)
    streams = []
    for source, target in zip(column_parts(ready, 2), column_parts(sums_out, 2)):
        part = scratch[SCATTER_REFS * len(streams) : SCATTER_REFS * (len(streams) + 1)]
        streams.append(ScatterStream(at, source, halves_out(target), *part[:5], part[5:]))
    one, two = streams
    events = {
        (0, "dense"): (one.stage_first,),
        (0, "end"): (two.stage_first,),
        (1, "dense"): (one.stage_second,),
        (1, "end"): (two.stage_second,),
        (2, "dense"): (one.stage_home,),
        (2, "end"): (two.stage_home,),
    }

    @pl.when(step == 0)
    def _():
        load = pltpu.make_async_copy(wts_in, wts, load_sem)
        load.start()
        all_here = greet(*scatter_greetings(at))
        up[...] = jnp.zeros_like(up)
        down[...] = jnp.zeros_like(down)
        all_here()
        one.start()
        two.start()
        load.wait()
        row_grads[...] = jnp.zeros_like(row_grads)

    d_result = dx[...]
    d_branch = d_result.astype(BF)
    row_grads[2:3] += jnp.sum(d_branch.astype(F32), 0, keepdims=True)
    xhat, rstd = norm_stats(middle[...])
    second = (xhat * vec[4:5] + vec[5:6]).astype(BF)
    run_events(events, step, "dense")
    d_second = jnp.zeros(d_result.shape, F32)
    for c in range(PARTS):
        cols = slice(c * WIDTH, (c + 1) * WIDTH)
        down[:, cols] += mm(d_branch, act[:, cols], TN)
        d_pre = (mm(d_branch, wts[1, :, cols]) * slope[:, cols].astype(F32)).astype(BF)
        put_beta(row_grads, 3, c, jnp.sum(d_pre.astype(F32), 0, keepdims=True), True)
        up[:, cols] += mm(second, d_pre, TN)
        d_second = d_second + mm(d_pre, wts[0, :, cols], NT)
    dn, d_gain, d_shift = norm_back(d_second, xhat, rstd, vec[4:5])
    row_grads[0:1] += d_gain
    row_grads[1:2] += d_shift
    dm_out[...] = d_result + dn
    run_events(events, step, "end")

    @pl.when(step == pl.num_programs(0) - 1)
    def _():
        d_feed[0] = up[...].astype(BF)
        d_feed[1] = down[...].astype(BF)
        one.finish()
        two.finish()


def halves_out(ref):
    return [ref.at[0], ref.at[1]]


def feed_back(dx, act, slope, middle, wts, vec, ready, wide, narrow):
    tokens = dx.shape[0]
    form = ready.shape[3:]

    def flat(width):
        return pl.BlockSpec((BLK, width), lambda i: (i, 0))

    return pl.pallas_call(
        functools.partial(feed_back_kernel, wide, narrow),
        grid=(tokens // BLK,),
        in_specs=[flat(D), flat(FF), flat(FF), flat(D), pl.BlockSpec(memory_space=pl.ANY), whole_spec(vec.shape)]
        + [pl.BlockSpec(memory_space=pl.ANY)],
        out_specs=[
            flat(D),
            whole_spec((2, D, FF)),
            whole_spec((8, D)),
            whole_spec((2,) + form),
        ],
        out_shape=[
            jax.ShapeDtypeStruct((tokens, D), F32),
            jax.ShapeDtypeStruct((2, D, FF), BF),
            jax.ShapeDtypeStruct((8, D), F32),
            jax.ShapeDtypeStruct((2,) + form, F32),
        ],
        scratch_shapes=[
            pltpu.VMEM(wts.shape, BF),
            pltpu.SemaphoreType.DMA,
            pltpu.VMEM((D, FF), F32),
            pltpu.VMEM((D, FF), F32),
        ]
        + scatter_scratch(wide, narrow, half_width(ready)) * 2,
        compiler_params=params(VMEM_MIB, collective_id=5, has_side_effects=True),
        name="feed_back",
    )(dx, act, slope, middle, wts, vec, ready)


def attention_back_kernel(
    long_blocks,
    wide,
    narrow,
    dm,
    aux,
    ot,
    lse,
    q_in,
    k_in,
    v_in,
    embed,
    wts,
    vec,
    rel,
    fold,
    ready_a,
    ready_b,
    d_attn,
    d_embed,
    row_grads,
    out_a,
    out_b,
    sums,
    q_all,
    k_all,
    v_all,
    load_sems,
    bias,
    tiles,
    kt_all,
    dk_all,
    dv_all,
    dq_t,
    d_att,
    inner,
    weights,
    d_mixed,
    *scratch,
):
    step = pl.program_id(0)
    blocks = pl.num_programs(0)
    i = blocks - 1 - step
    at = Place(wide, narrow)
    streams = []
    for ready, out in ((ready_a, out_a), (ready_b, out_b)):
        for source, target in zip(column_parts(ready, 2), column_parts(out, 2)):
            part = scratch[SCATTER_REFS * len(streams) : SCATTER_REFS * (len(streams) + 1)]
            streams.append(ScatterStream(at, source, halves_out(target), *part[:5], part[5:]))
    one, two, three, four = streams
    events = {
        (0, 0): (one.stage_first,),
        (0, 1): (two.stage_first,),
        (0, "end"): (three.stage_first,),
        (1, "dense"): (four.stage_first,),
        (1, 0): (one.stage_second,),
        (1, 1): (two.stage_second,),
        (1, "end"): (one.stage_home,),
        (2, 0): (three.stage_second, two.stage_home),
        (2, 1): (four.stage_second,),
        (2, "end"): (three.stage_home,),
        (3, 1): (four.stage_home,),
    }

    @pl.when(step == 0)
    def _():
        loads = [
            pltpu.make_async_copy(source, target, load_sems.at[k])
            for k, (source, target) in enumerate(((k_in, k_all), (q_in, q_all), (v_in, v_all)))
        ]
        for load in loads:
            load.start()
        all_here = greet(*scatter_greetings(at))
        build_bias(rel, 0, bias, bias.shape[1])
        all_here()
        for stream in streams:
            stream.start()
        tiles[...] = jnp.zeros_like(tiles)
        dk_all[...] = jnp.zeros_like(dk_all)
        dv_all[...] = jnp.zeros_like(dv_all)
        weights[...] = jnp.zeros_like(weights)
        d_embed[...] = jnp.zeros_like(d_embed)
        row_grads[...] = jnp.zeros_like(row_grads)

        for load in loads:
            load.wait()

        def turn(n, carry):
            for pair in range(PAIRS):
                kt_all[n, pair] = k_all[n, pair].T
            return carry

        lax.fori_loop(0, blocks, turn, 0)

    d_middle = dm[...]
    d_mix = d_middle.astype(BF)
    weights[1, :, D:] += mm(ot[0].reshape(D, BLK), d_mix)
    out = mm(d_mix, wts[1, :, D : 2 * D], NT).astype(BF)
    for pair in range(PAIRS):
        d_att[pair] = out[:, pair * PW : (pair + 1) * PW]
    product = mm(wts[1, :, D : 2 * D], d_mix, NT).astype(BF).astype(F32) * ot[0].reshape(
        D, BLK
    ).astype(F32)
    for pair in range(PAIRS):
        top = pair * PW
        inner[pair] = interleave(
            jnp.sum(product[top : top + HD], 0, keepdims=True),
            jnp.sum(product[top + HD : top + PW], 0, keepdims=True),
        )
    run_events(events, step, "dense")
    first = jnp.where(i >= long_blocks, long_blocks, 0)

    def two_pairs(turn, carry):
        pairs = [turn * TOGETHER + k for k in range(TOGETHER)]
        queries = [split_heads(q_all[i, pair]) for pair in pairs]
        grads = [split_heads(d_att[pair]) for pair in pairs]
        dq_t[...] = jnp.zeros_like(dq_t)

        def with_block(j, far, diag):
            for k, pair in enumerate(pairs):
                dv, dk, dq = score_back(
                    k_all[j, pair],
                    v_all[j, pair],
                    kt_all[j, pair],
                    queries[k],
                    grads[k],
                    lse[0, pair],
                    inner[pair],
                    bias,
                    pair,
                    far,
                    diag,
                    SUB,
                    SUB,
                    tiles,
                )
                dv_all[j, pair] += dv
                dk_all[j, pair] += dk
                dq_t[k] += dq

        def earlier(j, inside):
            with_block(j, SUB * (i - j), False)
            return inside

        lax.fori_loop(first, i, earlier, 0)
        with_block(i, 0, True)
        for k, pair in enumerate(pairs):
            d_mixed[0, pair] = (merge_heads(dq_t[k]) * HD**-0.5).T.astype(BF)
            d_mixed[1, pair] = dk_all[i, pair].astype(BF)
            d_mixed[2, pair] = dv_all[i, pair].astype(BF)
        run_events(events, step, turn)
        return carry

    lax.fori_loop(0, PAIRS // TOGETHER, two_pairs, 0)
    d_in = jnp.concatenate([d_mixed[part, pair] for part in range(3) for pair in range(PAIRS)], 1)
    hot = one_hot(aux[:, 0:1]).astype(BF)
    xhat, rstd = norm_stats(mm(hot, embed[0]))
    normed = (xhat * vec[2:3] + vec[3:4]).astype(BF)
    weights[0] += mm(normed, d_in[:, : 2 * D], TN)
    weights[1, :, :D] += mm(normed, d_in[:, 2 * D :], TN)
    dx, d_gain, d_shift = norm_back(mm(d_in[:, : 2 * D], wts[0, :, : 2 * D], NT) + mm(d_in[:, 2 * D :], wts[1, :, :D], NT), xhat, rstd, vec[2:3])
    row_grads[0:1] += d_gain
    row_grads[1:2] += d_shift
    d_embed[...] += mm(hot, (d_middle + dx).astype(BF), TN)

    run_events(events, step, "end")

    @pl.when(step == blocks - 1)
    def _():
        d_attn[...] = weights[...].astype(BF)
        rel = rel_row(tiles, sums, fold, tiles.shape[1])
        row_grads[2:3] = jnp.concatenate([rel, jnp.zeros_like(rel)], 1)
        for stream in streams:
            stream.finish()


def half_width(x):
    return x.shape[3:-1] + (x.shape[-1] // 2,)


def attention_back(
    dm, aux, ot, lse, q, k, v, tables, wts, vec, ready_a, ready_b, long_blocks, wide, narrow
):
    tokens = dm.shape[0]
    blocks = tokens // BLK
    far = SUB * long_blocks
    fold = fold_matrix(far)

    def turned(shape):
        return pl.BlockSpec(shape, lambda s: (blocks - 1 - s,) + (0,) * (len(shape) - 1))

    return pl.pallas_call(
        functools.partial(attention_back_kernel, long_blocks, wide, narrow),
        grid=(blocks,),
        in_specs=[
            turned((BLK, D)),
            turned((BLK, aux.shape[1])),
            turned((1, PAIRS, PW, BLK)),
            turned((1, PAIRS, 1, 2 * BLK)),
            pl.BlockSpec(memory_space=pl.ANY),
            pl.BlockSpec(memory_space=pl.ANY),
            pl.BlockSpec(memory_space=pl.ANY),
            whole_spec((1, V, D)),
            whole_spec((2, D, 2 * D)),
            whole_spec(vec.shape),
            pl.BlockSpec(memory_space=pltpu.SMEM),
            whole_spec(fold.shape),
            pl.BlockSpec(memory_space=pl.ANY),
            pl.BlockSpec(memory_space=pl.ANY),
        ],
        out_specs=[
            whole_spec((2, D, 2 * D)),
            whole_spec((V, D)),
            whole_spec((8, D)),
            whole_spec((2,) + ready_a.shape[3:]),
            whole_spec((2,) + ready_b.shape[3:]),
        ],
        out_shape=[
            jax.ShapeDtypeStruct((2, D, 2 * D), BF),
            jax.ShapeDtypeStruct((V, D), F32),
            jax.ShapeDtypeStruct((8, D), F32),
            jax.ShapeDtypeStruct((2,) + ready_a.shape[3:], F32),
            jax.ShapeDtypeStruct((2,) + ready_b.shape[3:], F32),
        ],
        scratch_shapes=[
            pltpu.VMEM((HEADS, fold_rows(far), TILE), F32),
            pltpu.VMEM(q.shape, BF),
            pltpu.VMEM(k.shape, BF),
            pltpu.VMEM(v.shape, BF),
            pltpu.SemaphoreType.DMA((3,)),
            pltpu.VMEM((HEADS, far, TILE, TILE), F32),
            pltpu.VMEM((HEADS, far, TILE, TILE), F32),
            pltpu.VMEM((blocks, PAIRS, PW, BLK), BF),
            pltpu.VMEM((blocks, PAIRS, BLK, PW), F32),
            pltpu.VMEM((blocks, PAIRS, BLK, PW), F32),
            pltpu.VMEM((TOGETHER, PW, 2 * BLK), F32),
            pltpu.VMEM((PAIRS, BLK, PW), BF),
            pltpu.VMEM((PAIRS, 1, 2 * BLK), F32),
            pltpu.VMEM((2, D, 2 * D), F32),
            pltpu.VMEM((3, PAIRS, BLK, PW), BF),
        ]
        + scatter_scratch(wide, narrow, half_width(ready_a)) * 2
        + scatter_scratch(wide, narrow, half_width(ready_b)) * 2,
        compiler_params=params(VMEM_MIB, collective_id=6, has_side_effects=True),
        name="attention_back",
    )(dm, aux, ot, lse, q, k, v, tables, wts, vec, vec, fold, ready_a, ready_b)


MESH = pl.DeviceIdType.MESH
MISC_ROWS = 32
SIDE = 128
MISC_COLS = D + SIDE
COUNT_ROW = 24


class Place:
    def __init__(self, wide, narrow):
        self.W, self.N = wide, narrow
        self.c = lax.axis_index("rep")
        self.w = lax.axis_index("wide")
        self.n = lax.axis_index("narrow")
        self.a0, self.b0 = self.digits(self.c)
        self.group = self.w // (wide // 2)

    def digits(self, c):
        hi, lo = self.n // 2, self.n % 2
        return (1 - c) * hi + c * lo, (1 - c) * lo + c * hi

    def narrow_of(self, a, b, c=None):
        c = self.c if c is None else c
        return a * (2 - c) + b * (1 + c)

    def chip(self, w, a, b):
        return {"wide": w, "narrow": self.narrow_of(a, b)}

    def sibling(self):
        return {"rep": 1 - self.c}


def greet(devices, more=()):
    barrier = pltpu.get_barrier_semaphore()
    count = len(devices)
    for device in devices:
        pl.semaphore_signal(barrier, inc=1, device_id=device, device_id_type=MESH)
    for condition, device in more:

        @pl.when(condition)
        def _(device=device):
            pl.semaphore_signal(barrier, inc=1, device_id=device, device_id_type=MESH)

        count = count + condition.astype(jnp.int32)
    return lambda: pl.semaphore_wait(barrier, count)


def slab_form(rows, cols):
    return (rows, cols) if rows % 16 == 0 else (16, rows * cols // 16)


def gather_greetings(at):
    out = [{"wide": lax.rem(at.w + k, at.W)} for k in range(1, at.W)]
    return out + [
        at.chip(at.w, at.a0, 1 - at.b0),
        at.chip(at.w, 1 - at.a0, at.b0),
        at.sibling(),
    ]


class GatherStream:
    def __init__(self, at, src, out, send_along, send, recv, recv_side, local):
        self.at, self.src, self.out = at, src, out
        self.send_along, self.send, self.recv, self.recv_side = send_along, send, recv, recv_side
        self.n0 = at.narrow_of(at.a0, at.b0)
        self.n1 = at.narrow_of(at.a0, 1 - at.b0)
        self.n2 = at.narrow_of(1 - at.a0, at.b0)
        self.n3 = at.narrow_of(1 - at.a0, 1 - at.b0)
        self.local = local

    @property
    def keep(self):
        at = self.at
        return pltpu.make_async_copy(self.src, self.out.at[at.c, at.w, self.n0], self.local)

    def copy(self, ref, w, n, sem, peer):
        return pltpu.make_async_remote_copy(
            src_ref=ref,
            dst_ref=self.out.at[self.at.c, w, n],
            send_sem=sem,
            recv_sem=self.recv.at[w, n],
            device_id=peer,
            device_id_type=MESH,
        )

    def arrived(self, w, n):
        self.copy(
            self.out.at[self.at.c, w, n], w, n, self.send.at[0], self.at.sibling()
        ).wait_recv()

    def other(self, k):
        return lax.rem(self.at.w + k, self.at.W)

    def along(self, k):
        at = self.at
        return self.copy(
            self.src, at.w, self.n0, self.send_along.at[k - 1], {"wide": self.other(k)}
        )

    def neighbours(self, w, mine):
        at = self.at
        ref = self.src if mine else self.out.at[at.c, w, self.n0]
        self.copy(ref, w, self.n0, self.send.at[0], at.chip(at.w, at.a0, 1 - at.b0)).start()
        self.copy(ref, w, self.n0, self.send.at[1], at.chip(at.w, 1 - at.a0, at.b0)).start()

    def side(self, n):
        at = self.at
        return pltpu.make_async_remote_copy(
            src_ref=self.out.at[at.c, :, n],
            dst_ref=self.out.at[at.c, :, n],
            send_sem=self.send.at[2 + n],
            recv_sem=self.recv_side.at[n],
            device_id=at.sibling(),
            device_id_type=MESH,
        )

    def start(self):
        self.start_along()
        self.neighbours(self.at.w, True)

    def start_along(self):
        self.keep.start()
        for k in self.order():
            self.along(k).start()

    def finish_along(self):
        self.keep.wait()
        for k in self.order():
            self.along(k).wait_send()
            self.arrived(self.other(k), self.n0)

    def start_across(self):
        at = self.at
        for k in range(at.W):
            self.neighbours(self.other(k), False)
        self.side(self.n0).start()

    def order(self):
        return sorted(range(1, self.at.W), key=lambda k: -min(k, self.at.W - k))

    def depth(self, d):
        at = self.at
        if d == 1:
            for k in self.order()[::-1]:
                w = self.other(k)
                self.arrived(w, self.n0)
                self.neighbours(w, False)
            self.keep.wait()
            self.side(self.n0).start()
        if d == 2:
            for k in [0] + self.order()[::-1]:
                w = self.other(k)
                self.arrived(w, self.n1)
                ref = self.out.at[at.c, w, self.n1]
                peer = at.chip(at.w, 1 - at.a0, at.b0)
                self.copy(ref, w, self.n1, self.send.at[1], peer).start()
            self.side(self.n1).start()
            for k in range(at.W):
                self.arrived(self.other(k), self.n2)
            self.side(self.n2).start()
        if d == 3:
            for k in range(at.W):
                self.arrived(self.other(k), self.n3)
            self.side(self.n3).start()

    def finish(self, along=True):
        at = self.at
        for k in self.order() if along else ():
            self.along(k).wait_send()
        column = self.out.at[at.c, :, self.n0]
        half = self.out.at[at.c, pl.ds(0, at.W // 2)]
        for sem, ref in ((self.send.at[0], column), (self.send.at[1], half)):
            pltpu.make_async_remote_copy(
                src_ref=ref,
                dst_ref=ref,
                send_sem=sem,
                recv_sem=self.recv.at[0, 0],
                device_id=at.sibling(),
                device_id_type=MESH,
            ).wait_send()
        for n in range(at.N):
            self.side(n).wait_send()
        for n in range(at.N):
            pltpu.make_async_remote_copy(
                src_ref=self.out.at[1 - at.c, :, n],
                dst_ref=self.out.at[1 - at.c, :, n],
                send_sem=self.send.at[2 + n],
                recv_sem=self.recv_side.at[n],
                device_id=at.sibling(),
                device_id_type=MESH,
            ).wait_recv()


class HostedStream(GatherStream):
    def column(self, half, n, count=None):
        return self.out.at[half, :, n] if count is None else self.out.at[half, pl.ds(0, count), n]

    def all_of(self, ref, send, recv):
        return pltpu.make_async_remote_copy(
            src_ref=ref,
            dst_ref=ref,
            send_sem=send,
            recv_sem=recv,
            device_id=self.at.sibling(),
            device_id_type=MESH,
        )

    def copy(self, ref, w, n, sem, peer):
        return pltpu.make_async_remote_copy(
            src_ref=ref,
            dst_ref=self.out.at[self.at.c, w, n],
            send_sem=sem,
            recv_sem=self.recv.at[0, n],
            device_id=peer,
            device_id_type=MESH,
        )

    def along(self, k):
        at = self.at
        return self.copy(self.src, at.w, self.n0, self.send_along.at[0], {"wide": self.other(k)})

    def second(self):
        at = self.at
        ref = self.column(at.c, self.n1)
        return pltpu.make_async_remote_copy(
            src_ref=ref,
            dst_ref=ref,
            send_sem=self.send_along.at[1],
            recv_sem=self.recv.at[0, self.n1],
            device_id=at.chip(at.w, 1 - at.a0, at.b0),
            device_id_type=MESH,
        )

    def arrived_all(self, n, count=None):
        self.all_of(self.column(self.at.c, n, count), self.send.at[0], self.recv.at[0, n]).wait_recv()

    def side(self, n):
        at = self.at
        ref = self.column(at.c, n)
        return pltpu.make_async_remote_copy(
            src_ref=ref,
            dst_ref=ref,
            send_sem=self.send.at[2],
            recv_sem=self.recv_side.at[0],
            device_id=at.sibling(),
            device_id_type=MESH,
        )

    def depth(self, d):
        at = self.at
        if d == 1:
            self.arrived_all(self.n0, at.W - 1)
            for k in self.order()[::-1]:
                self.neighbours(self.other(k), False)
            self.keep.wait()
            self.side(self.n0).start()
        if d == 2:
            self.arrived_all(self.n1)
            self.second().start()
            self.side(self.n1).start()
            self.arrived_all(self.n2)
            self.side(self.n2).start()
        if d == 3:
            self.arrived_all(self.n3)
            self.side(self.n3).start()

    def finish(self):
        at = self.at
        far = self.column(at.c, self.n0, at.W - 1)
        self.all_of(far, self.send_along.at[0], self.recv.at[0, 0]).wait_send()
        for k in range(2):
            self.all_of(
                self.column(at.c, self.n0), self.send.at[k], self.recv.at[0, 0]
            ).wait_send()
        self.second().wait_send()
        self.all_of(self.out.at[at.c], self.send.at[2], self.recv.at[0, 0]).wait_send()
        self.all_of(self.out.at[1 - at.c], self.send.at[2], self.recv_side.at[0]).wait_recv()


GATHER_SEMS = 5


def gather_sems(wide, narrow):
    dma = pltpu.SemaphoreType.DMA
    return [dma((wide,)), dma((2 + narrow,)), dma((wide, narrow)), dma((narrow,)), dma]


class ScatterStream:
    def __init__(self, at, src, out, own, side, first, second, fin, sems):
        self.at, self.src, self.out = at, src, out
        self.own, self.side, self.first, self.second, self.fin = own, side, first, second, fin
        self.local, self.side_sem, self.first_sem, self.second_sem, self.home_sem, self.fin_sem = sems
        self.n0 = at.narrow_of(at.a0, at.b0)
        self.n1 = at.narrow_of(at.a0, 1 - at.b0)

    def remote(self, src, dst, sems, index, device):
        return pltpu.make_async_remote_copy(
            src_ref=src,
            dst_ref=dst,
            send_sem=sems.at[(0,) + index],
            recv_sem=sems.at[(1,) + index],
            device_id=device,
            device_id_type=MESH,
        )

    def side_copy(self, n):
        at = self.at
        return self.remote(
            self.src.at[1 - at.c, :, n], self.side.at[:, n], self.side_sem, (n,), at.sibling()
        )

    def own_copy(self):
        return pltpu.make_async_copy(self.src.at[self.at.c], self.own, self.local)

    def first_copy(self, b):
        at = self.at
        return self.remote(
            self.own.at[:, at.narrow_of(1 - at.a0, b)],
            self.first.at[b],
            self.first_sem,
            (b,),
            at.chip(at.w, 1 - at.a0, at.b0),
        )

    def second_copy(self):
        at = self.at
        return self.remote(
            self.own.at[:, self.n1],
            self.second,
            self.second_sem,
            (),
            at.chip(at.w, at.a0, 1 - at.b0),
        )

    def home_copy(self, w):
        at = self.at
        return pltpu.make_async_remote_copy(
            src_ref=self.own.at[w, self.n0],
            dst_ref=self.fin.at[at.w % (at.W // 2), at.c],
            send_sem=self.home_sem.at[w],
            recv_sem=self.fin_sem.at[at.w % (at.W // 2), at.c],
            device_id={"wide": w, "rep": at.group},
            device_id_type=MESH,
        )

    def elsewhere(self, w):
        return (w != self.at.w) | (self.at.c != self.at.group)

    def start(self):
        at = self.at
        self.own_copy().start()
        other = 1 - at.c
        a1, b1 = at.digits(other)
        for a, b in ((1 - a1, 1 - b1), (1 - a1, b1), (a1, 1 - b1), (a1, b1)):
            self.side_copy(at.narrow_of(a, b, other)).start()

    def stage_first(self):
        at = self.at
        self.own_copy().wait()
        for b in (1 - at.b0, at.b0):
            n = at.narrow_of(1 - at.a0, b)
            self.side_copy(n).wait_recv()

            def body(w, carry, n=n):
                self.own[w, n] = (self.own[w, n].astype(F32) + self.side[w, n].astype(F32)).astype(BF)
                return carry

            lax.fori_loop(0, at.W, body, 0)
            self.first_copy(b).start()

    def stage_second(self):
        at = self.at
        self.side_copy(self.n1).wait_recv()
        self.first_copy(1 - at.b0).wait_recv()

        def body(w, carry):
            value = self.own[w, self.n1].astype(F32) + self.side[w, self.n1].astype(F32)
            self.own[w, self.n1] = (value + self.first[1 - at.b0, w].astype(F32)).astype(BF)
            return carry

        lax.fori_loop(0, at.W, body, 0)
        self.second_copy().start()

    def stage_home(self):
        at = self.at
        n = self.n0
        self.side_copy(n).wait_recv()
        self.first_copy(at.b0).wait_recv()
        self.second_copy().wait_recv()

        def body(k, carry):
            w = lax.rem(at.w + at.W // 2 + k, at.W)
            value = self.own[w, n].astype(F32) + self.side[w, n].astype(F32)
            value = value + self.first[at.b0, w].astype(F32) + self.second[w].astype(F32)
            self.own[w, n] = value.astype(BF)

            @pl.when(self.elsewhere(w))
            def _():
                self.home_copy(w).start()

            @pl.when(jnp.logical_not(self.elsewhere(w)))
            def _():
                self.fin[at.w % (at.W // 2), at.c] = value.astype(BF)

            return carry

        lax.fori_loop(0, at.W, body, 0)

    def finish(self):
        at = self.at
        half = at.W // 2
        for h in range(2):
            total = None
            for k in range(half):

                @pl.when((at.c * half + k != at.w) | (at.c != h))
                def _(k=k, h=h):
                    pltpu.make_async_remote_copy(
                        src_ref=self.fin.at[k, h],
                        dst_ref=self.fin.at[k, h],
                        send_sem=self.home_sem.at[0],
                        recv_sem=self.fin_sem.at[k, h],
                        device_id=at.sibling(),
                        device_id_type=MESH,
                    ).wait_recv()

                value = self.fin[k, h].astype(F32)
                total = value if total is None else total + value
            self.out[h][...] = total
        for n in range(at.N):
            self.side_copy(n).wait_send()
        for b in range(2):
            self.first_copy(b).wait_send()
        self.second_copy().wait_send()

        def homes(w, carry):
            @pl.when(self.elsewhere(w))
            def _():
                self.home_copy(w).wait_send()

            return carry

        lax.fori_loop(0, at.W, homes, 0)


SCATTER_REFS = 11


def scatter_scratch(wide, narrow, form):
    sizes = ((wide, narrow), (wide, narrow), (2, wide), (wide,), (wide // 2, 2))
    dma = pltpu.SemaphoreType.DMA
    buffers = [pltpu.VMEM(size + form, BF) for size in sizes]
    return buffers + [dma, dma((2, narrow)), dma((2, 2)), dma((2,)), dma((wide,)), dma((wide // 2, 2))]


def scatter_greetings(at):
    out = [
        at.chip(at.w, at.a0, 1 - at.b0),
        at.chip(at.w, 1 - at.a0, at.b0),
        at.sibling(),
    ]
    more = []
    for k in range(at.W // 2):
        for h in range(2):
            w = at.c * (at.W // 2) + k
            more.append(((w != at.w) | (at.c != h), {"rep": h, "wide": w}))
    return out, more


def place_columns(slabs, cols):
    feature = lax.broadcasted_iota(jnp.int32, (D, slabs * SIDE), 0)
    column = lax.broadcasted_iota(jnp.int32, (D, slabs * SIDE), 1)
    lane = column % SIDE
    return jnp.where((feature == column // SIDE * cols + lane) & (lane < cols), 1.0, 0.0).astype(BF)


def view_half(ref, layer, half, width, natural):
    if natural:
        return ref.at[layer, :, pl.ds(pl.multiple_of(half * width, width), width)]
    return ref.at[layer, half]


def column_parts(ref, count):
    width = ref.shape[-1] // count
    lead = (slice(None),) * (len(ref.shape) - 1)
    return [ref.at[lead + (slice(k * width, (k + 1) * width),)] for k in range(count)]


def prepare_kernel(wide, narrow, natural, *refs):
    take = iter(refs)

    def some(n):
        return [next(take) for _ in range(n)]

    ids, live, tables, attention, feed, vectors = some(6)
    attn_low, feed_low, attn_out, misc_out, aux, scalars = some(6)
    full_tables, vec = some(2) if natural else (None, None)
    misc, misc_low, packed, moved, move_sems = some(5)
    streams = [some(GATHER_SEMS) for _ in range(2)]
    at = Place(wide, narrow)
    seq = ids.shape[1]
    table_rows, cols = tables.shape[1], vectors.shape[1]

    to_core, to_wide = at.w % 2, at.c * (wide // 2) + at.w // 2
    from_wide = 2 * (at.w % (wide // 2)) + at.c
    leaves = (to_core != at.c) | (to_wide != at.w)
    greet(gather_greetings(at), [(leaves, {"rep": at.group, "wide": from_wide})])()
    packed[...] = ids[...] + V * live[...]
    move = pltpu.make_async_remote_copy(
        src_ref=packed,
        dst_ref=moved,
        send_sem=move_sems.at[0],
        recv_sem=move_sems.at[1],
        device_id={"rep": to_core, "wide": to_wide},
        device_id_type=MESH,
    )
    stay = pltpu.make_async_copy(packed, moved, move_sems.at[0])
    pl.when(leaves)(move.start)
    pl.when(jnp.logical_not(leaves))(stay.start)

    position = lax.broadcasted_iota(jnp.int32, live.shape, 1)
    tally = jnp.sum(jnp.where(position > 0, live[...], 0).astype(F32), 1, keepdims=True)
    tally = jnp.sum(tally, 0, keepdims=True)
    high = jnp.floor(tally / 64.0)
    lane = lax.broadcasted_iota(jnp.int32, (1, SIDE), 1)
    misc[...] = jnp.zeros_like(misc)
    misc[0:table_rows, 0:D] = tables[at.c]
    misc[0:VEC, D : D + cols] = vectors[...]
    misc[COUNT_ROW : COUNT_ROW + 1, D:] = jnp.where(
        lane == 0, high, jnp.where(lane == 1, tally - 64.0 * high, 0.0)
    )
    misc_low[...] = misc[...].astype(BF)
    attn_low[...] = attention[...].astype(BF)
    small = GatherStream(at, misc_low, misc_out, *streams[0])
    attn = GatherStream(
        at, view_half(attn_low, 0, at.c, 2 * D, natural), attn_out, *streams[1]
    )
    small.start()
    attn.start()
    feed_low[...] = feed[...].astype(BF)

    pl.when(leaves)(move.wait)
    pl.when(jnp.logical_not(leaves))(stay.wait)
    live_at = lax.broadcasted_iota(jnp.int32, (8, seq), 1)
    row_at = lax.broadcasted_iota(jnp.int32, (8, seq), 0)
    start = 0
    for r, length in ((0, seq), (1, BLK)):
        row = moved[r : r + 1]
        after = jnp.concatenate([row[:, 1:], row[:, :1]], 1)
        weight = jnp.where(live_at[0:1] < seq - 1, after // V, 0)
        info = jnp.where(
            row_at == 0, row % V, jnp.where(row_at == 1, after % V, jnp.where(row_at == 2, weight, 0))
        )
        aux[start : start + length] = info[:, :length].astype(F32).T
        start += length
    for stream, d in (
        (small, 1),
        (attn, 1),
        (small, 2),
        (attn, 2),
        (small, 3),
    ):
        stream.depth(d)
    small.finish()
    sides = [
        sum(
            misc_out[h, w, n, :, D:].astype(F32) for w in range(wide) for n in range(narrow)
        )
        for h in range(2)
    ]
    counts = [
        side[COUNT_ROW : COUNT_ROW + 1, 0:1] * 64.0 + side[COUNT_ROW : COUNT_ROW + 1, 1:2]
        for side in sides
    ]
    mine = jnp.where(at.group == 0, counts[0], counts[1])
    line = lax.broadcasted_iota(jnp.int32, (8, 128), 0)
    kept = jnp.where(at.c == 0, counts[0], counts[1])
    scalars[...] = jnp.where(line == 0, kept, jnp.where(line == 1, 1.0 / (mine * LOG_TWO), 0.0))
    if natural:
        for h in range(2):
            for w in range(wide):
                for n in range(narrow):
                    s = w * narrow + n
                    full_tables[h, s * table_rows : (s + 1) * table_rows] = misc_out[
                        h, w, n, :table_rows, :D
                    ]
        blocks = [misc_out[0, w, n, :, D:] for w in range(wide) for n in range(narrow)]
        spread = mm(jnp.concatenate(blocks, 1), place_columns(wide * narrow, cols), NT)
        vec[...] = spread[: vec.shape[0]]
    attn.depth(3)
    attn.finish()


def prepare(ids, live, tables, attention, feed, vectors, wide, narrow, natural):
    vm = pl.BlockSpec(memory_space=pltpu.VMEM)
    anywhere = pl.BlockSpec(memory_space=pl.ANY)
    seq = ids.shape[1]
    half_form = attention.shape[1:] if natural else attention.shape[2:]
    half_form = (half_form[0], 2 * D) if natural else half_form
    misc = (MISC_ROWS, MISC_COLS)
    outs = [
        (attention.shape, BF, vm),
        (feed.shape, BF, vm),
        ((2, wide, narrow) + half_form, BF, anywhere),
        ((2, wide, narrow) + misc, BF, vm),
        ((seq + BLK, 8), F32, vm),
        ((8, 128), F32, vm),
    ]
    if natural:
        outs += [((2, V, D), BF, vm), ((24, D), F32, vm)]
    return pl.pallas_call(
        functools.partial(prepare_kernel, wide, narrow, natural),
        in_specs=[vm] * 6,
        out_specs=[spec for _, _, spec in outs],
        out_shape=[jax.ShapeDtypeStruct(shape, kind) for shape, kind, _ in outs],
        scratch_shapes=[
            pltpu.VMEM(misc, F32),
            pltpu.VMEM(misc, BF),
            pltpu.VMEM(ids.shape, jnp.int32),
            pltpu.VMEM(ids.shape, jnp.int32),
            pltpu.SemaphoreType.DMA((2,)),
        ]
        + gather_sems(wide, narrow) * 2,
        compiler_params=params(VMEM_MIB, collective_id=1, has_side_effects=True),
        name="prepare",
    )(ids, live, tables, attention, feed, vectors)


def halves_of(ref, layer, width, natural):
    if natural:
        return [ref.at[layer, :, h * width : (h + 1) * width] for h in range(2)]
    return [ref.at[layer, h] for h in range(2)]


def adam_update(weight, moment, square, gradient, decay, rate):
    moment = BETA_ONE * moment + (1.0 - BETA_ONE) * gradient
    square = BETA_TWO * square + (1.0 - BETA_TWO) * gradient * gradient
    fixed_moment = moment / (1.0 - BETA_ONE**STEP)
    fixed_square = square / (1.0 - BETA_TWO**STEP)
    delta = -rate * (fixed_moment / (jnp.sqrt(fixed_square) + ADAM_EPS) + decay * weight)
    return (moment, square, delta)


DECAYS = (DECAY, DECAY, DECAY, 0.0)
RATES = (RATE_TABLE, RATE, RATE, RATE_TABLE)
SUMMED = ((1, 1), (2, 1), (2, 0))


def sum_stages(wide, narrow):
    if wide * narrow <= 16:
        return wide * narrow - 1
    return narrow - 1 + wide.bit_length() - 1


def sum_rounds(at):
    W, N = at.W, at.N
    if W * N <= 16:
        peers = []
        for k in range(1, W * N):
            device = {"wide": lax.rem(at.w + k // N, W), "narrow": lax.rem(at.n + k % N, N)}
            peers.append((k - 1, device))
        rounds = [peers]
    else:
        rounds = [[(k, {"narrow": lax.rem(at.n + 1 + k, N)}) for k in range(N - 1)]]
        slot, unit = N - 1, 1
        while unit < W:
            rounds.append([(slot, {"wide": at.w + unit * (1 - 2 * ((at.w // unit) % 2))})])
            slot += 1
            unit *= 2
    return [device for peers in rounds for _, device in peers], rounds


def ordered_sum(at, peers, total, arrived):
    if len(peers) == 1:
        return total + arrived[peers[0][0]]
    whole = len(peers) + 1 == at.W * at.N
    values = [(at.w * at.N + at.n if whole else at.n, total)]
    for slot, _ in peers:
        k = slot + 1
        if whole:
            source = lax.rem(at.w + at.W - k // at.N, at.W) * at.N
            source = source + lax.rem(at.n + at.N - k % at.N, at.N)
        else:
            source = lax.rem(at.n + at.N - k, at.N)
        values.append((source, arrived[slot]))
    out = None
    for index in range(len(values)):
        value = jnp.zeros_like(total)
        for source, piece in values:
            value = jnp.where(source == index, piece, value)
        out = value if out is None else out + value
    return out


def pack_misc(at, d_tables, row_sums, rows, packed, cols):
    short_rows, feed_rows, attn_rows = row_sums
    rows[0:2] = short_rows[0:2]
    rows[2:4] = attn_rows[0:2]
    rows[4:7] = feed_rows[0:3]
    rows[7:12] = short_rows[2:7]
    rows[BETA_ROW : BETA_ROW + CHUNKS] = feed_rows[3 : 3 + CHUNKS]
    rows[BETA_ROW + CHUNKS : REL_ROW] = short_rows[7 : 7 + CHUNKS]
    rows[REL_ROW : REL_ROW + 1] = attn_rows[2:3] + short_rows[11:12]
    rows[VEC:] = jnp.zeros((rows.shape[0] - VEC, D), F32)
    tall = jnp.concatenate([rows[...], jnp.zeros((MISC_ROWS - rows.shape[0], D), F32)], 0).astype(BF)
    spread = mm(tall, place_columns(at.W * at.N, cols)).astype(BF)
    count = V // (at.W * at.N)
    for w in range(at.W):
        for n in range(at.N):
            s = w * at.N + n
            for h in range(2):
                packed[h, w, n, :count, :D] = d_tables[h][s * count : (s + 1) * count].astype(BF)
                packed[h, w, n, count:, :D] = jnp.zeros((MISC_ROWS - count, D), BF)
            packed[0, w, n, :, D:] = spread[:, s * SIDE : (s + 1) * SIDE]
            packed[1, w, n, :, D:] = jnp.zeros((MISC_ROWS, SIDE), BF)


def reduce_kernel(wide, narrow, natural, *refs):
    at = Place(wide, narrow)
    take = iter(refs)

    def some(n):
        return [next(take) for _ in range(n)]

    if natural:
        d_tables, row_sums = some(2), some(3)
    else:
        d_misc = next(take)
    d_attn, ready, bits = next(take), some(3), next(take)
    hbm_states = some(12)
    grads, deltas, scalars = some(4), some(4), next(take)
    states, state_sems = some(12), next(take)
    misc_sum, bits_in, bits_sem = some(3)
    sums, arrived, sum_sems = some(3)
    mine, other, delta_sems = some(4), some(4), next(take)
    if natural:
        misc_rows, d_misc = some(2)
    greetings, rounds = sum_rounds(at)
    devices, more = scatter_greetings(at)
    all_here = greet(devices + greetings, more)

    tiny = pltpu.make_async_remote_copy(
        src_ref=bits,
        dst_ref=bits_in,
        send_sem=bits_sem.at[0],
        recv_sem=bits_sem.at[1],
        device_id=at.sibling(),
        device_id_type=MESH,
    )
    attn_views = halves_of(grads[1], 0, 2 * D, natural)
    attn_outs = list(zip(*(column_parts(view, 2) for view in attn_views)))
    streams = []
    for source, out in list(zip(column_parts(d_attn, 2), attn_outs)) + [(d_misc, halves_out(misc_sum))]:
        part = some(SCATTER_REFS)
        streams.append(ScatterStream(at, source, out, *part[:5], part[5:]))
    one, two, small = streams
    all_here()
    one.start()
    two.start()
    tiny.start()
    if natural:
        pack_misc(at, d_tables, row_sums, misc_rows, d_misc, grads[3].shape[1])
    small.start()
    loads = [
        pltpu.make_async_copy(src, dst, state_sems.at[i])
        for i, (src, dst) in enumerate(zip(hbm_states, states))
    ]
    for load in loads:
        load.start()
    one.stage_first()
    views = attn_views
    for (which, layer), source in zip(SUMMED, ready):
        targets = halves_of(grads[which], layer, 2 * D if which == 1 else FF, natural)
        views += targets
        for half in range(2):
            targets[half][...] = source[half]
    two.stage_first()
    small.stage_first()
    one.stage_second()
    two.stage_second()
    one.stage_home()
    small.stage_second()
    two.stage_home()
    small.stage_home()
    for stream in streams:
        stream.finish()
    tiny.wait()

    table_rows, columns = grads[0].shape[1], grads[3].shape[1]
    for layer in range(2):
        grads[0][layer] = misc_sum[layer, :table_rows, :D]
    grads[3][...] = misc_sum[0, :VEC, D : D + columns]
    squared = jnp.zeros((1, 1), F32)
    for ref in halves_out(misc_sum) + views:
        value = ref[...]
        value = jnp.sum(value * value, 0, keepdims=True)
        squared = squared + jnp.sum(value, 1, keepdims=True)
    row = lax.broadcasted_iota(jnp.int32, (8, 128), 0)
    lost = jnp.where(at.c == at.group, bits[...] + bits_in[...], 0.0)
    total = jnp.where(row == 0, squared, jnp.where(row == 1, lost, 0.0))
    for peers in rounds:
        copies = []
        for k, partner in peers:
            sums[k] = total
            copies.append(
                pltpu.make_async_remote_copy(
                    src_ref=sums.at[k],
                    dst_ref=arrived.at[k],
                    send_sem=sum_sems.at[0, k],
                    recv_sem=sum_sems.at[1, k],
                    device_id=partner,
                    device_id_type=MESH,
                )
            )
        for copy in copies:
            copy.start()
        for copy in copies:
            copy.wait()
        total = ordered_sum(at, peers, total, arrived)
    norm = jnp.sqrt(total[0:1, 0:1])
    factor = jnp.minimum(1.0, CLIP_AT / (norm + 1e-06))
    scalars[...] = jnp.where(row == 0, norm, jnp.where(row == 2, factor, total))
    for load in loads:
        load.wait()

    copies = [
        pltpu.make_async_remote_copy(
            src_ref=mine[which],
            dst_ref=other[which],
            send_sem=delta_sems.at[0, which],
            recv_sem=delta_sems.at[1, which],
            device_id=at.sibling(),
            device_id_type=MESH,
        )
        for which in range(4)
    ]
    order = (2, 1, 0, 3)
    for which in order:
        refs_of = [states[which], states[4 + which], states[8 + which], grads[which], mine[which]]
        if which in (1, 2):
            width = 2 * D if which == 1 else FF
            views = [[ref.at[l] for ref in refs_of] for l in range(2)]
            if natural:
                views = [
                    [ref.at[l, :, h * width : (h + 1) * width] for ref in refs_of]
                    for l in range(2)
                    for h in range(2)
                ]
        else:
            views = [refs_of]
        for weight, moment, square, gradient, target in views:
            _, _, delta = adam_update(
                weight[...],
                moment[...],
                square[...],
                gradient[...] * factor,
                DECAYS[which],
                RATES[which],
            )
            target[...] = delta.astype(target.dtype)
        copies[which].start()
    for which in order:
        copies[which].wait()
        deltas[which][...] = (mine[which][...].astype(F32) + other[which][...].astype(F32)) * 0.5


def reduce_all(small, d_attn, ready, bits, states, wide, narrow, natural, collective_id):
    vm = pl.BlockSpec(memory_space=pltpu.VMEM)
    anywhere = pl.BlockSpec(memory_space=pl.ANY)
    like = [jax.ShapeDtypeStruct(x.shape, F32) for x in states[:4]]
    kinds = [BF if x.shape[-2] % 16 == 0 else F32 for x in states[:4]]
    exchanged = [pltpu.VMEM(x.shape, kind) for x, kind in zip(states[:4], kinds)]
    dma = pltpu.SemaphoreType.DMA
    stages = sum_stages(wide, narrow)
    misc = (MISC_ROWS, MISC_COLS)
    scratch = [pltpu.VMEM(x.shape, F32) for x in states] + [dma((12,))]
    scratch += [pltpu.VMEM((2,) + misc, F32), pltpu.VMEM(bits.shape, F32), dma((2,))]
    scratch += [pltpu.VMEM((stages, 8, 128), F32)] * 2 + [dma((2, stages))]
    scratch += exchanged + exchanged + [dma((2, 4))]
    if natural:
        scratch += [pltpu.VMEM((24, D), F32), pltpu.VMEM((2, wide, narrow) + misc, BF)]
    for form in (half_width(d_attn), half_width(d_attn), misc):
        scratch += scatter_scratch(wide, narrow, form)
    return pl.pallas_call(
        functools.partial(reduce_kernel, wide, narrow, natural),
        in_specs=[vm if natural else anywhere] * len(small)
        + [anywhere]
        + [vm] * 4
        + [anywhere] * 12,
        out_specs=[vm] * 9,
        out_shape=like + like + [jax.ShapeDtypeStruct((8, 128), F32)],
        scratch_shapes=scratch,
        compiler_params=params(VMEM_MIB, collective_id=collective_id, has_side_effects=True),
        name="reduce_all",
    )(*small, d_attn, *ready, bits, *states)


def update_kernel(scalars, totals, counted, *refs):
    grads, deltas, weights, moments, squares, outers, averages = (
        refs[4 * k : 4 * k + 4] for k in range(7)
    )
    new_m, new_s, new_w, new_o, new_a = (refs[28 + 4 * k : 32 + 4 * k] for k in range(5))
    factor = scalars[2:3, 0:1]
    loss, count, norm = refs[48:]
    loss[0] = totals[1, 0]
    count[0] = counted[0, 0]
    norm[0] = totals[0, 0]
    for which in range(4):
        moment, square, _ = adam_update(
            weights[which][...],
            moments[which][...],
            squares[which][...],
            grads[which][...] * factor,
            DECAYS[which],
            RATES[which],
        )
        put_moment(new_m[which], moment)
        put_moment(new_s[which], square)
        delta = deltas[which][...]
        outer = OUTER_MOM * outers[which][...] + delta
        weight = weights[which][...] + OUTER_RATE * (delta + OUTER_MOM * outer)
        new_o[which][...] = outer
        new_w[which][...] = weight
        new_a[which][...] = EVAL_KEEP * averages[which][...] + (1.0 - EVAL_KEEP) * weight


def put_moment(ref, value):
    if len(ref.shape) == 3 and value.ndim == 2:
        for r in range(value.shape[0]):
            ref[r] = value[r : r + 1]
    else:
        ref[...] = value


def update(totals, counted, grads, deltas, arrays):
    weights = arrays[:4]
    rows = weights[1].shape[1]

    def half(width):
        return pl.BlockSpec((1, rows, width // 2), lambda i: (i // 2, 0, i % 2))

    specs = [
        pl.BlockSpec((1,) + weights[0].shape[1:], lambda i: (i // 2, 0, 0)),
        half(4 * D),
        half(2 * FF),
        pl.BlockSpec(weights[3].shape, lambda i: (0, 0)),
    ]
    like = [jax.ShapeDtypeStruct(x.shape, F32) for x in weights]
    vec_rows, cols = weights[3].shape
    lined = (vec_rows, 1, cols)
    own_specs = specs[:3] + [pl.BlockSpec(lined, lambda i: (0, 0, 0))]
    own_like = like[:3] + [jax.ShapeDtypeStruct(lined, F32)]
    scalar = pl.BlockSpec(memory_space=pltpu.SMEM)
    *new, loss, count, norm = pl.pallas_call(
        update_kernel,
        grid=(4,),
        in_specs=[pl.BlockSpec((8, 128), lambda i: (0, 0)), scalar, scalar] + specs * 7,
        out_specs=own_specs * 2 + specs * 3 + [scalar] * 3,
        out_shape=own_like * 2 + like * 3 + [jax.ShapeDtypeStruct((1,), F32)] * 3,
        compiler_params=params(VMEM_MIB),
        name="update",
    )(totals, totals, counted, *grads, *deltas, *arrays)
    for k in (3, 7):
        new[k] = new[k].transpose(1, 0, 2)
    new = [x[None] if k < 8 and k % 4 != 3 else x for k, x in enumerate(new)]
    return (loss, count, norm, *new)


def pad_to(x, rows, cols):
    return jnp.pad(x, [(0, 0)] * (x.ndim - 2) + [(0, rows - x.shape[-2]), (0, cols - x.shape[-1])])


def per_device(wide, narrow, byte_ids, live_mask, *arrays):
    tables, attention, feed_forward, vectors = arrays[:4]
    rows, table_rows, cols = attention.shape[1], tables.shape[1], vectors.shape[1]
    seq = byte_ids.shape[1]
    long_blocks = seq // BLK
    natural = rows % 16 == 0
    place = (2, wide, narrow)

    def formed(k, x):
        if natural or k % 4 not in (1, 2):
            return x
        half = x.shape[-1] // 2
        return x.reshape(2, rows, 2, half).swapaxes(1, 2).reshape((2, 2) + slab_form(rows, half))

    def unformed(k, x):
        if natural or k % 4 not in (1, 2):
            return x
        return x.reshape(2, 2, rows, -1).swapaxes(1, 2).reshape(arrays[k].shape)

    def slabs_of(d):
        return d.reshape(place + slab_form(rows, d.shape[-1]))

    arrays = [x[0] if 4 <= k < 12 else x for k, x in enumerate(arrays)]
    states = [formed(k, x) for k, x in enumerate(arrays[:12])]
    attn_low, feed_low, attn, misc, aux, scalars, *more = prepare(
        byte_ids, live_mask, tables, states[1], states[2], vectors, wide, narrow, natural
    )
    if natural:
        full_tables, vec = more
    else:
        full_tables = misc[:, :, :, :table_rows, :D].reshape(2, V, D)
        side = misc[0, :, :, :VEC, D : D + cols].astype(F32).reshape(-1, VEC, cols)
        vec = pad_to(side.transpose(1, 0, 2).reshape(VEC, D), 24, D)
    attn = attn.reshape(2, D, 2 * D)
    x1, middle, q, k, v, ot, lse, act, slope, feed, short_attn, short_feed = full_forward(
        aux, full_tables, attn, attn_low, feed_low, vec, long_blocks, wide, narrow, natural
    )
    feed = feed.reshape(2, D, FF)
    d_x1, d_short_attn, d_short_feed, d_head, short_rows, bits = middle_stage(
        x1,
        aux,
        full_tables,
        short_attn.reshape(2, D, 2 * D),
        short_feed.reshape(2, D, FF),
        vec,
        scalars,
        seq,
    )
    d_middle, d_feed, feed_rows, sum_short_attn = feed_back(
        d_x1, act, slope, middle, feed, vec, slabs_of(d_short_attn), wide, narrow
    )
    d_attn, d_embed, attn_rows, sum_short_feed, sum_feed = attention_back(
        d_middle,
        aux,
        ot,
        lse,
        q,
        k,
        v,
        full_tables,
        attn,
        vec,
        slabs_of(d_short_feed),
        slabs_of(d_feed),
        long_blocks,
        wide,
        narrow,
    )
    if natural:
        small = (d_embed, d_head, short_rows, feed_rows, attn_rows)
    else:
        d_vec = jnp.concatenate(
            [
                short_rows[0:2],
                attn_rows[0:2],
                feed_rows[0:3],
                short_rows[2:7],
                feed_rows[3 : 3 + CHUNKS],
                short_rows[7 : 7 + CHUNKS],
                attn_rows[2:3] + short_rows[11:12],
            ],
            0,
        )
        side = pad_to(d_vec.reshape(VEC, -1, cols).transpose(1, 0, 2), MISC_ROWS, SIDE)
        halves = [
            jnp.concatenate([pad_to(d.reshape(-1, table_rows, D), MISC_ROWS, D), extra], -1)
            for d, extra in ((d_embed, side), (d_head, jnp.zeros_like(side)))
        ]
        small = (jnp.stack(halves).astype(BF).reshape(place + (MISC_ROWS, MISC_COLS)),)
    *sums, totals = reduce_all(
        small,
        slabs_of(d_attn),
        (sum_short_attn, sum_short_feed, sum_feed),
        bits,
        states,
        wide,
        narrow,
        natural,
        2,
    )
    grads = [unformed(k, x) for k, x in enumerate(sums[:4])]
    deltas = [unformed(k, x) for k, x in enumerate(sums[4:])]
    return update(totals, scalars, grads, deltas, arrays)


def solution(mesh):
    rows = P(("rep", "wide", "narrow"), None)
    split = (
        P(None, ("wide", "narrow"), None),
        P(None, ("wide", "narrow"), None),
        P(None, ("wide", "narrow"), None),
        P(None, ("wide", "narrow")),
    )
    own = tuple(P("rep", *spec) for spec in split)
    return jax.shard_map(
        functools.partial(per_device, mesh.shape["wide"], mesh.shape["narrow"]),
        mesh=mesh,
        in_specs=(rows, rows) + split + own + own + split + split,
        out_specs=(P("rep"),) * 3 + own + own + split * 3,
        check_vma=False,
    )
```
